32 devices in a mesh: groups: 2 (over y), cells: 4 (over x, core), sharers: 4 (over z).
Axes of the slice: x: 2, y: 2, z: 4, core: 2. Of those that a mesh axis runs over, the one named last changes fastest.
Arguments:
- velocities: float32 [8, 3, 2048], P(('groups', 'cells'), None, 'sharers'), parts along dimension 0, may hold values from -12 to 12
- weights: float32 [8, 2048], P(('groups', 'cells'), 'sharers'), parts along dimension 0, may hold values from 0.5 to 2
- counts: int32 [8], P(('groups', 'cells')), parts along dimension 0, may hold values from 1024 to 2048, as said below
Outputs:
- new_velocities: float32 [8, 3, 2048], P(('groups', 'cells'), None, 'sharers'), parts along dimension 0
- scores: float32 [8, 3, 2048], P(('groups', 'cells'), None, 'sharers'), parts along dimension 0
The draws below stay inside these ranges and needn't reach their ends.
There are 2 independent parts, one for each index of `groups`. The reference program is written for one: setup_inputs(seed, part) draws one part's arguments, and reference() takes and returns one part's arrays. A program takes and returns all parts, laid end to end along the dimension named above; each array names one. Nothing has to cross between parts.
Inputs may be any that keep to these rules, and one draw needn't show every extreme that they name: Each count is a multiple of 128; the slots below counts[c] hold cell c's particles and the others are padding; in every draw some cell has all 2048 slots live.
All inputs are finite; a program needn't handle non-finite values.
Results may differ from the reference program's by a relative error of at most 0.0003.
Values sent between devices are 32-bit elements; how exact they have to be, the bound alone decides.
No kernel may reach another device: no remote copies, remote signals or barrier semaphores. Data moves between devices by JAX's collectives and lax.ppermute only.
A program may use at most 64 MiB of HBM per device.

```python
import math
import jax
import jax.numpy as jnp
from jax import lax

NP_DEV = 512
CAP = 2048
GROUP_CELLS = 4


def draw_velocities(key, part):
    key = jax.random.fold_in(key, 11)
    initial_key, second_key, third_key = jax.random.split(key, 3)
    warmup_factor = 3.0 ** (jnp.arange(GROUP_CELLS, dtype=jnp.float32) / (GROUP_CELLS - 1))
    thermal_spread = warmup_factor * jax.random.uniform(initial_key, (GROUP_CELLS,), minval=0.85, maxval=1.15)
    average_drift = 0.5 * jax.random.normal(second_key, (GROUP_CELLS, 3, 1))
    standard_sample = jax.random.normal(third_key, (GROUP_CELLS, 3, CAP))
    return jnp.clip(average_drift + jnp.sqrt(thermal_spread)[:, None, None] * standard_sample, -12.0, 12.0)


def draw_counts(key, part):
    key = jax.random.fold_in(key, 23)
    initial_key, second_key = jax.random.split(key)
    tiles = jax.random.randint(initial_key, (GROUP_CELLS,), CAP // 256, CAP // 128 + 1)
    full_cell = jax.random.randint(second_key, (), 0, GROUP_CELLS)
    tiles = jnp.where(jnp.arange(GROUP_CELLS) == full_cell, CAP // 128, tiles)
    return (128 * tiles).astype(jnp.int32)


def block_levels(own_key, dims, shards, low, high):
    factor_of = 1.0
    for axis_at, blocks in shards:
        draws = jax.random.uniform(jax.random.fold_in(jax.random.fold_in(own_key, 6), axis_at), (blocks,), jnp.float32, low / len(shards), high / len(shards))
        factor_of = factor_of * jnp.repeat(jnp.exp(draws), dims[axis_at] // blocks).reshape((-1,) + (1,) * (len(dims) - 1 - axis_at))
    return factor_of


def setup_inputs(seed: int = 0, part: int = 0) -> dict:
    arg_keys = jax.random.split(jax.random.key(seed), 4)
    own_keys = jax.random.split(jax.random.fold_in(arg_keys[3], part), 4)
    return {
        "velocities": draw_velocities(jax.random.fold_in(jax.random.fold_in(arg_keys[3], part), 71), part),
        "weights": jnp.clip(jnp.exp(math.log(2.0) - 1.3862944 * jax.random.uniform(own_keys[1], (GROUP_CELLS, CAP), jnp.float32) ** block_levels(own_keys[1], (GROUP_CELLS, CAP), ((0, 4), (1, 4)), -0.2, 0.2)), 0.5, 2.0),
        "counts": draw_counts(jax.random.fold_in(jax.random.fold_in(arg_keys[3], part), 71), part),
    }


EPS = 0.35
NORM = (2.0 * math.pi * EPS * EPS) ** (-1.5)

def density_block(query, key_vel, key_weight):
    offset = query[:, :, None] - key_vel[:, None, :]
    square_dist = lax.optimization_barrier(jnp.sum(offset * offset, axis=0))
    kernel = NORM * jnp.exp(-square_dist / (2.0 * EPS * EPS)) * key_weight[None, :]
    return (lax.optimization_barrier(jnp.sum(kernel, axis=1)), lax.optimization_barrier(jnp.sum(kernel[None] * offset, axis=2)))

def drift_block(query, query_score, key_vel, key_score, key_weight):
    offset = query[:, :, None] - key_vel[:, None, :]
    score_gap = query_score[:, :, None] - key_score[:, None, :]
    square_dist = lax.optimization_barrier(jnp.sum(offset * offset, axis=0))
    distance = jnp.sqrt(square_dist)
    along = lax.optimization_barrier(jnp.sum(offset * score_gap, axis=0))
    contrib = distance[None] * (square_dist[None] * score_gap - offset * along[None]) * key_weight[None, None, :]
    return lax.optimization_barrier(jnp.sum(contrib, axis=2))

def one_cell(inputs):
    velocity, weight_row, filled = inputs
    slot_index = jnp.arange(CAP, dtype=jnp.int32)
    is_live = slot_index < filled
    key_weight = jnp.where(is_live, weight_row, 0.0)
    block_count = CAP // NP_DEV
    query_blocks = velocity.reshape(3, block_count, NP_DEV).transpose(1, 0, 2)
    density_sum, pull_sum = lax.map(lambda query: density_block(query, velocity, key_weight), query_blocks)
    density_sum = density_sum.reshape(CAP)
    pull_sum = pull_sum.transpose(1, 0, 2).reshape(3, CAP)
    clamped_density = jnp.where(is_live, density_sum, 1.0)
    scores_cell = jnp.where(is_live[None], -pull_sum / (EPS * EPS * clamped_density[None]), 0.0)
    score_blocks = scores_cell.reshape(3, block_count, NP_DEV).transpose(1, 0, 2)
    drift_sum = lax.map(lambda pair: drift_block(pair[0], pair[1], velocity, scores_cell, key_weight), (query_blocks, score_blocks))
    drift_sum = drift_sum.transpose(1, 0, 2).reshape(3, CAP)
    drift_cell = jnp.where(is_live[None], -drift_sum / CAP, 0.0)
    return (scores_cell, drift_cell)

def reference(velocities, weights, counts):
    scores, drifts = lax.map(one_cell, (velocities, weights, counts))
    speeds = jnp.sqrt(lax.optimization_barrier(jnp.sum(drifts * drifts, axis=1)))
    largest = jnp.max(speeds)
    time_step = 0.5 / (largest + 1e-06)
    return (velocities + time_step * drifts, scores)
```

```python
import math

import jax
import jax.numpy as jnp
from jax import lax
from jax.sharding import PartitionSpec as P

EPS = 0.35
NORM = (2.0 * math.pi * EPS * EPS) ** (-1.5)


def density_block(query, key_vel, key_weight):
    offset = query[:, :, None] - key_vel[:, None, :]
    square_dist = jnp.sum(offset * offset, axis=0)
    kernel = NORM * jnp.exp(-square_dist / (2.0 * EPS * EPS)) * key_weight[None, :]
    return (jnp.sum(kernel, axis=1), jnp.sum(kernel[None] * offset, axis=2))


def drift_block(query, query_score, key_vel, key_score, key_weight):
    offset = query[:, :, None] - key_vel[:, None, :]
    score_gap = query_score[:, :, None] - key_score[:, None, :]
    square_dist = jnp.sum(offset * offset, axis=0)
    distance = jnp.sqrt(square_dist)
    along = jnp.sum(offset * score_gap, axis=0)
    contrib = (
        distance[None]
        * (square_dist[None] * score_gap - offset * along[None])
        * key_weight[None, None, :]
    )
    return jnp.sum(contrib, axis=2)


def exchange(value, axis):
    size = lax.axis_size(axis)
    blocks = [value]
    for shift in range(1, size):
        pairs = [(i, (i + shift) % size) for i in range(size)]
        blocks.append(lax.ppermute(value, axis, pairs))
    return blocks


def local(velocities, weights, counts):
    velocity = velocities[0]
    filled = counts[0]
    local_rows = velocity.shape[1]
    total_slots = local_rows * lax.axis_size("sharers")
    shifted_rows = lax.axis_index("sharers") * local_rows
    slot_index = jnp.arange(local_rows, dtype=jnp.int32)
    is_live = shifted_rows + slot_index < filled
    live_weight = jnp.where(is_live, weights[0], 0.0)

    density_sum = jnp.zeros((local_rows,), jnp.float32)
    pull_sum = jnp.zeros((3, local_rows), jnp.float32)
    key_blocks = exchange(jnp.concatenate([velocity, live_weight[None]], axis=0), "sharers")

    def density_step(totals, key_block):
        density_part, pull_part = density_block(velocity, key_block[:3], key_block[3])
        return (totals[0] + density_part, totals[1] + pull_part), None

    (density_sum, pull_sum), _ = lax.scan(
        density_step, (density_sum, pull_sum), jnp.stack(key_blocks)
    )
    clamped_density = jnp.where(is_live, density_sum, 1.0)
    scores_here = jnp.where(is_live[None], -pull_sum / (EPS * EPS * clamped_density[None]), 0.0)

    drift_sum = jnp.zeros((3, local_rows), jnp.float32)
    score_blocks = exchange(scores_here, "sharers")

    def drift_step(total, blocks):
        key_block, key_score = blocks
        part = drift_block(velocity, scores_here, key_block[:3], key_score, key_block[3])
        return total + part, None

    drift_sum, _ = lax.scan(
        drift_step, drift_sum, (jnp.stack(key_blocks), jnp.stack(score_blocks))
    )
    drift_local = jnp.where(is_live[None], -drift_sum / total_slots, 0.0)
    speeds = jnp.sqrt(jnp.sum(drift_local * drift_local, axis=0))
    largest = jnp.max(speeds).reshape(1, 1)
    for axis in ("sharers", "cells"):
        for other in exchange(largest, axis)[1:]:
            largest = jnp.maximum(largest, other)
    time_step = 0.5 / (largest + 1e-06)
    return ((velocity + time_step * drift_local)[None], scores_here[None])


def solution(mesh):
    in_specs = (
        P(("groups", "cells"), None, "sharers"),
        P(("groups", "cells"), "sharers"),
        P(("groups", "cells")),
    )
    out_specs = (P(("groups", "cells"), None, "sharers"), P(("groups", "cells"), None, "sharers"))
    return jax.shard_map(local, mesh=mesh, in_specs=in_specs, out_specs=out_specs, check_vma=False)
```

```python
import math

import jax
import jax.numpy as jnp
from jax import lax
from jax.sharding import PartitionSpec as P

EPS = 0.35
NORM = (2.0 * math.pi * EPS * EPS) ** (-1.5)


def density_block(query, key_vel, key_weight):
    offset = query[:, :, None] - key_vel[:, None, :]
    square_dist = jnp.sum(offset * offset, axis=0)
    kernel = NORM * jnp.exp(-square_dist / (2.0 * EPS * EPS)) * key_weight[None, :]
    return (jnp.sum(kernel, axis=1), jnp.sum(kernel[None] * offset, axis=2))


def drift_block(query, query_score, key_vel, key_score, key_weight):
    offset = query[:, :, None] - key_vel[:, None, :]
    score_gap = query_score[:, :, None] - key_score[:, None, :]
    square_dist = jnp.sum(offset * offset, axis=0)
    distance = jnp.sqrt(square_dist)
    along = jnp.sum(offset * score_gap, axis=0)
    contrib = (
        distance[None]
        * (square_dist[None] * score_gap - offset * along[None])
        * key_weight[None, None, :]
    )
    return jnp.sum(contrib, axis=2)


def exchange(value, axis):
    copies = jnp.broadcast_to(value[None], (lax.axis_size(axis),) + value.shape)
    return lax.all_to_all(copies, axis, 0, 0, tiled=True)


def local(velocities, weights, counts):
    velocity = velocities[0]
    filled = counts[0]
    local_rows = velocity.shape[1]
    total_slots = local_rows * lax.axis_size("sharers")
    shifted_rows = lax.axis_index("sharers") * local_rows
    slot_index = jnp.arange(local_rows, dtype=jnp.int32)
    is_live = shifted_rows + slot_index < filled
    live_weight = jnp.where(is_live, weights[0], 0.0)

    density_sum = jnp.zeros((local_rows,), jnp.float32)
    pull_sum = jnp.zeros((3, local_rows), jnp.float32)
    key_blocks = exchange(jnp.concatenate([velocity, live_weight[None]], axis=0), "sharers")

    def density_step(totals, key_block):
        density_part, pull_part = density_block(velocity, key_block[:3], key_block[3])
        return (totals[0] + density_part, totals[1] + pull_part), None

    (density_sum, pull_sum), _ = lax.scan(
        density_step, (density_sum, pull_sum), key_blocks
    )
    clamped_density = jnp.where(is_live, density_sum, 1.0)
    scores_here = jnp.where(is_live[None], -pull_sum / (EPS * EPS * clamped_density[None]), 0.0)

    drift_sum = jnp.zeros((3, local_rows), jnp.float32)
    score_blocks = exchange(scores_here, "sharers")

    def drift_step(total, blocks):
        key_block, key_score = blocks
        part = drift_block(velocity, scores_here, key_block[:3], key_score, key_block[3])
        return total + part, None

    drift_sum, _ = lax.scan(
        drift_step, drift_sum, (key_blocks, score_blocks)
    )
    drift_local = jnp.where(is_live[None], -drift_sum / total_slots, 0.0)
    speeds = jnp.sqrt(jnp.sum(drift_local * drift_local, axis=0))
    largest = jnp.max(exchange(jnp.max(speeds).reshape(1), ("cells", "sharers")))
    time_step = 0.5 / (largest + 1e-06)
    return ((velocity + time_step * drift_local)[None], scores_here[None])


def solution(mesh):
    in_specs = (
        P(("groups", "cells"), None, "sharers"),
        P(("groups", "cells"), "sharers"),
        P(("groups", "cells")),
    )
    out_specs = (P(("groups", "cells"), None, "sharers"), P(("groups", "cells"), None, "sharers"))
    return jax.shard_map(local, mesh=mesh, in_specs=in_specs, out_specs=out_specs, check_vma=False)
```

```python
import functools
import math

import jax
import jax.numpy as jnp
from jax import lax
from jax.experimental import pallas as pl
from jax.experimental.pallas import tpu as pltpu
from jax.sharding import PartitionSpec as P

EPS = 0.35
SCALE = math.sqrt(math.log2(math.e) / (2.0 * EPS * EPS))
GRID = 4.0
TINY = 1e-30
CHUNK = 256
FEATURES = 48
bf16, f32 = jnp.bfloat16, jnp.float32


def round_bf16(value):
    return value.astype(bf16).astype(f32)


def pieces(value, count):
    parts = []
    for _ in range(count):
        part = round_bf16(value)
        parts.append(part)
        value = value - part
    return parts


def padded(rows, height):
    filled = sum(row.shape[0] for row in rows)
    width = rows[0].shape[1]
    if filled < height:
        rows = rows + [jnp.zeros((height - filled, width), f32)]
    return jnp.concatenate(rows, axis=0)


def row_sum(value):
    return value[0:1] + value[1:2] + value[2:3]


def grid_parts(place):
    coarse = jnp.floor(place * GRID + 0.5) * (1.0 / GRID)
    return [coarse] + pieces(place - coarse, 2)


def distance_features(place):
    coarse, fine, rest = grid_parts(place)
    minor = place - coarse
    ones = jnp.ones_like(place)
    coarse_norm = jnp.concatenate(pieces(-row_sum(coarse * coarse), 3), axis=0)
    minor_norm = jnp.concatenate(
        pieces(-row_sum(minor * (2.0 * coarse + minor)), 3), axis=0
    )
    key_rows = [coarse, ones, coarse_norm, coarse, coarse, fine, rest, ones, minor_norm]
    key_rows += [fine, fine, rest, rest]
    query_rows = [coarse, coarse_norm, ones, fine, rest, coarse, coarse, minor_norm, ones]
    query_rows += [fine, rest, fine, rest]
    doubled = (0, 3, 4, 5, 6, 9, 10, 11, 12)
    query_rows = [row * 2.0 if i in doubled else row for i, row in enumerate(query_rows)]
    return padded(key_rows, FEATURES), padded(query_rows, FEATURES)


def along_key_features(place, score):
    coarse, fine, rest = grid_parts(place)
    first, second, third = pieces(score, 3)
    ones = jnp.ones_like(place)
    dot = jnp.concatenate(pieces(row_sum(place * score), 3), axis=0)
    rows = [ones, dot, -first, -second, -third, -first, -second, -first]
    rows += [coarse, coarse, coarse, fine, fine, rest]
    return padded(rows, FEATURES)


def along_query_features(place, score):
    coarse, fine, rest = grid_parts(place)
    first, second, third = pieces(score, 3)
    ones = jnp.ones_like(place)
    dot = jnp.concatenate(pieces(row_sum(place * score), 3), axis=0)
    rows = [dot, ones, coarse, coarse, coarse, fine, fine, rest]
    rows += [-first, -second, -third, -first, -second, -first]
    return padded(rows, FEATURES)


def weighted_rows(weight, value):
    whole = jnp.concatenate([weight, weight * value], axis=0)
    return padded(pieces(whole, 3), 16).astype(bf16)


def product(left, right):
    return jnp.dot(left, right, preferred_element_type=f32)


def split_product(left, matrix):
    upper = matrix.astype(bf16)
    lower = (matrix - upper.astype(f32)).astype(bf16)
    return product(left, upper) + product(left, lower)


def joined(total):
    return total[0:4] + total[4:8] + total[8:12]


def sweep_kernel(blocks, scores_out, drift_out, speed_out, place_ref, weight_ref,
                 key_ref, query_ref, own_ref, moment_ref, score_ref, along_ref, flux_ref):
    count, _, width = blocks.shape
    total_slots = count * width
    chunks = total_slots // CHUNK

    def columns(block):
        return pl.ds(pl.multiple_of(block * width, width), width)

    def build(block, carry):
        place = blocks[block, 0:3] * SCALE
        weight = blocks[block, 3:4]
        key, query = distance_features(place)
        place_ref[:, columns(block)] = place
        weight_ref[:, columns(block)] = weight
        key_ref[columns(block), :] = key.T.astype(bf16)
        query_ref[:, columns(block)] = query.astype(bf16)
        moment_ref[:, columns(block)] = weighted_rows(weight, place)
        return carry

    lax.fori_loop(0, count, build, 0, unroll=count <= 4)
    own_ref[...] = -query_ref[:, 0:width]

    def density(block, carry):
        query = query_ref[:, columns(block)]

        def add(chunk, total):
            keys = pl.ds(pl.multiple_of(chunk * CHUNK, CHUNK), CHUNK)
            blob = jnp.exp2(product(key_ref[keys, :], query))
            return total + split_product(moment_ref[:, keys], blob)

        total = lax.fori_loop(0, chunks, add, jnp.zeros((16, width), f32), unroll=8)
        sums = joined(total)
        place = place_ref[:, columns(block)]
        weight = weight_ref[:, columns(block)]
        live = weight > 0.0
        clamped = jnp.where(live, sums[0:1], 1.0)
        pull = place * sums[0:1] - sums[1:4]
        score = jnp.where(live, -pull / (SCALE * EPS * EPS * clamped), 0.0)
        score_ref[:, columns(block)] = score
        along_ref[columns(block), :] = along_key_features(place, score).T.astype(bf16)
        flux_ref[:, columns(block)] = weighted_rows(weight, score)
        return carry

    lax.fori_loop(0, count, density, 0)

    place = place_ref[:, 0:width]
    score = score_ref[:, 0:width]
    own = own_ref[...]
    own_along = along_query_features(place, score).astype(bf16)

    def add_drift(chunk, totals):
        keys = pl.ds(pl.multiple_of(chunk * CHUNK, CHUNK), CHUNK)
        square = jnp.maximum(product(key_ref[keys, :], own), TINY)
        along = product(along_ref[keys, :], own_along)
        distance = square * lax.rsqrt(square)
        return (
            totals[0] + split_product(flux_ref[:, keys], square * distance),
            totals[1] + split_product(moment_ref[:, keys], along * distance),
        )

    zero = jnp.zeros((16, width), f32)
    cubes, linear = lax.fori_loop(0, chunks, add_drift, (zero, zero), unroll=8)
    cubes, linear = joined(cubes), joined(linear)
    drift = score * cubes[0:1] - cubes[1:4] - place * linear[0:1] + linear[1:4]
    live = weight_ref[:, 0:width] > 0.0
    drift = jnp.where(live, drift * (-1.0 / (SCALE * SCALE * SCALE * total_slots)), 0.0)
    largest = jnp.max(row_sum(drift * drift), axis=1, keepdims=True)
    speed_out[...] = jnp.broadcast_to(jnp.sqrt(largest), speed_out.shape)
    for part in range(width // 128):
        lanes = slice(part * 128, part * 128 + 128)
        for axis in range(3):
            scores_out[axis, part : part + 1, :] = score[axis : axis + 1, lanes]
            drift_out[axis, part : part + 1, :] = drift[axis : axis + 1, lanes]


def sweep(blocks):
    count, _, width = blocks.shape
    slots = count * width
    parts = jax.ShapeDtypeStruct((3, width // 128, 128), f32)
    whole = pl.BlockSpec(memory_space=pltpu.VMEM)
    return pl.pallas_call(
        sweep_kernel,
        out_shape=(parts, parts, jax.ShapeDtypeStruct((8, 128), f32)),
        in_specs=[whole],
        out_specs=(whole, whole, whole),
        scratch_shapes=[
            pltpu.VMEM((3, slots), f32),
            pltpu.VMEM((1, slots), f32),
            pltpu.VMEM((slots, FEATURES), bf16),
            pltpu.VMEM((FEATURES, slots), bf16),
            pltpu.VMEM((FEATURES, width), bf16),
            pltpu.VMEM((16, slots), bf16),
            pltpu.VMEM((3, slots), f32),
            pltpu.VMEM((slots, FEATURES), bf16),
            pltpu.VMEM((16, slots), bf16),
        ],
        compiler_params=pltpu.CompilerParams(vmem_limit_bytes=48 * 1024 * 1024),
        name="sweep",
    )(blocks)


def swapped(value, axis, step):
    pairs = [(i, i ^ step) for i in range(lax.axis_size(axis))]
    return lax.ppermute(value, axis, pairs)


def steps(axis):
    step = 1
    while step < lax.axis_size(axis):
        yield step
        step *= 2


def local(velocities, weights, counts):
    velocity = velocities[0]
    width = velocity.shape[1]
    slot = lax.axis_index("sharers") * width + jnp.arange(width, dtype=jnp.int32)
    live_weight = jnp.where(slot < counts[0], weights[0], 0.0)
    blocks = jnp.concatenate([velocity, live_weight[None]], axis=0)[None]
    for step in steps("sharers"):
        blocks = jnp.concatenate([blocks, swapped(blocks, "sharers", step)], axis=0)
    scores, drift, largest = sweep(blocks)
    for axis in ("cells", "sharers"):
        for step in steps(axis):
            largest = jnp.maximum(largest, swapped(largest, axis, step))
    time_step = 0.5 / (largest[0:1, :] + 1e-06)
    moved = velocity.reshape(drift.shape) + time_step[None] * drift
    return moved.reshape(velocities.shape), scores.reshape(velocities.shape)


def solution(mesh):
    in_specs = (
        P(("groups", "cells"), None, "sharers"),
        P(("groups", "cells"), "sharers"),
        P(("groups", "cells")),
    )
    out_specs = (P(("groups", "cells"), None, "sharers"), P(("groups", "cells"), None, "sharers"))
    return jax.shard_map(local, mesh=mesh, in_specs=in_specs, out_specs=out_specs, check_vma=False)
```

```python
import functools
import functools
import math

import jax
import jax.numpy as jnp
from jax import lax
from jax.experimental import pallas as pl
from jax.experimental.pallas import tpu as pltpu
from jax.sharding import PartitionSpec as P

EPS = 0.35
SCALE = math.sqrt(math.log2(math.e) / (2.0 * EPS * EPS))
GRID = 4.0
TINY = 1e-30
CHUNK = 256
TILE = 256
FEATURES = 48
bf16, f32 = jnp.bfloat16, jnp.float32


def round_bf16(value):
    return value.astype(bf16).astype(f32)


def pieces(value, count):
    parts = []
    for _ in range(count):
        part = round_bf16(value)
        parts.append(part)
        value = value - part
    return parts


def padded(rows, height):
    filled = sum(row.shape[0] for row in rows)
    width = rows[0].shape[1]
    if filled < height:
        rows = rows + [jnp.zeros((height - filled, width), f32)]
    return jnp.concatenate(rows, axis=0)


def row_sum(value):
    return value[0:1] + value[1:2] + value[2:3]


def grid_parts(place):
    coarse = jnp.floor(place * GRID + 0.5) * (1.0 / GRID)
    return [coarse] + pieces(place - coarse, 2)


def distance_features(place):
    coarse, fine, rest = grid_parts(place)
    minor = place - coarse
    ones = jnp.ones_like(place)
    coarse_norm = jnp.concatenate(pieces(-row_sum(coarse * coarse), 3), axis=0)
    minor_norm = jnp.concatenate(
        pieces(-row_sum(minor * (2.0 * coarse + minor)), 3), axis=0
    )
    key_rows = [coarse, ones, coarse_norm, coarse, coarse, fine, rest, ones, minor_norm]
    key_rows += [fine, fine, rest, rest]
    query_rows = [coarse, coarse_norm, ones, fine, rest, coarse, coarse, minor_norm, ones]
    query_rows += [fine, rest, fine, rest]
    doubled = (0, 3, 4, 5, 6, 9, 10, 11, 12)
    query_rows = [row * 2.0 if i in doubled else row for i, row in enumerate(query_rows)]
    return padded(key_rows, FEATURES), padded(query_rows, FEATURES)


def along_key_features(place, score):
    coarse, fine, rest = grid_parts(place)
    first, second, third = pieces(score, 3)
    ones = jnp.ones_like(place)
    dot = jnp.concatenate(pieces(row_sum(place * score), 3), axis=0)
    rows = [ones, dot, -first, -second, -third, -first, -second, -first]
    rows += [coarse, coarse, coarse, fine, fine, rest]
    return padded(rows, FEATURES)


def along_query_features(place, score):
    coarse, fine, rest = grid_parts(place)
    first, second, third = pieces(score, 3)
    ones = jnp.ones_like(place)
    dot = jnp.concatenate(pieces(row_sum(place * score), 3), axis=0)
    rows = [dot, ones, coarse, coarse, coarse, fine, fine, rest]
    rows += [-first, -second, -third, -first, -second, -first]
    return padded(rows, FEATURES)


def weighted_rows(weight, value):
    whole = jnp.concatenate([weight, weight * value], axis=0)
    return padded(pieces(whole, 3), 16).astype(bf16)


def product(left, right):
    return jnp.dot(left, right, preferred_element_type=f32)


def split_product(left, matrix):
    upper = matrix.astype(bf16)
    lower = (matrix - upper.astype(f32)).astype(bf16)
    return product(left, upper) + product(left, lower)


def joined(total):
    return total[0:4] + total[4:8] + total[8:12]


def sweep_kernel(blocks, scores_out, drift_out, speed_out, place_ref, weight_ref,
                 key_ref, query_ref, own_ref, moment_ref, score_ref, along_ref, flux_ref,
                 own_along_ref, sums_ref):
    count, _, width = blocks.shape
    total_slots = count * width
    chunks = total_slots // CHUNK

    def columns(block):
        return pl.ds(pl.multiple_of(block * width, width), width)

    def build(block, carry):
        place = blocks[block, 0:3] * SCALE
        weight = blocks[block, 3:4]
        key, query = distance_features(place)
        place_ref[:, columns(block)] = place
        weight_ref[:, columns(block)] = weight
        key_ref[columns(block), :] = key.T.astype(bf16)
        query_ref[:, columns(block)] = query.astype(bf16)
        moment_ref[:, columns(block)] = weighted_rows(weight, place)
        return carry

    lax.fori_loop(0, count, build, 0, unroll=count <= 4)
    own_ref[...] = -query_ref[:, 0:width]

    def density(tile, carry):
        here = pl.ds(pl.multiple_of(tile * TILE, TILE), TILE)
        query = query_ref[:, here]

        def add(chunk, total):
            keys = pl.ds(pl.multiple_of(chunk * CHUNK, CHUNK), CHUNK)
            blob = jnp.exp2(product(key_ref[keys, :], query))
            return total + split_product(moment_ref[:, keys], blob)

        total = lax.fori_loop(0, chunks, add, jnp.zeros((16, TILE), f32), unroll=8)
        sums = joined(total)
        place = place_ref[:, here]
        weight = weight_ref[:, here]
        live = weight > 0.0
        clamped = jnp.where(live, sums[0:1], 1.0)
        pull = place * sums[0:1] - sums[1:4]
        score = jnp.where(live, -pull / (SCALE * EPS * EPS * clamped), 0.0)
        score_ref[:, here] = score
        along_ref[here, :] = along_key_features(place, score).T.astype(bf16)
        flux_ref[:, here] = weighted_rows(weight, score)
        return carry

    lax.fori_loop(0, total_slots // TILE, density, 0)

    place = place_ref[:, 0:width]
    score = score_ref[:, 0:width]
    own_along_ref[...] = along_query_features(place, score).astype(bf16)

    def add_drift(own, own_along, chunk, totals):
        keys = pl.ds(pl.multiple_of(chunk * CHUNK, CHUNK), CHUNK)
        square = jnp.maximum(product(key_ref[keys, :], own), TINY)
        along = product(along_ref[keys, :], own_along)
        distance = square * lax.rsqrt(square)
        return (
            totals[0] + split_product(flux_ref[:, keys], square * distance),
            totals[1] + split_product(moment_ref[:, keys], along * distance),
        )

    def drift_tile(tile, carry):
        here = pl.ds(pl.multiple_of(tile * TILE, TILE), TILE)
        step = functools.partial(add_drift, own_ref[:, here], own_along_ref[:, here])
        zero = jnp.zeros((16, TILE), f32)
        cubes, linear = lax.fori_loop(0, chunks, step, (zero, zero), unroll=8)
        sums_ref[0:4, here] = joined(cubes)
        sums_ref[4:8, here] = joined(linear)
        return carry

    lax.fori_loop(0, width // TILE, drift_tile, 0)
    cubes, linear = sums_ref[0:4, :], sums_ref[4:8, :]
    drift = score * cubes[0:1] - cubes[1:4] - place * linear[0:1] + linear[1:4]
    live = weight_ref[:, 0:width] > 0.0
    drift = jnp.where(live, drift * (-1.0 / (SCALE * SCALE * SCALE * total_slots)), 0.0)
    largest = jnp.max(row_sum(drift * drift), axis=1, keepdims=True)
    speed_out[...] = jnp.broadcast_to(jnp.sqrt(largest), speed_out.shape)
    for part in range(width // 128):
        lanes = slice(part * 128, part * 128 + 128)
        for axis in range(3):
            scores_out[axis, part : part + 1, :] = score[axis : axis + 1, lanes]
            drift_out[axis, part : part + 1, :] = drift[axis : axis + 1, lanes]


def sweep(blocks):
    count, _, width = blocks.shape
    slots = count * width
    parts = jax.ShapeDtypeStruct((3, width // 128, 128), f32)
    whole = pl.BlockSpec(memory_space=pltpu.VMEM)
    return pl.pallas_call(
        sweep_kernel,
        out_shape=(parts, parts, jax.ShapeDtypeStruct((8, 128), f32)),
        in_specs=[whole],
        out_specs=(whole, whole, whole),
        scratch_shapes=[
            pltpu.VMEM((3, slots), f32),
            pltpu.VMEM((1, slots), f32),
            pltpu.VMEM((slots, FEATURES), bf16),
            pltpu.VMEM((FEATURES, slots), bf16),
            pltpu.VMEM((FEATURES, width), bf16),
            pltpu.VMEM((16, slots), bf16),
            pltpu.VMEM((3, slots), f32),
            pltpu.VMEM((slots, FEATURES), bf16),
            pltpu.VMEM((16, slots), bf16),
            pltpu.VMEM((FEATURES, width), bf16),
            pltpu.VMEM((8, width), f32),
        ],
        compiler_params=pltpu.CompilerParams(vmem_limit_bytes=48 * 1024 * 1024),
        name="sweep",
    )(blocks)


def pack_kernel(velocity, weight, place, filled, packed):
    parts = velocity.shape[1]
    lane = lax.broadcasted_iota(jnp.int32, (1, 128), 1)
    first = place[0] * (parts * 128)
    for part in range(parts):
        lanes = slice(part * 128, part * 128 + 128)
        live = first + part * 128 + lane < filled[0]
        for axis in range(3):
            packed[0, axis : axis + 1, lanes] = velocity[axis, part : part + 1, :]
        packed[0, 3:4, lanes] = jnp.where(live, weight[part : part + 1, :], 0.0)


def pack(velocities, weights, counts):
    width = weights.shape[1]
    place = lax.axis_index("sharers").astype(jnp.int32).reshape(1)
    vector = pl.BlockSpec(memory_space=pltpu.VMEM)
    scalar = pl.BlockSpec(memory_space=pltpu.SMEM)
    return pl.pallas_call(
        pack_kernel,
        out_shape=jax.ShapeDtypeStruct((1, 4, width), f32),
        in_specs=[vector, vector, scalar, scalar],
        out_specs=vector,
        name="pack",
    )(velocities.reshape(3, width // 128, 128), weights.reshape(width // 128, 128), place, counts)


def swapped(value, axis, step):
    pairs = [(i, i ^ step) for i in range(lax.axis_size(axis))]
    return lax.ppermute(value, axis, pairs)


def bits(size):
    return [1 << bit for bit in range(size.bit_length() - 1)]


def gathered(block):
    size = lax.axis_size("sharers")
    if size == 4:
        third, first, second = (swapped(block, "sharers", step) for step in (3, 1, 2))
        return jnp.concatenate([block, first, second, third], axis=0)
    for step in bits(size):
        block = jnp.concatenate([block, swapped(block, "sharers", step)], axis=0)
    return block


def group_maximum(value):
    cells, sharers = lax.axis_size("cells"), lax.axis_size("sharers")
    axes = ("cells", "sharers")
    odd = [i for i in range(cells * sharers) if (i // sharers) % 2]

    def among_odd(value, step):
        return lax.ppermute(value, axes, [(i, i ^ step) for i in odd])

    value = jnp.maximum(value, swapped(value, "cells", 1))
    for step in bits(cells)[1:]:
        value = jnp.maximum(value, among_odd(value, step * sharers))
    if sharers == 4:
        others = [among_odd(value, step) for step in (3, 1, 2)]
        for other in others:
            value = jnp.maximum(value, other)
    else:
        for step in bits(sharers):
            value = jnp.maximum(value, among_odd(value, step))
    back = lax.ppermute(value, "cells", [(i, i ^ 1) for i in range(1, cells, 2)])
    return jnp.maximum(value, back)


def local(velocities, weights, counts):
    scores, drift, largest = sweep(gathered(pack(velocities, weights, counts)))
    time_step = 0.5 / (group_maximum(largest)[0:1, :] + 1e-06)
    moved = velocities.reshape(drift.shape) + time_step[None] * drift
    return moved.reshape(velocities.shape), scores.reshape(velocities.shape)


def solution(mesh):
    in_specs = (
        P(("groups", "cells"), None, "sharers"),
        P(("groups", "cells"), "sharers"),
        P(("groups", "cells")),
    )
    out_specs = (P(("groups", "cells"), None, "sharers"), P(("groups", "cells"), None, "sharers"))
    return jax.shard_map(local, mesh=mesh, in_specs=in_specs, out_specs=out_specs, check_vma=False)
```

```python
import functools
import functools
import math

import jax
import jax.numpy as jnp
from jax import lax
from jax.experimental import pallas as pl
from jax.experimental.pallas import tpu as pltpu
from jax.sharding import PartitionSpec as P

EPS = 0.35
SCALE = math.sqrt(math.log2(math.e) / (2.0 * EPS * EPS))
GRID = 4.0
TINY = 1e-30
CHUNK = 256
TILE = 512
FEATURES = 48
bf16, f32 = jnp.bfloat16, jnp.float32


def round_bf16(value):
    return value.astype(bf16).astype(f32)


def pieces(value, count):
    parts = []
    for _ in range(count):
        part = round_bf16(value)
        parts.append(part)
        value = value - part
    return parts


def padded(rows, height):
    filled = sum(row.shape[0] for row in rows)
    width = rows[0].shape[1]
    if filled < height:
        rows = rows + [jnp.zeros((height - filled, width), f32)]
    return jnp.concatenate(rows, axis=0)


def row_sum(value):
    return value[0:1] + value[1:2] + value[2:3]


def grid_parts(place):
    coarse = jnp.floor(place * GRID + 0.5) * (1.0 / GRID)
    return [coarse] + pieces(place - coarse, 2)


def distance_features(place):
    coarse, fine, rest = grid_parts(place)
    minor = place - coarse
    ones = jnp.ones_like(place)
    coarse_norm = jnp.concatenate(pieces(-row_sum(coarse * coarse), 3), axis=0)
    minor_norm = jnp.concatenate(
        pieces(-row_sum(minor * (2.0 * coarse + minor)), 3), axis=0
    )
    key_rows = [coarse, ones, coarse_norm, coarse, coarse, fine, rest, ones, minor_norm]
    key_rows += [fine, fine, rest, rest]
    query_rows = [coarse, coarse_norm, ones, fine, rest, coarse, coarse, minor_norm, ones]
    query_rows += [fine, rest, fine, rest]
    doubled = (0, 3, 4, 5, 6, 9, 10, 11, 12)
    query_rows = [row * 2.0 if i in doubled else row for i, row in enumerate(query_rows)]
    return padded(key_rows, FEATURES), padded(query_rows, FEATURES)


def along_key_features(place, score):
    coarse, fine, rest = grid_parts(place)
    first, second, third = pieces(score, 3)
    ones = jnp.ones_like(place)
    dot = jnp.concatenate(pieces(row_sum(place * score), 3), axis=0)
    rows = [ones, dot, -first, -second, -third, -first, -second, -first]
    rows += [coarse, coarse, coarse, fine, fine, rest]
    return padded(rows, FEATURES)


def along_query_features(place, score):
    coarse, fine, rest = grid_parts(place)
    first, second, third = pieces(score, 3)
    ones = jnp.ones_like(place)
    dot = jnp.concatenate(pieces(row_sum(place * score), 3), axis=0)
    rows = [dot, ones, coarse, coarse, coarse, fine, fine, rest]
    rows += [-first, -second, -third, -first, -second, -first]
    return padded(rows, FEATURES)


def weighted_rows(weight, value):
    whole = jnp.concatenate([weight, weight * value], axis=0)
    return padded(pieces(whole, 3), 16).astype(bf16)


def product(left, right):
    return jnp.dot(left, right, preferred_element_type=f32)


def split_product(left, matrix):
    upper = matrix.astype(bf16)
    lower = (matrix - upper.astype(f32)).astype(bf16)
    return product(left, upper) + product(left, lower)


def joined(total):
    return total[0:4] + total[4:8] + total[8:12]


def sweep_kernel(count, *refs):
    blocks, refs = refs[:count], refs[count:]
    scores_out, drift_out, speed_out, key_ref, query_ref, moment_ref, along_ref, flux_ref, sums_ref = refs
    width = blocks[0].shape[2]
    total_slots = count * width
    chunks = total_slots // CHUNK
    tiles = total_slots // TILE
    small = count <= 4

    place = jnp.concatenate([block[0, 0:3] for block in blocks], axis=1) * SCALE
    weight = jnp.concatenate([block[0, 3:4] for block in blocks], axis=1)
    key, query = distance_features(place)
    key_ref[...] = key.T.astype(bf16)
    query_ref[...] = query.astype(bf16)
    moment_ref[...] = weighted_rows(weight, place)

    def slots(index, size):
        return pl.ds(pl.multiple_of(index * size, size), size)

    def density(tile, carry):
        query = query_ref[:, slots(tile, TILE)]

        def add(chunk, total):
            keys = slots(chunk, CHUNK)
            blob = jnp.exp2(product(key_ref[keys, :], query))
            return total + split_product(moment_ref[:, keys], blob)

        total = lax.fori_loop(0, chunks, add, jnp.zeros((16, TILE), f32), unroll=8)
        sums_ref[:, slots(tile, TILE)] = joined(total)
        return carry

    lax.fori_loop(0, tiles, density, 0, unroll=small)
    sums = sums_ref[...]
    live = weight > 0.0
    clamped = jnp.where(live, sums[0:1], 1.0)
    pull = place * sums[0:1] - sums[1:4]
    score = jnp.where(live, -pull / (SCALE * EPS * EPS * clamped), 0.0)
    along_ref[...] = along_key_features(place, score).T.astype(bf16)
    flux_ref[...] = weighted_rows(weight, score)

    place, score, live = place[:, 0:width], score[:, 0:width], live[:, 0:width]
    own_along = along_query_features(place, score).astype(bf16)
    own = -query_ref[:, 0:width]

    def add_drift(chunk, totals):
        keys = slots(chunk, CHUNK)
        square = jnp.maximum(product(key_ref[keys, :], own), TINY)
        along = product(along_ref[keys, :], own_along)
        distance = square * lax.rsqrt(square)
        return (
            totals[0] + split_product(flux_ref[:, keys], square * distance),
            totals[1] + split_product(moment_ref[:, keys], along * distance),
        )

    zero = jnp.zeros((16, width), f32)
    cubes, linear = lax.fori_loop(0, chunks, add_drift, (zero, zero), unroll=8)
    cubes, linear = joined(cubes), joined(linear)
    drift = score * cubes[0:1] - cubes[1:4] - place * linear[0:1] + linear[1:4]
    drift = jnp.where(live, drift * (-1.0 / (SCALE * SCALE * SCALE * total_slots)), 0.0)
    largest = jnp.max(row_sum(drift * drift), axis=1, keepdims=True)
    speed_out[...] = jnp.broadcast_to(jnp.sqrt(largest), speed_out.shape)
    for part in range(width // 128):
        lanes = slice(part * 128, part * 128 + 128)
        for axis in range(3):
            scores_out[axis, part : part + 1, :] = score[axis : axis + 1, lanes]
            drift_out[axis, part : part + 1, :] = drift[axis : axis + 1, lanes]


def sweep(blocks):
    count, width = len(blocks), blocks[0].shape[2]
    slots = count * width
    parts = jax.ShapeDtypeStruct((3, width // 128, 128), f32)
    whole = pl.BlockSpec(memory_space=pltpu.VMEM)
    return pl.pallas_call(
        functools.partial(sweep_kernel, count),
        out_shape=(parts, parts, jax.ShapeDtypeStruct((8, 128), f32)),
        in_specs=[whole] * count,
        out_specs=(whole, whole, whole),
        scratch_shapes=[
            pltpu.VMEM((slots, FEATURES), bf16),
            pltpu.VMEM((FEATURES, slots), bf16),
            pltpu.VMEM((16, slots), bf16),
            pltpu.VMEM((slots, FEATURES), bf16),
            pltpu.VMEM((16, slots), bf16),
            pltpu.VMEM((4, slots), f32),
        ],
        compiler_params=pltpu.CompilerParams(vmem_limit_bytes=48 * 1024 * 1024),
        name="sweep",
    )(*blocks)


def pack_kernel(velocity, weight, filled, packed):
    parts = velocity.shape[1]
    lane = lax.broadcasted_iota(jnp.int32, (1, 128), 1)
    first = lax.axis_index("sharers") * (parts * 128)
    for part in range(parts):
        lanes = slice(part * 128, part * 128 + 128)
        live = first + part * 128 + lane < filled[0]
        for axis in range(3):
            packed[0, axis : axis + 1, lanes] = velocity[axis, part : part + 1, :]
        packed[0, 3:4, lanes] = jnp.where(live, weight[part : part + 1, :], 0.0)


def pack(velocities, weights, counts):
    width = weights.shape[1]
    vector = pl.BlockSpec(memory_space=pltpu.VMEM)
    scalar = pl.BlockSpec(memory_space=pltpu.SMEM)
    return pl.pallas_call(
        pack_kernel,
        out_shape=jax.ShapeDtypeStruct((1, 4, width), f32),
        in_specs=[vector, vector, scalar],
        out_specs=vector,
        name="pack",
    )(velocities.reshape(3, width // 128, 128), weights.reshape(width // 128, 128), counts)


def swapped(value, axis, step):
    pairs = [(i, i ^ step) for i in range(lax.axis_size(axis))]
    return lax.ppermute(value, axis, pairs)


def bits(size):
    return [1 << bit for bit in range(size.bit_length() - 1)]


def gathered(block):
    size = lax.axis_size("sharers")
    if size == 4:
        return [block] + [swapped(block, "sharers", step) for step in (3, 1, 2)]
    for step in bits(size):
        block = jnp.concatenate([block, swapped(block, "sharers", step)], axis=0)
    return [block[i : i + 1] for i in range(size)]


def group_maximum(value):
    cells, sharers = lax.axis_size("cells"), lax.axis_size("sharers")

    def among_odd(value, step):
        pairs = [(i, i ^ step if (i // sharers) % 2 else i) for i in range(cells * sharers)]
        return lax.ppermute(value, ("cells", "sharers"), pairs)

    value = jnp.maximum(value, swapped(value, "cells", 1))
    for step in bits(cells)[1:]:
        value = jnp.maximum(value, among_odd(value, step * sharers))
    if sharers == 4:
        others = [among_odd(value, step) for step in (3, 1, 2)]
        for other in others:
            value = jnp.maximum(value, other)
    else:
        for step in bits(sharers):
            value = jnp.maximum(value, among_odd(value, step))
    return jnp.maximum(value, swapped(value, "cells", 1))


def local(velocities, weights, counts):
    scores, drift, largest = sweep(gathered(pack(velocities, weights, counts)))
    time_step = 0.5 / (group_maximum(largest)[0:1, :] + 1e-06)
    moved = velocities.reshape(drift.shape) + time_step[None] * drift
    return moved.reshape(velocities.shape), scores.reshape(velocities.shape)


def solution(mesh):
    in_specs = (
        P(("groups", "cells"), None, "sharers"),
        P(("groups", "cells"), "sharers"),
        P(("groups", "cells")),
    )
    out_specs = (P(("groups", "cells"), None, "sharers"), P(("groups", "cells"), None, "sharers"))
    return jax.shard_map(local, mesh=mesh, in_specs=in_specs, out_specs=out_specs, check_vma=False)
```

```python
import functools
import functools
import math

import jax
import jax.numpy as jnp
from jax import lax
from jax.experimental import pallas as pl
from jax.experimental.pallas import tpu as pltpu
from jax.sharding import PartitionSpec as P

EPS = 0.35
SCALE = math.sqrt(math.log2(math.e) / (2.0 * EPS * EPS))
GRID = 4.0
TINY = 1e-30
CHUNK = 256
FEATURES = 48
bf16, f32 = jnp.bfloat16, jnp.float32


def round_bf16(value):
    return value.astype(bf16).astype(f32)


def pieces(value, count):
    parts = []
    for _ in range(count):
        part = round_bf16(value)
        parts.append(part)
        value = value - part
    return parts


def padded(rows, height):
    filled = sum(row.shape[0] for row in rows)
    width = rows[0].shape[1]
    if filled < height:
        rows = rows + [jnp.zeros((height - filled, width), f32)]
    return jnp.concatenate(rows, axis=0)


def row_sum(value):
    return value[0:1] + value[1:2] + value[2:3]


def grid_parts(place):
    coarse = jnp.floor(place * GRID + 0.5) * (1.0 / GRID)
    return [coarse] + pieces(place - coarse, 2)


def distance_features(place):
    coarse, fine, rest = grid_parts(place)
    minor = place - coarse
    ones = jnp.ones_like(place)
    coarse_norm = jnp.concatenate(pieces(-row_sum(coarse * coarse), 3), axis=0)
    minor_norm = jnp.concatenate(
        pieces(-row_sum(minor * (2.0 * coarse + minor)), 3), axis=0
    )
    key_rows = [coarse, ones, coarse_norm, coarse, coarse, fine, rest, ones, minor_norm]
    key_rows += [fine, fine, rest, rest]
    query_rows = [coarse, coarse_norm, ones, fine, rest, coarse, coarse, minor_norm, ones]
    query_rows += [fine, rest, fine, rest]
    doubled = (0, 3, 4, 5, 6, 9, 10, 11, 12)
    query_rows = [row * 2.0 if i in doubled else row for i, row in enumerate(query_rows)]
    return padded(key_rows, FEATURES), padded(query_rows, FEATURES)


def along_key_features(place, score):
    coarse, fine, rest = grid_parts(place)
    first, second, third = pieces(score, 3)
    ones = jnp.ones_like(place)
    dot = jnp.concatenate(pieces(row_sum(place * score), 3), axis=0)
    rows = [ones, dot, -first, -second, -third, -first, -second, -first]
    rows += [coarse, coarse, coarse, fine, fine, rest]
    return padded(rows, FEATURES)


def along_query_features(place, score):
    coarse, fine, rest = grid_parts(place)
    first, second, third = pieces(score, 3)
    ones = jnp.ones_like(place)
    dot = jnp.concatenate(pieces(row_sum(place * score), 3), axis=0)
    rows = [dot, ones, coarse, coarse, coarse, fine, fine, rest]
    rows += [-first, -second, -third, -first, -second, -first]
    return padded(rows, FEATURES)


def weighted_rows(weight, value):
    whole = jnp.concatenate([weight, weight * value], axis=0)
    return padded(pieces(whole, 3), 16).astype(bf16)


def product(left, right):
    return jnp.dot(left, right, preferred_element_type=f32)


def split_product(left, matrix):
    upper = matrix.astype(bf16)
    lower = (matrix - upper.astype(f32)).astype(bf16)
    return product(left, upper) + product(left, lower)


def joined(total):
    return total[0:4] + total[4:8] + total[8:12]


def sweep_kernel(count, *refs):
    filled, blocks, refs = refs[0], refs[1 : count + 1], refs[count + 1 :]
    scores_out, drift_out, speed_out, key_ref, query_ref, moment_ref, along_ref, flux_ref = refs[:8]
    sums_ref, cubes_ref, linear_ref, even_ref, odd_ref, even_along_ref, odd_along_ref, own_ref = refs[8:]
    width = blocks[0].shape[2]
    total_slots = count * width
    chunks = total_slots // CHUNK
    steps = chunks * count
    here = lax.axis_index("sharers")

    def slots(index, size):
        return pl.ds(pl.multiple_of(index * size, size), size)

    lane = lax.broadcasted_iota(jnp.int32, (1, width), 1)
    live = [lane + (here ^ step) * width < filled[0] for step in range(count)]
    weight = jnp.concatenate(
        [jnp.where(on, block[0, 3:4], 0.0) for on, block in zip(live, blocks)], axis=1
    )
    place = jnp.concatenate([block[0, 0:3] for block in blocks], axis=1) * SCALE
    key, query = distance_features(place)
    key_ref[...] = key.T.astype(bf16)
    query_ref[...] = query.astype(bf16)
    moment_ref[...] = weighted_rows(weight, place)
    sums_ref[...] = jnp.zeros_like(sums_ref)

    def exponent(step):
        step = jnp.minimum(step, steps - 1)
        tile, chunk = step // chunks, step % chunks
        return product(key_ref[slots(chunk, CHUNK), :], query_ref[:, slots(tile, width)])

    def add_blobs(step, ref):
        tile, chunk = step // chunks, step % chunks
        sums_ref[:, slots(tile, width)] += split_product(
            moment_ref[:, slots(chunk, CHUNK)], jnp.exp2(ref[...])
        )

    even_ref[...] = exponent(0)

    def density(pair, carry):
        step = pair * 2
        odd_ref[...] = exponent(step + 1)
        add_blobs(step, even_ref)
        even_ref[...] = exponent(step + 2)
        add_blobs(step + 1, odd_ref)
        return carry

    lax.fori_loop(0, steps // 2, density, 0)

    sums = joined(sums_ref[...])
    live = weight > 0.0
    clamped = jnp.where(live, sums[0:1], 1.0)
    pull = place * sums[0:1] - sums[1:4]
    score = jnp.where(live, -pull / (SCALE * EPS * EPS * clamped), 0.0)
    along_ref[...] = along_key_features(place, score).T.astype(bf16)
    flux_ref[...] = weighted_rows(weight, score)

    place, score, live = place[:, 0:width], score[:, 0:width], live[:, 0:width]
    own_ref[0] = -query_ref[:, 0:width]
    own_ref[1] = along_query_features(place, score).astype(bf16)
    cubes_ref[...] = jnp.zeros_like(cubes_ref)
    linear_ref[...] = jnp.zeros_like(linear_ref)

    def pair_products(chunk, square_ref, dot_ref):
        keys = slots(jnp.minimum(chunk, chunks - 1), CHUNK)
        square_ref[...] = product(key_ref[keys, :], own_ref[0])
        dot_ref[...] = product(along_ref[keys, :], own_ref[1])

    def add_drift(chunk, square_ref, dot_ref):
        keys = slots(chunk, CHUNK)
        square = jnp.maximum(square_ref[...], TINY)
        distance = square * lax.rsqrt(square)
        cubes_ref[...] += split_product(flux_ref[:, keys], square * distance)
        linear_ref[...] += split_product(moment_ref[:, keys], dot_ref[...] * distance)

    pair_products(0, even_ref, even_along_ref)

    def drift_pair(pair, carry):
        chunk = pair * 2
        pair_products(chunk + 1, odd_ref, odd_along_ref)
        add_drift(chunk, even_ref, even_along_ref)
        pair_products(chunk + 2, even_ref, even_along_ref)
        add_drift(chunk + 1, odd_ref, odd_along_ref)
        return carry

    lax.fori_loop(0, chunks // 2, drift_pair, 0)
    cubes, linear = joined(cubes_ref[...]), joined(linear_ref[...])
    drift = score * cubes[0:1] - cubes[1:4] - place * linear[0:1] + linear[1:4]
    drift = jnp.where(live, drift * (-1.0 / (SCALE * SCALE * SCALE * total_slots)), 0.0)
    largest = jnp.max(row_sum(drift * drift), axis=1, keepdims=True)
    speed_out[...] = jnp.broadcast_to(jnp.sqrt(largest), speed_out.shape)
    for part in range(width // 128):
        lanes = slice(part * 128, part * 128 + 128)
        for axis in range(3):
            scores_out[axis, part : part + 1, :] = score[axis : axis + 1, lanes]
            drift_out[axis, part : part + 1, :] = drift[axis : axis + 1, lanes]


def sweep(counts, blocks, copies):
    count, width = len(blocks), blocks[0].shape[2]
    slots = count * width
    parts = jax.ShapeDtypeStruct((3, width // 128, 128), f32)
    whole = pl.BlockSpec(memory_space=pltpu.VMEM)
    return pl.pallas_call(
        functools.partial(sweep_kernel, count),
        out_shape=(parts, parts, jax.ShapeDtypeStruct((copies, 128), f32)),
        in_specs=[pl.BlockSpec(memory_space=pltpu.SMEM)] + [whole] * count,
        out_specs=(whole, whole, whole),
        scratch_shapes=[
            pltpu.VMEM((slots, FEATURES), bf16),
            pltpu.VMEM((FEATURES, slots), bf16),
            pltpu.VMEM((16, slots), bf16),
            pltpu.VMEM((slots, FEATURES), bf16),
            pltpu.VMEM((16, slots), bf16),
            pltpu.VMEM((16, slots), f32),
            pltpu.VMEM((16, width), f32),
            pltpu.VMEM((16, width), f32),
            pltpu.VMEM((CHUNK, width), f32),
            pltpu.VMEM((CHUNK, width), f32),
            pltpu.VMEM((CHUNK, width), f32),
            pltpu.VMEM((CHUNK, width), f32),
            pltpu.VMEM((2, FEATURES, width), bf16),
        ],
        compiler_params=pltpu.CompilerParams(vmem_limit_bytes=48 * 1024 * 1024),
        name="sweep",
    )(counts, *blocks)


def swapped(value, axis, step):
    pairs = [(i, i ^ step) for i in range(lax.axis_size(axis))]
    return lax.ppermute(value, axis, pairs)


def bits(size):
    return [1 << bit for bit in range(size.bit_length() - 1)]


def gathered(block):
    size = lax.axis_size("sharers")
    if size == 4:
        second, first, third = (swapped(block, "sharers", step) for step in (2, 1, 3))
        return [block, first, second, third]
    for step in bits(size):
        block = jnp.concatenate([block, swapped(block, "sharers", step)], axis=0)
    return [block[i : i + 1] for i in range(size)]


def local(velocities, weights, counts):
    axes = ("cells", "sharers")
    blocks = gathered(jnp.concatenate([velocities, weights[:, None]], axis=1))
    copies = lax.axis_size(axes)
    scores, drift, speeds = sweep(counts, blocks, copies)
    speeds = lax.all_to_all(speeds.reshape(copies, 1, 128), axes, 0, 0, tiled=True)
    time_step = 0.5 / (jnp.max(speeds, axis=0, keepdims=True) + 1e-06)
    moved = velocities.reshape(drift.shape) + time_step * drift
    return moved.reshape(velocities.shape), scores.reshape(velocities.shape)


def solution(mesh):
    in_specs = (
        P(("groups", "cells"), None, "sharers"),
        P(("groups", "cells"), "sharers"),
        P(("groups", "cells")),
    )
    out_specs = (P(("groups", "cells"), None, "sharers"), P(("groups", "cells"), None, "sharers"))
    return jax.shard_map(local, mesh=mesh, in_specs=in_specs, out_specs=out_specs, check_vma=False)
```

```python
import functools
import functools
import math

import jax
import jax.numpy as jnp
from jax import lax
from jax.experimental import pallas as pl
from jax.experimental.pallas import tpu as pltpu
from jax.sharding import PartitionSpec as P

EPS = 0.35
SCALE = math.sqrt(math.log2(math.e) / (2.0 * EPS * EPS))
GRID = 4.0
TINY = 1e-30
CHUNK = 512
FEATURES = 48
bf16, f32 = jnp.bfloat16, jnp.float32


def round_bf16(value):
    return value.astype(bf16).astype(f32)


def pieces(value, count):
    parts = []
    for _ in range(count):
        part = round_bf16(value)
        parts.append(part)
        value = value - part
    return parts


def padded(rows, height):
    filled = sum(row.shape[0] for row in rows)
    width = rows[0].shape[1]
    if filled < height:
        rows = rows + [jnp.zeros((height - filled, width), f32)]
    return jnp.concatenate(rows, axis=0)


def row_sum(value):
    return value[0:1] + value[1:2] + value[2:3]


def grid_parts(place):
    coarse = jnp.floor(place * GRID + 0.5) * (1.0 / GRID)
    return [coarse] + pieces(place - coarse, 2)


def distance_features(place):
    coarse, fine, rest = grid_parts(place)
    minor = place - coarse
    ones = jnp.ones_like(place)
    coarse_norm = jnp.concatenate(pieces(-row_sum(coarse * coarse), 3), axis=0)
    minor_norm = jnp.concatenate(
        pieces(-row_sum(minor * (2.0 * coarse + minor)), 3), axis=0
    )
    key_rows = [coarse, ones, coarse_norm, coarse, coarse, fine, rest, ones, minor_norm]
    key_rows += [fine, fine, rest, rest]
    query_rows = [coarse, coarse_norm, ones, fine, rest, coarse, coarse, minor_norm, ones]
    query_rows += [fine, rest, fine, rest]
    doubled = (0, 3, 4, 5, 6, 9, 10, 11, 12)
    query_rows = [row * 2.0 if i in doubled else row for i, row in enumerate(query_rows)]
    return padded(key_rows, FEATURES), padded(query_rows, FEATURES)


def along_key_features(place, score):
    coarse, fine, rest = grid_parts(place)
    first, second, third = pieces(score, 3)
    ones = jnp.ones_like(place)
    dot = jnp.concatenate(pieces(row_sum(place * score), 3), axis=0)
    rows = [ones, dot, -first, -second, -third, -first, -second, -first]
    rows += [coarse, coarse, coarse, fine, fine, rest]
    return padded(rows, FEATURES)


def along_query_features(place, score):
    coarse, fine, rest = grid_parts(place)
    first, second, third = pieces(score, 3)
    ones = jnp.ones_like(place)
    dot = jnp.concatenate(pieces(row_sum(place * score), 3), axis=0)
    rows = [dot, ones, coarse, coarse, coarse, fine, fine, rest]
    rows += [-first, -second, -third, -first, -second, -first]
    return padded(rows, FEATURES)


def weighted_rows(weight, value):
    whole = jnp.concatenate([weight, weight * value], axis=0)
    return padded(pieces(whole, 3), 16).astype(bf16)


def product(left, right):
    return jnp.dot(left, right, preferred_element_type=f32)


def split_product(left, matrix):
    upper = matrix.astype(bf16)
    lower = (matrix - upper.astype(f32)).astype(bf16)
    return product(
        jnp.concatenate([left, left], axis=1), jnp.concatenate([upper, lower], axis=0)
    )


def joined(total):
    return total[0:4] + total[4:8] + total[8:12]


def sweep_kernel(order, *refs):
    count = len(order)
    filled, blocks, refs = refs[0], refs[1 : count + 1], refs[count + 1 :]
    scores_out, drift_out, start_out, speed_out, key_ref, query_ref, moment_ref = refs[:7]
    along_ref, flux_ref, sums_ref, cubes_ref, linear_ref, even_ref, odd_ref = refs[7:14]
    even_along_ref, odd_along_ref, own_ref = refs[14:]
    width = blocks[0].shape[2]
    total_slots = count * width
    chunks = total_slots // CHUNK
    steps = chunks * count
    here = lax.axis_index("sharers")

    def slots(index, size):
        return pl.ds(pl.multiple_of(index * size, size), size)

    lane = lax.broadcasted_iota(jnp.int32, (1, width), 1)
    live = [lane + (here ^ step) * width < filled[0] for step in order]
    weight = jnp.concatenate(
        [jnp.where(on, block[0, 3:4], 0.0) for on, block in zip(live, blocks)], axis=1
    )
    place = jnp.concatenate([block[0, 0:3] for block in blocks], axis=1) * SCALE
    key, query = distance_features(place)
    key_ref[...] = key.T.astype(bf16)
    query_ref[...] = query.astype(bf16)
    moment_ref[...] = weighted_rows(weight, place)
    sums_ref[...] = jnp.zeros_like(sums_ref)

    def exponent(step):
        step = jnp.minimum(step, steps - 1)
        tile, chunk = step // chunks, step % chunks
        return product(key_ref[slots(chunk, CHUNK), :], query_ref[:, slots(tile, width)])

    def add_blobs(step, ref):
        tile, chunk = step // chunks, step % chunks
        sums_ref[:, slots(tile, width)] += split_product(
            moment_ref[:, slots(chunk, CHUNK)], jnp.exp2(ref[...])
        )

    even_ref[...] = exponent(0)

    def density(pair, carry):
        step = pair * 2
        odd_ref[...] = exponent(step + 1)
        add_blobs(step, even_ref)
        even_ref[...] = exponent(step + 2)
        add_blobs(step + 1, odd_ref)
        return carry

    lax.fori_loop(0, steps // 2, density, 0)

    sums = joined(sums_ref[...])
    live = weight > 0.0
    clamped = jnp.where(live, sums[0:1], 1.0)
    pull = place * sums[0:1] - sums[1:4]
    score = jnp.where(live, -pull / (SCALE * EPS * EPS * clamped), 0.0)
    along_ref[...] = along_key_features(place, score).T.astype(bf16)
    flux_ref[...] = weighted_rows(weight, score)

    place, score, live = place[:, 0:width], score[:, 0:width], live[:, 0:width]
    own_ref[0] = -query_ref[:, 0:width]
    own_ref[1] = along_query_features(place, score).astype(bf16)
    cubes_ref[...] = jnp.zeros_like(cubes_ref)
    linear_ref[...] = jnp.zeros_like(linear_ref)

    def pair_products(chunk, square_ref, dot_ref):
        keys = slots(jnp.minimum(chunk, chunks - 1), CHUNK)
        square_ref[...] = product(key_ref[keys, :], own_ref[0])
        dot_ref[...] = product(along_ref[keys, :], own_ref[1])

    def add_drift(chunk, square_ref, dot_ref):
        keys = slots(chunk, CHUNK)
        square = jnp.maximum(square_ref[...], TINY)
        distance = square * lax.rsqrt(square)
        cubes_ref[...] += split_product(flux_ref[:, keys], square * distance)
        linear_ref[...] += split_product(moment_ref[:, keys], dot_ref[...] * distance)

    pair_products(0, even_ref, even_along_ref)

    def drift_pair(pair, carry):
        chunk = pair * 2
        pair_products(chunk + 1, odd_ref, odd_along_ref)
        add_drift(chunk, even_ref, even_along_ref)
        pair_products(chunk + 2, even_ref, even_along_ref)
        add_drift(chunk + 1, odd_ref, odd_along_ref)
        return carry

    lax.fori_loop(0, chunks // 2, drift_pair, 0)
    cubes, linear = joined(cubes_ref[...]), joined(linear_ref[...])
    drift = score * cubes[0:1] - cubes[1:4] - place * linear[0:1] + linear[1:4]
    drift = jnp.where(live, drift * (-1.0 / (SCALE * SCALE * SCALE * total_slots)), 0.0)
    largest = jnp.max(row_sum(drift * drift), axis=1, keepdims=True)
    speed_out[...] = jnp.broadcast_to(jnp.sqrt(largest), speed_out.shape)
    for part in range(width // 128):
        lanes = slice(part * 128, part * 128 + 128)
        for axis in range(3):
            scores_out[axis, part : part + 1, :] = score[axis : axis + 1, lanes]
            drift_out[axis, part : part + 1, :] = drift[axis : axis + 1, lanes]
            start_out[axis, part : part + 1, :] = blocks[0][0, axis : axis + 1, lanes]


def sweep(counts, blocks, order, copies):
    count, width = len(blocks), blocks[0].shape[2]
    slots = count * width
    parts = jax.ShapeDtypeStruct((3, width // 128, 128), f32)
    whole = pl.BlockSpec(memory_space=pltpu.VMEM)
    return pl.pallas_call(
        functools.partial(sweep_kernel, order),
        out_shape=(parts, parts, parts, jax.ShapeDtypeStruct((copies, 128), f32)),
        in_specs=[pl.BlockSpec(memory_space=pltpu.SMEM)] + [whole] * count,
        out_specs=(whole, whole, whole, whole),
        scratch_shapes=[
            pltpu.VMEM((slots, FEATURES), bf16),
            pltpu.VMEM((FEATURES, slots), bf16),
            pltpu.VMEM((16, slots), bf16),
            pltpu.VMEM((slots, FEATURES), bf16),
            pltpu.VMEM((16, slots), bf16),
            pltpu.VMEM((16, slots), f32),
            pltpu.VMEM((16, width), f32),
            pltpu.VMEM((16, width), f32),
            pltpu.VMEM((CHUNK, width), f32),
            pltpu.VMEM((CHUNK, width), f32),
            pltpu.VMEM((CHUNK, width), f32),
            pltpu.VMEM((CHUNK, width), f32),
            pltpu.VMEM((2, FEATURES, width), bf16),
        ],
        compiler_params=pltpu.CompilerParams(vmem_limit_bytes=48 * 1024 * 1024),
        name="sweep",
    )(counts, *blocks)


def swapped(value, axis, step):
    pairs = [(i, i ^ step) for i in range(lax.axis_size(axis))]
    return lax.ppermute(value, axis, pairs)


def bits(size):
    return [1 << bit for bit in range(size.bit_length() - 1)]


def gathered(block):
    size = lax.axis_size("sharers")
    if size == 4:
        order = [0, 2, 1, 3]
        return [block] + [swapped(block, "sharers", step) for step in order[1:]], order
    for step in bits(size):
        block = jnp.concatenate([block, swapped(block, "sharers", step)], axis=0)
    return [block[i : i + 1] for i in range(size)], list(range(size))


def local(velocities, weights, counts):
    axes = ("cells", "sharers")
    blocks, order = gathered(jnp.concatenate([velocities, weights[:, None]], axis=1))
    copies = lax.axis_size(axes)
    scores, drift, start, speeds = sweep(counts, blocks, order, copies)
    speeds = lax.all_to_all(speeds.reshape(copies, 1, 128), axes, 0, 0, tiled=True)
    time_step = 0.5 / (jnp.max(speeds, axis=0, keepdims=True) + 1e-06)
    moved = start + time_step * drift
    return moved.reshape(velocities.shape), scores.reshape(velocities.shape)


def solution(mesh):
    in_specs = (
        P(("groups", "cells"), None, "sharers"),
        P(("groups", "cells"), "sharers"),
        P(("groups", "cells")),
    )
    out_specs = (P(("groups", "cells"), None, "sharers"), P(("groups", "cells"), None, "sharers"))
    return jax.shard_map(local, mesh=mesh, in_specs=in_specs, out_specs=out_specs, check_vma=False)
```

```python
import functools
import functools
import math

import jax
import jax.numpy as jnp
from jax import lax
from jax.experimental import pallas as pl
from jax.experimental.pallas import tpu as pltpu
from jax.sharding import PartitionSpec as P

EPS = 0.35
SCALE = math.sqrt(math.log2(math.e) / (2.0 * EPS * EPS))
GRID = 4.0
TINY = 1e-30
DENSITY_CHUNK = 2048
DRIFT_CHUNK = 1024
FEATURES = 48
bf16, f32 = jnp.bfloat16, jnp.float32


def round_bf16(value):
    return value.astype(bf16).astype(f32)


def pieces(value, count):
    parts = []
    for _ in range(count):
        part = round_bf16(value)
        parts.append(part)
        value = value - part
    return parts


def padded(rows, height):
    filled = sum(row.shape[0] for row in rows)
    width = rows[0].shape[1]
    if filled < height:
        rows = rows + [jnp.zeros((height - filled, width), f32)]
    return jnp.concatenate(rows, axis=0)


def row_sum(value):
    return value[0:1] + value[1:2] + value[2:3]


def grid_parts(place):
    coarse = jnp.floor(place * GRID + 0.5) * (1.0 / GRID)
    return [coarse] + pieces(place - coarse, 2)


def distance_features(place):
    coarse, fine, rest = grid_parts(place)
    minor = place - coarse
    ones = jnp.ones_like(place)
    coarse_norm = jnp.concatenate(pieces(-row_sum(coarse * coarse), 3), axis=0)
    minor_norm = jnp.concatenate(
        pieces(-row_sum(minor * (2.0 * coarse + minor)), 3), axis=0
    )
    key_rows = [coarse, ones, coarse_norm, coarse, coarse, fine, rest, ones, minor_norm]
    key_rows += [fine, fine, rest, rest]
    query_rows = [coarse, coarse_norm, ones, fine, rest, coarse, coarse, minor_norm, ones]
    query_rows += [fine, rest, fine, rest]
    doubled = (0, 3, 4, 5, 6, 9, 10, 11, 12)
    query_rows = [row * 2.0 if i in doubled else row for i, row in enumerate(query_rows)]
    return padded(key_rows, FEATURES), padded(query_rows, FEATURES)


def along_key_features(place, score):
    coarse, fine, rest = grid_parts(place)
    first, second, third = pieces(score, 3)
    ones = jnp.ones_like(place)
    dot = jnp.concatenate(pieces(row_sum(place * score), 3), axis=0)
    rows = [ones, dot, -first, -second, -third, -first, -second, -first]
    rows += [coarse, coarse, coarse, fine, fine, rest]
    return padded(rows, FEATURES)


def along_query_features(place, score):
    coarse, fine, rest = grid_parts(place)
    first, second, third = pieces(score, 3)
    ones = jnp.ones_like(place)
    dot = jnp.concatenate(pieces(row_sum(place * score), 3), axis=0)
    rows = [dot, ones, coarse, coarse, coarse, fine, fine, rest]
    rows += [-first, -second, -third, -first, -second, -first]
    return padded(rows, FEATURES)


def weighted_rows(weight, value):
    whole = jnp.concatenate([weight, weight * value], axis=0)
    return padded(pieces(whole, 3), 16).astype(bf16)


def product(left, right):
    return jnp.dot(left, right, preferred_element_type=f32)


def split_product(left, matrix):
    upper = matrix.astype(bf16)
    lower = (matrix - upper.astype(f32)).astype(bf16)
    return product(
        jnp.concatenate([left, left], axis=1), jnp.concatenate([upper, lower], axis=0)
    )


def joined(total):
    return total[0:4] + total[4:8] + total[8:12]


def sweep_kernel(order, *refs):
    count = len(order)
    filled, blocks, refs = refs[0], refs[1 : count + 1], refs[count + 1 :]
    scores_out, drift_out, start_out, speed_out, key_ref, query_ref, moment_ref = refs[:7]
    along_ref, flux_ref, sums_ref, cubes_ref, linear_ref, even_ref, odd_ref = refs[7:14]
    even_square_ref, odd_square_ref, even_along_ref, odd_along_ref, own_ref = refs[14:]
    width = blocks[0].shape[2]
    total_slots = count * width
    size = min(total_slots, DENSITY_CHUNK)
    chunks = total_slots // size
    steps = chunks * count
    drift_size = min(total_slots // 2, DRIFT_CHUNK)
    drift_chunks = total_slots // drift_size
    here = lax.axis_index("sharers")

    def slots(index, size):
        return pl.ds(pl.multiple_of(index * size, size), size)

    lane = lax.broadcasted_iota(jnp.int32, (1, width), 1)
    live = [lane + (here ^ step) * width < filled[0] for step in order]
    weight = jnp.concatenate(
        [jnp.where(on, block[0, 3:4], 0.0) for on, block in zip(live, blocks)], axis=1
    )
    place = jnp.concatenate([block[0, 0:3] for block in blocks], axis=1) * SCALE
    key, query = distance_features(place)
    key_ref[...] = key.T.astype(bf16)
    query_ref[...] = query.astype(bf16)
    moment_ref[...] = weighted_rows(weight, place)
    sums_ref[...] = jnp.zeros_like(sums_ref)

    def exponent(step):
        step = jnp.minimum(step, steps - 1)
        tile, chunk = step // chunks, step % chunks
        return product(key_ref[slots(chunk, size), :], query_ref[:, slots(tile, width)])

    def add_blobs(step, ref):
        tile, chunk = step // chunks, step % chunks
        sums_ref[:, slots(tile, width)] += split_product(
            moment_ref[:, slots(chunk, size)], jnp.exp2(ref[...])
        )

    even_ref[...] = exponent(0)

    def density(pair, carry):
        step = pair * 2
        odd_ref[...] = exponent(step + 1)
        add_blobs(step, even_ref)
        even_ref[...] = exponent(step + 2)
        add_blobs(step + 1, odd_ref)
        return carry

    lax.fori_loop(0, steps // 2, density, 0)

    sums = joined(sums_ref[...])
    live = weight > 0.0
    clamped = jnp.where(live, sums[0:1], 1.0)
    pull = place * sums[0:1] - sums[1:4]
    score = jnp.where(live, -pull / (SCALE * EPS * EPS * clamped), 0.0)
    along_ref[...] = along_key_features(place, score).T.astype(bf16)
    flux_ref[...] = weighted_rows(weight, score)

    place, score, live = place[:, 0:width], score[:, 0:width], live[:, 0:width]
    own_ref[0] = -query_ref[:, 0:width]
    own_ref[1] = along_query_features(place, score).astype(bf16)
    cubes_ref[...] = jnp.zeros_like(cubes_ref)
    linear_ref[...] = jnp.zeros_like(linear_ref)

    def pair_products(chunk, square_ref, dot_ref):
        keys = slots(jnp.minimum(chunk, drift_chunks - 1), drift_size)
        square_ref[...] = product(key_ref[keys, :], own_ref[0])
        dot_ref[...] = product(along_ref[keys, :], own_ref[1])

    def add_drift(chunk, square_ref, dot_ref):
        keys = slots(chunk, drift_size)
        square = jnp.maximum(square_ref[...], TINY)
        distance = square * lax.rsqrt(square)
        cubes_ref[...] += split_product(flux_ref[:, keys], square * distance)
        linear_ref[...] += split_product(moment_ref[:, keys], dot_ref[...] * distance)

    pair_products(0, even_square_ref, even_along_ref)

    def drift_pair(pair, carry):
        chunk = pair * 2
        pair_products(chunk + 1, odd_square_ref, odd_along_ref)
        add_drift(chunk, even_square_ref, even_along_ref)
        pair_products(chunk + 2, even_square_ref, even_along_ref)
        add_drift(chunk + 1, odd_square_ref, odd_along_ref)
        return carry

    lax.fori_loop(0, drift_chunks // 2, drift_pair, 0)
    cubes, linear = joined(cubes_ref[...]), joined(linear_ref[...])
    drift = score * cubes[0:1] - cubes[1:4] - place * linear[0:1] + linear[1:4]
    drift = jnp.where(live, drift * (-1.0 / (SCALE * SCALE * SCALE * total_slots)), 0.0)
    largest = jnp.max(row_sum(drift * drift), axis=1, keepdims=True)
    speed_out[...] = jnp.broadcast_to(jnp.sqrt(largest), speed_out.shape)
    for part in range(width // 128):
        lanes = slice(part * 128, part * 128 + 128)
        for axis in range(3):
            scores_out[axis, part : part + 1, :] = score[axis : axis + 1, lanes]
            drift_out[axis, part : part + 1, :] = drift[axis : axis + 1, lanes]
            start_out[axis, part : part + 1, :] = blocks[0][0, axis : axis + 1, lanes]


def sweep(counts, blocks, order, copies):
    count, width = len(blocks), blocks[0].shape[2]
    slots = count * width
    parts = jax.ShapeDtypeStruct((3, width // 128, 128), f32)
    whole = pl.BlockSpec(memory_space=pltpu.VMEM)
    return pl.pallas_call(
        functools.partial(sweep_kernel, order),
        out_shape=(parts, parts, parts, jax.ShapeDtypeStruct((copies, 128), f32)),
        in_specs=[pl.BlockSpec(memory_space=pltpu.SMEM)] + [whole] * count,
        out_specs=(whole, whole, whole, whole),
        scratch_shapes=[
            pltpu.VMEM((slots, FEATURES), bf16),
            pltpu.VMEM((FEATURES, slots), bf16),
            pltpu.VMEM((16, slots), bf16),
            pltpu.VMEM((slots, FEATURES), bf16),
            pltpu.VMEM((16, slots), bf16),
            pltpu.VMEM((16, slots), f32),
            pltpu.VMEM((16, width), f32),
            pltpu.VMEM((16, width), f32),
            pltpu.VMEM((min(slots, DENSITY_CHUNK), width), f32),
            pltpu.VMEM((min(slots, DENSITY_CHUNK), width), f32),
            pltpu.VMEM((min(slots // 2, DRIFT_CHUNK), width), f32),
            pltpu.VMEM((min(slots // 2, DRIFT_CHUNK), width), f32),
            pltpu.VMEM((min(slots // 2, DRIFT_CHUNK), width), f32),
            pltpu.VMEM((min(slots // 2, DRIFT_CHUNK), width), f32),
            pltpu.VMEM((2, FEATURES, width), bf16),
        ],
        compiler_params=pltpu.CompilerParams(vmem_limit_bytes=48 * 1024 * 1024),
        name="sweep",
    )(counts, *blocks)


def swapped(value, axis, step):
    pairs = [(i, i ^ step) for i in range(lax.axis_size(axis))]
    return lax.ppermute(value, axis, pairs)


def bits(size):
    return [1 << bit for bit in range(size.bit_length() - 1)]


def gathered(block):
    size = lax.axis_size("sharers")
    if size == 4:
        order = [0, 2, 1, 3]
        return [block] + [swapped(block, "sharers", step) for step in order[1:]], order
    for step in bits(size):
        block = jnp.concatenate([block, swapped(block, "sharers", step)], axis=0)
    return [block[i : i + 1] for i in range(size)], list(range(size))


def local(velocities, weights, counts):
    axes = ("cells", "sharers")
    blocks, order = gathered(jnp.concatenate([velocities, weights[:, None]], axis=1))
    copies = lax.axis_size(axes)
    scores, drift, start, speeds = sweep(counts, blocks, order, copies)
    speeds = lax.all_to_all(speeds.reshape(copies, 1, 128), axes, 0, 0, tiled=True)
    time_step = 0.5 / (jnp.max(speeds, axis=0, keepdims=True) + 1e-06)
    moved = start + time_step * drift
    return moved.reshape(velocities.shape), scores.reshape(velocities.shape)


def solution(mesh):
    in_specs = (
        P(("groups", "cells"), None, "sharers"),
        P(("groups", "cells"), "sharers"),
        P(("groups", "cells")),
    )
    out_specs = (P(("groups", "cells"), None, "sharers"), P(("groups", "cells"), None, "sharers"))
    return jax.shard_map(local, mesh=mesh, in_specs=in_specs, out_specs=out_specs, check_vma=False)
```

```python
import functools
import functools
import math

import jax
import jax.numpy as jnp
from jax import lax
from jax.experimental import pallas as pl
from jax.experimental.pallas import tpu as pltpu
from jax.sharding import PartitionSpec as P

EPS = 0.35
SCALE = math.sqrt(math.log2(math.e) / (2.0 * EPS * EPS))
GRID = 4.0
TINY = 1e-30
CHUNK = 512
FEATURES = 48
EXTRA_ROW = 39
DEAD = -20000.0
bf16, f32 = jnp.bfloat16, jnp.float32


def round_bf16(value):
    return value.astype(bf16).astype(f32)


def pieces(value, count):
    parts = []
    for _ in range(count):
        part = round_bf16(value)
        parts.append(part)
        value = value - part
    return parts


def padded(rows, height):
    filled = sum(row.shape[0] for row in rows)
    width = rows[0].shape[1]
    if filled < height:
        rows = rows + [jnp.zeros((height - filled, width), f32)]
    return jnp.concatenate(rows, axis=0)


def row_sum(value):
    return value[0:1] + value[1:2] + value[2:3]


def grid_parts(place):
    coarse = jnp.floor(place * GRID + 0.5) * (1.0 / GRID)
    return [coarse] + pieces(place - coarse, 2)


def distance_features(parts, extra):
    coarse, fine, rest = parts
    minor = fine + rest
    place = coarse + minor
    ones = jnp.ones_like(place)
    coarse_norm = jnp.concatenate(pieces(-row_sum(coarse * coarse), 3), axis=0)
    minor_norm = jnp.concatenate(
        pieces(-row_sum(minor * (2.0 * coarse + minor)), 3), axis=0
    )
    key_rows = [coarse, ones, coarse_norm, coarse, coarse, fine, rest, ones, minor_norm]
    key_rows += [fine, fine, rest, rest] + pieces(extra, 3)
    query_rows = [coarse, coarse_norm, ones, fine, rest, coarse, coarse, minor_norm, ones]
    query_rows += [fine, rest, fine, rest, ones]
    doubled = (0, 3, 4, 5, 6, 9, 10, 11, 12)
    query_rows = [row * 2.0 if i in doubled else row for i, row in enumerate(query_rows)]
    return padded(key_rows, FEATURES), padded(query_rows, FEATURES)


def along_key_features(parts, score):
    coarse, fine, rest = parts
    place = coarse + fine + rest
    first, second, third = pieces(score, 3)
    ones = jnp.ones_like(place)
    dot = jnp.concatenate(pieces(row_sum(place * score), 3), axis=0)
    rows = [ones, dot, -first, -second, -third, -first, -second, -first]
    rows += [coarse, coarse, coarse, fine, fine, rest]
    return padded(rows, FEATURES)


def along_query_features(parts, score):
    coarse, fine, rest = parts
    place = coarse + fine + rest
    first, second, third = pieces(score, 3)
    ones = jnp.ones_like(place)
    dot = jnp.concatenate(pieces(row_sum(place * score), 3), axis=0)
    rows = [dot, ones, coarse, coarse, coarse, fine, fine, rest]
    rows += [-first, -second, -third, -first, -second, -first]
    return padded(rows, FEATURES)


def weighted_rows(weight, value):
    whole = jnp.concatenate([weight, weight * value], axis=0)
    return padded(pieces(whole, 3), 16).astype(bf16)


def product(left, right):
    return jnp.dot(left, right, preferred_element_type=f32)


def split_product(left, matrix):
    upper = matrix.astype(bf16)
    lower = (matrix - upper.astype(f32)).astype(bf16)
    return product(
        jnp.concatenate([left, left], axis=1), jnp.concatenate([upper, lower], axis=0)
    )


def joined(total):
    return total[0:4] + total[4:8] + total[8:12]


def sweep_kernel(order, *refs):
    count = len(order)
    filled, blocks, refs = refs[0], refs[1 : count + 1], refs[count + 1 :]
    scores_out, drift_out, start_out, speed_out, key_ref, query_ref, column_ref = refs[:7]
    along_ref, flux_ref, sums_ref, cubes_ref, linear_ref, even_ref, odd_ref = refs[7:14]
    even_along_ref, odd_along_ref, own_ref, moment_ref = refs[14:]
    width = blocks[0].shape[2]
    total_slots = count * width
    chunks = total_slots // CHUNK
    steps = chunks * count
    here = lax.axis_index("sharers")

    def slots(index, size):
        return pl.ds(pl.multiple_of(index * size, size), size)

    lane = lax.broadcasted_iota(jnp.int32, (1, width), 1)
    live = [lane + (here ^ step) * width < filled[0] for step in order]
    weight = jnp.concatenate(
        [jnp.where(on, block[0, 3:4], 0.0) for on, block in zip(live, blocks)], axis=1
    )
    live = weight > 0.0
    parts = grid_parts(jnp.concatenate([block[0, 0:3] for block in blocks], axis=1) * SCALE)
    place = parts[0] + parts[1] + parts[2]
    extra = jnp.where(live, jnp.log2(jnp.where(live, weight, 1.0)), DEAD)
    key, query = distance_features(parts, extra)
    key_ref[...] = key.T.astype(bf16)
    query_ref[...] = query.astype(bf16)
    moment_ref[...] = weighted_rows(weight, place)
    across = padded([place], 8).T
    for axis in range(3):
        column_ref[axis] = jnp.broadcast_to(across[:, axis : axis + 1], column_ref.shape[1:])
    sums_ref[...] = jnp.zeros_like(sums_ref)

    def exponent(step):
        step = jnp.minimum(step, steps - 1)
        tile, chunk = step // chunks, step % chunks
        return product(key_ref[slots(chunk, CHUNK), :], query_ref[:, slots(tile, width)])

    def add_blobs(step, ref):
        tile, chunk = step // chunks, step % chunks
        columns = [column_ref[axis, slots(chunk, CHUNK), :] for axis in range(3)]
        for part in range(width // 128):
            blob = jnp.exp2(ref[:, part * 128 : part * 128 + 128])
            lanes = pl.ds(pl.multiple_of(tile * width + part * 128, 128), 128)
            for i, term in enumerate([blob] + [blob * column for column in columns]):
                sums_ref[i, :, lanes] += jnp.sum(term.reshape(CHUNK // 8, 8, 128), axis=0)

    even_ref[...] = exponent(0)

    def density(pair, carry):
        step = pair * 2
        odd_ref[...] = exponent(step + 1)
        add_blobs(step, even_ref)
        even_ref[...] = exponent(step + 2)
        add_blobs(step + 1, odd_ref)
        return carry

    lax.fori_loop(0, steps // 2, density, 0)

    sums = jnp.sum(sums_ref[...], axis=1)
    clamped = jnp.where(live, sums[0:1], 1.0)
    pull = place * sums[0:1] - sums[1:4]
    score = jnp.where(live, -pull / (SCALE * EPS * EPS * clamped), 0.0)
    along_ref[...] = along_key_features(parts, score).T.astype(bf16)
    flux_ref[...] = weighted_rows(weight, score)

    place, score, live = place[:, 0:width], score[:, 0:width], live[:, 0:width]
    parts = [part[:, 0:width] for part in parts]
    row = lax.broadcasted_iota(jnp.int32, (FEATURES, width), 0)
    own_ref[0] = jnp.where(row < EXTRA_ROW, -query[:, 0:width], 0.0).astype(bf16)
    own_ref[1] = along_query_features(parts, score).astype(bf16)
    cubes_ref[...] = jnp.zeros_like(cubes_ref)
    linear_ref[...] = jnp.zeros_like(linear_ref)

    def pair_products(chunk, square_ref, dot_ref):
        keys = slots(jnp.minimum(chunk, chunks - 1), CHUNK)
        square_ref[...] = product(key_ref[keys, :], own_ref[0])
        dot_ref[...] = product(along_ref[keys, :], own_ref[1])

    def add_drift(chunk, square_ref, dot_ref):
        keys = slots(chunk, CHUNK)
        square = jnp.maximum(square_ref[...], TINY)
        distance = square * lax.rsqrt(square)
        cubes_ref[...] += split_product(flux_ref[:, keys], square * distance)
        linear_ref[...] += split_product(moment_ref[:, keys], dot_ref[...] * distance)

    pair_products(0, even_ref, even_along_ref)

    def drift_pair(pair, carry):
        chunk = pair * 2
        pair_products(chunk + 1, odd_ref, odd_along_ref)
        add_drift(chunk, even_ref, even_along_ref)
        pair_products(chunk + 2, even_ref, even_along_ref)
        add_drift(chunk + 1, odd_ref, odd_along_ref)
        return carry

    lax.fori_loop(0, chunks // 2, drift_pair, 0)
    cubes, linear = joined(cubes_ref[...]), joined(linear_ref[...])
    drift = score * cubes[0:1] - cubes[1:4] - place * linear[0:1] + linear[1:4]
    drift = jnp.where(live, drift * (-1.0 / (SCALE * SCALE * SCALE * total_slots)), 0.0)
    largest = jnp.max(row_sum(drift * drift), axis=1, keepdims=True)
    speed_out[...] = jnp.broadcast_to(jnp.sqrt(largest), speed_out.shape)
    for part in range(width // 128):
        lanes = slice(part * 128, part * 128 + 128)
        for axis in range(3):
            scores_out[axis, part : part + 1, :] = score[axis : axis + 1, lanes]
            drift_out[axis, part : part + 1, :] = drift[axis : axis + 1, lanes]
            start_out[axis, part : part + 1, :] = blocks[0][0, axis : axis + 1, lanes]


def sweep(counts, blocks, order, copies):
    count, width = len(blocks), blocks[0].shape[2]
    slots = count * width
    parts = jax.ShapeDtypeStruct((3, width // 128, 128), f32)
    whole = pl.BlockSpec(memory_space=pltpu.VMEM)
    return pl.pallas_call(
        functools.partial(sweep_kernel, order),
        out_shape=(parts, parts, parts, jax.ShapeDtypeStruct((copies, 128), f32)),
        in_specs=[pl.BlockSpec(memory_space=pltpu.SMEM)] + [whole] * count,
        out_specs=(whole, whole, whole, whole),
        scratch_shapes=[
            pltpu.VMEM((slots, FEATURES), bf16),
            pltpu.VMEM((FEATURES, slots), bf16),
            pltpu.VMEM((3, slots, 128), f32),
            pltpu.VMEM((slots, FEATURES), bf16),
            pltpu.VMEM((16, slots), bf16),
            pltpu.VMEM((4, 8, slots), f32),
            pltpu.VMEM((16, width), f32),
            pltpu.VMEM((16, width), f32),
            pltpu.VMEM((CHUNK, width), f32),
            pltpu.VMEM((CHUNK, width), f32),
            pltpu.VMEM((CHUNK, width), f32),
            pltpu.VMEM((CHUNK, width), f32),
            pltpu.VMEM((2, FEATURES, width), bf16),
            pltpu.VMEM((16, slots), bf16),
        ],
        compiler_params=pltpu.CompilerParams(vmem_limit_bytes=(16 << 20) + slots * 2688),
        name="sweep",
    )(counts, *blocks)


def swapped(value, axis, step):
    pairs = [(i, i ^ step) for i in range(lax.axis_size(axis))]
    return lax.ppermute(value, axis, pairs)


def bits(size):
    return [1 << bit for bit in range(size.bit_length() - 1)]


def gathered(block):
    size = lax.axis_size("sharers")
    if size == 4:
        order = [0, 2, 1, 3]
        return [block] + [swapped(block, "sharers", step) for step in order[1:]], order
    for step in bits(size):
        block = jnp.concatenate([block, swapped(block, "sharers", step)], axis=0)
    return [block[i : i + 1] for i in range(size)], list(range(size))


def local(velocities, weights, counts):
    axes = ("cells", "sharers")
    blocks, order = gathered(jnp.concatenate([velocities, weights[:, None]], axis=1))
    copies = lax.axis_size(axes)
    scores, drift, start, speeds = sweep(counts, blocks, order, copies)
    speeds = lax.all_to_all(speeds.reshape(copies, 1, 128), axes, 0, 0, tiled=True)
    time_step = 0.5 / (jnp.max(speeds, axis=0, keepdims=True) + 1e-06)
    moved = start + time_step * drift
    return moved.reshape(velocities.shape), scores.reshape(velocities.shape)


def solution(mesh):
    in_specs = (
        P(("groups", "cells"), None, "sharers"),
        P(("groups", "cells"), "sharers"),
        P(("groups", "cells")),
    )
    out_specs = (P(("groups", "cells"), None, "sharers"), P(("groups", "cells"), None, "sharers"))
    return jax.shard_map(local, mesh=mesh, in_specs=in_specs, out_specs=out_specs, check_vma=False)
```

```python
import functools
import functools
import math

import jax
import jax.numpy as jnp
from jax import lax
from jax.experimental import pallas as pl
from jax.experimental.pallas import tpu as pltpu
from jax.sharding import PartitionSpec as P

EPS = 0.35
SCALE = math.sqrt(math.log2(math.e) / (2.0 * EPS * EPS))
GRID = 4.0
TINY = 1e-30
CHUNK = 512
FEATURES = 48
bf16, f32 = jnp.bfloat16, jnp.float32


def round_bf16(value):
    return value.astype(bf16).astype(f32)


def pieces(value, count):
    parts = []
    for _ in range(count):
        part = round_bf16(value)
        parts.append(part)
        value = value - part
    return parts


def padded(rows, height):
    filled = sum(row.shape[0] for row in rows)
    width = rows[0].shape[1]
    if filled < height:
        rows = rows + [jnp.zeros((height - filled, width), f32)]
    return jnp.concatenate(rows, axis=0)


def row_sum(value):
    return value[0:1] + value[1:2] + value[2:3]


def grid_parts(place):
    coarse = jnp.floor(place * GRID + 0.5) * (1.0 / GRID)
    return [coarse] + pieces(place - coarse, 2)


def distance_features(place):
    coarse, fine, rest = grid_parts(place)
    minor = place - coarse
    ones = jnp.ones_like(place)
    coarse_norm = jnp.concatenate(pieces(-row_sum(coarse * coarse), 3), axis=0)
    minor_norm = jnp.concatenate(
        pieces(-row_sum(minor * (2.0 * coarse + minor)), 3), axis=0
    )
    key_rows = [coarse, ones, coarse_norm, coarse, coarse, fine, rest, ones, minor_norm]
    key_rows += [fine, fine, rest, rest]
    query_rows = [coarse, coarse_norm, ones, fine, rest, coarse, coarse, minor_norm, ones]
    query_rows += [fine, rest, fine, rest]
    doubled = (0, 3, 4, 5, 6, 9, 10, 11, 12)
    query_rows = [row * 2.0 if i in doubled else row for i, row in enumerate(query_rows)]
    return padded(key_rows, FEATURES), padded(query_rows, FEATURES)


def along_key_features(place, score):
    coarse, fine, rest = grid_parts(place)
    first, second, third = pieces(score, 3)
    ones = jnp.ones_like(place)
    dot = jnp.concatenate(pieces(row_sum(place * score), 3), axis=0)
    rows = [ones, dot, -first, -second, -third, -first, -second, -first]
    rows += [coarse, coarse, coarse, fine, fine, rest]
    return padded(rows, FEATURES)


def along_query_features(place, score):
    coarse, fine, rest = grid_parts(place)
    first, second, third = pieces(score, 3)
    ones = jnp.ones_like(place)
    dot = jnp.concatenate(pieces(row_sum(place * score), 3), axis=0)
    rows = [dot, ones, coarse, coarse, coarse, fine, fine, rest]
    rows += [-first, -second, -third, -first, -second, -first]
    return padded(rows, FEATURES)


def weighted_rows(weight, value):
    whole = jnp.concatenate([weight, weight * value], axis=0)
    return padded(pieces(whole, 3), 16).astype(bf16)


def product(left, right):
    return jnp.dot(left, right, preferred_element_type=f32)


def split_product(left, matrix):
    upper = matrix.astype(bf16)
    lower = (matrix - upper.astype(f32)).astype(bf16)
    return product(
        jnp.concatenate([left, left], axis=1), jnp.concatenate([upper, lower], axis=0)
    )


def joined(total):
    return total[0:4] + total[4:8] + total[8:12]


def sweep_kernel(order, *refs):
    count = len(order)
    filled, blocks, refs = refs[0], refs[1 : count + 1], refs[count + 1 :]
    scores_out, drift_out, start_out, speed_out, key_ref, query_ref, moment_ref = refs[:7]
    along_ref, flux_ref, sums_ref, cubes_ref, linear_ref, even_ref, odd_ref = refs[7:14]
    own_exponent_ref, own_along_ref = refs[14:]
    width = blocks[0].shape[2]
    total_slots = count * width
    chunks = total_slots // CHUNK
    steps = chunks * count
    here = lax.axis_index("sharers")

    def slots(index, size):
        return pl.ds(pl.multiple_of(index * size, size), size)

    lane = lax.broadcasted_iota(jnp.int32, (1, width), 1)
    live = [lane + (here ^ step) * width < filled[0] for step in order]
    weight = jnp.concatenate(
        [jnp.where(on, block[0, 3:4], 0.0) for on, block in zip(live, blocks)], axis=1
    )
    place = jnp.concatenate([block[0, 0:3] for block in blocks], axis=1) * SCALE
    key, query = distance_features(place)
    key_ref[...] = key.T.astype(bf16)
    query_ref[...] = query.astype(bf16)
    moment_ref[...] = weighted_rows(weight, place)
    sums_ref[...] = jnp.zeros_like(sums_ref)

    def exponent(step):
        step = jnp.minimum(step, steps - 1)
        tile, chunk = step // chunks, step % chunks
        return product(key_ref[slots(chunk, CHUNK), :], query_ref[:, slots(tile, width)])

    def add_blobs(step, ref):
        tile, chunk = step // chunks, step % chunks
        sums_ref[:, slots(tile, width)] += split_product(
            moment_ref[:, slots(chunk, CHUNK)], jnp.exp2(ref[...])
        )

    own_exponent_ref[slots(0, CHUNK), :] = exponent(0)

    def own_density(chunk, carry):
        later = jnp.minimum(chunk + 1, chunks - 1)
        own_exponent_ref[slots(later, CHUNK), :] = exponent(later)
        add_blobs(chunk, own_exponent_ref.at[slots(chunk, CHUNK), :])
        return carry

    lax.fori_loop(0, chunks, own_density, 0, unroll=count <= 4)
    even_ref[...] = exponent(chunks)

    def density(pair, carry):
        step = chunks + pair * 2
        odd_ref[...] = exponent(step + 1)
        add_blobs(step, even_ref)
        even_ref[...] = exponent(step + 2)
        add_blobs(step + 1, odd_ref)
        return carry

    lax.fori_loop(0, (steps - chunks) // 2, density, 0)

    sums = joined(sums_ref[...])
    live = weight > 0.0
    clamped = jnp.where(live, sums[0:1], 1.0)
    pull = place * sums[0:1] - sums[1:4]
    score = jnp.where(live, -pull / (SCALE * EPS * EPS * clamped), 0.0)
    along_ref[...] = along_key_features(place, score).T.astype(bf16)
    flux_ref[...] = weighted_rows(weight, score)

    place, score, live = place[:, 0:width], score[:, 0:width], live[:, 0:width]
    own_along_ref[...] = along_query_features(place, score).astype(bf16)
    cubes_ref[...] = jnp.zeros_like(cubes_ref)
    linear_ref[...] = jnp.zeros_like(linear_ref)

    def along(chunk):
        keys = slots(jnp.minimum(chunk, chunks - 1), CHUNK)
        return product(along_ref[keys, :], own_along_ref[...])

    def add_drift(chunk, ref):
        keys = slots(chunk, CHUNK)
        negative = jnp.minimum(own_exponent_ref[keys, :], -TINY)
        distance = negative * lax.rsqrt(-negative)
        cubes_ref[...] += split_product(flux_ref[:, keys], negative * distance)
        linear_ref[...] += split_product(moment_ref[:, keys], ref[...] * distance)

    even_ref[...] = along(0)

    def drift_pair(pair, carry):
        chunk = pair * 2
        odd_ref[...] = along(chunk + 1)
        add_drift(chunk, even_ref)
        even_ref[...] = along(chunk + 2)
        add_drift(chunk + 1, odd_ref)
        return carry

    lax.fori_loop(0, chunks // 2, drift_pair, 0)
    cubes, linear = joined(cubes_ref[...]), joined(linear_ref[...])
    drift = score * cubes[0:1] - cubes[1:4] + place * linear[0:1] - linear[1:4]
    drift = jnp.where(live, drift * (-1.0 / (SCALE * SCALE * SCALE * total_slots)), 0.0)
    largest = jnp.max(row_sum(drift * drift), axis=1, keepdims=True)
    speed_out[...] = jnp.broadcast_to(jnp.sqrt(largest), speed_out.shape)
    for part in range(width // 128):
        lanes = slice(part * 128, part * 128 + 128)
        for axis in range(3):
            scores_out[axis, part : part + 1, :] = score[axis : axis + 1, lanes]
            drift_out[axis, part : part + 1, :] = drift[axis : axis + 1, lanes]
            start_out[axis, part : part + 1, :] = blocks[0][0, axis : axis + 1, lanes]


def sweep(counts, blocks, order, copies):
    count, width = len(blocks), blocks[0].shape[2]
    slots = count * width
    parts = jax.ShapeDtypeStruct((3, width // 128, 128), f32)
    whole = pl.BlockSpec(memory_space=pltpu.VMEM)
    return pl.pallas_call(
        functools.partial(sweep_kernel, order),
        out_shape=(parts, parts, parts, jax.ShapeDtypeStruct((copies, 128), f32)),
        in_specs=[pl.BlockSpec(memory_space=pltpu.SMEM)] + [whole] * count,
        out_specs=(whole, whole, whole, whole),
        scratch_shapes=[
            pltpu.VMEM((slots, FEATURES), bf16),
            pltpu.VMEM((FEATURES, slots), bf16),
            pltpu.VMEM((16, slots), bf16),
            pltpu.VMEM((slots, FEATURES), bf16),
            pltpu.VMEM((16, slots), bf16),
            pltpu.VMEM((16, slots), f32),
            pltpu.VMEM((16, width), f32),
            pltpu.VMEM((16, width), f32),
            pltpu.VMEM((CHUNK, width), f32),
            pltpu.VMEM((CHUNK, width), f32),
            pltpu.VMEM((slots, width), f32),
            pltpu.VMEM((FEATURES, width), bf16),
        ],
        compiler_params=pltpu.CompilerParams(vmem_limit_bytes=(16 << 20) + slots * 2688),
        name="sweep",
    )(counts, *blocks)


def swapped(value, axis, step):
    pairs = [(i, i ^ step) for i in range(lax.axis_size(axis))]
    return lax.ppermute(value, axis, pairs)


def bits(size):
    return [1 << bit for bit in range(size.bit_length() - 1)]


def gathered(block):
    size = lax.axis_size("sharers")
    if size == 4:
        order = [0, 2, 1, 3]
        return [block] + [swapped(block, "sharers", step) for step in order[1:]], order
    for step in bits(size):
        block = jnp.concatenate([block, swapped(block, "sharers", step)], axis=0)
    return [block[i : i + 1] for i in range(size)], list(range(size))


def local(velocities, weights, counts):
    axes = ("cells", "sharers")
    blocks, order = gathered(jnp.concatenate([velocities, weights[:, None]], axis=1))
    copies = lax.axis_size(axes)
    scores, drift, start, speeds = sweep(counts, blocks, order, copies)
    speeds = lax.all_to_all(speeds.reshape(copies, 1, 128), axes, 0, 0, tiled=True)
    time_step = 0.5 / (jnp.max(speeds, axis=0, keepdims=True) + 1e-06)
    moved = start + time_step * drift
    return moved.reshape(velocities.shape), scores.reshape(velocities.shape)


def solution(mesh):
    in_specs = (
        P(("groups", "cells"), None, "sharers"),
        P(("groups", "cells"), "sharers"),
        P(("groups", "cells")),
    )
    out_specs = (P(("groups", "cells"), None, "sharers"), P(("groups", "cells"), None, "sharers"))
    return jax.shard_map(local, mesh=mesh, in_specs=in_specs, out_specs=out_specs, check_vma=False)
```

```python
import functools
import functools
import math

import jax
import jax.numpy as jnp
from jax import lax
from jax.experimental import pallas as pl
from jax.experimental.pallas import tpu as pltpu
from jax.sharding import PartitionSpec as P

EPS = 0.35
SCALE = math.sqrt(math.log2(math.e) / (2.0 * EPS * EPS))
GRID = 4.0
TINY = 1e-30
CHUNK = 512
DISTANCE_ROWS = 96
ALONG_ROWS = 112
bf16, f32 = jnp.bfloat16, jnp.float32


def round_bf16(value):
    return value.astype(bf16).astype(f32)


def pieces(value, count):
    parts = []
    for _ in range(count):
        part = round_bf16(value)
        parts.append(part)
        value = value - part
    return parts


def row_of(value):
    return lax.broadcasted_iota(jnp.int32, value.shape, 0)


def rows_sum(value):
    return jnp.sum(value, axis=0, keepdims=True)


def stacked(groups):
    if len(groups) % 2:
        groups = groups + [jnp.zeros_like(groups[0])]
    return jnp.concatenate(groups, axis=0).astype(bf16)


def scalar_groups(value, like):
    row = row_of(like)
    first, second, third = pieces(value, 3)
    low = jnp.where(row == 0, first, jnp.where(row == 1, second, jnp.where(row == 2, third, 0.0)))
    high = jnp.where(row == 3, first, jnp.where(row == 4, second, jnp.where(row == 5, third, 0.0)))
    ones_low, ones_high = row < 3, (row >= 3) & (row < 6)
    return jnp.where(ones_high, 1.0, low), jnp.where(ones_low, 1.0, high)


def grid_parts(place):
    coarse = jnp.floor(place * GRID + 0.5) * (1.0 / GRID)
    return [coarse] + pieces(place - coarse, 2)


def distance_features(parts):
    coarse, fine, rest = parts
    minor = fine + rest
    query_norm, key_norm = scalar_groups(-rows_sum(coarse * coarse), coarse)
    query_less, key_less = scalar_groups(-rows_sum(minor * (2.0 * coarse + minor)), coarse)
    key = [coarse, key_norm, coarse, coarse, fine, rest, key_less, fine, fine, rest, rest]
    coarse, fine, rest = coarse * 2.0, fine * 2.0, rest * 2.0
    query = [coarse, query_norm, fine, rest, coarse, coarse, query_less, fine, rest, fine, rest]
    return stacked(key), stacked(query)


def along_features(parts, score, is_key):
    coarse, fine, rest = parts
    first, second, third = pieces(-score, 3)
    query_dot, key_dot = scalar_groups(rows_sum((coarse + fine + rest) * score), coarse)
    places = [coarse, coarse, coarse, fine, fine, rest]
    turns = [first, second, third, first, second, first]
    if is_key:
        return stacked([key_dot] + turns + places)
    return stacked([query_dot] + places + turns)


def weighted_rows(weight, value):
    row = row_of(value)
    whole = jnp.where(row < 3, value, jnp.where(row == 3, 1.0, 0.0)) * weight
    first, second, third = pieces(whole, 3)
    return stacked([first, second + pltpu.roll(third, 4, 0)])


def product(left, right):
    return jnp.dot(left, right, preferred_element_type=f32)


def split_product(left, matrix):
    upper = matrix.astype(bf16)
    lower = (matrix - upper.astype(f32)).astype(bf16)
    return product(
        jnp.concatenate([left, left], axis=1), jnp.concatenate([upper, lower], axis=0)
    )


def joined(total):
    upper, lower = total[0:8], total[8:16]
    return upper + lower + pltpu.roll(lower, 4, 0)


def sweep_kernel(order, *refs):
    count = len(order)
    filled, blocks, refs = refs[0], refs[1 : count + 1], refs[count + 1 :]
    scores_out, drift_out, start_out, speed_out, key_ref, query_ref, moment_ref = refs[:7]
    along_ref, flux_ref, sums_ref, cubes_ref, linear_ref, even_ref, odd_ref = refs[7:14]
    own_exponent_ref, own_along_ref = refs[14:]
    width = blocks[0].shape[2]
    total_slots = count * width
    chunks = total_slots // CHUNK
    steps = chunks * count
    here = lax.axis_index("sharers")

    def slots(index, size):
        return pl.ds(pl.multiple_of(index * size, size), size)

    lane = lax.broadcasted_iota(jnp.int32, (1, width), 1)
    live = [lane + (here ^ step) * width < filled[0] for step in order]
    weight = jnp.concatenate(
        [jnp.where(on, block[0, 3:4], 0.0) for on, block in zip(live, blocks)], axis=1
    )
    whole = jnp.concatenate([block[0] for block in blocks], axis=1)
    vector = row_of(whole) < 3
    parts = grid_parts(jnp.where(vector, whole * SCALE, 0.0))
    place = parts[0] + parts[1] + parts[2]
    key, query = distance_features(parts)
    key_ref[...] = key.T
    query_ref[...] = query
    moment_ref[...] = weighted_rows(weight, place)
    sums_ref[...] = jnp.zeros_like(sums_ref)

    def exponent(step):
        step = jnp.minimum(step, steps - 1)
        tile, chunk = step // chunks, step % chunks
        return product(key_ref[slots(chunk, CHUNK), :], query_ref[:, slots(tile, width)])

    def add_blobs(step, ref):
        tile, chunk = step // chunks, step % chunks
        sums_ref[:, slots(tile, width)] += split_product(
            moment_ref[:, slots(chunk, CHUNK)], jnp.exp2(ref[...])
        )

    own_exponent_ref[slots(0, CHUNK), :] = exponent(0)

    def own_density(chunk, carry):
        later = jnp.minimum(chunk + 1, chunks - 1)
        own_exponent_ref[slots(later, CHUNK), :] = exponent(later)
        add_blobs(chunk, own_exponent_ref.at[slots(chunk, CHUNK), :])
        return carry

    lax.fori_loop(0, chunks, own_density, 0, unroll=count <= 4)
    even_ref[...] = exponent(chunks)

    def density(pair, carry):
        step = chunks + pair * 2
        odd_ref[...] = exponent(step + 1)
        add_blobs(step, even_ref)
        even_ref[...] = exponent(step + 2)
        add_blobs(step + 1, odd_ref)
        return carry

    lax.fori_loop(0, (steps - chunks) // 2, density, 0)

    sums = joined(sums_ref[...])
    live = weight > 0.0
    density_sum = jnp.where(live, sums[3:4], 1.0)
    pull = place * density_sum - sums
    score = jnp.where(vector & live, pull / (-SCALE * EPS * EPS * density_sum), 0.0)
    along_ref[...] = along_features(parts, score, True).T
    flux_ref[...] = weighted_rows(weight, score)

    place, score, live = place[:, 0:width], score[:, 0:width], live[:, 0:width]
    own_along_ref[...] = along_features([part[:, 0:width] for part in parts], score, False)
    cubes_ref[...] = jnp.zeros_like(cubes_ref)
    linear_ref[...] = jnp.zeros_like(linear_ref)

    def along(chunk):
        keys = slots(jnp.minimum(chunk, chunks - 1), CHUNK)
        return product(along_ref[keys, :], own_along_ref[...])

    def add_drift(chunk, ref):
        keys = slots(chunk, CHUNK)
        negative = jnp.minimum(own_exponent_ref[keys, :], -TINY)
        distance = negative * lax.rsqrt(-negative)
        cubes_ref[...] += split_product(flux_ref[:, keys], negative * distance)
        linear_ref[...] += split_product(moment_ref[:, keys], ref[...] * distance)

    even_ref[...] = along(0)

    def drift_pair(pair, carry):
        chunk = pair * 2
        odd_ref[...] = along(chunk + 1)
        add_drift(chunk, even_ref)
        even_ref[...] = along(chunk + 2)
        add_drift(chunk + 1, odd_ref)
        return carry

    lax.fori_loop(0, chunks // 2, drift_pair, 0)
    cubes, linear = joined(cubes_ref[...]), joined(linear_ref[...])
    drift = score * cubes[3:4] - cubes + place * linear[3:4] - linear
    factor = -1.0 / (SCALE * SCALE * SCALE * total_slots)
    drift = jnp.where(live & vector[:, 0:width], drift * factor, 0.0)
    largest = jnp.max(rows_sum(drift * drift), axis=1, keepdims=True)
    speed_out[...] = jnp.broadcast_to(jnp.sqrt(largest), speed_out.shape)
    for part in range(width // 128):
        lanes = slice(part * 128, part * 128 + 128)
        for axis in range(3):
            scores_out[axis, part : part + 1, :] = score[axis : axis + 1, lanes]
            drift_out[axis, part : part + 1, :] = drift[axis : axis + 1, lanes]
            start_out[axis, part : part + 1, :] = blocks[0][0, axis : axis + 1, lanes]


def sweep(counts, blocks, order, copies):
    count, width = len(blocks), blocks[0].shape[2]
    slots = count * width
    parts = jax.ShapeDtypeStruct((3, width // 128, 128), f32)
    whole = pl.BlockSpec(memory_space=pltpu.VMEM)
    return pl.pallas_call(
        functools.partial(sweep_kernel, order),
        out_shape=(parts, parts, parts, jax.ShapeDtypeStruct((copies, 128), f32)),
        in_specs=[pl.BlockSpec(memory_space=pltpu.SMEM)] + [whole] * count,
        out_specs=(whole, whole, whole, whole),
        scratch_shapes=[
            pltpu.VMEM((slots, DISTANCE_ROWS), bf16),
            pltpu.VMEM((DISTANCE_ROWS, slots), bf16),
            pltpu.VMEM((16, slots), bf16),
            pltpu.VMEM((slots, ALONG_ROWS), bf16),
            pltpu.VMEM((16, slots), bf16),
            pltpu.VMEM((16, slots), f32),
            pltpu.VMEM((16, width), f32),
            pltpu.VMEM((16, width), f32),
            pltpu.VMEM((CHUNK, width), f32),
            pltpu.VMEM((CHUNK, width), f32),
            pltpu.VMEM((slots, width), f32),
            pltpu.VMEM((ALONG_ROWS, width), bf16),
        ],
        compiler_params=pltpu.CompilerParams(vmem_limit_bytes=(16 << 20) + slots * 2688),
        name="sweep",
    )(counts, *blocks)


def swapped(value, axis, step):
    pairs = [(i, i ^ step) for i in range(lax.axis_size(axis))]
    return lax.ppermute(value, axis, pairs)


def bits(size):
    return [1 << bit for bit in range(size.bit_length() - 1)]


def gathered(block):
    size = lax.axis_size("sharers")
    if size == 4:
        order = [0, 2, 1, 3]
        return [block] + [swapped(block, "sharers", step) for step in order[1:]], order
    for step in bits(size):
        block = jnp.concatenate([block, swapped(block, "sharers", step)], axis=0)
    return [block[i : i + 1] for i in range(size)], list(range(size))


def local(velocities, weights, counts):
    axes = ("cells", "sharers")
    blocks, order = gathered(
        jnp.pad(jnp.concatenate([velocities, weights[:, None]], axis=1), ((0, 0), (0, 4), (0, 0)))
    )
    copies = lax.axis_size(axes)
    scores, drift, start, speeds = sweep(counts, blocks, order, copies)
    speeds = lax.all_to_all(speeds.reshape(copies, 1, 128), axes, 0, 0, tiled=True)
    time_step = 0.5 / (jnp.max(speeds, axis=0, keepdims=True) + 1e-06)
    moved = start + time_step * drift
    return moved.reshape(velocities.shape), scores.reshape(velocities.shape)


def solution(mesh):
    in_specs = (
        P(("groups", "cells"), None, "sharers"),
        P(("groups", "cells"), "sharers"),
        P(("groups", "cells")),
    )
    out_specs = (P(("groups", "cells"), None, "sharers"), P(("groups", "cells"), None, "sharers"))
    return jax.shard_map(local, mesh=mesh, in_specs=in_specs, out_specs=out_specs, check_vma=False)
```

```python
import functools
import functools
import math

import jax
import jax.numpy as jnp
from jax import lax
from jax.experimental import pallas as pl
from jax.experimental.pallas import tpu as pltpu
from jax.sharding import PartitionSpec as P

EPS = 0.35
SCALE = math.sqrt(math.log2(math.e) / (2.0 * EPS * EPS))
GRID = 4.0
TINY = 1e-30
DEAD = -20000.0
CHUNK = 512
KEPT_BLOCKS = 4
DISTANCE_ROWS = 96
ALONG_ROWS = 112
bf16, f32 = jnp.bfloat16, jnp.float32


def round_bf16(value):
    return value.astype(bf16).astype(f32)


def pieces(value, count):
    parts = []
    for _ in range(count):
        part = round_bf16(value)
        parts.append(part)
        value = value - part
    return parts


def row_of(value):
    return lax.broadcasted_iota(jnp.int32, value.shape, 0)


def rows_sum(value):
    return jnp.sum(value, axis=0, keepdims=True)


def stacked(groups):
    if len(groups) % 2:
        groups = groups + [jnp.zeros_like(groups[0])]
    return jnp.concatenate(groups, axis=0).astype(bf16)


def scalar_groups(value, like):
    row = row_of(like)
    first, second, third = pieces(value, 3)
    low = jnp.where(row == 0, first, jnp.where(row == 1, second, jnp.where(row == 2, third, 0.0)))
    high = jnp.where(row == 3, first, jnp.where(row == 4, second, jnp.where(row == 5, third, 0.0)))
    ones_low, ones_high = row < 3, (row >= 3) & (row < 6)
    return jnp.where(ones_high, 1.0, low), jnp.where(ones_low, 1.0, high)


def grid_parts(place):
    coarse = jnp.floor(place * GRID + 0.5) * (1.0 / GRID)
    return [coarse] + pieces(place - coarse, 2)


def distance_features(parts, key_extra, query_extra):
    coarse, fine, rest = parts
    minor = fine + rest
    query_norm, key_norm = scalar_groups(-rows_sum(coarse * coarse), coarse)
    query_less, key_less = scalar_groups(-rows_sum(minor * (2.0 * coarse + minor)), coarse)
    key = [coarse, key_norm, coarse, coarse, fine, rest, key_less, fine, fine, rest, rest]
    coarse, fine, rest = coarse * 2.0, fine * 2.0, rest * 2.0
    query = [coarse, query_norm, fine, rest, coarse, coarse, query_less, fine, rest, fine, rest]
    return stacked(key + [key_extra]), stacked(query + [query_extra])


def along_features(parts, score, is_key):
    coarse, fine, rest = parts
    first, second, third = pieces(-score, 3)
    query_dot, key_dot = scalar_groups(rows_sum((coarse + fine + rest) * score), coarse)
    places = [coarse, coarse, coarse, fine, fine, rest]
    turns = [first, second, third, first, second, first]
    if is_key:
        return stacked([key_dot] + turns + places)
    return stacked([query_dot] + places + turns)


def weighted_rows(weight, value):
    row = row_of(value)
    whole = jnp.where(row < 3, value, jnp.where(row == 3, 1.0, 0.0)) * weight
    first, second, third = pieces(whole, 3)
    return stacked([first, second + pltpu.roll(third, 4, 0)])


def product(left, right):
    return jnp.dot(left, right, preferred_element_type=f32)


def store_split(ref, rows, matrix):
    upper = matrix.astype(bf16)
    ref[rows, :] = upper
    half = ref.shape[0] // 2
    ref[pl.ds(half + rows.start, rows.size), :] = (matrix - upper.astype(f32)).astype(bf16)


def split_product(left, ref):
    return product(jnp.concatenate([left, left], axis=1), ref[...])


def joined(total):
    upper, lower = total[0:8], total[8:16]
    return upper + lower + pltpu.roll(lower, 4, 0)


def sweep_kernel(order, *refs):
    count = len(order)
    filled, blocks, refs = refs[0], refs[1 : count + 1], refs[count + 1 :]
    scores_out, drift_out, start_out, speed_out, key_ref, query_ref, moment_ref = refs[:7]
    along_ref, flux_ref, sums_ref, cubes_ref, linear_ref, even_ref, odd_ref = refs[7:14]
    own_exponent_ref, own_along_ref, across_ref = refs[14:17]
    even_cubes_ref, even_linear_ref, odd_cubes_ref, odd_linear_ref = refs[17:]
    width = blocks[0].shape[2]
    total_slots = count * width
    chunks = total_slots // CHUNK
    steps = chunks * count
    kept = count <= KEPT_BLOCKS
    here = lax.axis_index("sharers")

    def slots(index, size):
        return pl.ds(pl.multiple_of(index * size, size), size)

    lane = lax.broadcasted_iota(jnp.int32, (1, width), 1)
    live = [lane + (here ^ step) * width < filled[0] for step in order]
    weight = jnp.concatenate(
        [jnp.where(on, block[0, 3:4], 0.0) for on, block in zip(live, blocks)], axis=1
    )
    whole = jnp.concatenate([block[0] for block in blocks], axis=1)
    vector = row_of(whole) < 3
    parts = grid_parts(jnp.where(vector, whole * SCALE, 0.0))
    place = parts[0] + parts[1] + parts[2]
    live = weight > 0.0
    row = row_of(whole)
    log_weight = jnp.where(live, jnp.log2(jnp.where(live, weight, 1.0)), DEAD)
    other = lax.broadcasted_iota(jnp.int32, whole.shape, 1) >= width
    key, query = distance_features(
        parts, scalar_groups(log_weight, whole)[0], jnp.where(other & (row < 3), 1.0, 0.0)
    )
    key_ref[...] = key.T
    query_ref[...] = query
    across_ref[...] = jnp.where(row == 3, weight, place).T
    moment_ref[...] = weighted_rows(weight, place)
    sums_ref[...] = jnp.zeros_like(sums_ref)

    def exponent(step):
        step = jnp.minimum(step, steps - 1)
        tile, chunk = step // chunks, step % chunks
        return product(key_ref[slots(chunk, CHUNK), :], query_ref[:, slots(tile, width)])

    def add_blobs(step, ref, first=0, weigh=False):
        tile, chunk = step // chunks, step % chunks
        parts = width // 128
        totals = [[jnp.zeros((8, 128), f32)] * 4 for _ in range(parts)]
        for group in range(0, CHUNK, 8):
            keys = pl.ds(pl.multiple_of(chunk * CHUNK + group, 8), 8)
            across = across_ref[keys, :]
            columns = [
                jnp.broadcast_to(across[:, axis : axis + 1], (8, 128))
                for axis in range(4 if weigh else 3)
            ]
            for part in range(parts):
                rows = pl.ds(first + group, 8)
                blob = jnp.exp2(ref[rows, part * 128 : part * 128 + 128])
                if weigh:
                    blob = blob * columns[3]
                terms = [blob * column for column in columns[:3]] + [blob]
                totals[part] = [total + term for total, term in zip(totals[part], terms)]
        for part in range(parts):
            lanes = pl.ds(pl.multiple_of(tile * width + part * 128, 128), 128)
            for i in range(4):
                sums_ref[i, :, lanes] += totals[part][i]

    own_exponent_ref[0:CHUNK, :] = exponent(0)
    if kept:
        for chunk in range(chunks):
            if chunk + 1 < chunks:
                own_exponent_ref[slots(chunk + 1, CHUNK), :] = exponent(chunk + 1)
            add_blobs(chunk, own_exponent_ref, chunk * CHUNK, True)
    else:

        def own_density(chunk, carry):
            add_blobs(chunk, own_exponent_ref, 0, True)
            own_exponent_ref[...] = exponent(chunk + 1)
            return carry

        lax.fori_loop(0, chunks, own_density, 0)
    even_ref[...] = exponent(chunks)

    def density(pair, carry):
        step = chunks + pair * 2
        odd_ref[...] = exponent(step + 1)
        add_blobs(step, even_ref)
        even_ref[...] = exponent(step + 2)
        add_blobs(step + 1, odd_ref)
        return carry

    lax.fori_loop(0, (steps - chunks) // 2, density, 0)

    sums = [rows_sum(sums_ref[i]) for i in range(4)]
    density_sum = jnp.where(live, sums[3], 1.0)
    sums = jnp.where(row == 0, sums[0], jnp.where(row == 1, sums[1], sums[2]))
    pull = place * density_sum - sums
    score = jnp.where(vector & live, pull / (-SCALE * EPS * EPS * density_sum), 0.0)
    along_ref[...] = along_features(parts, score, True).T
    flux_ref[...] = weighted_rows(weight, score)

    place, score, live = place[:, 0:width], score[:, 0:width], live[:, 0:width]
    own_along_ref[...] = along_features([part[:, 0:width] for part in parts], score, False)
    cubes_ref[...] = jnp.zeros_like(cubes_ref)
    linear_ref[...] = jnp.zeros_like(linear_ref)

    def along(chunk):
        keys = slots(jnp.minimum(chunk, chunks - 1), CHUNK)
        return product(along_ref[keys, :], own_along_ref[...])

    def add_drift(chunk, ref, cubes_split, linear_split):
        if not kept:
            own_exponent_ref[...] = exponent(chunk)
        for group in range(0, CHUNK, 16):
            rows = pl.ds(group, 16)
            keys = pl.ds(pl.multiple_of(chunk * CHUNK + group, 16), 16)
            negative = jnp.minimum(own_exponent_ref[keys if kept else rows, :], -TINY)
            distance = negative * lax.rsqrt(-negative)
            store_split(cubes_split, rows, negative * distance)
            store_split(linear_split, rows, ref[rows, :] * distance)
        keys = slots(chunk, CHUNK)
        cubes_ref[...] += split_product(flux_ref[:, keys], cubes_split)
        linear_ref[...] += split_product(moment_ref[:, keys], linear_split)

    even_ref[...] = along(0)

    def drift_pair(pair, carry):
        chunk = pair * 2
        odd_ref[...] = along(chunk + 1)
        add_drift(chunk, even_ref, even_cubes_ref, even_linear_ref)
        even_ref[...] = along(chunk + 2)
        add_drift(chunk + 1, odd_ref, odd_cubes_ref, odd_linear_ref)
        return carry

    lax.fori_loop(0, chunks // 2, drift_pair, 0)
    cubes, linear = joined(cubes_ref[...]), joined(linear_ref[...])
    drift = score * cubes[3:4] - cubes + place * linear[3:4] - linear
    factor = -1.0 / (SCALE * SCALE * SCALE * total_slots)
    drift = jnp.where(live & vector[:, 0:width], drift * factor, 0.0)
    largest = jnp.max(rows_sum(drift * drift), axis=1, keepdims=True)
    speed_out[...] = jnp.broadcast_to(jnp.sqrt(largest), speed_out.shape)
    for part in range(width // 128):
        lanes = slice(part * 128, part * 128 + 128)
        for axis in range(3):
            scores_out[axis, part : part + 1, :] = score[axis : axis + 1, lanes]
            drift_out[axis, part : part + 1, :] = drift[axis : axis + 1, lanes]
            start_out[axis, part : part + 1, :] = blocks[0][0, axis : axis + 1, lanes]


def sweep(counts, blocks, order, copies):
    count, width = len(blocks), blocks[0].shape[2]
    slots = count * width
    parts = jax.ShapeDtypeStruct((3, width // 128, 128), f32)
    whole = pl.BlockSpec(memory_space=pltpu.VMEM)
    return pl.pallas_call(
        functools.partial(sweep_kernel, order),
        out_shape=(parts, parts, parts, jax.ShapeDtypeStruct((copies, 128), f32)),
        in_specs=[pl.BlockSpec(memory_space=pltpu.SMEM)] + [whole] * count,
        out_specs=(whole, whole, whole, whole),
        scratch_shapes=[
            pltpu.VMEM((slots, DISTANCE_ROWS), bf16),
            pltpu.VMEM((DISTANCE_ROWS, slots), bf16),
            pltpu.VMEM((16, slots), bf16),
            pltpu.VMEM((slots, ALONG_ROWS), bf16),
            pltpu.VMEM((16, slots), bf16),
            pltpu.VMEM((4, 8, slots), f32),
            pltpu.VMEM((16, width), f32),
            pltpu.VMEM((16, width), f32),
            pltpu.VMEM((CHUNK, width), f32),
            pltpu.VMEM((CHUNK, width), f32),
            pltpu.VMEM((slots if count <= KEPT_BLOCKS else CHUNK, width), f32),
            pltpu.VMEM((ALONG_ROWS, width), bf16),
            pltpu.VMEM((slots, 8), f32),
            pltpu.VMEM((2 * CHUNK, width), bf16),
            pltpu.VMEM((2 * CHUNK, width), bf16),
            pltpu.VMEM((2 * CHUNK, width), bf16),
            pltpu.VMEM((2 * CHUNK, width), bf16),
        ],
        compiler_params=pltpu.CompilerParams(vmem_limit_bytes=(16 << 20) + slots * 2688),
        name="sweep",
    )(counts, *blocks)


def swapped(value, axis, step):
    pairs = [(i, i ^ step) for i in range(lax.axis_size(axis))]
    return lax.ppermute(value, axis, pairs)


def bits(size):
    return [1 << bit for bit in range(size.bit_length() - 1)]


def gathered(block):
    size = lax.axis_size("sharers")
    if size == 4:
        order = [0, 2, 1, 3]
        return [block] + [swapped(block, "sharers", step) for step in order[1:]], order
    for step in bits(size):
        block = jnp.concatenate([block, swapped(block, "sharers", step)], axis=0)
    return [block[i : i + 1] for i in range(size)], list(range(size))


def local(velocities, weights, counts):
    axes = ("cells", "sharers")
    blocks, order = gathered(
        jnp.pad(jnp.concatenate([velocities, weights[:, None]], axis=1), ((0, 0), (0, 4), (0, 0)))
    )
    copies = lax.axis_size(axes)
    scores, drift, start, speeds = sweep(counts, blocks, order, copies)
    speeds = lax.all_to_all(speeds.reshape(copies, 1, 128), axes, 0, 0, tiled=True)
    time_step = 0.5 / (jnp.max(speeds, axis=0, keepdims=True) + 1e-06)
    moved = start + time_step * drift
    return moved.reshape(velocities.shape), scores.reshape(velocities.shape)


def solution(mesh):
    in_specs = (
        P(("groups", "cells"), None, "sharers"),
        P(("groups", "cells"), "sharers"),
        P(("groups", "cells")),
    )
    out_specs = (P(("groups", "cells"), None, "sharers"), P(("groups", "cells"), None, "sharers"))
    return jax.shard_map(local, mesh=mesh, in_specs=in_specs, out_specs=out_specs, check_vma=False)
```

```python
import functools
import functools
import math

import jax
import jax.numpy as jnp
from jax import lax
from jax.experimental import pallas as pl
from jax.experimental.pallas import tpu as pltpu
from jax.sharding import PartitionSpec as P

EPS = 0.35
SCALE = math.sqrt(1.0 / (2.0 * EPS * EPS))
GRID = 4.0
TINY = 1e-30
CHUNK = 512
DISTANCE_ROWS = 96
ALONG_ROWS = 112
bf16, f32 = jnp.bfloat16, jnp.float32


def round_bf16(value):
    return value.astype(bf16).astype(f32)


def pieces(value, count):
    parts = []
    for _ in range(count):
        part = round_bf16(value)
        parts.append(part)
        value = value - part
    return parts


def row_of(value):
    return lax.broadcasted_iota(jnp.int32, value.shape, 0)


def rows_sum(value):
    return jnp.sum(value, axis=0, keepdims=True)


def stacked(groups):
    if len(groups) % 2:
        groups = groups + [jnp.zeros_like(groups[0])]
    return jnp.concatenate(groups, axis=0).astype(bf16)


def scalar_groups(value, like):
    row = row_of(like)
    first, second, third = pieces(value, 3)
    low = jnp.where(row == 0, first, jnp.where(row == 1, second, jnp.where(row == 2, third, 0.0)))
    high = jnp.where(row == 3, first, jnp.where(row == 4, second, jnp.where(row == 5, third, 0.0)))
    ones_low, ones_high = row < 3, (row >= 3) & (row < 6)
    return jnp.where(ones_high, 1.0, low), jnp.where(ones_low, 1.0, high)


def grid_parts(place):
    coarse = jnp.floor(place * GRID + 0.5) * (1.0 / GRID)
    return [coarse] + pieces(place - coarse, 2)


def distance_features(parts):
    coarse, fine, rest = parts
    minor = fine + rest
    query_norm, key_norm = scalar_groups(-rows_sum(coarse * coarse), coarse)
    query_less, key_less = scalar_groups(-rows_sum(minor * (2.0 * coarse + minor)), coarse)
    key = [coarse, key_norm, coarse, coarse, fine, rest, key_less, fine, fine, rest, rest]
    coarse, fine, rest = coarse * 2.0, fine * 2.0, rest * 2.0
    query = [coarse, query_norm, fine, rest, coarse, coarse, query_less, fine, rest, fine, rest]
    return stacked(key), stacked(query)


def along_features(parts, score, is_key):
    coarse, fine, rest = parts
    first, second, third = pieces(-score, 3)
    query_dot, key_dot = scalar_groups(rows_sum((coarse + fine + rest) * score), coarse)
    places = [coarse, coarse, coarse, fine, fine, rest]
    turns = [first, second, third, first, second, first]
    if is_key:
        return stacked([key_dot] + turns + places)
    return stacked([query_dot] + places + turns)


def weighted_rows(weight, value):
    row = row_of(value)
    whole = jnp.where(row < 3, value, jnp.where(row == 3, 1.0, 0.0)) * weight
    first, second, third = pieces(whole, 3)
    return stacked([first, second + pltpu.roll(third, 4, 0)])


def product(left, right):
    return jnp.dot(left, right, preferred_element_type=f32)


def split_product(left, matrix):
    upper = matrix.astype(bf16)
    lower = (matrix - upper.astype(f32)).astype(bf16)
    return product(
        jnp.concatenate([left, left], axis=1), jnp.concatenate([upper, lower], axis=0)
    )


def joined(total):
    upper, lower = total[0:8], total[8:16]
    return upper + lower + pltpu.roll(lower, 4, 0)


def sweep_kernel(order, *refs):
    count = len(order)
    filled, blocks, refs = refs[0], refs[1 : count + 1], refs[count + 1 :]
    scores_out, drift_out, start_out, speed_out, key_ref, query_ref, moment_ref = refs[:7]
    along_ref, flux_ref, sums_ref, cubes_ref, linear_ref, even_ref, odd_ref = refs[7:14]
    own_exponent_ref, own_along_ref = refs[14:]
    width = blocks[0].shape[2]
    total_slots = count * width
    chunks = total_slots // CHUNK
    steps = chunks * count
    here = lax.axis_index("sharers")

    def slots(index, size):
        return pl.ds(pl.multiple_of(index * size, size), size)

    lane = lax.broadcasted_iota(jnp.int32, (1, width), 1)
    live = [lane + (here ^ step) * width < filled[0] for step in order]
    weight = jnp.concatenate(
        [jnp.where(on, block[0, 3:4], 0.0) for on, block in zip(live, blocks)], axis=1
    )
    whole = jnp.concatenate([block[0] for block in blocks], axis=1)
    vector = row_of(whole) < 3
    parts = grid_parts(jnp.where(vector, whole * SCALE, 0.0))
    place = parts[0] + parts[1] + parts[2]
    key, query = distance_features(parts)
    key_ref[...] = key.T
    query_ref[...] = query
    moment_ref[...] = weighted_rows(weight, place)
    sums_ref[...] = jnp.zeros_like(sums_ref)

    def exponent(step):
        step = jnp.minimum(step, steps - 1)
        tile, chunk = step // chunks, step % chunks
        return product(key_ref[slots(chunk, CHUNK), :], query_ref[:, slots(tile, width)])

    def add_blobs(step, ref):
        tile, chunk = step // chunks, step % chunks
        sums_ref[:, slots(tile, width)] += split_product(
            moment_ref[:, slots(chunk, CHUNK)], jnp.exp(ref[...])
        )

    own_exponent_ref[slots(0, CHUNK), :] = exponent(0)

    def own_density(chunk, carry):
        later = jnp.minimum(chunk + 1, chunks - 1)
        own_exponent_ref[slots(later, CHUNK), :] = exponent(later)
        add_blobs(chunk, own_exponent_ref.at[slots(chunk, CHUNK), :])
        return carry

    lax.fori_loop(0, chunks, own_density, 0, unroll=count <= 4)
    even_ref[...] = exponent(chunks)

    def density(pair, carry):
        step = chunks + pair * 2
        odd_ref[...] = exponent(step + 1)
        add_blobs(step, even_ref)
        even_ref[...] = exponent(step + 2)
        add_blobs(step + 1, odd_ref)
        return carry

    lax.fori_loop(0, (steps - chunks) // 2, density, 0)

    sums = joined(sums_ref[...])
    live = weight > 0.0
    density_sum = jnp.where(live, sums[3:4], 1.0)
    pull = place * density_sum - sums
    score = jnp.where(vector & live, pull / (-SCALE * EPS * EPS * density_sum), 0.0)
    along_ref[...] = along_features(parts, score, True).T
    flux_ref[...] = weighted_rows(weight, score)

    place, score, live = place[:, 0:width], score[:, 0:width], live[:, 0:width]
    own_along_ref[...] = along_features([part[:, 0:width] for part in parts], score, False)
    cubes_ref[...] = jnp.zeros_like(cubes_ref)
    linear_ref[...] = jnp.zeros_like(linear_ref)

    def along(chunk):
        keys = slots(jnp.minimum(chunk, chunks - 1), CHUNK)
        return product(along_ref[keys, :], own_along_ref[...])

    def add_drift(chunk, ref):
        keys = slots(chunk, CHUNK)
        negative = jnp.minimum(own_exponent_ref[keys, :], -TINY)
        distance = negative * lax.rsqrt(-negative)
        cubes_ref[...] += split_product(flux_ref[:, keys], negative * distance)
        linear_ref[...] += split_product(moment_ref[:, keys], ref[...] * distance)

    even_ref[...] = along(0)

    def drift_pair(pair, carry):
        chunk = pair * 2
        odd_ref[...] = along(chunk + 1)
        add_drift(chunk, even_ref)
        even_ref[...] = along(chunk + 2)
        add_drift(chunk + 1, odd_ref)
        return carry

    lax.fori_loop(0, chunks // 2, drift_pair, 0)
    cubes, linear = joined(cubes_ref[...]), joined(linear_ref[...])
    drift = score * cubes[3:4] - cubes + place * linear[3:4] - linear
    factor = -1.0 / (SCALE * SCALE * SCALE * total_slots)
    drift = jnp.where(live & vector[:, 0:width], drift * factor, 0.0)
    largest = jnp.max(rows_sum(drift * drift), axis=1, keepdims=True)
    speed_out[...] = jnp.broadcast_to(jnp.sqrt(largest), speed_out.shape)
    for part in range(width // 128):
        lanes = slice(part * 128, part * 128 + 128)
        for axis in range(3):
            scores_out[axis, part : part + 1, :] = score[axis : axis + 1, lanes]
            drift_out[axis, part : part + 1, :] = drift[axis : axis + 1, lanes]
            start_out[axis, part : part + 1, :] = blocks[0][0, axis : axis + 1, lanes]


def sweep(counts, blocks, order, copies):
    count, width = len(blocks), blocks[0].shape[2]
    slots = count * width
    parts = jax.ShapeDtypeStruct((3, width // 128, 128), f32)
    whole = pl.BlockSpec(memory_space=pltpu.VMEM)
    return pl.pallas_call(
        functools.partial(sweep_kernel, order),
        out_shape=(parts, parts, parts, jax.ShapeDtypeStruct((copies, 128), f32)),
        in_specs=[pl.BlockSpec(memory_space=pltpu.SMEM)] + [whole] * count,
        out_specs=(whole, whole, whole, whole),
        scratch_shapes=[
            pltpu.VMEM((slots, DISTANCE_ROWS), bf16),
            pltpu.VMEM((DISTANCE_ROWS, slots), bf16),
            pltpu.VMEM((16, slots), bf16),
            pltpu.VMEM((slots, ALONG_ROWS), bf16),
            pltpu.VMEM((16, slots), bf16),
            pltpu.VMEM((16, slots), f32),
            pltpu.VMEM((16, width), f32),
            pltpu.VMEM((16, width), f32),
            pltpu.VMEM((CHUNK, width), f32),
            pltpu.VMEM((CHUNK, width), f32),
            pltpu.VMEM((slots, width), f32),
            pltpu.VMEM((ALONG_ROWS, width), bf16),
        ],
        compiler_params=pltpu.CompilerParams(vmem_limit_bytes=(16 << 20) + slots * 2688),
        name="sweep",
    )(counts, *blocks)


def swapped(value, axis, step):
    pairs = [(i, i ^ step) for i in range(lax.axis_size(axis))]
    return lax.ppermute(value, axis, pairs)


def bits(size):
    return [1 << bit for bit in range(size.bit_length() - 1)]


def gathered(block):
    size = lax.axis_size("sharers")
    if size == 4:
        order = [0, 2, 1, 3]
        return [block] + [swapped(block, "sharers", step) for step in order[1:]], order
    for step in bits(size):
        block = jnp.concatenate([block, swapped(block, "sharers", step)], axis=0)
    return [block[i : i + 1] for i in range(size)], list(range(size))


def local(velocities, weights, counts):
    axes = ("cells", "sharers")
    blocks, order = gathered(
        jnp.pad(jnp.concatenate([velocities, weights[:, None]], axis=1), ((0, 0), (0, 4), (0, 0)))
    )
    copies = lax.axis_size(axes)
    scores, drift, start, speeds = sweep(counts, blocks, order, copies)
    speeds = lax.all_to_all(speeds.reshape(copies, 1, 128), axes, 0, 0, tiled=True)
    time_step = 0.5 / (jnp.max(speeds, axis=0, keepdims=True) + 1e-06)
    moved = start + time_step * drift
    return moved.reshape(velocities.shape), scores.reshape(velocities.shape)


def solution(mesh):
    in_specs = (
        P(("groups", "cells"), None, "sharers"),
        P(("groups", "cells"), "sharers"),
        P(("groups", "cells")),
    )
    out_specs = (P(("groups", "cells"), None, "sharers"), P(("groups", "cells"), None, "sharers"))
    return jax.shard_map(local, mesh=mesh, in_specs=in_specs, out_specs=out_specs, check_vma=False)
```

```python
import functools
import functools
import math

import jax
import jax.numpy as jnp
from jax import lax
from jax.experimental import pallas as pl
from jax.experimental.pallas import tpu as pltpu
from jax.sharding import PartitionSpec as P

EPS = 0.35
SCALE = math.sqrt(math.log2(math.e) / (2.0 * EPS * EPS))
GRID = 4.0
TINY = 1e-30
GROUP = 16
KEPT_BLOCKS = 4
DISTANCE_ROWS = 96
ALONG_ROWS = 112
bf16, f32 = jnp.bfloat16, jnp.float32


def round_bf16(value):
    return value.astype(bf16).astype(f32)


def pieces(value, count):
    parts = []
    for _ in range(count):
        part = round_bf16(value)
        parts.append(part)
        value = value - part
    return parts


def row_of(value):
    return lax.broadcasted_iota(jnp.int32, value.shape, 0)


def rows_sum(value):
    return jnp.sum(value, axis=0, keepdims=True)


def stacked(groups):
    if len(groups) % 2:
        groups = groups + [jnp.zeros_like(groups[0])]
    return jnp.concatenate(groups, axis=0).astype(bf16)


def scalar_groups(value, like):
    row = row_of(like)
    first, second, third = pieces(value, 3)
    low = jnp.where(row == 0, first, jnp.where(row == 1, second, jnp.where(row == 2, third, 0.0)))
    high = jnp.where(row == 3, first, jnp.where(row == 4, second, jnp.where(row == 5, third, 0.0)))
    ones_low, ones_high = row < 3, (row >= 3) & (row < 6)
    return jnp.where(ones_high, 1.0, low), jnp.where(ones_low, 1.0, high)


def grid_parts(place):
    coarse = jnp.floor(place * GRID + 0.5) * (1.0 / GRID)
    return [coarse] + pieces(place - coarse, 2)


def distance_features(parts):
    coarse, fine, rest = parts
    minor = fine + rest
    query_norm, key_norm = scalar_groups(-rows_sum(coarse * coarse), coarse)
    query_less, key_less = scalar_groups(-rows_sum(minor * (2.0 * coarse + minor)), coarse)
    key = [coarse, key_norm, coarse, coarse, fine, rest, key_less, fine, fine, rest, rest]
    coarse, fine, rest = coarse * 2.0, fine * 2.0, rest * 2.0
    query = [coarse, query_norm, fine, rest, coarse, coarse, query_less, fine, rest, fine, rest]
    return stacked(key), stacked(query)


def along_features(parts, score, is_key):
    coarse, fine, rest = parts
    first, second, third = pieces(-score, 3)
    query_dot, key_dot = scalar_groups(rows_sum((coarse + fine + rest) * score), coarse)
    places = [coarse, coarse, coarse, fine, fine, rest]
    turns = [first, second, third, first, second, first]
    if is_key:
        return stacked([key_dot] + turns + places)
    return stacked([query_dot] + places + turns)


def weighted_rows(weight, value):
    row = row_of(value)
    whole = jnp.where(row < 3, value, jnp.where(row == 3, 1.0, 0.0)) * weight
    first, second, third = pieces(whole, 3)
    return stacked([first, second + pltpu.roll(third, 4, 0)])


def product(left, right):
    return jnp.dot(left, right, preferred_element_type=f32)


def store_split(ref, rows, matrix):
    half = ref.shape[0] // 2
    upper = matrix.astype(bf16)
    ref[rows, :] = upper
    ref[pl.ds(half + rows.start, rows.size), :] = (matrix - upper.astype(f32)).astype(bf16)


def sum_rows(left, ref):
    return product(jnp.concatenate([left, left], axis=1), ref[...])


def sum_columns(left, ref):
    both = lax.dot_general(left, ref[...], (((1,), (1,)), ((), ())), preferred_element_type=f32)
    half = ref.shape[0] // 2
    return both[:, :half] + both[:, half:]


def joined(total):
    upper, lower = total[0:8], total[8:16]
    return upper + lower + pltpu.roll(lower, 4, 0)


def sweep_kernel(order, *refs):
    count = len(order)
    filled, blocks, refs = refs[0], refs[1 : count + 1], refs[count + 1 :]
    scores_out, drift_out, start_out, speed_out, key_ref, query_ref, moment_ref = refs[:7]
    along_ref, flux_ref, sums_ref, cubes_ref, linear_ref, even_ref, odd_ref = refs[7:14]
    own_exponent_ref, own_along_ref, *split_refs = refs[14:]
    width = blocks[0].shape[2]
    total_slots = count * width
    kept = count <= KEPT_BLOCKS
    here = lax.axis_index("sharers")

    def slots(index, size):
        return pl.ds(pl.multiple_of(index * size, size), size)

    lane = lax.broadcasted_iota(jnp.int32, (1, width), 1)
    live = [lane + (here ^ step) * width < filled[0] for step in order]
    weight = jnp.concatenate(
        [jnp.where(on, block[0, 3:4], 0.0) for on, block in zip(live, blocks)], axis=1
    )
    whole = jnp.concatenate([block[0] for block in blocks], axis=1)
    vector = row_of(whole) < 3
    parts = grid_parts(jnp.where(vector, whole * SCALE, 0.0))
    place = parts[0] + parts[1] + parts[2]
    key, query = distance_features(parts)
    key_ref[...] = key.T
    query_ref[...] = query
    moment_ref[...] = weighted_rows(weight, place)
    sums_ref[...] = jnp.zeros_like(sums_ref)

    def exponent(key_block, query_block):
        return product(key_ref[slots(key_block, width), :], query_ref[:, slots(query_block, width)])

    def add_blobs(key_block, query_block, ref, split, both):
        for group in range(0, width, GROUP):
            rows = pl.ds(group, GROUP)
            store_split(split, rows, jnp.exp2(ref[rows, :]))
        keys, queries = slots(key_block, width), slots(query_block, width)
        sums_ref[:, queries] += sum_rows(moment_ref[:, keys], split)
        if both:
            sums_ref[:, keys] += sum_columns(moment_ref[:, queries], split)

    if kept:
        pairs = [(key, query) for query in range(count) for key in range(query, count)]
        buffers = [even_ref, odd_ref]

        def buffer(index):
            key, query = pairs[index]
            return own_exponent_ref.at[slots(key, width), :] if query == 0 else buffers[index % 2]

        buffer(0)[...] = exponent(*pairs[0])
        for index, (key, query) in enumerate(pairs):
            if index + 1 < len(pairs):
                buffer(index + 1)[...] = exponent(*pairs[index + 1])
            add_blobs(key, query, buffer(index), split_refs[index % 2], key != query)
    else:

        def whole_row(query, carry):
            even_ref[...] = exponent(query, query)
            add_blobs(query, query, even_ref, split_refs[0], False)

            def one(key, carry):
                even_ref[...] = exponent(key, query)
                add_blobs(key, query, even_ref, split_refs[0], True)
                return carry

            return lax.fori_loop(query + 1, count, one, carry)

        lax.fori_loop(0, count, whole_row, 0)

    sums = joined(sums_ref[...])
    live = weight > 0.0
    density_sum = jnp.where(live, sums[3:4], 1.0)
    pull = place * density_sum - sums
    score = jnp.where(vector & live, pull / (-SCALE * EPS * EPS * density_sum), 0.0)
    along_ref[...] = along_features(parts, score, True).T
    flux_ref[...] = weighted_rows(weight, score)

    place, score, live = place[:, 0:width], score[:, 0:width], live[:, 0:width]
    own_along_ref[...] = along_features([part[:, 0:width] for part in parts], score, False)
    cubes_ref[...] = jnp.zeros_like(cubes_ref)
    linear_ref[...] = jnp.zeros_like(linear_ref)

    def along(block):
        return product(along_ref[slots(block, width), :], own_along_ref[...])

    def add_drift(block, ref, cubes_split, linear_split):
        if not kept:
            own_exponent_ref[...] = exponent(block, 0)
        for group in range(0, width, GROUP):
            rows = pl.ds(group, GROUP)
            first = block * width + group if kept else group
            negative = jnp.minimum(own_exponent_ref[pl.ds(first, GROUP), :], -TINY)
            distance = negative * lax.rsqrt(-negative)
            store_split(cubes_split, rows, negative * distance)
            store_split(linear_split, rows, ref[rows, :] * distance)
        keys = slots(block, width)
        cubes_ref[...] += sum_rows(flux_ref[:, keys], cubes_split)
        linear_ref[...] += sum_rows(moment_ref[:, keys], linear_split)

    if kept:
        even_ref[...] = along(0)
        for block in range(count):
            if block + 1 < count:
                buffers[(block + 1) % 2][...] = along(block + 1)
            first = 2 * (block % 2)
            add_drift(block, buffers[block % 2], *split_refs[first : first + 2])
    else:

        def drift_block(block, carry):
            even_ref[...] = along(block)
            add_drift(block, even_ref, *split_refs[0:2])
            return carry

        lax.fori_loop(0, count, drift_block, 0)
    cubes, linear = joined(cubes_ref[...]), joined(linear_ref[...])
    drift = score * cubes[3:4] - cubes + place * linear[3:4] - linear
    factor = -1.0 / (SCALE * SCALE * SCALE * total_slots)
    drift = jnp.where(live & vector[:, 0:width], drift * factor, 0.0)
    largest = jnp.max(rows_sum(drift * drift), axis=1, keepdims=True)
    speed_out[...] = jnp.broadcast_to(jnp.sqrt(largest), speed_out.shape)
    for part in range(width // 128):
        lanes = slice(part * 128, part * 128 + 128)
        for axis in range(3):
            scores_out[axis, part : part + 1, :] = score[axis : axis + 1, lanes]
            drift_out[axis, part : part + 1, :] = drift[axis : axis + 1, lanes]
            start_out[axis, part : part + 1, :] = blocks[0][0, axis : axis + 1, lanes]


def sweep(counts, blocks, order, copies):
    count, width = len(blocks), blocks[0].shape[2]
    slots = count * width
    parts = jax.ShapeDtypeStruct((3, width // 128, 128), f32)
    whole = pl.BlockSpec(memory_space=pltpu.VMEM)
    return pl.pallas_call(
        functools.partial(sweep_kernel, order),
        out_shape=(parts, parts, parts, jax.ShapeDtypeStruct((copies, 128), f32)),
        in_specs=[pl.BlockSpec(memory_space=pltpu.SMEM)] + [whole] * count,
        out_specs=(whole, whole, whole, whole),
        scratch_shapes=[
            pltpu.VMEM((slots, DISTANCE_ROWS), bf16),
            pltpu.VMEM((DISTANCE_ROWS, slots), bf16),
            pltpu.VMEM((16, slots), bf16),
            pltpu.VMEM((slots, ALONG_ROWS), bf16),
            pltpu.VMEM((16, slots), bf16),
            pltpu.VMEM((16, slots), f32),
            pltpu.VMEM((16, width), f32),
            pltpu.VMEM((16, width), f32),
            pltpu.VMEM((width, width), f32),
            pltpu.VMEM((width, width), f32),
            pltpu.VMEM((slots if count <= KEPT_BLOCKS else width, width), f32),
            pltpu.VMEM((ALONG_ROWS, width), bf16),
        ]
        + [pltpu.VMEM((2 * width, width), bf16)] * 4,
        compiler_params=pltpu.CompilerParams(vmem_limit_bytes=(16 << 20) + slots * 2688),
        name="sweep",
    )(counts, *blocks)


def swapped(value, axis, step):
    pairs = [(i, i ^ step) for i in range(lax.axis_size(axis))]
    return lax.ppermute(value, axis, pairs)


def bits(size):
    return [1 << bit for bit in range(size.bit_length() - 1)]


def gathered(block):
    size = lax.axis_size("sharers")
    if size == 4:
        order = [0, 2, 1, 3]
        return [block] + [swapped(block, "sharers", step) for step in order[1:]], order
    for step in bits(size):
        block = jnp.concatenate([block, swapped(block, "sharers", step)], axis=0)
    return [block[i : i + 1] for i in range(size)], list(range(size))


def local(velocities, weights, counts):
    axes = ("cells", "sharers")
    blocks, order = gathered(
        jnp.pad(jnp.concatenate([velocities, weights[:, None]], axis=1), ((0, 0), (0, 4), (0, 0)))
    )
    copies = lax.axis_size(axes)
    scores, drift, start, speeds = sweep(counts, blocks, order, copies)
    speeds = lax.all_to_all(speeds.reshape(copies, 1, 128), axes, 0, 0, tiled=True)
    time_step = 0.5 / (jnp.max(speeds, axis=0, keepdims=True) + 1e-06)
    moved = start + time_step * drift
    return moved.reshape(velocities.shape), scores.reshape(velocities.shape)


def solution(mesh):
    in_specs = (
        P(("groups", "cells"), None, "sharers"),
        P(("groups", "cells"), "sharers"),
        P(("groups", "cells")),
    )
    out_specs = (P(("groups", "cells"), None, "sharers"), P(("groups", "cells"), None, "sharers"))
    return jax.shard_map(local, mesh=mesh, in_specs=in_specs, out_specs=out_specs, check_vma=False)
```

```python
import functools
import functools
import math

import jax
import jax.numpy as jnp
from jax import lax
from jax.experimental import pallas as pl
from jax.experimental.pallas import tpu as pltpu
from jax.sharding import PartitionSpec as P

EPS = 0.35
SCALE = math.sqrt(math.log2(math.e) / (2.0 * EPS * EPS))
GRID = 4.0
TINY = 1e-30
GROUP = 16
KEPT_BLOCKS = 4
DISTANCE_ROWS = 96
DRIFT_ROWS = 64
bf16, f32 = jnp.bfloat16, jnp.float32


def round_bf16(value):
    return value.astype(bf16).astype(f32)


def pieces(value, count):
    parts = []
    for _ in range(count):
        part = round_bf16(value)
        parts.append(part)
        value = value - part
    return parts


def row_of(value):
    return lax.broadcasted_iota(jnp.int32, value.shape, 0)


def rows_sum(value):
    return jnp.sum(value, axis=0, keepdims=True)


def stacked(groups):
    if len(groups) % 2:
        groups = groups + [jnp.zeros_like(groups[0])]
    return jnp.concatenate(groups, axis=0).astype(bf16)


def scalar_groups(value, like):
    row = row_of(like)
    first, second, third = pieces(value, 3)
    low = jnp.where(row == 0, first, jnp.where(row == 1, second, jnp.where(row == 2, third, 0.0)))
    high = jnp.where(row == 3, first, jnp.where(row == 4, second, jnp.where(row == 5, third, 0.0)))
    ones_low, ones_high = row < 3, (row >= 3) & (row < 6)
    return jnp.where(ones_high, 1.0, low), jnp.where(ones_low, 1.0, high)


def grid_parts(place):
    coarse = jnp.floor(place * GRID + 0.5) * (1.0 / GRID)
    return [coarse] + pieces(place - coarse, 2)


def distance_features(parts):
    coarse, fine, rest = parts
    minor = fine + rest
    query_norm, key_norm = scalar_groups(-rows_sum(coarse * coarse), coarse)
    query_less, key_less = scalar_groups(-rows_sum(minor * (2.0 * coarse + minor)), coarse)
    key = [coarse, key_norm, coarse, coarse, fine, rest, key_less, fine, fine, rest, rest]
    coarse, fine, rest = coarse * 2.0, fine * 2.0, rest * 2.0
    query = [coarse, query_norm, fine, rest, coarse, coarse, query_less, fine, rest, fine, rest]
    return stacked(key), stacked(query)


def weighted_rows(weight, value):
    row = row_of(value)
    whole = jnp.where(row < 3, value, jnp.where(row == 3, 1.0, 0.0)) * weight
    first, second, third = pieces(whole, 3)
    return stacked([first, second + pltpu.roll(third, 4, 0)])


def product(left, right):
    return jnp.dot(left, right, preferred_element_type=f32)


def store_split(ref, rows, matrix):
    half = ref.shape[0] // 2
    upper = matrix.astype(bf16)
    ref[rows, :] = upper
    ref[pl.ds(half + rows.start, rows.size), :] = (matrix - upper.astype(f32)).astype(bf16)


def sum_rows(left, ref):
    return product(jnp.concatenate([left, left], axis=1), ref[...])


def sum_columns(left, ref):
    both = lax.dot_general(left, ref[...], (((1,), (1,)), ((), ())), preferred_element_type=f32)
    half = ref.shape[0] // 2
    return both[:, :half] + both[:, half:]


def joined(total):
    upper, lower = total[0:8], total[8:16]
    return upper + lower + pltpu.roll(lower, 4, 0)


def drift_rows(weight, place, score):
    row = row_of(place)
    base = place + jnp.where(row == 3, 1.0, 0.0) + pltpu.roll(score, 4, 0)
    cubic = rows_sum(place * place) * score - rows_sum(place * score) * place
    groups = [weight * base]
    for i in range(3):
        here = slice(i, i + 1)
        groups.append(weight * jnp.where(row == 3, cubic[here], place[here] * base))
    return stacked(sum(map(list, zip(*[pieces(group, 2) for group in groups])), []))


def drift_sum(total, place, score):
    row = row_of(place)
    total = total[0:32] + total[32:64]
    first, *rest = [total[8 * i : 8 * i + 8] for i in range(4)]
    turned = [pltpu.roll(group, 4, 0) for group in rest]
    count, scores = first[3:4], pltpu.roll(first, 4, 0)
    square, both = rows_sum(place * place), rows_sum(place * score)
    trace = rest[0][0:1] + rest[1][1:2] + rest[2][2:3]
    cross = turned[0][0:1] + turned[1][1:2] + turned[2][2:3]
    drift = score * (square * count - 2.0 * rows_sum(place * first) + trace) - square * scores
    drift += both * first + place * (
        rows_sum(place * scores) + rows_sum(score * first) - both * count - cross
    )
    ends = []
    for i in range(3):
        here = slice(i, i + 1)
        drift += 2.0 * place[here] * turned[i] - score[here] * rest[i]
        ends.append(rows_sum(place * turned[i]) + rest[i][3:4])
    return drift - jnp.where(row == 0, ends[0], jnp.where(row == 1, ends[1], ends[2]))


def sweep_kernel(order, *refs):
    count = len(order)
    filled, blocks, refs = refs[0], refs[1 : count + 1], refs[count + 1 :]
    scores_out, drift_out, start_out, speed_out, key_ref, query_ref, moment_ref = refs[:7]
    flux_ref, sums_ref, totals_ref, exponent_ref, *split_refs = refs[7:]
    width = blocks[0].shape[2]
    total_slots = count * width
    kept = count <= KEPT_BLOCKS
    pairs = [(key, query) for query in range(count) for key in range(query, count)]
    here = lax.axis_index("sharers")

    def slots(index, size):
        return pl.ds(pl.multiple_of(index * size, size), size)

    lane = lax.broadcasted_iota(jnp.int32, (1, width), 1)
    live = [lane + (here ^ step) * width < filled[0] for step in order]
    weight = jnp.concatenate(
        [jnp.where(on, block[0, 3:4], 0.0) for on, block in zip(live, blocks)], axis=1
    )
    whole = jnp.concatenate([block[0] for block in blocks], axis=1)
    vector = row_of(whole) < 3
    parts = grid_parts(jnp.where(vector, whole * SCALE, 0.0))
    place = parts[0] + parts[1] + parts[2]
    key, query = distance_features(parts)
    key_ref[...] = key.T
    query_ref[...] = query
    moment_ref[...] = weighted_rows(weight, place)
    middle = jnp.sum(place * weight, axis=1, keepdims=True)
    middle = middle / jnp.sum(weight, axis=1, keepdims=True)
    sums_ref[...] = jnp.zeros_like(sums_ref)

    def exponent(key_block, query_block):
        return product(key_ref[slots(key_block, width), :], query_ref[:, slots(query_block, width)])

    def add_blobs(key_block, query_block, ref, split, both):
        for group in range(0, width, GROUP):
            rows = pl.ds(group, GROUP)
            store_split(split, rows, jnp.exp2(ref[rows, :]))
        keys, queries = slots(key_block, width), slots(query_block, width)
        sums_ref[:, queries] += sum_rows(moment_ref[:, keys], split)
        if both:
            sums_ref[:, keys] += sum_columns(moment_ref[:, queries], split)

    if kept:

        def tile(index):
            return exponent_ref.at[slots(index, width), :]

        tile(0)[...] = exponent(*pairs[0])
        for index, (key, query) in enumerate(pairs):
            if index + 1 < len(pairs):
                tile(index + 1)[...] = exponent(*pairs[index + 1])
            add_blobs(key, query, tile(index), split_refs[index % 2], key != query)
    else:

        def whole_row(query, carry):
            exponent_ref[...] = exponent(query, query)
            add_blobs(query, query, exponent_ref, split_refs[0], False)

            def one(key, carry):
                exponent_ref[...] = exponent(key, query)
                add_blobs(key, query, exponent_ref, split_refs[0], True)
                return carry

            return lax.fori_loop(query + 1, count, one, carry)

        lax.fori_loop(0, count, whole_row, 0)

    sums = joined(sums_ref[...])
    live = weight > 0.0
    density_sum = jnp.where(live, sums[3:4], 1.0)
    pull = place * density_sum - sums
    score = jnp.where(vector & live, pull / (-SCALE * EPS * EPS * density_sum), 0.0)
    centred = jnp.where(vector, place - middle, 0.0)
    flux_ref[...] = drift_rows(weight, centred, score)
    totals_ref[...] = jnp.zeros_like(totals_ref)

    def add_distances(key_block, query_block, ref, split, both):
        for group in range(0, width, GROUP):
            rows = pl.ds(group, GROUP)
            negative = jnp.minimum(ref[rows, :], -TINY)
            store_split(split, rows, negative * lax.rsqrt(-negative))
        keys, queries = slots(key_block, width), slots(query_block, width)
        totals_ref[:, queries] += sum_rows(flux_ref[:, keys], split)
        if both:
            totals_ref[:, keys] += sum_columns(flux_ref[:, queries], split)

    if kept:
        for index, (key, query) in enumerate(pairs):
            add_distances(key, query, tile(index), split_refs[index % 2], key != query)
        spread = total_slots
    else:

        def one_block(key, carry):
            exponent_ref[...] = exponent(key, 0)
            add_distances(key, 0, exponent_ref, split_refs[0], False)
            return carry

        lax.fori_loop(0, count, one_block, 0)
        spread = width

    drift = drift_sum(totals_ref[...], centred[:, 0:spread], score[:, 0:spread])
    factor = 1.0 / (SCALE * SCALE * SCALE * total_slots)
    drift = jnp.where((vector & live)[:, 0:spread], drift * factor, 0.0)
    largest = jnp.max(rows_sum(drift * drift), axis=1, keepdims=True)
    speed_out[...] = jnp.broadcast_to(jnp.sqrt(largest), speed_out.shape)
    for part in range(width // 128):
        lanes = slice(part * 128, part * 128 + 128)
        for axis in range(3):
            scores_out[axis, part : part + 1, :] = score[axis : axis + 1, lanes]
            drift_out[axis, part : part + 1, :] = drift[axis : axis + 1, lanes]
            start_out[axis, part : part + 1, :] = blocks[0][0, axis : axis + 1, lanes]


def sweep(counts, blocks, order, copies):
    count, width = len(blocks), blocks[0].shape[2]
    slots = count * width
    kept = count <= KEPT_BLOCKS
    parts = jax.ShapeDtypeStruct((3, width // 128, 128), f32)
    whole = pl.BlockSpec(memory_space=pltpu.VMEM)
    return pl.pallas_call(
        functools.partial(sweep_kernel, order),
        out_shape=(parts, parts, parts, jax.ShapeDtypeStruct((copies, 128), f32)),
        in_specs=[pl.BlockSpec(memory_space=pltpu.SMEM)] + [whole] * count,
        out_specs=(whole, whole, whole, whole),
        scratch_shapes=[
            pltpu.VMEM((slots, DISTANCE_ROWS), bf16),
            pltpu.VMEM((DISTANCE_ROWS, slots), bf16),
            pltpu.VMEM((16, slots), bf16),
            pltpu.VMEM((DRIFT_ROWS, slots), bf16),
            pltpu.VMEM((16, slots), f32),
            pltpu.VMEM((DRIFT_ROWS, slots if kept else width), f32),
            pltpu.VMEM((count * (count + 1) // 2 * width if kept else width, width), f32),
        ]
        + [pltpu.VMEM((2 * width, width), bf16)] * 2,
        compiler_params=pltpu.CompilerParams(vmem_limit_bytes=(16 << 20) + slots * 2688),
        name="sweep",
    )(counts, *blocks)


def swapped(value, axis, step):
    pairs = [(i, i ^ step) for i in range(lax.axis_size(axis))]
    return lax.ppermute(value, axis, pairs)


def bits(size):
    return [1 << bit for bit in range(size.bit_length() - 1)]


def gathered(block):
    size = lax.axis_size("sharers")
    if size == 4:
        order = [0, 2, 1, 3]
        return [block] + [swapped(block, "sharers", step) for step in order[1:]], order
    for step in bits(size):
        block = jnp.concatenate([block, swapped(block, "sharers", step)], axis=0)
    return [block[i : i + 1] for i in range(size)], list(range(size))


def largest_speed(speeds, whole_cell):
    if not whole_cell:
        axes = ("cells", "sharers")
        return jnp.max(lax.all_to_all(speeds[:, None], axes, 0, 0, tiled=True), axis=0)
    for step in bits(lax.axis_size("cells")):
        speeds = jnp.maximum(speeds, swapped(speeds, "cells", step))
    return speeds[0:1]


def local(velocities, weights, counts):
    package = jnp.concatenate([velocities, weights[:, None]], axis=1)
    blocks, order = gathered(jnp.pad(package, ((0, 0), (0, 4), (0, 0))))
    whole_cell = len(blocks) <= KEPT_BLOCKS
    copies = 8 if whole_cell else lax.axis_size(("cells", "sharers"))
    scores, drift, start, speeds = sweep(counts, blocks, order, copies)
    time_step = 0.5 / (largest_speed(speeds, whole_cell) + 1e-06)
    moved = start + time_step[None] * drift
    return moved.reshape(velocities.shape), scores.reshape(velocities.shape)


def solution(mesh):
    in_specs = (
        P(("groups", "cells"), None, "sharers"),
        P(("groups", "cells"), "sharers"),
        P(("groups", "cells")),
    )
    out_specs = (P(("groups", "cells"), None, "sharers"), P(("groups", "cells"), None, "sharers"))
    return jax.shard_map(local, mesh=mesh, in_specs=in_specs, out_specs=out_specs, check_vma=False)
```

```python
import functools
import functools
import math

import jax
import jax.numpy as jnp
from jax import lax
from jax.experimental import pallas as pl
from jax.experimental.pallas import tpu as pltpu
from jax.sharding import PartitionSpec as P

EPS = 0.35
SCALE = math.sqrt(math.log2(math.e) / (2.0 * EPS * EPS))
GRID = 4.0
TINY = 1e-30
GROUP = 16
KEPT_BLOCKS = 4
DISTANCE_ROWS = 96
DRIFT_ROWS = 64
bf16, f32 = jnp.bfloat16, jnp.float32


def round_bf16(value):
    return value.astype(bf16).astype(f32)


def pieces(value, count):
    parts = []
    for _ in range(count):
        part = round_bf16(value)
        parts.append(part)
        value = value - part
    return parts


def row_of(value):
    return lax.broadcasted_iota(jnp.int32, value.shape, 0)


def rows_sum(value):
    return jnp.sum(value, axis=0, keepdims=True)


def stacked(groups):
    if len(groups) % 2:
        groups = groups + [jnp.zeros_like(groups[0])]
    return jnp.concatenate(groups, axis=0).astype(bf16)


def scalar_groups(value, like):
    row = row_of(like)
    first, second, third = pieces(value, 3)
    low = jnp.where(row == 0, first, jnp.where(row == 1, second, jnp.where(row == 2, third, 0.0)))
    high = jnp.where(row == 3, first, jnp.where(row == 4, second, jnp.where(row == 5, third, 0.0)))
    ones_low, ones_high = row < 3, (row >= 3) & (row < 6)
    return jnp.where(ones_high, 1.0, low), jnp.where(ones_low, 1.0, high)


def grid_parts(place):
    coarse = jnp.floor(place * GRID + 0.5) * (1.0 / GRID)
    return [coarse] + pieces(place - coarse, 2)


def distance_features(parts):
    coarse, fine, rest = parts
    minor = fine + rest
    query_norm, key_norm = scalar_groups(-rows_sum(coarse * coarse), coarse)
    query_less, key_less = scalar_groups(-rows_sum(minor * (2.0 * coarse + minor)), coarse)
    key = [coarse, key_norm, coarse, coarse, fine, rest, key_less, fine, fine, rest, rest]
    coarse, fine, rest = coarse * 2.0, fine * 2.0, rest * 2.0
    query = [coarse, query_norm, fine, rest, coarse, coarse, query_less, fine, rest, fine, rest]
    return stacked(key), stacked(query)


def weighted_rows(weight, value):
    row = row_of(value)
    whole = jnp.where(row < 3, value, jnp.where(row == 3, 1.0, 0.0)) * weight
    first, second, third = pieces(whole, 3)
    return stacked([first, second + pltpu.roll(third, 4, 0)])


def product(left, right):
    return jnp.dot(left, right, preferred_element_type=f32)


def store_split(ref, rows, matrix):
    half = ref.shape[0] // 2
    upper = matrix.astype(bf16)
    ref[rows, :] = upper
    ref[pl.ds(half + rows.start, rows.size), :] = (matrix - upper.astype(f32)).astype(bf16)


def sum_rows(left, ref):
    return product(jnp.concatenate([left, left], axis=1), ref[...])


def sum_columns(left, ref):
    both = lax.dot_general(left, ref[...], (((1,), (1,)), ((), ())), preferred_element_type=f32)
    half = ref.shape[0] // 2
    return both[:, :half] + both[:, half:]


def sum_rows_less(left, ref):
    half = ref.shape[0] // 2
    both = product(left, ref[:half, :])
    few = left.shape[0] // 2
    return both[:few] + product(left[:few], ref[half:, :]), both[few:]


def sum_columns_less(left, ref):
    half, few = ref.shape[0] // 2, left.shape[0] // 2
    turned = (((1,), (1,)), ((), ()))
    both = lax.dot_general(left, ref[:half, :], turned, preferred_element_type=f32)
    less = lax.dot_general(left[:few], ref[half:, :], turned, preferred_element_type=f32)
    return both[:few] + less, both[few:]


def joined(total):
    upper, lower = total[0:8], total[8:16]
    return upper + lower + pltpu.roll(lower, 4, 0)


def drift_rows(weight, place, score):
    row = row_of(place)
    base = place + jnp.where(row == 3, 1.0, 0.0) + pltpu.roll(score, 4, 0)
    cubic = rows_sum(place * place) * score - rows_sum(place * score) * place
    groups = [weight * base]
    for i in range(3):
        here = slice(i, i + 1)
        groups.append(weight * jnp.where(row == 3, cubic[here], place[here] * base))
    return stacked(sum(map(list, zip(*[pieces(group, 2) for group in groups])), []))


def drift_sum(total, place, score):
    row = row_of(place)
    first, *rest = [total[8 * i : 8 * i + 8] for i in range(4)]
    turned = [pltpu.roll(group, 4, 0) for group in rest]
    count, scores = first[3:4], pltpu.roll(first, 4, 0)
    square, both = rows_sum(place * place), rows_sum(place * score)
    trace = rest[0][0:1] + rest[1][1:2] + rest[2][2:3]
    cross = turned[0][0:1] + turned[1][1:2] + turned[2][2:3]
    drift = score * (square * count - 2.0 * rows_sum(place * first) + trace) - square * scores
    drift += both * first + place * (
        rows_sum(place * scores) + rows_sum(score * first) - both * count - cross
    )
    ends = []
    for i in range(3):
        here = slice(i, i + 1)
        drift += 2.0 * place[here] * turned[i] - score[here] * rest[i]
        ends.append(rows_sum(place * turned[i]) + rest[i][3:4])
    return drift - jnp.where(row == 0, ends[0], jnp.where(row == 1, ends[1], ends[2]))


def sweep_kernel(sources, *refs):
    count = len(sources)
    filled, blocks, refs = refs[0], refs[1 : count + 1], refs[count + 1 :]
    scores_out, drift_out, start_out, speed_out, key_ref, query_ref, moment_ref = refs[:7]
    flux_ref, sums_ref, totals_ref, exponent_ref, *split_refs = refs[7:]
    width = blocks[0].shape[2]
    total_slots = count * width
    kept = count <= KEPT_BLOCKS
    pairs = [(key, query) for query in range(count) for key in range(query, count)]
    here = lax.axis_index("sharers")

    def slots(index, size):
        return pl.ds(pl.multiple_of(index * size, size), size)

    lane = lax.broadcasted_iota(jnp.int32, (1, width), 1)
    live = []
    for source in sources:
        owner = sum(jnp.where(here == i, source[i], 0) for i in range(count))
        live.append(lane + owner * width < filled[0])
    weight = jnp.concatenate(
        [jnp.where(on, block[0, 3:4], 0.0) for on, block in zip(live, blocks)], axis=1
    )
    whole = jnp.concatenate([block[0] for block in blocks], axis=1)
    vector = row_of(whole) < 3
    parts = grid_parts(jnp.where(vector, whole * SCALE, 0.0))
    place = parts[0] + parts[1] + parts[2]
    key, query = distance_features(parts)
    key_ref[...] = key.T
    query_ref[...] = query
    moment_ref[...] = weighted_rows(weight, place)
    middle = jnp.sum(place * weight, axis=1, keepdims=True)
    middle = middle / jnp.sum(weight, axis=1, keepdims=True)
    sums_ref[...] = jnp.zeros_like(sums_ref)

    def exponent(key_block, query_block):
        return product(key_ref[slots(key_block, width), :], query_ref[:, slots(query_block, width)])

    def add_blobs(key_block, query_block, ref, split, both):
        for group in range(0, width, GROUP):
            rows = pl.ds(group, GROUP)
            store_split(split, rows, jnp.exp2(ref[rows, :]))
        keys, queries = slots(key_block, width), slots(query_block, width)
        sums_ref[:, queries] += sum_rows(moment_ref[:, keys], split)
        if both:
            sums_ref[:, keys] += sum_columns(moment_ref[:, queries], split)

    if kept:

        def tile(index):
            return exponent_ref.at[slots(index, width), :]

        tile(0)[...] = exponent(*pairs[0])
        for index, (key, query) in enumerate(pairs):
            if index + 1 < len(pairs):
                tile(index + 1)[...] = exponent(*pairs[index + 1])
            add_blobs(key, query, tile(index), split_refs[index % 2], key != query)
    else:

        def whole_row(query, carry):
            exponent_ref[...] = exponent(query, query)
            add_blobs(query, query, exponent_ref, split_refs[0], False)

            def one(key, carry):
                exponent_ref[...] = exponent(key, query)
                add_blobs(key, query, exponent_ref, split_refs[0], True)
                return carry

            return lax.fori_loop(query + 1, count, one, carry)

        lax.fori_loop(0, count, whole_row, 0)

    sums = joined(sums_ref[...])
    live = weight > 0.0
    density_sum = jnp.where(live, sums[3:4], 1.0)
    pull = place * density_sum - sums
    score = jnp.where(vector & live, pull / (-SCALE * EPS * EPS * density_sum), 0.0)
    centred = jnp.where(vector, place - middle, 0.0)
    flux_ref[...] = drift_rows(weight, centred, score)
    totals_ref[...] = jnp.zeros_like(totals_ref)

    def add_distances(key_block, query_block, ref, split, both):
        for group in range(0, width, GROUP):
            rows = pl.ds(group, GROUP)
            negative = jnp.minimum(ref[rows, :], -TINY)
            store_split(split, rows, negative * lax.rsqrt(-negative))
        keys, queries = slots(key_block, width), slots(query_block, width)
        upper, lower = sum_rows_less(flux_ref[:, keys], split)
        totals_ref[:, queries] += upper + lower
        if both:
            upper, lower = sum_columns_less(flux_ref[:, queries], split)
            totals_ref[:, keys] += upper + lower

    if kept:
        for index, (key, query) in enumerate(pairs):
            add_distances(key, query, tile(index), split_refs[index % 2], key != query)
        spread = total_slots
    else:

        def one_block(key, carry):
            exponent_ref[...] = exponent(key, 0)
            add_distances(key, 0, exponent_ref, split_refs[0], False)
            return carry

        lax.fori_loop(0, count, one_block, 0)
        spread = width

    drift = drift_sum(totals_ref[...], centred[:, 0:spread], score[:, 0:spread])
    factor = 1.0 / (SCALE * SCALE * SCALE * total_slots)
    drift = jnp.where((vector & live)[:, 0:spread], drift * factor, 0.0)
    largest = jnp.max(rows_sum(drift * drift), axis=1, keepdims=True)
    speed_out[...] = jnp.broadcast_to(jnp.sqrt(largest), speed_out.shape)
    scores_out[...] = score[:, 0:width]
    for part in range(width // 128):
        lanes = slice(part * 128, part * 128 + 128)
        for axis in range(3):
            drift_out[axis, part : part + 1, :] = drift[axis : axis + 1, lanes]
            start_out[axis, part : part + 1, :] = blocks[0][0, axis : axis + 1, lanes]


def sweep(counts, blocks, sources, copies):
    count, width = len(blocks), blocks[0].shape[2]
    slots = count * width
    kept = count <= KEPT_BLOCKS
    parts = jax.ShapeDtypeStruct((3, width // 128, 128), f32)
    whole = pl.BlockSpec(memory_space=pltpu.VMEM)
    return pl.pallas_call(
        functools.partial(sweep_kernel, sources),
        out_shape=(jax.ShapeDtypeStruct((8, width), f32), parts, parts, jax.ShapeDtypeStruct((copies, 128), f32)),
        in_specs=[pl.BlockSpec(memory_space=pltpu.SMEM)] + [whole] * count,
        out_specs=(whole, whole, whole, whole),
        scratch_shapes=[
            pltpu.VMEM((slots, DISTANCE_ROWS), bf16),
            pltpu.VMEM((DISTANCE_ROWS, slots), bf16),
            pltpu.VMEM((16, slots), bf16),
            pltpu.VMEM((DRIFT_ROWS, slots), bf16),
            pltpu.VMEM((16, slots), f32),
            pltpu.VMEM((DRIFT_ROWS // 2, slots if kept else width), f32),
            pltpu.VMEM((count * (count + 1) // 2 * width if kept else width, width), f32),
        ]
        + [pltpu.VMEM((2 * width, width), bf16)] * 2,
        compiler_params=pltpu.CompilerParams(vmem_limit_bytes=(16 << 20) + slots * 2688),
        name="sweep",
    )(counts, *blocks)


def swapped(value, axis, step):
    pairs = [(i, i ^ step) for i in range(lax.axis_size(axis))]
    return lax.ppermute(value, axis, pairs)


def bits(size):
    return [1 << bit for bit in range(size.bit_length() - 1)]


ROUNDS = ((2, 3, 1, 0), (3, 2, 0, 1), (1, 0, 3, 2))


def gathered(block):
    size = lax.axis_size("sharers")
    if size == 4:
        blocks, sources = [block], [(0, 1, 2, 3)]
        for targets in reversed(ROUNDS):
            blocks.append(lax.ppermute(block, "sharers", list(enumerate(targets))))
            sources.append(tuple(targets.index(i) for i in range(size)))
        return blocks, sources
    for step in bits(size):
        block = jnp.concatenate([block, swapped(block, "sharers", step)], axis=0)
    sources = [tuple(i ^ step for i in range(size)) for step in range(size)]
    return [block[i : i + 1] for i in range(size)], sources


def largest_speed(speeds, whole_cell):
    if not whole_cell:
        axes = ("cells", "sharers")
        return jnp.max(lax.all_to_all(speeds[:, None], axes, 0, 0, tiled=True), axis=0)
    for step in bits(lax.axis_size("cells")):
        speeds = jnp.maximum(speeds, swapped(speeds, "cells", step))
    return speeds[0:1]


def local(velocities, weights, counts):
    package = jnp.concatenate([velocities, weights[:, None]], axis=1)
    blocks, sources = gathered(jnp.pad(package, ((0, 0), (0, 4), (0, 0))))
    whole_cell = len(blocks) <= KEPT_BLOCKS
    copies = 8 if whole_cell else lax.axis_size(("cells", "sharers"))
    scores, drift, start, speeds = sweep(counts, blocks, sources, copies)
    time_step = 0.5 / (largest_speed(speeds, whole_cell) + 1e-06)
    moved = start + time_step[None] * drift
    return moved.reshape(velocities.shape), scores[None, 0:3]


def solution(mesh):
    in_specs = (
        P(("groups", "cells"), None, "sharers"),
        P(("groups", "cells"), "sharers"),
        P(("groups", "cells")),
    )
    out_specs = (P(("groups", "cells"), None, "sharers"), P(("groups", "cells"), None, "sharers"))
    return jax.shard_map(local, mesh=mesh, in_specs=in_specs, out_specs=out_specs, check_vma=False)
```

```python
import functools
import functools
import math

import jax
import jax.numpy as jnp
from jax import lax
from jax.experimental import pallas as pl
from jax.experimental.pallas import tpu as pltpu
from jax.sharding import PartitionSpec as P

EPS = 0.35
SCALE = math.sqrt(math.log2(math.e) / (2.0 * EPS * EPS))
GRID = 4.0
TINY = 1e-30
GROUP = 16
KEPT_BLOCKS = 4
DISTANCE_ROWS = 96
DRIFT_ROWS = 64
bf16, f32 = jnp.bfloat16, jnp.float32


def round_bf16(value):
    return value.astype(bf16).astype(f32)


def pieces(value, count):
    parts = []
    for _ in range(count):
        part = round_bf16(value)
        parts.append(part)
        value = value - part
    return parts


def row_of(value):
    return lax.broadcasted_iota(jnp.int32, value.shape, 0)


def rows_sum(value):
    return jnp.sum(value, axis=0, keepdims=True)


def stacked(groups):
    if len(groups) % 2:
        groups = groups + [jnp.zeros_like(groups[0])]
    return jnp.concatenate(groups, axis=0).astype(bf16)


def scalar_groups(value, like):
    row = row_of(like)
    first, second, third = pieces(value, 3)
    low = jnp.where(row == 0, first, jnp.where(row == 1, second, jnp.where(row == 2, third, 0.0)))
    high = jnp.where(row == 3, first, jnp.where(row == 4, second, jnp.where(row == 5, third, 0.0)))
    ones_low, ones_high = row < 3, (row >= 3) & (row < 6)
    return jnp.where(ones_high, 1.0, low), jnp.where(ones_low, 1.0, high)


def grid_parts(place):
    coarse = jnp.floor(place * GRID + 0.5) * (1.0 / GRID)
    return [coarse] + pieces(place - coarse, 2)


def distance_features(parts):
    coarse, fine, rest = parts
    minor = fine + rest
    query_norm, key_norm = scalar_groups(-rows_sum(coarse * coarse), coarse)
    query_less, key_less = scalar_groups(-rows_sum(minor * (2.0 * coarse + minor)), coarse)
    key = [coarse, key_norm, coarse, coarse, fine, rest, key_less, fine, fine, rest, rest]
    coarse, fine, rest = coarse * 2.0, fine * 2.0, rest * 2.0
    query = [coarse, query_norm, fine, rest, coarse, coarse, query_less, fine, rest, fine, rest]
    return stacked(key), stacked(query)


def weighted_rows(weight, value):
    row = row_of(value)
    whole = jnp.where(row < 3, value, jnp.where(row == 3, 1.0, 0.0)) * weight
    first, second, third = pieces(whole, 3)
    return stacked([first, second + pltpu.roll(third, 4, 0)])


def product(left, right):
    return jnp.dot(left, right, preferred_element_type=f32)


def store_split(ref, rows, matrix):
    half = ref.shape[0] // 2
    upper = matrix.astype(bf16)
    ref[rows, :] = upper
    ref[pl.ds(half + rows.start, rows.size), :] = (matrix - upper.astype(f32)).astype(bf16)


def sum_rows(left, ref):
    return product(jnp.concatenate([left, left], axis=1), ref[...])


def sum_columns(left, ref):
    both = lax.dot_general(left, ref[...], (((1,), (1,)), ((), ())), preferred_element_type=f32)
    half = ref.shape[0] // 2
    return both[:, :half] + both[:, half:]


def sum_rows_less(left, ref):
    half = ref.shape[0] // 2
    both = product(left, ref[:half, :])
    few = left.shape[0] // 2
    return both[:few] + product(left[:few], ref[half:, :]), both[few:]


def sum_columns_less(left, ref):
    half, few = ref.shape[0] // 2, left.shape[0] // 2
    turned = (((1,), (1,)), ((), ()))
    both = lax.dot_general(left, ref[:half, :], turned, preferred_element_type=f32)
    less = lax.dot_general(left[:few], ref[half:, :], turned, preferred_element_type=f32)
    return both[:few] + less, both[few:]


def joined(total):
    upper, lower = total[0:8], total[8:16]
    return upper + lower + pltpu.roll(lower, 4, 0)


def drift_rows(weight, place, score):
    row = row_of(place)
    base = place + jnp.where(row == 3, 1.0, 0.0) + pltpu.roll(score, 4, 0)
    cubic = rows_sum(place * place) * score - rows_sum(place * score) * place
    groups = [weight * base]
    for i in range(3):
        here = slice(i, i + 1)
        groups.append(weight * jnp.where(row == 3, cubic[here], place[here] * base))
    return stacked(sum(map(list, zip(*[pieces(group, 2) for group in groups])), []))


def drift_sum(total, place, score):
    row = row_of(place)
    first, *rest = [total[8 * i : 8 * i + 8] for i in range(4)]
    turned = [pltpu.roll(group, 4, 0) for group in rest]
    count, scores = first[3:4], pltpu.roll(first, 4, 0)
    square, both = rows_sum(place * place), rows_sum(place * score)
    trace = rest[0][0:1] + rest[1][1:2] + rest[2][2:3]
    cross = turned[0][0:1] + turned[1][1:2] + turned[2][2:3]
    drift = score * (square * count - 2.0 * rows_sum(place * first) + trace) - square * scores
    drift += both * first + place * (
        rows_sum(place * scores) + rows_sum(score * first) - both * count - cross
    )
    ends = []
    for i in range(3):
        here = slice(i, i + 1)
        drift += 2.0 * place[here] * turned[i] - score[here] * rest[i]
        ends.append(rows_sum(place * turned[i]) + rest[i][3:4])
    return drift - jnp.where(row == 0, ends[0], jnp.where(row == 1, ends[1], ends[2]))


def sweep_kernel(sources, *refs):
    count = len(sources)
    filled, blocks, refs = refs[0], refs[1 : count + 1], refs[count + 1 :]
    scores_out, drift_out, start_out, speed_out, key_ref, query_ref, moment_ref = refs[:7]
    flux_ref, sums_ref, totals_ref, exponent_ref, *split_refs = refs[7:]
    width = blocks[0].shape[2]
    total_slots = count * width
    kept = count <= KEPT_BLOCKS
    half = width // 2
    tiles = []
    for query in range(count if kept else 0):
        start = query * width
        tiles += [(start, half, start, half, 0), (start + half, half, start, width, half)]
        tiles += [(key * width, width, start, width, width) for key in range(query + 1, count)]
    here = lax.axis_index("sharers")

    lane = lax.broadcasted_iota(jnp.int32, (1, width), 1)
    live = []
    for source in sources:
        owner = sum(jnp.where(here == i, source[i], 0) for i in range(count))
        live.append(lane + owner * width < filled[0])
    weight = jnp.concatenate(
        [jnp.where(on, block[0, 3:4], 0.0) for on, block in zip(live, blocks)], axis=1
    )
    whole = jnp.concatenate([block[0] for block in blocks], axis=1)
    vector = row_of(whole) < 3
    parts = grid_parts(jnp.where(vector, whole * SCALE, 0.0))
    place = parts[0] + parts[1] + parts[2]
    key, query = distance_features(parts)
    key_ref[...] = key.T
    query_ref[...] = query
    moment_ref[...] = weighted_rows(weight, place)
    middle = jnp.sum(place * weight, axis=1, keepdims=True)
    middle = middle / jnp.sum(weight, axis=1, keepdims=True)
    sums_ref[...] = jnp.zeros_like(sums_ref)

    def exponent(key, keys, query, queries):
        return product(key_ref[pl.ds(key, keys), :], query_ref[:, pl.ds(query, queries)])

    def add_blobs(tile, ref, split):
        key, keys, query, queries, turned = tile
        split = split.at[0 : 2 * keys, 0:queries]
        for group in range(0, keys, GROUP):
            rows = pl.ds(group, GROUP)
            store_split(split, rows, jnp.exp2(ref[rows, :]))
        sums_ref[:, pl.ds(query, queries)] += sum_rows(moment_ref[:, pl.ds(key, keys)], split)
        if turned:
            left, right = moment_ref[:, pl.ds(query, turned)], split.at[:, 0:turned]
            sums_ref[:, pl.ds(key, keys)] += sum_columns(left, right)

    def block_tile(key, query, both):
        start, first = (pl.multiple_of(block * width, width) for block in (key, query))
        return (start, width, first, width, width if both else 0)

    if kept:
        exponents = []
        for index, (_, keys, _, queries, _) in enumerate(tiles):
            exponents.append(exponent_ref.at[index, 0:keys, 0:queries])
        exponents[0][...] = exponent(*tiles[0][:4])
        for index, tile in enumerate(tiles):
            if index + 1 < len(tiles):
                exponents[index + 1][...] = exponent(*tiles[index + 1][:4])
            add_blobs(tile, exponents[index], split_refs[index % 2])
    else:

        def whole_row(query, carry):
            def one(key, both, carry):
                tile = block_tile(key, query, both)
                exponent_ref[0] = exponent(*tile[:4])
                add_blobs(tile, exponent_ref.at[0], split_refs[0])
                return carry

            carry = one(query, False, carry)
            return lax.fori_loop(query + 1, count, lambda key, c: one(key, True, c), carry)

        lax.fori_loop(0, count, whole_row, 0)

    sums = joined(sums_ref[...])
    live = weight > 0.0
    density_sum = jnp.where(live, sums[3:4], 1.0)
    pull = place * density_sum - sums
    score = jnp.where(vector & live, pull / (-SCALE * EPS * EPS * density_sum), 0.0)
    centred = jnp.where(vector, place - middle, 0.0)
    flux_ref[...] = drift_rows(weight, centred, score)
    totals_ref[...] = jnp.zeros_like(totals_ref)

    def add_distances(tile, ref, split):
        key, keys, query, queries, turned = tile
        split = split.at[0 : 2 * keys, 0:queries]
        for group in range(0, keys, GROUP):
            rows = pl.ds(group, GROUP)
            negative = jnp.minimum(ref[rows, :], -TINY)
            store_split(split, rows, negative * lax.rsqrt(-negative))
        upper, lower = sum_rows_less(flux_ref[:, pl.ds(key, keys)], split)
        totals_ref[:, pl.ds(query, queries)] += upper + lower
        if turned:
            left, right = flux_ref[:, pl.ds(query, turned)], split.at[:, 0:turned]
            upper, lower = sum_columns_less(left, right)
            totals_ref[:, pl.ds(key, keys)] += upper + lower

    if kept:
        for index, tile in enumerate(tiles):
            add_distances(tile, exponents[index], split_refs[index % 2])
        spread = total_slots
    else:

        def one_block(key, carry):
            tile = block_tile(key, 0, False)
            exponent_ref[0] = exponent(*tile[:4])
            add_distances(tile, exponent_ref.at[0], split_refs[0])
            return carry

        lax.fori_loop(0, count, one_block, 0)
        spread = width

    drift = drift_sum(totals_ref[...], centred[:, 0:spread], score[:, 0:spread])
    factor = 1.0 / (SCALE * SCALE * SCALE * total_slots)
    drift = jnp.where((vector & live)[:, 0:spread], drift * factor, 0.0)
    largest = jnp.max(rows_sum(drift * drift), axis=1, keepdims=True)
    speed_out[...] = jnp.broadcast_to(jnp.sqrt(largest), speed_out.shape)
    scores_out[...] = score[:, 0:width]
    for part in range(width // 128):
        lanes = slice(part * 128, part * 128 + 128)
        for axis in range(3):
            drift_out[axis, part : part + 1, :] = drift[axis : axis + 1, lanes]
            start_out[axis, part : part + 1, :] = blocks[0][0, axis : axis + 1, lanes]


def sweep(counts, blocks, sources, copies):
    count, width = len(blocks), blocks[0].shape[2]
    slots = count * width
    kept = count <= KEPT_BLOCKS
    parts = jax.ShapeDtypeStruct((3, width // 128, 128), f32)
    whole = pl.BlockSpec(memory_space=pltpu.VMEM)
    return pl.pallas_call(
        functools.partial(sweep_kernel, sources),
        out_shape=(jax.ShapeDtypeStruct((8, width), f32), parts, parts, jax.ShapeDtypeStruct((copies, 128), f32)),
        in_specs=[pl.BlockSpec(memory_space=pltpu.SMEM)] + [whole] * count,
        out_specs=(whole, whole, whole, whole),
        scratch_shapes=[
            pltpu.VMEM((slots, DISTANCE_ROWS), bf16),
            pltpu.VMEM((DISTANCE_ROWS, slots), bf16),
            pltpu.VMEM((16, slots), bf16),
            pltpu.VMEM((DRIFT_ROWS, slots), bf16),
            pltpu.VMEM((16, slots), f32),
            pltpu.VMEM((DRIFT_ROWS // 2, slots if kept else width), f32),
            pltpu.VMEM((count * (count + 3) // 2 if kept else 1, width, width), f32),
        ]
        + [pltpu.VMEM((2 * width, width), bf16)] * 2,
        compiler_params=pltpu.CompilerParams(vmem_limit_bytes=(16 << 20) + slots * 2688),
        name="sweep",
    )(counts, *blocks)


def swapped(value, axis, step):
    pairs = [(i, i ^ step) for i in range(lax.axis_size(axis))]
    return lax.ppermute(value, axis, pairs)


def bits(size):
    return [1 << bit for bit in range(size.bit_length() - 1)]


ROUNDS = ((2, 3, 1, 0), (3, 2, 0, 1), (1, 0, 3, 2))


def gathered(block):
    size = lax.axis_size("sharers")
    if size == 4:
        blocks, sources = [block], [(0, 1, 2, 3)]
        for targets in reversed(ROUNDS):
            blocks.append(lax.ppermute(block, "sharers", list(enumerate(targets))))
            sources.append(tuple(targets.index(i) for i in range(size)))
        return blocks, sources
    for step in bits(size):
        block = jnp.concatenate([block, swapped(block, "sharers", step)], axis=0)
    sources = [tuple(i ^ step for i in range(size)) for step in range(size)]
    return [block[i : i + 1] for i in range(size)], sources


def largest_speed(speeds, whole_cell):
    if not whole_cell:
        axes = ("cells", "sharers")
        return jnp.max(lax.all_to_all(speeds[:, None], axes, 0, 0, tiled=True), axis=0)
    size = lax.axis_size("cells")
    if size == 4:
        for other in [swapped(speeds, "cells", step) for step in (2, 3, 1)]:
            speeds = jnp.maximum(speeds, other)
    else:
        for step in bits(size):
            speeds = jnp.maximum(speeds, swapped(speeds, "cells", step))
    return speeds[0:1]


def local(velocities, weights, counts):
    package = jnp.concatenate([velocities, weights[:, None]], axis=1)
    blocks, sources = gathered(jnp.pad(package, ((0, 0), (0, 4), (0, 0))))
    whole_cell = len(blocks) <= KEPT_BLOCKS
    copies = 8 if whole_cell else lax.axis_size(("cells", "sharers"))
    scores, drift, start, speeds = sweep(counts, blocks, sources, copies)
    time_step = 0.5 / (largest_speed(speeds, whole_cell) + 1e-06)
    moved = start + time_step[None] * drift
    return moved.reshape(velocities.shape), scores[None, 0:3]


def solution(mesh):
    in_specs = (
        P(("groups", "cells"), None, "sharers"),
        P(("groups", "cells"), "sharers"),
        P(("groups", "cells")),
    )
    out_specs = (P(("groups", "cells"), None, "sharers"), P(("groups", "cells"), None, "sharers"))
    return jax.shard_map(local, mesh=mesh, in_specs=in_specs, out_specs=out_specs, check_vma=False)
```

```python
import functools
import functools
import math

import jax
import jax.numpy as jnp
from jax import lax
from jax.experimental import pallas as pl
from jax.experimental.pallas import tpu as pltpu
from jax.sharding import PartitionSpec as P

EPS = 0.35
SCALE = math.sqrt(math.log2(math.e) / (2.0 * EPS * EPS))
GRID = 4.0
TINY = 1e-30
GROUP = 16
KEPT_BLOCKS = 4
DISTANCE_ROWS = 96
DRIFT_ROWS = 64
bf16, f32 = jnp.bfloat16, jnp.float32


def round_bf16(value):
    return value.astype(bf16).astype(f32)


def pieces(value, count):
    parts = []
    for _ in range(count):
        part = round_bf16(value)
        parts.append(part)
        value = value - part
    return parts


def row_of(value):
    return lax.broadcasted_iota(jnp.int32, value.shape, 0)


def rows_sum(value):
    return jnp.sum(value, axis=0, keepdims=True)


def stacked(groups):
    if len(groups) % 2:
        groups = groups + [jnp.zeros_like(groups[0])]
    return jnp.concatenate(groups, axis=0).astype(bf16)


def scalar_groups(value, like):
    row = row_of(like)
    first, second, third = pieces(value, 3)
    low = jnp.where(row == 0, first, jnp.where(row == 1, second, jnp.where(row == 2, third, 0.0)))
    high = jnp.where(row == 3, first, jnp.where(row == 4, second, jnp.where(row == 5, third, 0.0)))
    ones_low, ones_high = row < 3, (row >= 3) & (row < 6)
    return jnp.where(ones_high, 1.0, low), jnp.where(ones_low, 1.0, high)


def grid_parts(place):
    coarse = jnp.floor(place * GRID + 0.5) * (1.0 / GRID)
    return [coarse] + pieces(place - coarse, 2)


def distance_features(parts):
    coarse, fine, rest = parts
    minor = fine + rest
    query_norm, key_norm = scalar_groups(-rows_sum(coarse * coarse), coarse)
    query_less, key_less = scalar_groups(-rows_sum(minor * (2.0 * coarse + minor)), coarse)
    key = [coarse, key_norm, coarse, coarse, fine, rest, key_less, fine, fine, rest, rest]
    coarse, fine, rest = coarse * 2.0, fine * 2.0, rest * 2.0
    query = [coarse, query_norm, fine, rest, coarse, coarse, query_less, fine, rest, fine, rest]
    return stacked(key), stacked(query)


def weighted_rows(weight, value):
    row = row_of(value)
    whole = jnp.where(row < 3, value, jnp.where(row == 3, 1.0, 0.0)) * weight
    first, second, third = pieces(whole, 3)
    return stacked([first, second + pltpu.roll(third, 4, 0)])


def product(left, right):
    return jnp.dot(left, right, preferred_element_type=f32)


def store_split(ref, rows, matrix):
    half = ref.shape[0] // 2
    upper = matrix.astype(bf16)
    ref[rows, :] = upper
    ref[pl.ds(half + rows.start, rows.size), :] = (matrix - upper.astype(f32)).astype(bf16)


def sum_rows(left, ref):
    return product(jnp.concatenate([left, left], axis=1), ref[...])


def sum_columns(left, ref):
    both = lax.dot_general(left, ref[...], (((1,), (1,)), ((), ())), preferred_element_type=f32)
    half = ref.shape[0] // 2
    return both[:, :half] + both[:, half:]


def sum_rows_less(left, ref):
    half = ref.shape[0] // 2
    both = product(left, ref[:half, :])
    few = left.shape[0] // 2
    return both[:few] + product(left[:few], ref[half:, :]), both[few:]


def sum_columns_less(left, ref):
    half, few = ref.shape[0] // 2, left.shape[0] // 2
    turned = (((1,), (1,)), ((), ()))
    both = lax.dot_general(left, ref[:half, :], turned, preferred_element_type=f32)
    less = lax.dot_general(left[:few], ref[half:, :], turned, preferred_element_type=f32)
    return both[:few] + less, both[few:]


def joined(total):
    upper, lower = total[0:8], total[8:16]
    return upper + lower + pltpu.roll(lower, 4, 0)


def drift_rows(weight, place, score):
    row = row_of(place)
    base = place + jnp.where(row == 3, 1.0, 0.0) + pltpu.roll(score, 4, 0)
    cubic = rows_sum(place * place) * score - rows_sum(place * score) * place
    groups = [weight * base]
    for i in range(3):
        here = slice(i, i + 1)
        groups.append(weight * jnp.where(row == 3, cubic[here], place[here] * base))
    return stacked(sum(map(list, zip(*[pieces(group, 2) for group in groups])), []))


def drift_sum(total, place, score):
    row = row_of(place)
    first, *rest = [total[8 * i : 8 * i + 8] for i in range(4)]
    turned = [pltpu.roll(group, 4, 0) for group in rest]
    count, scores = first[3:4], pltpu.roll(first, 4, 0)
    square, both = rows_sum(place * place), rows_sum(place * score)
    trace = rest[0][0:1] + rest[1][1:2] + rest[2][2:3]
    cross = turned[0][0:1] + turned[1][1:2] + turned[2][2:3]
    drift = score * (square * count - 2.0 * rows_sum(place * first) + trace) - square * scores
    drift += both * first + place * (
        rows_sum(place * scores) + rows_sum(score * first) - both * count - cross
    )
    ends = []
    for i in range(3):
        here = slice(i, i + 1)
        drift += 2.0 * place[here] * turned[i] - score[here] * rest[i]
        ends.append(rows_sum(place * turned[i]) + rest[i][3:4])
    return drift - jnp.where(row == 0, ends[0], jnp.where(row == 1, ends[1], ends[2]))


def prepared(whole, live):
    weight = jnp.where(live, whole[3:4], 0.0)
    parts = grid_parts(jnp.where(row_of(whole) < 3, whole * SCALE, 0.0))
    place = parts[0] + parts[1] + parts[2]
    key, query = distance_features(parts)
    return weight, place, key.T, query, weighted_rows(weight, place)


def split_blobs(exponent, split):
    for group in range(0, exponent.shape[0], GROUP):
        rows = pl.ds(group, GROUP)
        store_split(split, rows, jnp.exp2(exponent[rows, :]))


def split_distances(exponent, split):
    for group in range(0, exponent.shape[0], GROUP):
        rows = pl.ds(group, GROUP)
        negative = jnp.minimum(exponent[rows, :], -TINY)
        store_split(split, rows, negative * lax.rsqrt(-negative))


def diagonal_tiles(start, width):
    half = width // 2
    return [(start, half, start, half, 0), (start + half, half, start, width, half)]


def add_blobs(tile, split, moments, sums_ref):
    key, keys, query, queries, turned = tile
    sums_ref[:, pl.ds(query, queries)] += sum_rows(moments(key, keys), split)
    if turned:
        sums_ref[:, pl.ds(key, keys)] += sum_columns(moments(query, turned), split.at[:, 0:turned])


def add_distances(tile, split, fluxes, totals_ref):
    key, keys, query, queries, turned = tile
    upper, lower = sum_rows_less(fluxes(key, keys), split)
    totals_ref[:, pl.ds(query, queries)] += upper + lower
    if turned:
        upper, lower = sum_columns_less(fluxes(query, turned), split.at[:, 0:turned])
        totals_ref[:, pl.ds(key, keys)] += upper + lower


def own_kernel(filled, block, key_out, query_out, moment_out, sums_out, first_out, second_out,
               exponent_ref, split_ref):
    width = block.shape[2]
    lane = lax.broadcasted_iota(jnp.int32, (1, width), 1)
    live = lane + lax.axis_index("sharers") * width < filled[0]
    _, _, key, query, moment = prepared(block[0], live)
    key_out[...] = key
    query_out[...] = query
    moment_out[...] = moment
    sums_out[...] = jnp.zeros_like(sums_out)

    def moments(start, size):
        return moment_out[:, pl.ds(start, size)]

    for tile, distances in zip(diagonal_tiles(0, width), (first_out, second_out)):
        first, keys, start, queries, _ = tile
        exponent = exponent_ref.at[0:keys, 0:queries]
        exponent[...] = product(key_out[pl.ds(first, keys), :], query_out[:, pl.ds(start, queries)])
        split = split_ref.at[:, 0:queries]
        split_blobs(exponent, split)
        add_blobs(tile, split, moments, sums_out)
        split_distances(exponent, distances)


def own_part(counts, block):
    width = block.shape[2]
    half = width // 2
    vector = pl.BlockSpec(memory_space=pltpu.VMEM)
    return pl.pallas_call(
        own_kernel,
        out_shape=(
            jax.ShapeDtypeStruct((width, DISTANCE_ROWS), bf16),
            jax.ShapeDtypeStruct((DISTANCE_ROWS, width), bf16),
            jax.ShapeDtypeStruct((16, width), bf16),
            jax.ShapeDtypeStruct((16, width), f32),
            jax.ShapeDtypeStruct((2 * half, half), bf16),
            jax.ShapeDtypeStruct((2 * half, width), bf16),
        ),
        in_specs=[pl.BlockSpec(memory_space=pltpu.SMEM), vector],
        out_specs=(vector,) * 6,
        scratch_shapes=[pltpu.VMEM((half, width), f32), pltpu.VMEM((2 * half, width), bf16)],
        compiler_params=pltpu.CompilerParams(vmem_limit_bytes=16 << 20),
        name="own",
    )(counts, block)


def sweep_kernel(sources, *refs):
    count = len(sources)
    kept = count <= KEPT_BLOCKS
    filled, blocks, refs = refs[0], refs[1 : count + 1], refs[count + 1 :]
    early, refs = (refs[:6], refs[6:]) if kept else ((), refs)
    scores_out, drift_out, start_out, speed_out, key_ref, query_ref, moment_ref = refs[:7]
    flux_ref, sums_ref, totals_ref, exponent_ref, *split_refs = refs[7:]
    width = blocks[0].shape[2]
    total_slots = count * width
    here = lax.axis_index("sharers")

    lane = lax.broadcasted_iota(jnp.int32, (1, width), 1)
    live = []
    for source in sources:
        owner = sum(jnp.where(here == i, source[i], 0) for i in range(count))
        live.append(lane + owner * width < filled[0])
    skipped = 1 if kept else 0
    rest = [prepared(block[0], on) for block, on in zip(blocks[skipped:], live[skipped:])]
    for index, (_, _, key, query, moment) in enumerate(rest):
        lanes = pl.ds(index * width, width)
        key_ref[lanes, :] = key
        query_ref[:, lanes] = query
        moment_ref[:, lanes] = moment
    whole = jnp.concatenate([block[0] for block in blocks], axis=1)
    vector = row_of(whole) < 3
    weight = jnp.concatenate(
        [jnp.where(on, block[0, 3:4], 0.0) for on, block in zip(live, blocks)], axis=1
    )
    place = grid_parts(jnp.where(vector, whole * SCALE, 0.0))
    place = place[0] + place[1] + place[2]
    middle = jnp.sum(place * weight, axis=1, keepdims=True)
    middle = middle / jnp.sum(weight, axis=1, keepdims=True)

    def feature(index, start):
        if kept and start < width:
            return early[index], start
        return (key_ref, query_ref, moment_ref)[index], start - skipped * width

    def moments(start, size):
        ref, start = feature(2, start)
        return ref[:, pl.ds(start, size)]

    def exponent(tile):
        (keys, key), (queries, query) = feature(0, tile[0]), feature(1, tile[2])
        return product(keys[pl.ds(key, tile[1]), :], queries[:, pl.ds(query, tile[3])])

    def block_tile(key, query, both):
        start, first = (pl.multiple_of(block * width, width) for block in (key, query))
        return (start, width, first, width, width if both else 0)

    def piece(ref, tile):
        return ref.at[0 : 2 * tile[1], 0 : tile[3]]

    sums_ref[...] = jnp.zeros_like(sums_ref)
    if kept:
        sums_ref[:, 0:width] = early[3][...]
        tiles = [(key * width, width, 0, width, width) for key in range(1, count)]
        for query in range(1, count):
            start = query * width
            tiles += diagonal_tiles(start, width)
            tiles += [(key * width, width, start, width, width) for key in range(query + 1, count)]
        exponents = []
        for index, (_, keys, _, queries, _) in enumerate(tiles):
            exponents.append(exponent_ref.at[index, 0:keys, 0:queries])
        exponents[0][...] = exponent(tiles[0])
        for index, tile in enumerate(tiles):
            if index + 1 < len(tiles):
                exponents[index + 1][...] = exponent(tiles[index + 1])
            split = piece(split_refs[index % 2], tile)
            split_blobs(exponents[index], split)
            add_blobs(tile, split, moments, sums_ref)
    else:

        def whole_row(query, carry):
            def one(key, both, carry):
                tile = block_tile(key, query, both)
                exponent_ref[0] = exponent(tile)
                split_blobs(exponent_ref.at[0], split_refs[0])
                add_blobs(tile, split_refs[0], moments, sums_ref)
                return carry

            carry = one(query, False, carry)
            return lax.fori_loop(query + 1, count, lambda key, c: one(key, True, c), carry)

        lax.fori_loop(0, count, whole_row, 0)

    sums = joined(sums_ref[...])
    live = weight > 0.0
    density_sum = jnp.where(live, sums[3:4], 1.0)
    pull = place * density_sum - sums
    score = jnp.where(vector & live, pull / (-SCALE * EPS * EPS * density_sum), 0.0)
    centred = jnp.where(vector, place - middle, 0.0)
    flux_ref[...] = drift_rows(weight, centred, score)
    totals_ref[...] = jnp.zeros_like(totals_ref)

    def fluxes(start, size):
        return flux_ref[:, pl.ds(start, size)]

    if kept:
        for tile, split in zip(diagonal_tiles(0, width), early[4:6]):
            add_distances(tile, split, fluxes, totals_ref)
        for index, tile in enumerate(tiles):
            split = piece(split_refs[index % 2], tile)
            split_distances(exponents[index], split)
            add_distances(tile, split, fluxes, totals_ref)
        spread = total_slots
    else:

        def one_block(key, carry):
            tile = block_tile(key, 0, False)
            exponent_ref[0] = exponent(tile)
            split_distances(exponent_ref.at[0], split_refs[0])
            add_distances(tile, split_refs[0], fluxes, totals_ref)
            return carry

        lax.fori_loop(0, count, one_block, 0)
        spread = width

    drift = drift_sum(totals_ref[...], centred[:, 0:spread], score[:, 0:spread])
    factor = 1.0 / (SCALE * SCALE * SCALE * total_slots)
    drift = jnp.where((vector & live)[:, 0:spread], drift * factor, 0.0)
    largest = jnp.max(rows_sum(drift * drift), axis=1, keepdims=True)
    speed_out[...] = jnp.broadcast_to(jnp.sqrt(largest), speed_out.shape)
    scores_out[...] = score[:, 0:width]
    for part in range(width // 128):
        lanes = slice(part * 128, part * 128 + 128)
        for axis in range(3):
            drift_out[axis, part : part + 1, :] = drift[axis : axis + 1, lanes]
            start_out[axis, part : part + 1, :] = blocks[0][0, axis : axis + 1, lanes]


def sweep(counts, blocks, early, sources, copies):
    count, width = len(blocks), blocks[0].shape[2]
    slots = count * width
    kept = count <= KEPT_BLOCKS
    built = slots - width if kept else slots
    parts = jax.ShapeDtypeStruct((3, width // 128, 128), f32)
    vector = pl.BlockSpec(memory_space=pltpu.VMEM)
    return pl.pallas_call(
        functools.partial(sweep_kernel, sources),
        out_shape=(
            jax.ShapeDtypeStruct((8, width), f32),
            parts,
            parts,
            jax.ShapeDtypeStruct((copies, 128), f32),
        ),
        in_specs=[pl.BlockSpec(memory_space=pltpu.SMEM)] + [vector] * (count + len(early)),
        out_specs=(vector,) * 4,
        scratch_shapes=[
            pltpu.VMEM((built, DISTANCE_ROWS), bf16),
            pltpu.VMEM((DISTANCE_ROWS, built), bf16),
            pltpu.VMEM((16, built), bf16),
            pltpu.VMEM((DRIFT_ROWS, slots), bf16),
            pltpu.VMEM((16, slots), f32),
            pltpu.VMEM((DRIFT_ROWS // 2, slots if kept else width), f32),
            pltpu.VMEM(((count - 1) * (count + 4) // 2 if kept else 1, width, width), f32),
        ]
        + [pltpu.VMEM((2 * width, width), bf16)] * 2,
        compiler_params=pltpu.CompilerParams(vmem_limit_bytes=(16 << 20) + slots * 2688),
        name="sweep",
    )(counts, *blocks, *early)


def swapped(value, axis, step):
    pairs = [(i, i ^ step) for i in range(lax.axis_size(axis))]
    return lax.ppermute(value, axis, pairs)


def bits(size):
    return [1 << bit for bit in range(size.bit_length() - 1)]


ROUNDS = ((2, 3, 1, 0), (3, 2, 0, 1), (1, 0, 3, 2))


def gathered(block):
    size = lax.axis_size("sharers")
    if size == 4:
        blocks, sources = [block], [(0, 1, 2, 3)]
        for targets in reversed(ROUNDS):
            blocks.append(lax.ppermute(block, "sharers", list(enumerate(targets))))
            sources.append(tuple(targets.index(i) for i in range(size)))
        return blocks, sources
    for step in bits(size):
        block = jnp.concatenate([block, swapped(block, "sharers", step)], axis=0)
    sources = [tuple(i ^ step for i in range(size)) for step in range(size)]
    return [block[i : i + 1] for i in range(size)], sources


def largest_speed(speeds, whole_cell):
    if not whole_cell:
        axes = ("cells", "sharers")
        return jnp.max(lax.all_to_all(speeds[:, None], axes, 0, 0, tiled=True), axis=0)
    for step in bits(lax.axis_size("cells")):
        speeds = jnp.maximum(speeds, swapped(speeds, "cells", 2 * step - 1))
    return speeds[0:1]


def local(velocities, weights, counts):
    package = jnp.concatenate([velocities, weights[:, None]], axis=1)
    blocks, sources = gathered(jnp.pad(package, ((0, 0), (0, 4), (0, 0))))
    whole_cell = len(blocks) <= KEPT_BLOCKS
    copies = 8 if whole_cell else lax.axis_size(("cells", "sharers"))
    early = own_part(counts, blocks[0]) if whole_cell else ()
    scores, drift, start, speeds = sweep(counts, blocks, early, sources, copies)
    time_step = 0.5 / (largest_speed(speeds, whole_cell) + 1e-06)
    moved = start + time_step[None] * drift
    return moved.reshape(velocities.shape), scores[None, 0:3]


def solution(mesh):
    in_specs = (
        P(("groups", "cells"), None, "sharers"),
        P(("groups", "cells"), "sharers"),
        P(("groups", "cells")),
    )
    out_specs = (P(("groups", "cells"), None, "sharers"), P(("groups", "cells"), None, "sharers"))
    return jax.shard_map(local, mesh=mesh, in_specs=in_specs, out_specs=out_specs, check_vma=False)
```

```python
import functools
import functools
import math

import jax
import jax.numpy as jnp
from jax import lax
from jax.experimental import pallas as pl
from jax.experimental.pallas import tpu as pltpu
from jax.sharding import PartitionSpec as P

EPS = 0.35
SCALE = math.sqrt(math.log2(math.e) / (2.0 * EPS * EPS))
GRID = 4.0
TINY = 1e-30
GROUP = 16
DISTANCE_ROWS = 96
DRIFT_ROWS = 64
bf16, f32 = jnp.bfloat16, jnp.float32


def round_bf16(value):
    return value.astype(bf16).astype(f32)


def pieces(value, count):
    parts = []
    for _ in range(count):
        part = round_bf16(value)
        parts.append(part)
        value = value - part
    return parts


def row_of(value):
    return lax.broadcasted_iota(jnp.int32, value.shape, 0)


def rows_sum(value):
    return jnp.sum(value, axis=0, keepdims=True)


def stacked(groups):
    if len(groups) % 2:
        groups = groups + [jnp.zeros_like(groups[0])]
    return jnp.concatenate(groups, axis=0).astype(bf16)


def scalar_groups(value, like):
    row = row_of(like)
    first, second, third = pieces(value, 3)
    low = jnp.where(row == 0, first, jnp.where(row == 1, second, jnp.where(row == 2, third, 0.0)))
    high = jnp.where(row == 3, first, jnp.where(row == 4, second, jnp.where(row == 5, third, 0.0)))
    ones_low, ones_high = row < 3, (row >= 3) & (row < 6)
    return jnp.where(ones_high, 1.0, low), jnp.where(ones_low, 1.0, high)


def grid_parts(place):
    coarse = jnp.floor(place * GRID + 0.5) * (1.0 / GRID)
    return [coarse] + pieces(place - coarse, 2)


def distance_features(parts):
    coarse, fine, rest = parts
    minor = fine + rest
    query_norm, key_norm = scalar_groups(-rows_sum(coarse * coarse), coarse)
    query_less, key_less = scalar_groups(-rows_sum(minor * (2.0 * coarse + minor)), coarse)
    key = [coarse, key_norm, coarse, coarse, fine, rest, key_less, fine, fine, rest, rest]
    coarse, fine, rest = coarse * 2.0, fine * 2.0, rest * 2.0
    query = [coarse, query_norm, fine, rest, coarse, coarse, query_less, fine, rest, fine, rest]
    return stacked(key), stacked(query)


def weighted_rows(weight, value):
    row = row_of(value)
    whole = jnp.where(row < 3, value, jnp.where(row == 3, 1.0, 0.0)) * weight
    first, second, third = pieces(whole, 3)
    return stacked([first, second + pltpu.roll(third, 4, 0)])


def product(left, right):
    return jnp.dot(left, right, preferred_element_type=f32)


def store_split(ref, rows, matrix):
    half = ref.shape[0] // 2
    upper = matrix.astype(bf16)
    ref[rows, :] = upper
    ref[pl.ds(half + rows.start, rows.size), :] = (matrix - upper.astype(f32)).astype(bf16)


def sum_rows(left, ref):
    return product(jnp.concatenate([left, left], axis=1), ref[...])


def sum_columns(left, ref):
    both = lax.dot_general(left, ref[...], (((1,), (1,)), ((), ())), preferred_element_type=f32)
    half = ref.shape[0] // 2
    return both[:, :half] + both[:, half:]


def sum_rows_less(left, ref):
    half = ref.shape[0] // 2
    both = product(left, ref[:half, :])
    few = left.shape[0] // 2
    return both[:few] + product(left[:few], ref[half:, :]), both[few:]


def sum_columns_less(left, ref):
    half, few = ref.shape[0] // 2, left.shape[0] // 2
    turned = (((1,), (1,)), ((), ()))
    both = lax.dot_general(left, ref[:half, :], turned, preferred_element_type=f32)
    less = lax.dot_general(left[:few], ref[half:, :], turned, preferred_element_type=f32)
    return both[:few] + less, both[few:]


def joined(total):
    upper, lower = total[0:8], total[8:16]
    return upper + lower + pltpu.roll(lower, 4, 0)


def drift_rows(weight, place, score):
    row = row_of(place)
    base = place + jnp.where(row == 3, 1.0, 0.0) + pltpu.roll(score, 4, 0)
    cubic = rows_sum(place * place) * score - rows_sum(place * score) * place
    groups = [weight * base]
    for i in range(3):
        here = slice(i, i + 1)
        groups.append(weight * jnp.where(row == 3, cubic[here], place[here] * base))
    return stacked(sum(map(list, zip(*[pieces(group, 2) for group in groups])), []))


def drift_sum(total, place, score):
    row = row_of(place)
    first, *rest = [total[8 * i : 8 * i + 8] for i in range(4)]
    turned = [pltpu.roll(group, 4, 0) for group in rest]
    count, scores = first[3:4], pltpu.roll(first, 4, 0)
    square, both = rows_sum(place * place), rows_sum(place * score)
    trace = rest[0][0:1] + rest[1][1:2] + rest[2][2:3]
    cross = turned[0][0:1] + turned[1][1:2] + turned[2][2:3]
    drift = score * (square * count - 2.0 * rows_sum(place * first) + trace) - square * scores
    drift += both * first + place * (
        rows_sum(place * scores) + rows_sum(score * first) - both * count - cross
    )
    ends = []
    for i in range(3):
        here = slice(i, i + 1)
        drift += 2.0 * place[here] * turned[i] - score[here] * rest[i]
        ends.append(rows_sum(place * turned[i]) + rest[i][3:4])
    return drift - jnp.where(row == 0, ends[0], jnp.where(row == 1, ends[1], ends[2]))


def prepared(whole, live):
    weight = jnp.where(live, whole[3:4], 0.0)
    parts = grid_parts(jnp.where(row_of(whole) < 3, whole * SCALE, 0.0))
    place = parts[0] + parts[1] + parts[2]
    key, query = distance_features(parts)
    return weight, place, key.T, query, weighted_rows(weight, place)


def split_blobs(exponent, split):
    for group in range(0, exponent.shape[0], GROUP):
        rows = pl.ds(group, GROUP)
        store_split(split, rows, jnp.exp2(exponent[rows, :]))


def split_distances(exponent, split):
    for group in range(0, exponent.shape[0], GROUP):
        rows = pl.ds(group, GROUP)
        negative = jnp.minimum(exponent[rows, :], -TINY)
        store_split(split, rows, negative * lax.rsqrt(-negative))


def diagonal_tiles(start, width):
    half = width // 2
    return [(start, half, start, half, 0), (start + half, half, start, width, half)]


def add_blobs(tile, split, moments, sums_ref):
    key, keys, query, queries, turned = tile
    sums_ref[:, pl.ds(query, queries)] += sum_rows(moments(key, keys), split)
    if turned:
        sums_ref[:, pl.ds(key, keys)] += sum_columns(moments(query, turned), split.at[:, 0:turned])


def add_distances(tile, split, fluxes, totals_ref):
    key, keys, query, queries, turned = tile
    upper, lower = sum_rows_less(fluxes(key, keys), split)
    totals_ref[:, pl.ds(query, queries)] += upper + lower
    if turned:
        upper, lower = sum_columns_less(fluxes(query, turned), split.at[:, 0:turned])
        totals_ref[:, pl.ds(key, keys)] += upper + lower


def stage(tiles, exponent, moments, sums_ref, exponent_refs, split_refs, distance_refs):
    def buffer(index):
        _, keys, _, queries, _ = tiles[index]
        return exponent_refs[index % 2].at[0:keys, 0:queries]

    buffer(0)[...] = exponent(tiles[0])
    for index, tile in enumerate(tiles):
        if index + 1 < len(tiles):
            buffer(index + 1)[...] = exponent(tiles[index + 1])
        split = split_refs[index % 2].at[0 : 2 * tile[1], 0 : tile[3]]
        split_blobs(buffer(index), split)
        add_blobs(tile, split, moments, sums_ref)
        split_distances(buffer(index), distance_refs[index])


def looked_up(refs, width, axis):
    def read(start, size):
        at = pl.ds(start % width, size)
        ref = refs[start // width]
        return ref[at, :] if axis == 0 else ref[:, at]

    return read


def exponent_of(keys, queries):
    return lambda tile: product(keys(tile[0], tile[1]), queries(tile[2], tile[3]))


def lanes_of(source, width):
    return lax.broadcasted_iota(jnp.int32, (1, width), 1) + source * width


def owner_of(sources):
    here = lax.axis_index("sharers")
    return sum(jnp.where(here == i, source, 0) for i, source in enumerate(sources))


def own_kernel(filled_hbm, block, filled_out, key_out, query_out, moment_out, sums_out, first_out,
               second_out, filled_ref, filled_sem, *scratch):
    width = block.shape[2]
    fetch = pltpu.make_async_copy(filled_hbm, filled_ref, filled_sem)
    fetch.start()
    everything = lax.broadcasted_iota(jnp.int32, (1, width), 1) >= 0
    _, place, key, query, _ = prepared(block[0], everything)
    key_out[...] = key
    query_out[...] = query
    sums_out[...] = jnp.zeros_like(sums_out)
    fetch.wait()
    live = lanes_of(lax.axis_index("sharers"), width) < filled_ref[0]
    moment_out[...] = weighted_rows(jnp.where(live, block[0, 3:4], 0.0), place)
    filled_out[...] = jnp.full(filled_out.shape, filled_ref[0], jnp.int32)
    exponent = exponent_of(looked_up([key_out], width, 0), looked_up([query_out], width, 1))
    moments = looked_up([moment_out], width, 1)
    tiles = diagonal_tiles(0, width)
    stage(tiles, exponent, moments, sums_out, scratch[:2], scratch[2:], (first_out, second_out))


def next_kernel(sources, filled, block, own_key, own_query, own_moment, own_sums, key_out,
                query_out, moment_out, sums_out, tile_out, first_out, second_out, *scratch):
    width = block.shape[2]
    live = lanes_of(owner_of(sources), width) < filled[0:1, :]
    _, _, key, query, moment = prepared(block[0], live)
    key_out[...] = key
    query_out[...] = query
    moment_out[...] = moment
    sums_out[:, 0:width] = own_sums[...]
    sums_out[:, width:] = jnp.zeros_like(own_sums)
    exponent = exponent_of(
        looked_up([own_key, key_out], width, 0), looked_up([own_query, query_out], width, 1)
    )
    moments = looked_up([own_moment, moment_out], width, 1)
    tiles = [(width, width, 0, width, width)] + diagonal_tiles(width, width)
    distances = (tile_out, first_out, second_out)
    stage(tiles, exponent, moments, sums_out, scratch[:2], scratch[2:], distances)


def feature_shapes(width):
    return [
        jax.ShapeDtypeStruct((width, DISTANCE_ROWS), bf16),
        jax.ShapeDtypeStruct((DISTANCE_ROWS, width), bf16),
        jax.ShapeDtypeStruct((16, width), bf16),
    ]


def diagonal_shapes(width):
    half = width // 2
    return [
        jax.ShapeDtypeStruct((2 * half, half), bf16),
        jax.ShapeDtypeStruct((2 * half, width), bf16),
    ]


def stage_scratch(width):
    return [pltpu.VMEM((width, width), f32)] * 2 + [pltpu.VMEM((2 * width, width), bf16)] * 2


def own_part(counts, block):
    width = block.shape[2]
    vector = pl.BlockSpec(memory_space=pltpu.VMEM)
    shapes = [jax.ShapeDtypeStruct((8, width), jnp.int32)] + feature_shapes(width)
    shapes += [jax.ShapeDtypeStruct((16, width), f32)] + diagonal_shapes(width)
    return pl.pallas_call(
        own_kernel,
        out_shape=shapes,
        in_specs=[pl.BlockSpec(memory_space=pltpu.HBM), vector],
        out_specs=[vector] * len(shapes),
        scratch_shapes=[pltpu.SMEM((1,), jnp.int32), pltpu.SemaphoreType.DMA]
        + stage_scratch(width),
        compiler_params=pltpu.CompilerParams(vmem_limit_bytes=16 << 20),
        name="own",
    )(counts, block)


def next_part(filled, block, features, sums, sources):
    width = block.shape[2]
    vector = pl.BlockSpec(memory_space=pltpu.VMEM)
    shapes = feature_shapes(width) + [jax.ShapeDtypeStruct((16, 2 * width), f32)]
    shapes += [jax.ShapeDtypeStruct((2 * width, width), bf16)] + diagonal_shapes(width)
    return pl.pallas_call(
        functools.partial(next_kernel, sources),
        out_shape=shapes,
        in_specs=[vector] * 6,
        out_specs=[vector] * len(shapes),
        scratch_shapes=stage_scratch(width),
        compiler_params=pltpu.CompilerParams(vmem_limit_bytes=20 << 20),
        name="next",
    )(filled, block, *features, sums)


def late_tiles(count, width):
    tiles = []
    for query in range(count):
        first = max(query + 1, 2)
        tiles += diagonal_tiles(query * width, width) if query >= 2 else []
        tiles += [(key * width, width, query * width, width, width) for key in range(first, count)]
    return tiles


def scored(weight, place, sums):
    vector, live = row_of(place) < 3, weight > 0.0
    density_sum = jnp.where(live, sums[3:4], 1.0)
    pull = place * density_sum - sums
    return jnp.where(vector & live, pull / (-SCALE * EPS * EPS * density_sum), 0.0)


def whole_cell(blocks, live):
    weight = jnp.concatenate(
        [jnp.where(on, block[0, 3:4], 0.0) for on, block in zip(live, blocks)], axis=1
    )
    whole = jnp.concatenate([block[0] for block in blocks], axis=1)
    vector = row_of(whole) < 3
    parts = grid_parts(jnp.where(vector, whole * SCALE, 0.0))
    place = parts[0] + parts[1] + parts[2]
    middle = jnp.sum(place * weight, axis=1, keepdims=True)
    middle = middle / jnp.sum(weight, axis=1, keepdims=True)
    return weight, place, jnp.where(vector, place - middle, 0.0)


def finish(blocks, total_slots, weight, centred, score, totals, outs):
    scores_out, drift_out, start_out, speed_out = outs
    width = blocks[0].shape[2]
    spread = totals.shape[1]
    drift = drift_sum(totals, centred[:, 0:spread], score[:, 0:spread])
    factor = 1.0 / (SCALE * SCALE * SCALE * total_slots)
    live = (row_of(drift) < 3) & (weight[:, 0:spread] > 0.0)
    drift = jnp.where(live, drift * factor, 0.0)
    largest = jnp.max(rows_sum(drift * drift), axis=1, keepdims=True)
    speed_out[...] = jnp.broadcast_to(jnp.sqrt(largest), speed_out.shape)
    scores_out[...] = score[:, 0:width]
    for part in range(width // 128):
        lanes = slice(part * 128, part * 128 + 128)
        for axis in range(3):
            drift_out[axis, part : part + 1, :] = drift[axis : axis + 1, lanes]
            start_out[axis, part : part + 1, :] = blocks[0][0, axis : axis + 1, lanes]


def sweep_kernel(sources, *refs):
    count = len(sources)
    filled, blocks, refs = refs[0], refs[1 : count + 1], list(refs[count + 1 :])
    blocks = blocks[:2] + blocks[:1:-1]
    own, following, refs = refs[:5], refs[5:12], refs[12:]
    outs, (key_ref, query_ref, moment_ref, flux_ref, sums_ref, totals_ref), refs = (
        refs[:4], refs[4:10], refs[10:]
    )
    width = blocks[0].shape[2]
    half = 2 * width
    scratch, distance_refs = refs[:4], refs[4:]

    live = [lanes_of(owner_of(source), width) < filled[0:1, :] for source in sources]
    late = range(2, count)
    for index in late:
        _, _, key, query, moment = prepared(blocks[index][0], live[index])
        lanes = pl.ds((index - 2) * width, width)
        key_ref[lanes, :] = key
        query_ref[:, lanes] = query
        moment_ref[:, lanes] = moment
    weight, place, centred = whole_cell(blocks, live)
    lanes = [pl.ds((index - 2) * width, width) for index in late]
    keys = [own[0], following[0]] + [key_ref.at[lane, :] for lane in lanes]
    queries = [own[1], following[1]] + [query_ref.at[:, lane] for lane in lanes]
    moments = [own[2], following[2]] + [moment_ref.at[:, lane] for lane in lanes]
    exponent = exponent_of(looked_up(keys, width, 0), looked_up(queries, width, 1))

    sums_ref[:, 0:half] = following[3][...]
    sums_ref[:, half:] = jnp.zeros_like(sums_ref[:, half:])
    tiles = late_tiles(count, width)
    stage(
        tiles, exponent, looked_up(moments, width, 1), sums_ref, scratch[:2], scratch[2:],
        distance_refs,
    )
    score = scored(weight, place, joined(sums_ref[...]))
    flux_ref[...] = drift_rows(weight, centred, score)
    totals_ref[...] = jnp.zeros_like(totals_ref)

    def fluxes(start, size):
        return flux_ref[:, pl.ds(start, size)]

    early = diagonal_tiles(0, width) + [(width, width, 0, width, width)]
    early += diagonal_tiles(width, width)
    for tile, split in zip(early + tiles, own[3:5] + following[4:7] + distance_refs):
        add_distances(tile, split, fluxes, totals_ref)
    finish(blocks, count * width, weight, centred, score, totals_ref[...], outs)


def sweep_shapes(width, copies):
    parts = jax.ShapeDtypeStruct((3, width // 128, 128), f32)
    speeds = jax.ShapeDtypeStruct((copies, 128), f32)
    return [jax.ShapeDtypeStruct((8, width), f32), parts, parts, speeds]


def sweep(counts, blocks, sources):
    count, width = len(blocks), blocks[0].shape[2]
    slots, late = count * width, (count - 2) * width
    filled, *own = own_part(counts, blocks[0])
    following = next_part(filled, blocks[1], own[:3], own[3], sources[1])
    early = [*own[:3], *own[4:], *following]
    vector = pl.BlockSpec(memory_space=pltpu.VMEM)
    distances = [pltpu.VMEM((2 * tile[1], tile[3]), bf16) for tile in late_tiles(count, width)]
    return pl.pallas_call(
        functools.partial(sweep_kernel, sources),
        out_shape=sweep_shapes(width, 8),
        in_specs=[vector] * (1 + count + len(early)),
        out_specs=[vector] * 4,
        scratch_shapes=[
            pltpu.VMEM((late, DISTANCE_ROWS), bf16),
            pltpu.VMEM((DISTANCE_ROWS, late), bf16),
            pltpu.VMEM((16, late), bf16),
            pltpu.VMEM((DRIFT_ROWS, slots), bf16),
            pltpu.VMEM((16, slots), f32),
            pltpu.VMEM((DRIFT_ROWS // 2, slots), f32),
        ]
        + stage_scratch(width)
        + distances,
        compiler_params=pltpu.CompilerParams(vmem_limit_bytes=24 << 20),
        name="sweep",
    )(filled, *blocks[:2], *blocks[:1:-1], *early)


def long_kernel(sources, filled, *refs):
    count = len(sources)
    blocks, outs, refs = refs[:count], refs[count : count + 4], refs[count + 4 :]
    key_ref, query_ref, moment_ref, flux_ref, sums_ref, totals_ref, exponent_ref, split_ref = refs
    width = blocks[0].shape[2]
    live = [lanes_of(owner_of(source), width) < filled[0] for source in sources]
    for index, (block, on) in enumerate(zip(blocks, live)):
        _, _, key, query, moment = prepared(block[0], on)
        lanes = pl.ds(index * width, width)
        key_ref[lanes, :] = key
        query_ref[:, lanes] = query
        moment_ref[:, lanes] = moment
    weight, place, centred = whole_cell(blocks, live)
    sums_ref[...] = jnp.zeros_like(sums_ref)
    totals_ref[...] = jnp.zeros_like(totals_ref)

    def block_tile(key, query, both):
        start, first = (pl.multiple_of(block * width, width) for block in (key, query))
        return (start, width, first, width, width if both else 0)

    def fill(tile):
        key, keys, query, queries, _ = tile
        exponent_ref[...] = product(key_ref[pl.ds(key, keys), :], query_ref[:, pl.ds(query, queries)])

    def blobs(key, query, both):
        tile = block_tile(key, query, both)
        fill(tile)
        split_blobs(exponent_ref, split_ref)
        add_blobs(tile, split_ref, lambda at, size: moment_ref[:, pl.ds(at, size)], sums_ref)

    @pl.loop(0, count)
    def _(query):
        blobs(query, query, False)

        @pl.loop(query + 1, count)
        def _(key):
            blobs(key, query, True)

    score = scored(weight, place, joined(sums_ref[...]))
    flux_ref[...] = drift_rows(weight, centred, score)

    @pl.loop(0, count)
    def _(key):
        tile = block_tile(key, 0, False)
        fill(tile)
        split_distances(exponent_ref, split_ref)
        add_distances(tile, split_ref, lambda at, size: flux_ref[:, pl.ds(at, size)], totals_ref)

    finish(blocks, count * width, weight, centred, score, totals_ref[...], outs)


def long_sweep(counts, blocks, sources, copies):
    count, width = len(blocks), blocks[0].shape[2]
    slots = count * width
    vector = pl.BlockSpec(memory_space=pltpu.VMEM)
    return pl.pallas_call(
        functools.partial(long_kernel, sources),
        out_shape=sweep_shapes(width, copies),
        in_specs=[pl.BlockSpec(memory_space=pltpu.SMEM)] + [vector] * count,
        out_specs=[vector] * 4,
        scratch_shapes=[
            pltpu.VMEM((slots, DISTANCE_ROWS), bf16),
            pltpu.VMEM((DISTANCE_ROWS, slots), bf16),
            pltpu.VMEM((16, slots), bf16),
            pltpu.VMEM((DRIFT_ROWS, slots), bf16),
            pltpu.VMEM((16, slots), f32),
            pltpu.VMEM((DRIFT_ROWS // 2, width), f32),
            pltpu.VMEM((width, width), f32),
            pltpu.VMEM((2 * width, width), bf16),
        ],
        compiler_params=pltpu.CompilerParams(vmem_limit_bytes=(16 << 20) + slots * 2688),
        name="sweep",
    )(counts, *blocks)


def swapped(value, axis, step):
    pairs = [(i, i ^ step) for i in range(lax.axis_size(axis))]
    return lax.ppermute(value, axis, pairs)


def bits(size):
    return [1 << bit for bit in range(size.bit_length() - 1)]


ROUNDS = ((2, 3, 1, 0), (3, 2, 0, 1), (1, 0, 3, 2))


def gathered(block):
    size = lax.axis_size("sharers")
    if size == len(ROUNDS) + 1:
        blocks, sources = [block], [tuple(range(size))]
        for targets in ROUNDS:
            blocks.append(lax.ppermute(block, "sharers", list(enumerate(targets))))
            sources.append(tuple(targets.index(i) for i in range(size)))
        return blocks, sources
    for step in bits(size):
        block = jnp.concatenate([block, swapped(block, "sharers", step)], axis=0)
    sources = [tuple(i ^ step for i in range(size)) for step in range(size)]
    return [block[i : i + 1] for i in range(size)], sources


def local(velocities, weights, counts):
    package = jnp.concatenate([velocities, weights[:, None]], axis=1)
    blocks, sources = gathered(jnp.pad(package, ((0, 0), (0, 4), (0, 0))))
    if len(blocks) == len(ROUNDS) + 1:
        scores, drift, start, speeds = sweep(counts, blocks, sources)
        for step in bits(lax.axis_size("cells")):
            speeds = jnp.maximum(speeds, swapped(speeds, "cells", 2 * step - 1))
        largest = speeds[0:1]
    else:
        axes = ("cells", "sharers")
        scores, drift, start, speeds = long_sweep(counts, blocks, sources, lax.axis_size(axes))
        largest = jnp.max(lax.all_to_all(speeds[:, None], axes, 0, 0, tiled=True), axis=0)
    time_step = 0.5 / (largest + 1e-06)
    moved = start + time_step[None] * drift
    return moved.reshape(velocities.shape), scores[None, 0:3]


def solution(mesh):
    in_specs = (
        P(("groups", "cells"), None, "sharers"),
        P(("groups", "cells"), "sharers"),
        P(("groups", "cells")),
    )
    out_specs = (P(("groups", "cells"), None, "sharers"), P(("groups", "cells"), None, "sharers"))
    return jax.shard_map(local, mesh=mesh, in_specs=in_specs, out_specs=out_specs, check_vma=False)
```

```python
import functools
import functools
import math

import jax
import jax.numpy as jnp
from jax import lax
from jax.experimental import pallas as pl
from jax.experimental.pallas import tpu as pltpu
from jax.sharding import PartitionSpec as P

EPS = 0.35
SCALE = math.sqrt(math.log2(math.e) / (2.0 * EPS * EPS))
GRID = 4.0
TINY = 1e-30
GROUP = 32
DISTANCE_ROWS = 96
DRIFT_ROWS = 64
bf16, f32 = jnp.bfloat16, jnp.float32


def round_bf16(value):
    return value.astype(bf16).astype(f32)


def pieces(value, count):
    parts = []
    for _ in range(count):
        part = round_bf16(value)
        parts.append(part)
        value = value - part
    return parts


def row_of(value):
    return lax.broadcasted_iota(jnp.int32, value.shape, 0)


def rows_sum(value):
    return jnp.sum(value, axis=0, keepdims=True)


def stacked(groups):
    if len(groups) % 2:
        groups = groups + [jnp.zeros_like(groups[0])]
    return jnp.concatenate(groups, axis=0).astype(bf16)


def scalar_groups(value, like):
    row = row_of(like)
    first, second, third = pieces(value, 3)
    low = jnp.where(row == 0, first, jnp.where(row == 1, second, jnp.where(row == 2, third, 0.0)))
    high = jnp.where(row == 3, first, jnp.where(row == 4, second, jnp.where(row == 5, third, 0.0)))
    ones_low, ones_high = row < 3, (row >= 3) & (row < 6)
    return jnp.where(ones_high, 1.0, low), jnp.where(ones_low, 1.0, high)


def grid_parts(place):
    coarse = jnp.floor(place * GRID + 0.5) * (1.0 / GRID)
    return [coarse] + pieces(place - coarse, 2)


def distance_features(parts):
    coarse, fine, rest = parts
    minor = fine + rest
    query_norm, key_norm = scalar_groups(-rows_sum(coarse * coarse), coarse)
    query_less, key_less = scalar_groups(-rows_sum(minor * (2.0 * coarse + minor)), coarse)
    key = [coarse, key_norm, coarse, coarse, fine, rest, key_less, fine, fine, rest, rest]
    coarse, fine, rest = coarse * 2.0, fine * 2.0, rest * 2.0
    query = [coarse, query_norm, fine, rest, coarse, coarse, query_less, fine, rest, fine, rest]
    return stacked(key), stacked(query)


def weighted_rows(weight, value):
    row = row_of(value)
    whole = jnp.where(row < 3, value, jnp.where(row == 3, 1.0, 0.0)) * weight
    first, second, third = pieces(whole, 3)
    return stacked([first, second + pltpu.roll(third, 4, 0)])


def product(left, right):
    return jnp.dot(left, right, preferred_element_type=f32)


def store_split(ref, rows, matrix):
    half = ref.shape[0] // 2
    upper = matrix.astype(bf16)
    ref[rows, :] = upper
    ref[pl.ds(half + rows.start, rows.size), :] = (matrix - upper.astype(f32)).astype(bf16)


def sum_rows(left, ref):
    return product(jnp.concatenate([left, left], axis=1), ref[...])


def sum_columns(left, ref):
    both = lax.dot_general(left, ref[...], (((1,), (1,)), ((), ())), preferred_element_type=f32)
    half = ref.shape[0] // 2
    return both[:, :half] + both[:, half:]


def sum_rows_less(left, ref):
    half = ref.shape[0] // 2
    both = product(left, ref[:half, :])
    few = left.shape[0] // 2
    return both[:few] + product(left[:few], ref[half:, :]), both[few:]


def sum_columns_less(left, ref):
    half, few = ref.shape[0] // 2, left.shape[0] // 2
    turned = (((1,), (1,)), ((), ()))
    both = lax.dot_general(left, ref[:half, :], turned, preferred_element_type=f32)
    less = lax.dot_general(left[:few], ref[half:, :], turned, preferred_element_type=f32)
    return both[:few] + less, both[few:]


def joined(total):
    upper, lower = total[0:8], total[8:16]
    return upper + lower + pltpu.roll(lower, 4, 0)


def drift_rows(weight, place, score):
    row = row_of(place)
    base = place + jnp.where(row == 3, 1.0, 0.0) + pltpu.roll(score, 4, 0)
    cubic = rows_sum(place * place) * score - rows_sum(place * score) * place
    groups = [weight * base]
    for i in range(3):
        here = slice(i, i + 1)
        groups.append(weight * jnp.where(row == 3, cubic[here], place[here] * base))
    return stacked(sum(map(list, zip(*[pieces(group, 2) for group in groups])), []))


def drift_sum(total, place, score):
    row = row_of(place)
    first, *rest = [total[8 * i : 8 * i + 8] for i in range(4)]
    turned = [pltpu.roll(group, 4, 0) for group in rest]
    count, scores = first[3:4], pltpu.roll(first, 4, 0)
    square, both = rows_sum(place * place), rows_sum(place * score)
    trace = rest[0][0:1] + rest[1][1:2] + rest[2][2:3]
    cross = turned[0][0:1] + turned[1][1:2] + turned[2][2:3]
    drift = score * (square * count - 2.0 * rows_sum(place * first) + trace) - square * scores
    drift += both * first + place * (
        rows_sum(place * scores) + rows_sum(score * first) - both * count - cross
    )
    ends = []
    for i in range(3):
        here = slice(i, i + 1)
        drift += 2.0 * place[here] * turned[i] - score[here] * rest[i]
        ends.append(rows_sum(place * turned[i]) + rest[i][3:4])
    return drift - jnp.where(row == 0, ends[0], jnp.where(row == 1, ends[1], ends[2]))


def widened(block):
    return jnp.concatenate([block[0], jnp.zeros_like(block[0])], axis=0)


def prepared(whole, live):
    weight = jnp.where(live, whole[3:4], 0.0)
    parts = grid_parts(jnp.where(row_of(whole) < 3, whole * SCALE, 0.0))
    place = parts[0] + parts[1] + parts[2]
    key, query = distance_features(parts)
    return weight, place, key.T, query, weighted_rows(weight, place)


def split_blobs(exponent, split):
    for group in range(0, exponent.shape[0], GROUP):
        rows = pl.ds(group, GROUP)
        store_split(split, rows, jnp.exp2(exponent[rows, :]))


def split_distances(exponent, split):
    for group in range(0, exponent.shape[0], GROUP):
        rows = pl.ds(group, GROUP)
        negative = jnp.minimum(exponent[rows, :], -TINY)
        store_split(split, rows, negative * lax.rsqrt(-negative))


def diagonal_tiles(start, width):
    half = width // 2
    return [(start, half, start, half, 0), (start + half, half, start, width, half)]


def add_blobs(tile, split, moments, sums_ref):
    key, keys, query, queries, turned = tile
    sums_ref[:, pl.ds(query, queries)] += sum_rows(moments(key, keys), split)
    if turned:
        sums_ref[:, pl.ds(key, keys)] += sum_columns(moments(query, turned), split.at[:, 0:turned])


def add_distances(tile, split, fluxes, totals_ref):
    key, keys, query, queries, turned = tile
    upper, lower = sum_rows_less(fluxes(key, keys), split)
    totals_ref[:, pl.ds(query, queries)] += upper + lower
    if turned:
        upper, lower = sum_columns_less(fluxes(query, turned), split.at[:, 0:turned])
        totals_ref[:, pl.ds(key, keys)] += upper + lower


def stage(tiles, exponent, moments, sums_ref, exponent_refs, split_refs, distance_refs):
    def buffer(index):
        _, keys, _, queries, _ = tiles[index]
        return exponent_refs[index % 2].at[0:keys, 0:queries]

    buffer(0)[...] = exponent(tiles[0])
    for index, tile in enumerate(tiles):
        if index + 1 < len(tiles):
            buffer(index + 1)[...] = exponent(tiles[index + 1])
        split = split_refs[index % 2].at[0 : 2 * tile[1], 0 : tile[3]]
        split_blobs(buffer(index), split)
        add_blobs(tile, split, moments, sums_ref)
        split_distances(buffer(index), distance_refs[index])


def looked_up(refs, width, axis):
    def read(start, size):
        at = pl.ds(start % width, size)
        ref = refs[start // width]
        return ref[at, :] if axis == 0 else ref[:, at]

    return read


def exponent_of(keys, queries):
    return lambda tile: product(keys(tile[0], tile[1]), queries(tile[2], tile[3]))


def lanes_of(source, width):
    return lax.broadcasted_iota(jnp.int32, (1, width), 1) + source * width


def owner_of(sources):
    here = lax.axis_index("sharers")
    return sum(jnp.where(here == i, source, 0) for i, source in enumerate(sources))


def own_kernel(filled, block, key_out, query_out, moment_out, sums_out, first_out, second_out,
               *scratch):
    width = block.shape[2]
    live = lanes_of(lax.axis_index("sharers"), width) < filled[...]
    _, _, key, query, moment = prepared(widened(block), live)
    key_out[...] = key
    query_out[...] = query
    moment_out[...] = moment
    sums_out[...] = jnp.zeros_like(sums_out)
    exponent = exponent_of(looked_up([key_out], width, 0), looked_up([query_out], width, 1))
    moments = looked_up([moment_out], width, 1)
    tiles = diagonal_tiles(0, width)
    stage(tiles, exponent, moments, sums_out, scratch[:2], scratch[2:], (first_out, second_out))


def next_kernel(sources, filled, block, own_key, own_query, own_moment, own_sums, key_out,
                query_out, moment_out, sums_out, tile_out, first_out, second_out, *scratch):
    width = block.shape[2]
    live = lanes_of(owner_of(sources), width) < filled[...]
    _, _, key, query, moment = prepared(widened(block), live)
    key_out[...] = key
    query_out[...] = query
    moment_out[...] = moment
    sums_out[:, 0:width] = own_sums[...]
    sums_out[:, width:] = jnp.zeros_like(own_sums)
    exponent = exponent_of(
        looked_up([own_key, key_out], width, 0), looked_up([own_query, query_out], width, 1)
    )
    moments = looked_up([own_moment, moment_out], width, 1)
    tiles = [(width, width, 0, width, width)] + diagonal_tiles(width, width)
    distances = (tile_out, first_out, second_out)
    stage(tiles, exponent, moments, sums_out, scratch[:2], scratch[2:], distances)


def feature_shapes(width):
    return [
        jax.ShapeDtypeStruct((width, DISTANCE_ROWS), bf16),
        jax.ShapeDtypeStruct((DISTANCE_ROWS, width), bf16),
        jax.ShapeDtypeStruct((16, width), bf16),
    ]


def diagonal_shapes(width):
    half = width // 2
    return [
        jax.ShapeDtypeStruct((2 * half, half), bf16),
        jax.ShapeDtypeStruct((2 * half, width), bf16),
    ]


def stage_scratch(width):
    return [pltpu.VMEM((width, width), f32)] * 2 + [pltpu.VMEM((2 * width, width), bf16)] * 2


def own_part(filled, block):
    width = block.shape[2]
    vector = pl.BlockSpec(memory_space=pltpu.VMEM)
    shapes = feature_shapes(width) + [jax.ShapeDtypeStruct((16, width), f32)] + diagonal_shapes(width)
    return pl.pallas_call(
        own_kernel,
        out_shape=shapes,
        in_specs=[vector] * 2,
        out_specs=[vector] * len(shapes),
        scratch_shapes=stage_scratch(width),
        compiler_params=pltpu.CompilerParams(vmem_limit_bytes=16 << 20),
        name="own",
    )(filled, block)


def next_part(filled, block, features, sums, sources):
    width = block.shape[2]
    vector = pl.BlockSpec(memory_space=pltpu.VMEM)
    shapes = feature_shapes(width) + [jax.ShapeDtypeStruct((16, 2 * width), f32)]
    shapes += [jax.ShapeDtypeStruct((2 * width, width), bf16)] + diagonal_shapes(width)
    return pl.pallas_call(
        functools.partial(next_kernel, sources),
        out_shape=shapes,
        in_specs=[vector] * 6,
        out_specs=[vector] * len(shapes),
        scratch_shapes=stage_scratch(width),
        compiler_params=pltpu.CompilerParams(vmem_limit_bytes=20 << 20),
        name="next",
    )(filled, block, *features, sums)


def late_tiles(count, width):
    tiles = []
    for query in range(count):
        first = max(query + 1, 2)
        tiles += diagonal_tiles(query * width, width) if query >= 2 else []
        tiles += [(key * width, width, query * width, width, width) for key in range(first, count)]
    return tiles


def scored(weight, place, sums):
    vector, live = row_of(place) < 3, weight > 0.0
    density_sum = jnp.where(live, sums[3:4], 1.0)
    pull = place * density_sum - sums
    return jnp.where(vector & live, pull / (-SCALE * EPS * EPS * density_sum), 0.0)


def whole_cell(blocks, live):
    weight = jnp.concatenate(
        [jnp.where(on, block[0, 3:4], 0.0) for on, block in zip(live, blocks)], axis=1
    )
    whole = jnp.concatenate([widened(block) for block in blocks], axis=1)
    vector = row_of(whole) < 3
    parts = grid_parts(jnp.where(vector, whole * SCALE, 0.0))
    place = parts[0] + parts[1] + parts[2]
    middle = jnp.sum(place * weight, axis=1, keepdims=True)
    middle = middle / jnp.sum(weight, axis=1, keepdims=True)
    return weight, place, jnp.where(vector, place - middle, 0.0)


def finish(blocks, total_slots, weight, centred, score, totals, outs):
    scores_out, drift_out, start_out, speed_out = outs
    width = blocks[0].shape[2]
    spread = totals.shape[1]
    drift = drift_sum(totals, centred[:, 0:spread], score[:, 0:spread])
    factor = 1.0 / (SCALE * SCALE * SCALE * total_slots)
    live = (row_of(drift) < 3) & (weight[:, 0:spread] > 0.0)
    drift = jnp.where(live, drift * factor, 0.0)
    largest = jnp.max(rows_sum(drift * drift), axis=1, keepdims=True)
    speed_out[...] = jnp.broadcast_to(jnp.sqrt(largest), speed_out.shape)
    scores_out[...] = score[:, 0:width]
    for part in range(width // 128):
        lanes = slice(part * 128, part * 128 + 128)
        for axis in range(3):
            drift_out[axis, part : part + 1, :] = drift[axis : axis + 1, lanes]
            start_out[axis, part : part + 1, :] = blocks[0][0, axis : axis + 1, lanes]


def sweep_kernel(sources, *refs):
    count = len(sources)
    filled, blocks, refs = refs[0], refs[1 : count + 1], list(refs[count + 1 :])
    blocks = blocks[:2] + blocks[:1:-1]
    own, following, refs = refs[:5], refs[5:12], refs[12:]
    outs, (key_ref, query_ref, moment_ref, flux_ref, sums_ref, totals_ref), refs = (
        refs[:4], refs[4:10], refs[10:]
    )
    width = blocks[0].shape[2]
    half = 2 * width
    scratch, distance_refs = refs[:4], refs[4:]

    live = [lanes_of(owner_of(source), width) < filled[...] for source in sources]
    late = range(2, count)
    for index in late:
        _, _, key, query, moment = prepared(widened(blocks[index]), live[index])
        lanes = pl.ds((index - 2) * width, width)
        key_ref[lanes, :] = key
        query_ref[:, lanes] = query
        moment_ref[:, lanes] = moment
    weight, place, centred = whole_cell(blocks, live)
    lanes = [pl.ds((index - 2) * width, width) for index in late]
    keys = [own[0], following[0]] + [key_ref.at[lane, :] for lane in lanes]
    queries = [own[1], following[1]] + [query_ref.at[:, lane] for lane in lanes]
    moments = [own[2], following[2]] + [moment_ref.at[:, lane] for lane in lanes]
    exponent = exponent_of(looked_up(keys, width, 0), looked_up(queries, width, 1))

    sums_ref[:, 0:half] = following[3][...]
    sums_ref[:, half:] = jnp.zeros_like(sums_ref[:, half:])
    tiles = late_tiles(count, width)
    stage(
        tiles, exponent, looked_up(moments, width, 1), sums_ref, scratch[:2], scratch[2:],
        distance_refs,
    )
    score = scored(weight, place, joined(sums_ref[...]))
    flux_ref[...] = drift_rows(weight, centred, score)
    totals_ref[...] = jnp.zeros_like(totals_ref)

    def fluxes(start, size):
        return flux_ref[:, pl.ds(start, size)]

    early = diagonal_tiles(0, width) + [(width, width, 0, width, width)]
    early += diagonal_tiles(width, width)
    for tile, split in zip(early + tiles, own[3:5] + following[4:7] + distance_refs):
        add_distances(tile, split, fluxes, totals_ref)
    finish(blocks, count * width, weight, centred, score, totals_ref[...], outs)


def sweep_shapes(width, copies):
    parts = jax.ShapeDtypeStruct((3, width // 128, 128), f32)
    speeds = jax.ShapeDtypeStruct((copies, 128), f32)
    return [jax.ShapeDtypeStruct((8, width), f32), parts, parts, speeds]


def sweep(filled, blocks, sources):
    count, width = len(blocks), blocks[0].shape[2]
    slots, late = count * width, (count - 2) * width
    own = own_part(filled, blocks[0])
    following = next_part(filled, blocks[1], own[:3], own[3], sources[1])
    early = [*own[:3], *own[4:], *following]
    vector = pl.BlockSpec(memory_space=pltpu.VMEM)
    distances = [pltpu.VMEM((2 * tile[1], tile[3]), bf16) for tile in late_tiles(count, width)]
    return pl.pallas_call(
        functools.partial(sweep_kernel, sources),
        out_shape=sweep_shapes(width, 1),
        in_specs=[vector] * (1 + count + len(early)),
        out_specs=[vector] * 4,
        scratch_shapes=[
            pltpu.VMEM((late, DISTANCE_ROWS), bf16),
            pltpu.VMEM((DISTANCE_ROWS, late), bf16),
            pltpu.VMEM((16, late), bf16),
            pltpu.VMEM((DRIFT_ROWS, slots), bf16),
            pltpu.VMEM((16, slots), f32),
            pltpu.VMEM((DRIFT_ROWS // 2, slots), f32),
        ]
        + stage_scratch(width)
        + distances,
        compiler_params=pltpu.CompilerParams(vmem_limit_bytes=24 << 20),
        name="sweep",
    )(filled, *blocks[:2], *blocks[:1:-1], *early)


def long_kernel(sources, filled, *refs):
    count = len(sources)
    blocks, outs, refs = refs[:count], refs[count : count + 4], refs[count + 4 :]
    key_ref, query_ref, moment_ref, flux_ref, sums_ref, totals_ref, exponent_ref, split_ref = refs
    width = blocks[0].shape[2]
    live = [lanes_of(owner_of(source), width) < filled[...] for source in sources]
    for index, (block, on) in enumerate(zip(blocks, live)):
        _, _, key, query, moment = prepared(widened(block), on)
        lanes = pl.ds(index * width, width)
        key_ref[lanes, :] = key
        query_ref[:, lanes] = query
        moment_ref[:, lanes] = moment
    weight, place, centred = whole_cell(blocks, live)
    sums_ref[...] = jnp.zeros_like(sums_ref)
    totals_ref[...] = jnp.zeros_like(totals_ref)

    def block_tile(key, query, both):
        start, first = (pl.multiple_of(block * width, width) for block in (key, query))
        return (start, width, first, width, width if both else 0)

    def fill(tile):
        key, keys, query, queries, _ = tile
        exponent_ref[...] = product(key_ref[pl.ds(key, keys), :], query_ref[:, pl.ds(query, queries)])

    def blobs(key, query, both):
        tile = block_tile(key, query, both)
        fill(tile)
        split_blobs(exponent_ref, split_ref)
        add_blobs(tile, split_ref, lambda at, size: moment_ref[:, pl.ds(at, size)], sums_ref)

    @pl.loop(0, count)
    def _(query):
        blobs(query, query, False)

        @pl.loop(query + 1, count)
        def _(key):
            blobs(key, query, True)

    score = scored(weight, place, joined(sums_ref[...]))
    flux_ref[...] = drift_rows(weight, centred, score)

    @pl.loop(0, count)
    def _(key):
        tile = block_tile(key, 0, False)
        fill(tile)
        split_distances(exponent_ref, split_ref)
        add_distances(tile, split_ref, lambda at, size: flux_ref[:, pl.ds(at, size)], totals_ref)

    finish(blocks, count * width, weight, centred, score, totals_ref[...], outs)


def long_sweep(filled, blocks, sources, copies):
    count, width = len(blocks), blocks[0].shape[2]
    slots = count * width
    vector = pl.BlockSpec(memory_space=pltpu.VMEM)
    return pl.pallas_call(
        functools.partial(long_kernel, sources),
        out_shape=sweep_shapes(width, copies),
        in_specs=[vector] * (1 + count),
        out_specs=[vector] * 4,
        scratch_shapes=[
            pltpu.VMEM((slots, DISTANCE_ROWS), bf16),
            pltpu.VMEM((DISTANCE_ROWS, slots), bf16),
            pltpu.VMEM((16, slots), bf16),
            pltpu.VMEM((DRIFT_ROWS, slots), bf16),
            pltpu.VMEM((16, slots), f32),
            pltpu.VMEM((DRIFT_ROWS // 2, width), f32),
            pltpu.VMEM((width, width), f32),
            pltpu.VMEM((2 * width, width), bf16),
        ],
        compiler_params=pltpu.CompilerParams(vmem_limit_bytes=(16 << 20) + slots * 2688),
        name="sweep",
    )(filled, *blocks)


def swapped(value, axis, step):
    pairs = [(i, i ^ step) for i in range(lax.axis_size(axis))]
    return lax.ppermute(value, axis, pairs)


def bits(size):
    return [1 << bit for bit in range(size.bit_length() - 1)]


ROUNDS = ((2, 3, 1, 0), (3, 2, 0, 1), (1, 0, 3, 2))


def gathered(block):
    size = lax.axis_size("sharers")
    if size == len(ROUNDS) + 1:
        blocks, sources = [block], [tuple(range(size))]
        for targets in ROUNDS:
            blocks.append(lax.ppermute(block, "sharers", list(enumerate(targets))))
            sources.append(tuple(targets.index(i) for i in range(size)))
        return blocks, sources
    for step in bits(size):
        block = jnp.concatenate([block, swapped(block, "sharers", step)], axis=0)
    sources = [tuple(i ^ step for i in range(size)) for step in range(size)]
    return [block[i : i + 1] for i in range(size)], sources


def local(velocities, weights, counts):
    filled = counts.reshape(1, 1)
    blocks, sources = gathered(jnp.concatenate([velocities, weights[:, None]], axis=1))
    if len(blocks) == len(ROUNDS) + 1:
        scores, drift, start, speeds = sweep(filled, blocks, sources)
        for step in bits(lax.axis_size("cells")):
            speeds = jnp.maximum(speeds, swapped(speeds, "cells", 2 * step - 1))
        largest = speeds
    else:
        axes = ("cells", "sharers")
        scores, drift, start, speeds = long_sweep(filled, blocks, sources, lax.axis_size(axes))
        largest = jnp.max(lax.all_to_all(speeds[:, None], axes, 0, 0, tiled=True), axis=0)
    time_step = 0.5 / (largest + 1e-06)
    moved = start + time_step[None] * drift
    return moved.reshape(velocities.shape), scores[None, 0:3]


def solution(mesh):
    in_specs = (
        P(("groups", "cells"), None, "sharers"),
        P(("groups", "cells"), "sharers"),
        P(("groups", "cells")),
    )
    out_specs = (P(("groups", "cells"), None, "sharers"), P(("groups", "cells"), None, "sharers"))
    return jax.shard_map(local, mesh=mesh, in_specs=in_specs, out_specs=out_specs, check_vma=False)
```

```python
import functools
import functools
import math

import jax
import jax.numpy as jnp
from jax import lax
from jax.experimental import pallas as pl
from jax.experimental.pallas import tpu as pltpu
from jax.sharding import PartitionSpec as P

EPS = 0.35
SCALE = math.sqrt(math.log2(math.e) / (2.0 * EPS * EPS))
GRID = 4.0
TINY = 1e-30
GROUP = 32
DISTANCE_ROWS = 96
DRIFT_ROWS = 64
bf16, f32 = jnp.bfloat16, jnp.float32


def round_bf16(value):
    return value.astype(bf16).astype(f32)


def pieces(value, count):
    parts = []
    for _ in range(count):
        part = round_bf16(value)
        parts.append(part)
        value = value - part
    return parts


def row_of(value):
    return lax.broadcasted_iota(jnp.int32, value.shape, 0)


def rows_sum(value):
    return jnp.sum(value, axis=0, keepdims=True)


def stacked(groups):
    if len(groups) % 2:
        groups = groups + [jnp.zeros_like(groups[0])]
    return jnp.concatenate(groups, axis=0).astype(bf16)


def scalar_groups(value, like):
    row = row_of(like)
    first, second, third = pieces(value, 3)
    low = jnp.where(row == 0, first, jnp.where(row == 1, second, jnp.where(row == 2, third, 0.0)))
    high = jnp.where(row == 3, first, jnp.where(row == 4, second, jnp.where(row == 5, third, 0.0)))
    ones_low, ones_high = row < 3, (row >= 3) & (row < 6)
    return jnp.where(ones_high, 1.0, low), jnp.where(ones_low, 1.0, high)


def grid_parts(place):
    coarse = jnp.floor(place * GRID + 0.5) * (1.0 / GRID)
    return [coarse] + pieces(place - coarse, 2)


def distance_features(parts):
    coarse, fine, rest = parts
    minor = fine + rest
    query_norm, key_norm = scalar_groups(-rows_sum(coarse * coarse), coarse)
    query_less, key_less = scalar_groups(-rows_sum(minor * (2.0 * coarse + minor)), coarse)
    key = [coarse, key_norm, coarse, coarse, fine, rest, key_less, fine, fine, rest, rest]
    coarse, fine, rest = coarse * 2.0, fine * 2.0, rest * 2.0
    query = [coarse, query_norm, fine, rest, coarse, coarse, query_less, fine, rest, fine, rest]
    return stacked(key), stacked(query)


def weighted_rows(weight, value):
    row = row_of(value)
    whole = jnp.where(row < 3, value, jnp.where(row == 3, 1.0, 0.0)) * weight
    first, second, third = pieces(whole, 3)
    return stacked([first, second + pltpu.roll(third, 4, 0)])


def product(left, right):
    return jnp.dot(left, right, preferred_element_type=f32)


def store_split(ref, rows, matrix):
    half = ref.shape[0] // 2
    upper = matrix.astype(bf16)
    ref[rows, :] = upper
    ref[pl.ds(half + rows.start, rows.size), :] = (matrix - upper.astype(f32)).astype(bf16)


def sum_rows(left, ref):
    return product(jnp.concatenate([left, left], axis=1), ref[...])


def sum_columns(left, ref):
    both = lax.dot_general(left, ref[...], (((1,), (1,)), ((), ())), preferred_element_type=f32)
    half = ref.shape[0] // 2
    return both[:, :half] + both[:, half:]


def sum_rows_less(left, ref):
    half = ref.shape[0] // 2
    both = product(left, ref[:half, :])
    few = left.shape[0] // 2
    return both[:few] + product(left[:few], ref[half:, :]), both[few:]


def sum_columns_less(left, ref):
    half, few = ref.shape[0] // 2, left.shape[0] // 2
    turned = (((1,), (1,)), ((), ()))
    both = lax.dot_general(left, ref[:half, :], turned, preferred_element_type=f32)
    less = lax.dot_general(left[:few], ref[half:, :], turned, preferred_element_type=f32)
    return both[:few] + less, both[few:]


def joined(total):
    upper, lower = total[0:8], total[8:16]
    return upper + lower + pltpu.roll(lower, 4, 0)


def drift_rows(weight, place, score):
    row = row_of(place)
    base = place + jnp.where(row == 3, 1.0, 0.0) + pltpu.roll(score, 4, 0)
    cubic = rows_sum(place * place) * score - rows_sum(place * score) * place
    groups = [weight * base]
    for i in range(3):
        here = slice(i, i + 1)
        groups.append(weight * jnp.where(row == 3, cubic[here], place[here] * base))
    return stacked(sum(map(list, zip(*[pieces(group, 2) for group in groups])), []))


def drift_sum(total, place, score):
    row = row_of(place)
    first, *rest = [total[8 * i : 8 * i + 8] for i in range(4)]
    turned = [pltpu.roll(group, 4, 0) for group in rest]
    count, scores = first[3:4], pltpu.roll(first, 4, 0)
    square, both = rows_sum(place * place), rows_sum(place * score)
    trace = rest[0][0:1] + rest[1][1:2] + rest[2][2:3]
    cross = turned[0][0:1] + turned[1][1:2] + turned[2][2:3]
    drift = score * (square * count - 2.0 * rows_sum(place * first) + trace) - square * scores
    drift += both * first + place * (
        rows_sum(place * scores) + rows_sum(score * first) - both * count - cross
    )
    ends = []
    for i in range(3):
        here = slice(i, i + 1)
        drift += 2.0 * place[here] * turned[i] - score[here] * rest[i]
        ends.append(rows_sum(place * turned[i]) + rest[i][3:4])
    return drift - jnp.where(row == 0, ends[0], jnp.where(row == 1, ends[1], ends[2]))


def widened(block):
    return jnp.concatenate([block[0], jnp.zeros_like(block[0])], axis=0)


def prepared(whole, live):
    weight = jnp.where(live, whole[3:4], 0.0)
    parts = grid_parts(jnp.where(row_of(whole) < 3, whole * SCALE, 0.0))
    place = parts[0] + parts[1] + parts[2]
    key, query = distance_features(parts)
    return weight, place, key.T, query, weighted_rows(weight, place)


def split_blobs(exponent, split):
    for group in range(0, exponent.shape[0], GROUP):
        rows = pl.ds(group, GROUP)
        store_split(split, rows, jnp.exp2(exponent[rows, :]))


def split_distances(exponent, split):
    for group in range(0, exponent.shape[0], GROUP):
        rows = pl.ds(group, GROUP)
        negative = jnp.minimum(exponent[rows, :], -TINY)
        store_split(split, rows, negative * lax.rsqrt(-negative))


def diagonal_tiles(start, width):
    half = width // 2
    return [(start, half, start, half, 0), (start + half, half, start, width, half)]


def add_blobs(tile, split, moments, sums_ref):
    key, keys, query, queries, turned = tile
    sums_ref[:, pl.ds(query, queries)] += sum_rows(moments(key, keys), split)
    if turned:
        sums_ref[:, pl.ds(key, keys)] += sum_columns(moments(query, turned), split.at[:, 0:turned])


def add_distances(tile, split, fluxes, totals_ref):
    key, keys, query, queries, turned = tile
    upper, lower = sum_rows_less(fluxes(key, keys), split)
    totals_ref[:, pl.ds(query, queries)] += upper + lower
    if turned:
        upper, lower = sum_columns_less(fluxes(query, turned), split.at[:, 0:turned])
        totals_ref[:, pl.ds(key, keys)] += upper + lower


def stage(tiles, exponent, moments, sums_ref, exponent_refs, split_refs, distance_refs):
    def buffer(index):
        _, keys, _, queries, _ = tiles[index]
        return exponent_refs[index % 2].at[0:keys, 0:queries]

    buffer(0)[...] = exponent(tiles[0])
    for index, tile in enumerate(tiles):
        if index + 1 < len(tiles):
            buffer(index + 1)[...] = exponent(tiles[index + 1])
        split = split_refs[index % 2].at[0 : 2 * tile[1], 0 : tile[3]]
        split_blobs(buffer(index), split)
        add_blobs(tile, split, moments, sums_ref)
        split_distances(buffer(index), distance_refs[index])


def looked_up(refs, width, axis):
    def read(start, size):
        at = pl.ds(start % width, size)
        ref = refs[start // width]
        return ref[at, :] if axis == 0 else ref[:, at]

    return read


def exponent_of(keys, queries):
    return lambda tile: product(keys(tile[0], tile[1]), queries(tile[2], tile[3]))


def lanes_of(source, width):
    return lax.broadcasted_iota(jnp.int32, (1, width), 1) + source * width


def owner_of(sources):
    here = lax.axis_index("sharers")
    return sum(jnp.where(here == i, source, 0) for i, source in enumerate(sources))


def own_kernel(filled, block, key_out, query_out, moment_out, sums_out, first_out, second_out,
               *scratch):
    width = block.shape[2]
    live = lanes_of(lax.axis_index("sharers"), width) < filled[...]
    _, _, key, query, moment = prepared(widened(block), live)
    key_out[...] = key
    query_out[...] = query
    moment_out[...] = moment
    sums_out[...] = jnp.zeros_like(sums_out)
    exponent = exponent_of(looked_up([key_out], width, 0), looked_up([query_out], width, 1))
    moments = looked_up([moment_out], width, 1)
    tiles = diagonal_tiles(0, width)
    stage(tiles, exponent, moments, sums_out, scratch[:2], scratch[2:], (first_out, second_out))


def next_kernel(sources, filled, block, own_key, own_query, own_moment, own_sums, key_out,
                query_out, moment_out, sums_out, tile_out, first_out, second_out, *scratch):
    width = block.shape[2]
    live = lanes_of(owner_of(sources), width) < filled[...]
    _, _, key, query, moment = prepared(widened(block), live)
    key_out[...] = key
    query_out[...] = query
    moment_out[...] = moment
    sums_out[:, 0:width] = own_sums[...]
    sums_out[:, width:] = jnp.zeros_like(own_sums)
    exponent = exponent_of(
        looked_up([own_key, key_out], width, 0), looked_up([own_query, query_out], width, 1)
    )
    moments = looked_up([own_moment, moment_out], width, 1)
    tiles = [(width, width, 0, width, width)] + diagonal_tiles(width, width)
    distances = (tile_out, first_out, second_out)
    stage(tiles, exponent, moments, sums_out, scratch[:2], scratch[2:], distances)


def feature_shapes(width):
    return [
        jax.ShapeDtypeStruct((width, DISTANCE_ROWS), bf16),
        jax.ShapeDtypeStruct((DISTANCE_ROWS, width), bf16),
        jax.ShapeDtypeStruct((16, width), bf16),
    ]


def diagonal_shapes(width):
    half = width // 2
    return [
        jax.ShapeDtypeStruct((2 * half, half), bf16),
        jax.ShapeDtypeStruct((2 * half, width), bf16),
    ]


def stage_scratch(width):
    return [pltpu.VMEM((width, width), f32)] * 2 + [pltpu.VMEM((2 * width, width), bf16)] * 2


def own_part(filled, block):
    width = block.shape[2]
    vector = pl.BlockSpec(memory_space=pltpu.VMEM)
    shapes = feature_shapes(width) + [jax.ShapeDtypeStruct((16, width), f32)] + diagonal_shapes(width)
    return pl.pallas_call(
        own_kernel,
        out_shape=shapes,
        in_specs=[vector] * 2,
        out_specs=[vector] * len(shapes),
        scratch_shapes=stage_scratch(width),
        compiler_params=pltpu.CompilerParams(vmem_limit_bytes=16 << 20),
        name="own",
    )(filled, block)


def next_part(filled, block, features, sums, sources):
    width = block.shape[2]
    vector = pl.BlockSpec(memory_space=pltpu.VMEM)
    shapes = feature_shapes(width) + [jax.ShapeDtypeStruct((16, 2 * width), f32)]
    shapes += [jax.ShapeDtypeStruct((2 * width, width), bf16)] + diagonal_shapes(width)
    return pl.pallas_call(
        functools.partial(next_kernel, sources),
        out_shape=shapes,
        in_specs=[vector] * 6,
        out_specs=[vector] * len(shapes),
        scratch_shapes=stage_scratch(width),
        compiler_params=pltpu.CompilerParams(vmem_limit_bytes=20 << 20),
        name="next",
    )(filled, block, *features, sums)


def late_tiles(count, width):
    tiles = []
    for query in range(count):
        first = max(query + 1, 2)
        tiles += diagonal_tiles(query * width, width) if query >= 2 else []
        tiles += [(key * width, width, query * width, width, width) for key in range(first, count)]
    return tiles


def scored(weight, place, sums):
    vector, live = row_of(place) < 3, weight > 0.0
    density_sum = jnp.where(live, sums[3:4], 1.0)
    pull = place * density_sum - sums
    return jnp.where(vector & live, pull / (-SCALE * EPS * EPS * density_sum), 0.0)


def whole_cell(blocks, live):
    weight = jnp.concatenate(
        [jnp.where(on, block[0, 3:4], 0.0) for on, block in zip(live, blocks)], axis=1
    )
    whole = jnp.concatenate([widened(block) for block in blocks], axis=1)
    vector = row_of(whole) < 3
    parts = grid_parts(jnp.where(vector, whole * SCALE, 0.0))
    place = parts[0] + parts[1] + parts[2]
    middle = jnp.sum(place * weight, axis=1, keepdims=True)
    middle = middle / jnp.sum(weight, axis=1, keepdims=True)
    return weight, place, jnp.where(vector, place - middle, 0.0)


def finish(blocks, total_slots, weight, centred, score, totals, outs):
    scores_out, drift_out, start_out, speed_out = outs
    width = blocks[0].shape[2]
    spread = totals.shape[1]
    drift = drift_sum(totals, centred[:, 0:spread], score[:, 0:spread])
    factor = 1.0 / (SCALE * SCALE * SCALE * total_slots)
    live = (row_of(drift) < 3) & (weight[:, 0:spread] > 0.0)
    drift = jnp.where(live, drift * factor, 0.0)
    largest = jnp.max(rows_sum(drift * drift), axis=1, keepdims=True)
    speed_out[...] = jnp.broadcast_to(jnp.sqrt(largest), speed_out.shape)
    scores_out[...] = score[:, 0:width]
    for part in range(width // 128):
        lanes = slice(part * 128, part * 128 + 128)
        for axis in range(3):
            drift_out[axis, part : part + 1, :] = drift[axis : axis + 1, lanes]
            start_out[axis, part : part + 1, :] = blocks[0][0, axis : axis + 1, lanes]


def sweep_kernel(sources, *refs):
    count = len(sources)
    filled, blocks, refs = refs[0], refs[1 : count + 1], list(refs[count + 1 :])
    own, following, refs = refs[:5], refs[5:12], refs[12:]
    outs, (key_ref, query_ref, moment_ref, flux_ref, sums_ref, totals_ref), refs = (
        refs[:4], refs[4:10], refs[10:]
    )
    width = blocks[0].shape[2]
    half = 2 * width
    scratch, distance_refs = refs[:4], refs[4:]

    live = [lanes_of(owner_of(source), width) < filled[...] for source in sources]
    late = range(2, count)
    for index in late:
        _, _, key, query, moment = prepared(widened(blocks[index]), live[index])
        lanes = pl.ds((index - 2) * width, width)
        key_ref[lanes, :] = key
        query_ref[:, lanes] = query
        moment_ref[:, lanes] = moment
    weight, place, centred = whole_cell(blocks, live)
    lanes = [pl.ds((index - 2) * width, width) for index in late]
    keys = [own[0], following[0]] + [key_ref.at[lane, :] for lane in lanes]
    queries = [own[1], following[1]] + [query_ref.at[:, lane] for lane in lanes]
    moments = [own[2], following[2]] + [moment_ref.at[:, lane] for lane in lanes]
    exponent = exponent_of(looked_up(keys, width, 0), looked_up(queries, width, 1))

    sums_ref[:, 0:half] = following[3][...]
    sums_ref[:, half:] = jnp.zeros_like(sums_ref[:, half:])
    tiles = late_tiles(count, width)
    stage(
        tiles, exponent, looked_up(moments, width, 1), sums_ref, scratch[:2], scratch[2:],
        distance_refs,
    )
    score = scored(weight, place, joined(sums_ref[...]))
    flux_ref[...] = drift_rows(weight, centred, score)
    totals_ref[...] = jnp.zeros_like(totals_ref)

    def fluxes(start, size):
        return flux_ref[:, pl.ds(start, size)]

    early = diagonal_tiles(0, width) + [(width, width, 0, width, width)]
    early += diagonal_tiles(width, width)
    for tile, split in zip(early + tiles, own[3:5] + following[4:7] + distance_refs):
        add_distances(tile, split, fluxes, totals_ref)
    finish(blocks, count * width, weight, centred, score, totals_ref[...], outs)


def sweep_shapes(width, copies):
    parts = jax.ShapeDtypeStruct((3, width // 128, 128), f32)
    speeds = jax.ShapeDtypeStruct((copies, 128), f32)
    return [jax.ShapeDtypeStruct((8, width), f32), parts, parts, speeds]


def sweep(filled, blocks, sources):
    count, width = len(blocks), blocks[0].shape[2]
    slots, late = count * width, (count - 2) * width
    own = own_part(filled, blocks[0])
    following = next_part(filled, blocks[1], own[:3], own[3], sources[1])
    early = [*own[:3], *own[4:], *following]
    vector = pl.BlockSpec(memory_space=pltpu.VMEM)
    distances = [pltpu.VMEM((2 * tile[1], tile[3]), bf16) for tile in late_tiles(count, width)]
    return pl.pallas_call(
        functools.partial(sweep_kernel, sources),
        out_shape=sweep_shapes(width, 1),
        in_specs=[vector] * (1 + count + len(early)),
        out_specs=[vector] * 4,
        scratch_shapes=[
            pltpu.VMEM((late, DISTANCE_ROWS), bf16),
            pltpu.VMEM((DISTANCE_ROWS, late), bf16),
            pltpu.VMEM((16, late), bf16),
            pltpu.VMEM((DRIFT_ROWS, slots), bf16),
            pltpu.VMEM((16, slots), f32),
            pltpu.VMEM((DRIFT_ROWS // 2, slots), f32),
        ]
        + stage_scratch(width)
        + distances,
        compiler_params=pltpu.CompilerParams(vmem_limit_bytes=24 << 20),
        name="sweep",
    )(filled, *blocks, *early)


def long_kernel(sources, filled, *refs):
    count = len(sources)
    blocks, outs, refs = refs[:count], refs[count : count + 4], refs[count + 4 :]
    key_ref, query_ref, moment_ref, flux_ref, sums_ref, totals_ref, exponent_ref, split_ref = refs
    width = blocks[0].shape[2]
    live = [lanes_of(owner_of(source), width) < filled[...] for source in sources]
    for index, (block, on) in enumerate(zip(blocks, live)):
        _, _, key, query, moment = prepared(widened(block), on)
        lanes = pl.ds(index * width, width)
        key_ref[lanes, :] = key
        query_ref[:, lanes] = query
        moment_ref[:, lanes] = moment
    weight, place, centred = whole_cell(blocks, live)
    sums_ref[...] = jnp.zeros_like(sums_ref)
    totals_ref[...] = jnp.zeros_like(totals_ref)

    def block_tile(key, query, both):
        start, first = (pl.multiple_of(block * width, width) for block in (key, query))
        return (start, width, first, width, width if both else 0)

    def fill(tile):
        key, keys, query, queries, _ = tile
        exponent_ref[...] = product(key_ref[pl.ds(key, keys), :], query_ref[:, pl.ds(query, queries)])

    def blobs(key, query, both):
        tile = block_tile(key, query, both)
        fill(tile)
        split_blobs(exponent_ref, split_ref)
        add_blobs(tile, split_ref, lambda at, size: moment_ref[:, pl.ds(at, size)], sums_ref)

    @pl.loop(0, count)
    def _(query):
        blobs(query, query, False)

        @pl.loop(query + 1, count)
        def _(key):
            blobs(key, query, True)

    score = scored(weight, place, joined(sums_ref[...]))
    flux_ref[...] = drift_rows(weight, centred, score)

    @pl.loop(0, count)
    def _(key):
        tile = block_tile(key, 0, False)
        fill(tile)
        split_distances(exponent_ref, split_ref)
        add_distances(tile, split_ref, lambda at, size: flux_ref[:, pl.ds(at, size)], totals_ref)

    finish(blocks, count * width, weight, centred, score, totals_ref[...], outs)


def long_sweep(filled, blocks, sources, copies):
    count, width = len(blocks), blocks[0].shape[2]
    slots = count * width
    vector = pl.BlockSpec(memory_space=pltpu.VMEM)
    return pl.pallas_call(
        functools.partial(long_kernel, sources),
        out_shape=sweep_shapes(width, copies),
        in_specs=[vector] * (1 + count),
        out_specs=[vector] * 4,
        scratch_shapes=[
            pltpu.VMEM((slots, DISTANCE_ROWS), bf16),
            pltpu.VMEM((DISTANCE_ROWS, slots), bf16),
            pltpu.VMEM((16, slots), bf16),
            pltpu.VMEM((DRIFT_ROWS, slots), bf16),
            pltpu.VMEM((16, slots), f32),
            pltpu.VMEM((DRIFT_ROWS // 2, width), f32),
            pltpu.VMEM((width, width), f32),
            pltpu.VMEM((2 * width, width), bf16),
        ],
        compiler_params=pltpu.CompilerParams(vmem_limit_bytes=(16 << 20) + slots * 2688),
        name="sweep",
    )(filled, *blocks)


def swapped(value, axis, step):
    pairs = [(i, i ^ step) for i in range(lax.axis_size(axis))]
    return lax.ppermute(value, axis, pairs)


def bits(size):
    return [1 << bit for bit in range(size.bit_length() - 1)]


ROUNDS = ((2, 3, 1, 0), (3, 2, 0, 1), (1, 0, 3, 2))


def gathered(block):
    size = lax.axis_size("sharers")
    if size == len(ROUNDS) + 1:
        blocks, sources = [block], [tuple(range(size))]
        for targets in ROUNDS:
            blocks.append(lax.ppermute(block, "sharers", list(enumerate(targets))))
            sources.append(tuple(targets.index(i) for i in range(size)))
        return blocks, sources
    for step in bits(size):
        block = jnp.concatenate([block, swapped(block, "sharers", step)], axis=0)
    sources = [tuple(i ^ step for i in range(size)) for step in range(size)]
    return [block[i : i + 1] for i in range(size)], sources


def local(velocities, weights, counts):
    filled = counts.reshape(1, 1)
    blocks, sources = gathered(jnp.concatenate([velocities, weights[:, None]], axis=1))
    if len(blocks) == len(ROUNDS) + 1:
        scores, drift, start, speeds = sweep(filled, blocks, sources)
        for step in bits(lax.axis_size("cells")):
            speeds = jnp.maximum(speeds, swapped(speeds, "cells", 2 * step - 1))
        largest = speeds
    else:
        axes = ("cells", "sharers")
        scores, drift, start, speeds = long_sweep(filled, blocks, sources, lax.axis_size(axes))
        largest = jnp.max(lax.all_to_all(speeds[:, None], axes, 0, 0, tiled=True), axis=0)
    time_step = 0.5 / (largest + 1e-06)
    moved = start + time_step[None] * drift
    return moved.reshape(velocities.shape), scores[None, 0:3]


def solution(mesh):
    in_specs = (
        P(("groups", "cells"), None, "sharers"),
        P(("groups", "cells"), "sharers"),
        P(("groups", "cells")),
    )
    out_specs = (P(("groups", "cells"), None, "sharers"), P(("groups", "cells"), None, "sharers"))
    return jax.shard_map(local, mesh=mesh, in_specs=in_specs, out_specs=out_specs, check_vma=False)
```

```python
import functools
import functools
import math

import jax
import jax.numpy as jnp
from jax import lax
from jax.experimental import pallas as pl
from jax.experimental.pallas import tpu as pltpu
from jax.sharding import PartitionSpec as P

EPS = 0.35
SCALE = math.sqrt(math.log2(math.e) / (2.0 * EPS * EPS))
GRID = 4.0
TINY = 1e-30
GROUP = 16
DISTANCE_ROWS = 96
DRIFT_ROWS = 64
bf16, f32 = jnp.bfloat16, jnp.float32


def round_bf16(value):
    return value.astype(bf16).astype(f32)


def pieces(value, count):
    parts = []
    for _ in range(count):
        part = round_bf16(value)
        parts.append(part)
        value = value - part
    return parts


def row_of(value):
    return lax.broadcasted_iota(jnp.int32, value.shape, 0)


def rows_sum(value):
    return jnp.sum(value, axis=0, keepdims=True)


def stacked(groups):
    if len(groups) % 2:
        groups = groups + [jnp.zeros_like(groups[0])]
    return jnp.concatenate(groups, axis=0).astype(bf16)


def scalar_groups(value, like):
    row = row_of(like)
    first, second, third = pieces(value, 3)
    low = jnp.where(row == 0, first, jnp.where(row == 1, second, jnp.where(row == 2, third, 0.0)))
    high = jnp.where(row == 3, first, jnp.where(row == 4, second, jnp.where(row == 5, third, 0.0)))
    ones_low, ones_high = row < 3, (row >= 3) & (row < 6)
    return jnp.where(ones_high, 1.0, low), jnp.where(ones_low, 1.0, high)


def grid_parts(place):
    coarse = jnp.floor(place * GRID + 0.5) * (1.0 / GRID)
    return [coarse] + pieces(place - coarse, 2)


def distance_features(parts):
    coarse, fine, rest = parts
    minor = fine + rest
    query_norm, key_norm = scalar_groups(-rows_sum(coarse * coarse), coarse)
    query_less, key_less = scalar_groups(-rows_sum(minor * (2.0 * coarse + minor)), coarse)
    key = [coarse, key_norm, coarse, coarse, fine, rest, key_less, fine, fine, rest, rest]
    coarse, fine, rest = coarse * 2.0, fine * 2.0, rest * 2.0
    query = [coarse, query_norm, fine, rest, coarse, coarse, query_less, fine, rest, fine, rest]
    return stacked(key), stacked(query)


def weighted_rows(weight, value):
    row = row_of(value)
    whole = jnp.where(row < 3, value, jnp.where(row == 3, 1.0, 0.0)) * weight
    first, second, third = pieces(whole, 3)
    return stacked([first, second + pltpu.roll(third, 4, 0)])


def product(left, right):
    return jnp.dot(left, right, preferred_element_type=f32)


def store_split(ref, rows, matrix):
    half = ref.shape[0] // 2
    spread = matrix * 65537.0
    upper = spread - (spread - matrix)
    ref[rows, :] = upper.astype(bf16)
    ref[pl.ds(half + rows.start, rows.size), :] = (matrix - upper).astype(bf16)


def sum_rows(left, ref):
    return product(jnp.concatenate([left, left], axis=1), ref[...])


def sum_columns(left, ref):
    both = lax.dot_general(left, ref[...], (((1,), (1,)), ((), ())), preferred_element_type=f32)
    half = ref.shape[0] // 2
    return both[:, :half] + both[:, half:]


def sum_rows_less(left, ref):
    half = ref.shape[0] // 2
    both = product(left, ref[:half, :])
    few = left.shape[0] // 2
    return both[:few] + product(left[:few], ref[half:, :]), both[few:]


def sum_columns_less(left, ref):
    half, few = ref.shape[0] // 2, left.shape[0] // 2
    turned = (((1,), (1,)), ((), ()))
    both = lax.dot_general(left, ref[:half, :], turned, preferred_element_type=f32)
    less = lax.dot_general(left[:few], ref[half:, :], turned, preferred_element_type=f32)
    return both[:few] + less, both[few:]


def joined(total):
    upper, lower = total[0:8], total[8:16]
    return upper + lower + pltpu.roll(lower, 4, 0)


def drift_rows(weight, place, score):
    row = row_of(place)
    base = place + jnp.where(row == 3, 1.0, 0.0) + pltpu.roll(score, 4, 0)
    cubic = rows_sum(place * place) * score - rows_sum(place * score) * place
    groups = [weight * base]
    for i in range(3):
        here = slice(i, i + 1)
        groups.append(weight * jnp.where(row == 3, cubic[here], place[here] * base))
    return stacked(sum(map(list, zip(*[pieces(group, 2) for group in groups])), []))


def drift_sum(total, place, score):
    row = row_of(place)
    first, *rest = [total[8 * i : 8 * i + 8] for i in range(4)]
    turned = [pltpu.roll(group, 4, 0) for group in rest]
    count, scores = first[3:4], pltpu.roll(first, 4, 0)
    square, both = rows_sum(place * place), rows_sum(place * score)
    trace = rest[0][0:1] + rest[1][1:2] + rest[2][2:3]
    cross = turned[0][0:1] + turned[1][1:2] + turned[2][2:3]
    drift = score * (square * count - 2.0 * rows_sum(place * first) + trace) - square * scores
    drift += both * first + place * (
        rows_sum(place * scores) + rows_sum(score * first) - both * count - cross
    )
    ends = []
    for i in range(3):
        here = slice(i, i + 1)
        drift += 2.0 * place[here] * turned[i] - score[here] * rest[i]
        ends.append(rows_sum(place * turned[i]) + rest[i][3:4])
    return drift - jnp.where(row == 0, ends[0], jnp.where(row == 1, ends[1], ends[2]))


def widened(block):
    return jnp.concatenate([block[0], jnp.zeros_like(block[0])], axis=0)


def prepared(whole, live):
    weight = jnp.where(live, whole[3:4], 0.0)
    parts = grid_parts(jnp.where(row_of(whole) < 3, whole * SCALE, 0.0))
    place = parts[0] + parts[1] + parts[2]
    key, query = distance_features(parts)
    return weight, place, key.T, query, weighted_rows(weight, place)


def split_blobs(exponent, split):
    for group in range(0, exponent.shape[0], GROUP):
        rows = pl.ds(group, GROUP)
        store_split(split, rows, jnp.exp2(exponent[rows, :]))


def split_distances(exponent, split):
    for group in range(0, exponent.shape[0], GROUP):
        rows = pl.ds(group, GROUP)
        negative = jnp.minimum(exponent[rows, :], -TINY)
        store_split(split, rows, negative * lax.rsqrt(-negative))


def split_both(exponent, blobs, distances):
    for group in range(0, exponent.shape[0], GROUP):
        rows = pl.ds(group, GROUP)
        values = exponent[rows, :]
        store_split(blobs, rows, jnp.exp2(values))
        negative = jnp.minimum(values, -TINY)
        store_split(distances, rows, negative * lax.rsqrt(-negative))


def diagonal_tiles(start, width):
    half = width // 2
    return [(start, half, start, half, 0), (start + half, half, start, width, half)]


def add_blobs(tile, split, moments, sums_ref):
    key, keys, query, queries, turned = tile
    sums_ref[:, pl.ds(query, queries)] += sum_rows(moments(key, keys), split)
    if turned:
        sums_ref[:, pl.ds(key, keys)] += sum_columns(moments(query, turned), split.at[:, 0:turned])


def add_distances(tile, split, fluxes, totals_ref):
    key, keys, query, queries, turned = tile
    upper, lower = sum_rows_less(fluxes(key, keys), split)
    totals_ref[:, pl.ds(query, queries)] += upper + lower
    if turned:
        upper, lower = sum_columns_less(fluxes(query, turned), split.at[:, 0:turned])
        totals_ref[:, pl.ds(key, keys)] += upper + lower


def stage(tiles, exponent, moments, sums_ref, exponent_refs, split_refs, distance_refs):
    def buffer(index):
        _, keys, _, queries, _ = tiles[index]
        return exponent_refs[index % 2].at[0:keys, 0:queries]

    buffer(0)[...] = exponent(tiles[0])
    for index, tile in enumerate(tiles):
        if index + 1 < len(tiles):
            buffer(index + 1)[...] = exponent(tiles[index + 1])
        split = split_refs[index % 2].at[0 : 2 * tile[1], 0 : tile[3]]
        split_both(buffer(index), split, distance_refs[index])
        add_blobs(tile, split, moments, sums_ref)


def looked_up(refs, width, axis):
    def read(start, size):
        at = pl.ds(start % width, size)
        ref = refs[start // width]
        return ref[at, :] if axis == 0 else ref[:, at]

    return read


def exponent_of(keys, queries):
    return lambda tile: product(keys(tile[0], tile[1]), queries(tile[2], tile[3]))


def lanes_of(source, width):
    return lax.broadcasted_iota(jnp.int32, (1, width), 1) + source * width


def owner_of(sources):
    here = lax.axis_index("sharers")
    return sum(jnp.where(here == i, source, 0) for i, source in enumerate(sources))


def own_kernel(filled, block, key_out, query_out, moment_out, sums_out, first_out, second_out,
               *scratch):
    width = block.shape[2]
    live = lanes_of(lax.axis_index("sharers"), width) < filled[...]
    _, _, key, query, moment = prepared(widened(block), live)
    key_out[...] = key
    query_out[...] = query
    moment_out[...] = moment
    sums_out[...] = jnp.zeros_like(sums_out)
    exponent = exponent_of(looked_up([key_out], width, 0), looked_up([query_out], width, 1))
    moments = looked_up([moment_out], width, 1)
    tiles = diagonal_tiles(0, width)
    stage(tiles, exponent, moments, sums_out, scratch[:2], scratch[2:], (first_out, second_out))


def next_kernel(sources, filled, block, own_key, own_query, own_moment, own_sums, key_out,
                query_out, moment_out, sums_out, tile_out, first_out, second_out, *scratch):
    width = block.shape[2]
    live = lanes_of(owner_of(sources), width) < filled[...]
    _, _, key, query, moment = prepared(widened(block), live)
    key_out[...] = key
    query_out[...] = query
    moment_out[...] = moment
    sums_out[:, 0:width] = own_sums[...]
    sums_out[:, width:] = jnp.zeros_like(own_sums)
    exponent = exponent_of(
        looked_up([own_key, key_out], width, 0), looked_up([own_query, query_out], width, 1)
    )
    moments = looked_up([own_moment, moment_out], width, 1)
    tiles = [(width, width, 0, width, width)] + diagonal_tiles(width, width)
    distances = (tile_out, first_out, second_out)
    stage(tiles, exponent, moments, sums_out, scratch[:2], scratch[2:], distances)


def feature_shapes(width):
    return [
        jax.ShapeDtypeStruct((width, DISTANCE_ROWS), bf16),
        jax.ShapeDtypeStruct((DISTANCE_ROWS, width), bf16),
        jax.ShapeDtypeStruct((16, width), bf16),
    ]


def diagonal_shapes(width):
    half = width // 2
    return [
        jax.ShapeDtypeStruct((2 * half, half), bf16),
        jax.ShapeDtypeStruct((2 * half, width), bf16),
    ]


def stage_scratch(width):
    return [pltpu.VMEM((width, width), f32)] * 2 + [pltpu.VMEM((2 * width, width), bf16)] * 2


def own_part(filled, block):
    width = block.shape[2]
    vector = pl.BlockSpec(memory_space=pltpu.VMEM)
    shapes = feature_shapes(width) + [jax.ShapeDtypeStruct((16, width), f32)] + diagonal_shapes(width)
    return pl.pallas_call(
        own_kernel,
        out_shape=shapes,
        in_specs=[vector] * 2,
        out_specs=[vector] * len(shapes),
        scratch_shapes=stage_scratch(width),
        compiler_params=pltpu.CompilerParams(vmem_limit_bytes=16 << 20),
        name="own",
    )(filled, block)


def next_part(filled, block, features, sums, sources):
    width = block.shape[2]
    vector = pl.BlockSpec(memory_space=pltpu.VMEM)
    shapes = feature_shapes(width) + [jax.ShapeDtypeStruct((16, 2 * width), f32)]
    shapes += [jax.ShapeDtypeStruct((2 * width, width), bf16)] + diagonal_shapes(width)
    return pl.pallas_call(
        functools.partial(next_kernel, sources),
        out_shape=shapes,
        in_specs=[vector] * 6,
        out_specs=[vector] * len(shapes),
        scratch_shapes=stage_scratch(width),
        compiler_params=pltpu.CompilerParams(vmem_limit_bytes=20 << 20),
        name="next",
    )(filled, block, *features, sums)


def late_tiles(count, width):
    tiles = []
    for query in range(count):
        first = max(query + 1, 2)
        tiles += diagonal_tiles(query * width, width) if query >= 2 else []
        tiles += [(key * width, width, query * width, width, width) for key in range(first, count)]
    return tiles


def scored(weight, place, sums):
    vector, live = row_of(place) < 3, weight > 0.0
    density_sum = jnp.where(live, sums[3:4], 1.0)
    pull = place * density_sum - sums
    return jnp.where(vector & live, pull / (-SCALE * EPS * EPS * density_sum), 0.0)


def whole_cell(blocks, live):
    weight = jnp.concatenate(
        [jnp.where(on, block[0, 3:4], 0.0) for on, block in zip(live, blocks)], axis=1
    )
    whole = jnp.concatenate([widened(block) for block in blocks], axis=1)
    vector = row_of(whole) < 3
    parts = grid_parts(jnp.where(vector, whole * SCALE, 0.0))
    place = parts[0] + parts[1] + parts[2]
    middle = jnp.sum(place * weight, axis=1, keepdims=True)
    middle = middle / jnp.sum(weight, axis=1, keepdims=True)
    return weight, place, jnp.where(vector, place - middle, 0.0)


def finish(blocks, total_slots, weight, centred, score, totals, outs):
    scores_out, drift_out, start_out, speed_out = outs
    width = blocks[0].shape[2]
    spread = totals.shape[1]
    drift = drift_sum(totals, centred[:, 0:spread], score[:, 0:spread])
    factor = 1.0 / (SCALE * SCALE * SCALE * total_slots)
    live = (row_of(drift) < 3) & (weight[:, 0:spread] > 0.0)
    drift = jnp.where(live, drift * factor, 0.0)
    largest = jnp.max(rows_sum(drift * drift), axis=1, keepdims=True)
    speed_out[...] = jnp.broadcast_to(jnp.sqrt(largest), speed_out.shape)
    scores_out[...] = score[:, 0:width]
    for part in range(width // 128):
        lanes = slice(part * 128, part * 128 + 128)
        for axis in range(3):
            drift_out[axis, part : part + 1, :] = drift[axis : axis + 1, lanes]
            start_out[axis, part : part + 1, :] = blocks[0][0, axis : axis + 1, lanes]


def sweep_kernel(sources, *refs):
    count = len(sources)
    filled, blocks, refs = refs[0], refs[1 : count + 1], list(refs[count + 1 :])
    own, following, refs = refs[:5], refs[5:12], refs[12:]
    outs, (key_ref, query_ref, moment_ref, flux_ref, sums_ref, totals_ref), refs = (
        refs[:4], refs[4:10], refs[10:]
    )
    width = blocks[0].shape[2]
    half = 2 * width
    scratch, distance_refs = refs[:4], refs[4:]

    live = [lanes_of(owner_of(source), width) < filled[...] for source in sources]
    late = range(2, count)
    for index in late:
        _, _, key, query, moment = prepared(widened(blocks[index]), live[index])
        lanes = pl.ds((index - 2) * width, width)
        key_ref[lanes, :] = key
        query_ref[:, lanes] = query
        moment_ref[:, lanes] = moment
    weight, place, centred = whole_cell(blocks, live)
    lanes = [pl.ds((index - 2) * width, width) for index in late]
    keys = [own[0], following[0]] + [key_ref.at[lane, :] for lane in lanes]
    queries = [own[1], following[1]] + [query_ref.at[:, lane] for lane in lanes]
    moments = [own[2], following[2]] + [moment_ref.at[:, lane] for lane in lanes]
    exponent = exponent_of(looked_up(keys, width, 0), looked_up(queries, width, 1))

    sums_ref[:, 0:half] = following[3][...]
    sums_ref[:, half:] = jnp.zeros_like(sums_ref[:, half:])
    tiles = late_tiles(count, width)
    stage(
        tiles, exponent, looked_up(moments, width, 1), sums_ref, scratch[:2], scratch[2:],
        distance_refs,
    )
    score = scored(weight, place, joined(sums_ref[...]))
    flux_ref[...] = drift_rows(weight, centred, score)
    totals_ref[...] = jnp.zeros_like(totals_ref)

    def fluxes(start, size):
        return flux_ref[:, pl.ds(start, size)]

    early = diagonal_tiles(0, width) + [(width, width, 0, width, width)]
    early += diagonal_tiles(width, width)
    for tile, split in zip(early + tiles, own[3:5] + following[4:7] + distance_refs):
        add_distances(tile, split, fluxes, totals_ref)
    finish(blocks, count * width, weight, centred, score, totals_ref[...], outs)


def sweep_shapes(width, copies):
    parts = jax.ShapeDtypeStruct((3, width // 128, 128), f32)
    speeds = jax.ShapeDtypeStruct((copies, 128), f32)
    return [jax.ShapeDtypeStruct((8, width), f32), parts, parts, speeds]


def sweep(filled, blocks, sources):
    count, width = len(blocks), blocks[0].shape[2]
    slots, late = count * width, (count - 2) * width
    own = own_part(filled, blocks[0])
    following = next_part(filled, blocks[1], own[:3], own[3], sources[1])
    early = [*own[:3], *own[4:], *following]
    vector = pl.BlockSpec(memory_space=pltpu.VMEM)
    distances = [pltpu.VMEM((2 * tile[1], tile[3]), bf16) for tile in late_tiles(count, width)]
    return pl.pallas_call(
        functools.partial(sweep_kernel, sources),
        out_shape=sweep_shapes(width, 1),
        in_specs=[vector] * (1 + count + len(early)),
        out_specs=[vector] * 4,
        scratch_shapes=[
            pltpu.VMEM((late, DISTANCE_ROWS), bf16),
            pltpu.VMEM((DISTANCE_ROWS, late), bf16),
            pltpu.VMEM((16, late), bf16),
            pltpu.VMEM((DRIFT_ROWS, slots), bf16),
            pltpu.VMEM((16, slots), f32),
            pltpu.VMEM((DRIFT_ROWS // 2, slots), f32),
        ]
        + stage_scratch(width)
        + distances,
        compiler_params=pltpu.CompilerParams(vmem_limit_bytes=24 << 20),
        name="sweep",
    )(filled, *blocks, *early)


def long_kernel(sources, filled, *refs):
    count = len(sources)
    blocks, outs, refs = refs[:count], refs[count : count + 4], refs[count + 4 :]
    key_ref, query_ref, moment_ref, flux_ref, sums_ref, totals_ref, exponent_ref, split_ref = refs
    width = blocks[0].shape[2]
    live = [lanes_of(owner_of(source), width) < filled[...] for source in sources]
    for index, (block, on) in enumerate(zip(blocks, live)):
        _, _, key, query, moment = prepared(widened(block), on)
        lanes = pl.ds(index * width, width)
        key_ref[lanes, :] = key
        query_ref[:, lanes] = query
        moment_ref[:, lanes] = moment
    weight, place, centred = whole_cell(blocks, live)
    sums_ref[...] = jnp.zeros_like(sums_ref)
    totals_ref[...] = jnp.zeros_like(totals_ref)

    def block_tile(key, query, both):
        start, first = (pl.multiple_of(block * width, width) for block in (key, query))
        return (start, width, first, width, width if both else 0)

    def fill(tile):
        key, keys, query, queries, _ = tile
        exponent_ref[...] = product(key_ref[pl.ds(key, keys), :], query_ref[:, pl.ds(query, queries)])

    def blobs(key, query, both):
        tile = block_tile(key, query, both)
        fill(tile)
        split_blobs(exponent_ref, split_ref)
        add_blobs(tile, split_ref, lambda at, size: moment_ref[:, pl.ds(at, size)], sums_ref)

    @pl.loop(0, count)
    def _(query):
        blobs(query, query, False)

        @pl.loop(query + 1, count)
        def _(key):
            blobs(key, query, True)

    score = scored(weight, place, joined(sums_ref[...]))
    flux_ref[...] = drift_rows(weight, centred, score)

    @pl.loop(0, count)
    def _(key):
        tile = block_tile(key, 0, False)
        fill(tile)
        split_distances(exponent_ref, split_ref)
        add_distances(tile, split_ref, lambda at, size: flux_ref[:, pl.ds(at, size)], totals_ref)

    finish(blocks, count * width, weight, centred, score, totals_ref[...], outs)


def long_sweep(filled, blocks, sources, copies):
    count, width = len(blocks), blocks[0].shape[2]
    slots = count * width
    vector = pl.BlockSpec(memory_space=pltpu.VMEM)
    return pl.pallas_call(
        functools.partial(long_kernel, sources),
        out_shape=sweep_shapes(width, copies),
        in_specs=[vector] * (1 + count),
        out_specs=[vector] * 4,
        scratch_shapes=[
            pltpu.VMEM((slots, DISTANCE_ROWS), bf16),
            pltpu.VMEM((DISTANCE_ROWS, slots), bf16),
            pltpu.VMEM((16, slots), bf16),
            pltpu.VMEM((DRIFT_ROWS, slots), bf16),
            pltpu.VMEM((16, slots), f32),
            pltpu.VMEM((DRIFT_ROWS // 2, width), f32),
            pltpu.VMEM((width, width), f32),
            pltpu.VMEM((2 * width, width), bf16),
        ],
        compiler_params=pltpu.CompilerParams(vmem_limit_bytes=(16 << 20) + slots * 2688),
        name="sweep",
    )(filled, *blocks)


def swapped(value, axis, step):
    pairs = [(i, i ^ step) for i in range(lax.axis_size(axis))]
    return lax.ppermute(value, axis, pairs)


def bits(size):
    return [1 << bit for bit in range(size.bit_length() - 1)]


ROUNDS = ((2, 3, 1, 0), (3, 2, 0, 1), (1, 0, 3, 2))


def gathered(block):
    size = lax.axis_size("sharers")
    if size == len(ROUNDS) + 1:
        blocks, sources = [block], [tuple(range(size))]
        for targets in ROUNDS:
            blocks.append(lax.ppermute(block, "sharers", list(enumerate(targets))))
            sources.append(tuple(targets.index(i) for i in range(size)))
        return blocks, sources
    for step in bits(size):
        block = jnp.concatenate([block, swapped(block, "sharers", step)], axis=0)
    sources = [tuple(i ^ step for i in range(size)) for step in range(size)]
    return [block[i : i + 1] for i in range(size)], sources


def local(velocities, weights, counts):
    filled = counts.reshape(1, 1)
    blocks, sources = gathered(jnp.concatenate([velocities, weights[:, None]], axis=1))
    if len(blocks) == len(ROUNDS) + 1:
        scores, drift, start, speeds = sweep(filled, blocks, sources)
        for step in bits(lax.axis_size("cells")):
            speeds = jnp.maximum(speeds, swapped(speeds, "cells", 2 * step - 1))
        largest = speeds
    else:
        axes = ("cells", "sharers")
        scores, drift, start, speeds = long_sweep(filled, blocks, sources, lax.axis_size(axes))
        largest = jnp.max(lax.all_to_all(speeds[:, None], axes, 0, 0, tiled=True), axis=0)
    time_step = 0.5 / (largest + 1e-06)
    moved = start + time_step[None] * drift
    return moved.reshape(velocities.shape), scores[None, 0:3]


def solution(mesh):
    in_specs = (
        P(("groups", "cells"), None, "sharers"),
        P(("groups", "cells"), "sharers"),
        P(("groups", "cells")),
    )
    out_specs = (P(("groups", "cells"), None, "sharers"), P(("groups", "cells"), None, "sharers"))
    return jax.shard_map(local, mesh=mesh, in_specs=in_specs, out_specs=out_specs, check_vma=False)
```

```python
import functools
import functools
import math

import jax
import jax.numpy as jnp
from jax import lax
from jax.experimental import pallas as pl
from jax.experimental.pallas import tpu as pltpu
from jax.sharding import PartitionSpec as P

EPS = 0.35
SCALE = math.sqrt(math.log2(math.e) / (2.0 * EPS * EPS))
GRID = 4.0
TINY = 1e-30
GROUP = 32
DISTANCE_ROWS = 96
DRIFT_ROWS = 64
bf16, f32 = jnp.bfloat16, jnp.float32


def round_bf16(value):
    return value.astype(bf16).astype(f32)


def pieces(value, count):
    parts = []
    for _ in range(count):
        part = round_bf16(value)
        parts.append(part)
        value = value - part
    return parts


def row_of(value):
    return lax.broadcasted_iota(jnp.int32, value.shape, 0)


def rows_sum(value):
    return jnp.sum(value, axis=0, keepdims=True)


def stacked(groups):
    if len(groups) % 2:
        groups = groups + [jnp.zeros_like(groups[0])]
    return jnp.concatenate(groups, axis=0).astype(bf16)


def scalar_groups(value, like):
    row = row_of(like)
    first, second, third = pieces(value, 3)
    low = jnp.where(row == 0, first, jnp.where(row == 1, second, jnp.where(row == 2, third, 0.0)))
    high = jnp.where(row == 3, first, jnp.where(row == 4, second, jnp.where(row == 5, third, 0.0)))
    ones_low, ones_high = row < 3, (row >= 3) & (row < 6)
    return jnp.where(ones_high, 1.0, low), jnp.where(ones_low, 1.0, high)


def grid_parts(place):
    coarse = jnp.floor(place * GRID + 0.5) * (1.0 / GRID)
    return [coarse] + pieces(place - coarse, 2)


def distance_features(parts):
    coarse, fine, rest = parts
    minor = fine + rest
    query_norm, key_norm = scalar_groups(-rows_sum(coarse * coarse), coarse)
    query_less, key_less = scalar_groups(-rows_sum(minor * (2.0 * coarse + minor)), coarse)
    key = [coarse, key_norm, coarse, coarse, fine, rest, key_less, fine, fine, rest, rest]
    coarse, fine, rest = coarse * 2.0, fine * 2.0, rest * 2.0
    query = [coarse, query_norm, fine, rest, coarse, coarse, query_less, fine, rest, fine, rest]
    return stacked(key), stacked(query)


def weighted_rows(weight, value):
    row = row_of(value)
    whole = jnp.where(row < 3, value, jnp.where(row == 3, 1.0, 0.0)) * weight
    first, second, third = pieces(whole, 3)
    return stacked([first, second + pltpu.roll(third, 4, 0)])


def product(left, right):
    return jnp.dot(left, right, preferred_element_type=f32)


def store_split(ref, rows, matrix):
    half = ref.shape[0] // 2
    upper = matrix.astype(bf16)
    ref[rows, :] = upper
    ref[pl.ds(half + rows.start, rows.size), :] = (matrix - upper.astype(f32)).astype(bf16)


def sum_rows(left, ref):
    return product(jnp.concatenate([left, left], axis=1), ref[...])


def sum_columns(left, ref):
    both = lax.dot_general(left, ref[...], (((1,), (1,)), ((), ())), preferred_element_type=f32)
    half = ref.shape[0] // 2
    return both[:, :half] + both[:, half:]


def sum_rows_less(left, ref):
    half = ref.shape[0] // 2
    both = product(left, ref[:half, :])
    few = left.shape[0] // 2
    return both[:few] + product(left[:few], ref[half:, :]), both[few:]


def sum_columns_less(left, ref):
    half, few = ref.shape[0] // 2, left.shape[0] // 2
    turned = (((1,), (1,)), ((), ()))
    both = lax.dot_general(left, ref[:half, :], turned, preferred_element_type=f32)
    less = lax.dot_general(left[:few], ref[half:, :], turned, preferred_element_type=f32)
    return both[:few] + less, both[few:]


def joined(total):
    upper, lower = total[0:8], total[8:16]
    return upper + lower + pltpu.roll(lower, 4, 0)


def drift_rows(weight, place, score):
    row = row_of(place)
    base = place + jnp.where(row == 3, 1.0, 0.0) + pltpu.roll(score, 4, 0)
    cubic = rows_sum(place * place) * score - rows_sum(place * score) * place
    groups = [weight * base]
    for i in range(3):
        here = slice(i, i + 1)
        groups.append(weight * jnp.where(row == 3, cubic[here], place[here] * base))
    return stacked(sum(map(list, zip(*[pieces(group, 2) for group in groups])), []))


def drift_sum(total, place, score):
    row = row_of(place)
    first, *rest = [total[8 * i : 8 * i + 8] for i in range(4)]
    turned = [pltpu.roll(group, 4, 0) for group in rest]
    count, scores = first[3:4], pltpu.roll(first, 4, 0)
    square, both = rows_sum(place * place), rows_sum(place * score)
    trace = rest[0][0:1] + rest[1][1:2] + rest[2][2:3]
    cross = turned[0][0:1] + turned[1][1:2] + turned[2][2:3]
    drift = score * (square * count - 2.0 * rows_sum(place * first) + trace) - square * scores
    drift += both * first + place * (
        rows_sum(place * scores) + rows_sum(score * first) - both * count - cross
    )
    ends = []
    for i in range(3):
        here = slice(i, i + 1)
        drift += 2.0 * place[here] * turned[i] - score[here] * rest[i]
        ends.append(rows_sum(place * turned[i]) + rest[i][3:4])
    return drift - jnp.where(row == 0, ends[0], jnp.where(row == 1, ends[1], ends[2]))


def widened(block):
    return jnp.concatenate([block[0], jnp.zeros_like(block[0])], axis=0)


def prepared(whole, live):
    weight = jnp.where(live, whole[3:4], 0.0)
    parts = grid_parts(jnp.where(row_of(whole) < 3, whole * SCALE, 0.0))
    place = parts[0] + parts[1] + parts[2]
    key, query = distance_features(parts)
    return weight, place, key.T, query, weighted_rows(weight, place)


def split_blobs(exponent, split):
    for group in range(0, exponent.shape[0], GROUP):
        rows = pl.ds(group, GROUP)
        store_split(split, rows, jnp.exp2(exponent[rows, :]))


def split_distances(exponent, split):
    for group in range(0, exponent.shape[0], GROUP):
        rows = pl.ds(group, GROUP)
        negative = jnp.minimum(exponent[rows, :], -TINY)
        store_split(split, rows, negative * lax.rsqrt(-negative))


def diagonal_tiles(start, width):
    half = width // 2
    return [(start, half, start, half, 0), (start + half, half, start, width, half)]


def add_blobs(tile, split, moments, sums_ref):
    key, keys, query, queries, turned = tile
    sums_ref[:, pl.ds(query, queries)] += sum_rows(moments(key, keys), split)
    if turned:
        sums_ref[:, pl.ds(key, keys)] += sum_columns(moments(query, turned), split.at[:, 0:turned])


def add_distances(tile, split, fluxes, totals_ref):
    key, keys, query, queries, turned = tile
    upper, lower = sum_rows_less(fluxes(key, keys), split)
    totals_ref[:, pl.ds(query, queries)] += upper + lower
    if turned:
        upper, lower = sum_columns_less(fluxes(query, turned), split.at[:, 0:turned])
        totals_ref[:, pl.ds(key, keys)] += upper + lower


def stage(tiles, exponent, moments, sums_ref, exponent_refs, split_refs, distance_refs):
    def buffer(index):
        _, keys, _, queries, _ = tiles[index]
        return exponent_refs[index % 2].at[0:keys, 0:queries]

    buffer(0)[...] = exponent(tiles[0])
    for index, tile in enumerate(tiles):
        if index + 1 < len(tiles):
            buffer(index + 1)[...] = exponent(tiles[index + 1])
        split = split_refs[index % 2].at[0 : 2 * tile[1], 0 : tile[3]]
        split_blobs(buffer(index), split)
        add_blobs(tile, split, moments, sums_ref)
        split_distances(buffer(index), distance_refs[index])


def looked_up(refs, width, axis):
    def read(start, size):
        at = pl.ds(start % width, size)
        ref = refs[start // width]
        return ref[at, :] if axis == 0 else ref[:, at]

    return read


def exponent_of(keys, queries):
    return lambda tile: product(keys(tile[0], tile[1]), queries(tile[2], tile[3]))


def lanes_of(source, width):
    return lax.broadcasted_iota(jnp.int32, (1, width), 1) + source * width


def owner_of(sources):
    here = lax.axis_index("sharers")
    return sum(jnp.where(here == i, source, 0) for i, source in enumerate(sources))


def own_kernel(filled, block, key_out, query_out, moment_out, sums_out, first_out, second_out,
               *scratch):
    width = block.shape[2]
    live = lanes_of(lax.axis_index("sharers"), width) < filled[...]
    _, _, key, query, moment = prepared(widened(block), live)
    key_out[...] = key
    query_out[...] = query
    moment_out[...] = moment
    sums_out[...] = jnp.zeros_like(sums_out)
    exponent = exponent_of(looked_up([key_out], width, 0), looked_up([query_out], width, 1))
    moments = looked_up([moment_out], width, 1)
    tiles = diagonal_tiles(0, width)
    stage(tiles, exponent, moments, sums_out, scratch[:2], scratch[2:], (first_out, second_out))


def next_kernel(sources, filled, block, own_key, own_query, own_moment, own_sums, key_out,
                query_out, moment_out, sums_out, *refs):
    width = block.shape[2]
    live = lanes_of(owner_of(sources), width) < filled[...]
    _, _, key, query, moment = prepared(widened(block), live)
    key_out[...] = key
    query_out[...] = query
    moment_out[...] = moment
    sums_out[:, 0:width] = own_sums[...]
    sums_out[:, width:] = jnp.zeros_like(own_sums)
    exponent = exponent_of(
        looked_up([own_key, key_out], width, 0), looked_up([own_query, query_out], width, 1)
    )
    moments = looked_up([own_moment, moment_out], width, 1)
    tiles = square_tiles(width, 0, width) + diagonal_tiles(width, width)
    distances, scratch = refs[: len(tiles)], refs[len(tiles) :]
    stage(tiles, exponent, moments, sums_out, scratch[:2], scratch[2:], distances)


def feature_shapes(width):
    return [
        jax.ShapeDtypeStruct((width, DISTANCE_ROWS), bf16),
        jax.ShapeDtypeStruct((DISTANCE_ROWS, width), bf16),
        jax.ShapeDtypeStruct((16, width), bf16),
    ]


def diagonal_shapes(width):
    half = width // 2
    return [
        jax.ShapeDtypeStruct((2 * half, half), bf16),
        jax.ShapeDtypeStruct((2 * half, width), bf16),
    ]


def stage_scratch(width):
    half = width // 2
    return [pltpu.VMEM((half, width), f32)] * 2 + [pltpu.VMEM((width, width), bf16)] * 2


def own_part(filled, block):
    width = block.shape[2]
    vector = pl.BlockSpec(memory_space=pltpu.VMEM)
    shapes = feature_shapes(width) + [jax.ShapeDtypeStruct((16, width), f32)] + diagonal_shapes(width)
    return pl.pallas_call(
        own_kernel,
        out_shape=shapes,
        in_specs=[vector] * 2,
        out_specs=[vector] * len(shapes),
        scratch_shapes=stage_scratch(width),
        compiler_params=pltpu.CompilerParams(vmem_limit_bytes=16 << 20),
        name="own",
    )(filled, block)


def next_part(filled, block, features, sums, sources):
    width = block.shape[2]
    vector = pl.BlockSpec(memory_space=pltpu.VMEM)
    shapes = feature_shapes(width) + [jax.ShapeDtypeStruct((16, 2 * width), f32)]
    shapes += [jax.ShapeDtypeStruct((width, width), bf16)] * 2 + diagonal_shapes(width)
    return pl.pallas_call(
        functools.partial(next_kernel, sources),
        out_shape=shapes,
        in_specs=[vector] * 6,
        out_specs=[vector] * len(shapes),
        scratch_shapes=stage_scratch(width),
        compiler_params=pltpu.CompilerParams(vmem_limit_bytes=20 << 20),
        name="next",
    )(filled, block, *features, sums)


def square_tiles(key, query, width):
    half = width // 2
    return [(key + part, half, query, width, width) for part in (0, half)]


def late_tiles(count, width):
    tiles = []
    for query in range(count):
        first = max(query + 1, 2)
        tiles += diagonal_tiles(query * width, width) if query >= 2 else []
        for key in range(first, count):
            tiles += square_tiles(key * width, query * width, width)
    return tiles


def scored(weight, place, sums):
    vector, live = row_of(place) < 3, weight > 0.0
    density_sum = jnp.where(live, sums[3:4], 1.0)
    pull = place * density_sum - sums
    return jnp.where(vector & live, pull / (-SCALE * EPS * EPS * density_sum), 0.0)


def whole_cell(blocks, live):
    weight = jnp.concatenate(
        [jnp.where(on, block[0, 3:4], 0.0) for on, block in zip(live, blocks)], axis=1
    )
    whole = jnp.concatenate([widened(block) for block in blocks], axis=1)
    vector = row_of(whole) < 3
    parts = grid_parts(jnp.where(vector, whole * SCALE, 0.0))
    place = parts[0] + parts[1] + parts[2]
    middle = jnp.sum(place * weight, axis=1, keepdims=True)
    middle = middle / jnp.sum(weight, axis=1, keepdims=True)
    return weight, place, jnp.where(vector, place - middle, 0.0)


def finish(blocks, total_slots, weight, centred, score, totals, outs):
    scores_out, drift_out, start_out, speed_out = outs
    width = blocks[0].shape[2]
    spread = totals.shape[1]
    drift = drift_sum(totals, centred[:, 0:spread], score[:, 0:spread])
    factor = 1.0 / (SCALE * SCALE * SCALE * total_slots)
    live = (row_of(drift) < 3) & (weight[:, 0:spread] > 0.0)
    drift = jnp.where(live, drift * factor, 0.0)
    largest = jnp.max(rows_sum(drift * drift), axis=1, keepdims=True)
    speed_out[...] = jnp.broadcast_to(jnp.sqrt(largest), speed_out.shape)
    scores_out[...] = score[:, 0:width]
    for part in range(width // 128):
        lanes = slice(part * 128, part * 128 + 128)
        for axis in range(3):
            drift_out[axis, part : part + 1, :] = drift[axis : axis + 1, lanes]
            start_out[axis, part : part + 1, :] = blocks[0][0, axis : axis + 1, lanes]


def sweep_kernel(sources, *refs):
    count = len(sources)
    filled, blocks, refs = refs[0], refs[1 : count + 1], list(refs[count + 1 :])
    own, following, refs = refs[:5], refs[5:13], refs[13:]
    outs, (key_ref, query_ref, moment_ref, flux_ref, sums_ref, totals_ref), refs = (
        refs[:4], refs[4:10], refs[10:]
    )
    width = blocks[0].shape[2]
    half = 2 * width
    scratch, distance_refs = refs[:4], refs[4:]

    live = [lanes_of(owner_of(source), width) < filled[...] for source in sources]
    late = range(2, count)
    for index in late:
        _, _, key, query, moment = prepared(widened(blocks[index]), live[index])
        lanes = pl.ds((index - 2) * width, width)
        key_ref[lanes, :] = key
        query_ref[:, lanes] = query
        moment_ref[:, lanes] = moment
    weight, place, centred = whole_cell(blocks, live)
    lanes = [pl.ds((index - 2) * width, width) for index in late]
    keys = [own[0], following[0]] + [key_ref.at[lane, :] for lane in lanes]
    queries = [own[1], following[1]] + [query_ref.at[:, lane] for lane in lanes]
    moments = [own[2], following[2]] + [moment_ref.at[:, lane] for lane in lanes]
    exponent = exponent_of(looked_up(keys, width, 0), looked_up(queries, width, 1))

    sums_ref[:, 0:half] = following[3][...]
    sums_ref[:, half:] = jnp.zeros_like(sums_ref[:, half:])
    tiles = late_tiles(count, width)
    stage(
        tiles, exponent, looked_up(moments, width, 1), sums_ref, scratch[:2], scratch[2:],
        distance_refs,
    )
    score = scored(weight, place, joined(sums_ref[...]))
    flux_ref[...] = drift_rows(weight, centred, score)
    totals_ref[...] = jnp.zeros_like(totals_ref)

    def fluxes(start, size):
        return flux_ref[:, pl.ds(start, size)]

    early = diagonal_tiles(0, width) + square_tiles(width, 0, width)
    early += diagonal_tiles(width, width)
    for tile, split in zip(early + tiles, own[3:5] + following[4:8] + distance_refs):
        add_distances(tile, split, fluxes, totals_ref)
    finish(blocks, count * width, weight, centred, score, totals_ref[...], outs)


def sweep_shapes(width, copies):
    parts = jax.ShapeDtypeStruct((3, width // 128, 128), f32)
    speeds = jax.ShapeDtypeStruct((copies, 128), f32)
    return [jax.ShapeDtypeStruct((8, width), f32), parts, parts, speeds]


def sweep(filled, blocks, sources):
    count, width = len(blocks), blocks[0].shape[2]
    slots, late = count * width, (count - 2) * width
    own = own_part(filled, blocks[0])
    following = next_part(filled, blocks[1], own[:3], own[3], sources[1])
    early = [*own[:3], *own[4:], *following]
    vector = pl.BlockSpec(memory_space=pltpu.VMEM)
    distances = [pltpu.VMEM((2 * tile[1], tile[3]), bf16) for tile in late_tiles(count, width)]
    return pl.pallas_call(
        functools.partial(sweep_kernel, sources),
        out_shape=sweep_shapes(width, 1),
        in_specs=[vector] * (1 + count + len(early)),
        out_specs=[vector] * 4,
        scratch_shapes=[
            pltpu.VMEM((late, DISTANCE_ROWS), bf16),
            pltpu.VMEM((DISTANCE_ROWS, late), bf16),
            pltpu.VMEM((16, late), bf16),
            pltpu.VMEM((DRIFT_ROWS, slots), bf16),
            pltpu.VMEM((16, slots), f32),
            pltpu.VMEM((DRIFT_ROWS // 2, slots), f32),
        ]
        + stage_scratch(width)
        + distances,
        compiler_params=pltpu.CompilerParams(vmem_limit_bytes=24 << 20),
        name="sweep",
    )(filled, *blocks, *early)


def long_kernel(sources, filled, *refs):
    count = len(sources)
    blocks, outs, refs = refs[:count], refs[count : count + 4], refs[count + 4 :]
    key_ref, query_ref, moment_ref, flux_ref, sums_ref, totals_ref, exponent_ref, split_ref = refs
    width = blocks[0].shape[2]
    live = [lanes_of(owner_of(source), width) < filled[...] for source in sources]
    for index, (block, on) in enumerate(zip(blocks, live)):
        _, _, key, query, moment = prepared(widened(block), on)
        lanes = pl.ds(index * width, width)
        key_ref[lanes, :] = key
        query_ref[:, lanes] = query
        moment_ref[:, lanes] = moment
    weight, place, centred = whole_cell(blocks, live)
    sums_ref[...] = jnp.zeros_like(sums_ref)
    totals_ref[...] = jnp.zeros_like(totals_ref)

    def block_tile(key, query, both):
        start, first = (pl.multiple_of(block * width, width) for block in (key, query))
        return (start, width, first, width, width if both else 0)

    def fill(tile):
        key, keys, query, queries, _ = tile
        exponent_ref[...] = product(key_ref[pl.ds(key, keys), :], query_ref[:, pl.ds(query, queries)])

    def blobs(key, query, both):
        tile = block_tile(key, query, both)
        fill(tile)
        split_blobs(exponent_ref, split_ref)
        add_blobs(tile, split_ref, lambda at, size: moment_ref[:, pl.ds(at, size)], sums_ref)

    @pl.loop(0, count)
    def _(query):
        blobs(query, query, False)

        @pl.loop(query + 1, count)
        def _(key):
            blobs(key, query, True)

    score = scored(weight, place, joined(sums_ref[...]))
    flux_ref[...] = drift_rows(weight, centred, score)

    @pl.loop(0, count)
    def _(key):
        tile = block_tile(key, 0, False)
        fill(tile)
        split_distances(exponent_ref, split_ref)
        add_distances(tile, split_ref, lambda at, size: flux_ref[:, pl.ds(at, size)], totals_ref)

    finish(blocks, count * width, weight, centred, score, totals_ref[...], outs)


def long_sweep(filled, blocks, sources, copies):
    count, width = len(blocks), blocks[0].shape[2]
    slots = count * width
    vector = pl.BlockSpec(memory_space=pltpu.VMEM)
    return pl.pallas_call(
        functools.partial(long_kernel, sources),
        out_shape=sweep_shapes(width, copies),
        in_specs=[vector] * (1 + count),
        out_specs=[vector] * 4,
        scratch_shapes=[
            pltpu.VMEM((slots, DISTANCE_ROWS), bf16),
            pltpu.VMEM((DISTANCE_ROWS, slots), bf16),
            pltpu.VMEM((16, slots), bf16),
            pltpu.VMEM((DRIFT_ROWS, slots), bf16),
            pltpu.VMEM((16, slots), f32),
            pltpu.VMEM((DRIFT_ROWS // 2, width), f32),
            pltpu.VMEM((width, width), f32),
            pltpu.VMEM((2 * width, width), bf16),
        ],
        compiler_params=pltpu.CompilerParams(vmem_limit_bytes=(16 << 20) + slots * 2688),
        name="sweep",
    )(filled, *blocks)


def swapped(value, axis, step):
    pairs = [(i, i ^ step) for i in range(lax.axis_size(axis))]
    return lax.ppermute(value, axis, pairs)


def bits(size):
    return [1 << bit for bit in range(size.bit_length() - 1)]


ROUNDS = ((2, 3, 1, 0), (3, 2, 0, 1), (1, 0, 3, 2))


def gathered(block):
    size = lax.axis_size("sharers")
    if size == len(ROUNDS) + 1:
        blocks, sources = [block], [tuple(range(size))]
        for targets in ROUNDS:
            blocks.append(lax.ppermute(block, "sharers", list(enumerate(targets))))
            sources.append(tuple(targets.index(i) for i in range(size)))
        return blocks, sources
    for step in bits(size):
        block = jnp.concatenate([block, swapped(block, "sharers", step)], axis=0)
    sources = [tuple(i ^ step for i in range(size)) for step in range(size)]
    return [block[i : i + 1] for i in range(size)], sources


def local(velocities, weights, counts):
    filled = counts.reshape(1, 1)
    blocks, sources = gathered(jnp.concatenate([velocities, weights[:, None]], axis=1))
    if len(blocks) == len(ROUNDS) + 1:
        scores, drift, start, speeds = sweep(filled, blocks, sources)
        for step in bits(lax.axis_size("cells")):
            speeds = jnp.maximum(speeds, swapped(speeds, "cells", 2 * step - 1))
        largest = speeds
    else:
        axes = ("cells", "sharers")
        scores, drift, start, speeds = long_sweep(filled, blocks, sources, lax.axis_size(axes))
        largest = jnp.max(lax.all_to_all(speeds[:, None], axes, 0, 0, tiled=True), axis=0)
    time_step = 0.5 / (largest + 1e-06)
    moved = start + time_step[None] * drift
    return moved.reshape(velocities.shape), scores[None, 0:3]


def solution(mesh):
    in_specs = (
        P(("groups", "cells"), None, "sharers"),
        P(("groups", "cells"), "sharers"),
        P(("groups", "cells")),
    )
    out_specs = (P(("groups", "cells"), None, "sharers"), P(("groups", "cells"), None, "sharers"))
    return jax.shard_map(local, mesh=mesh, in_specs=in_specs, out_specs=out_specs, check_vma=False)
```

```python
import functools
import functools
import math

import jax
import jax.numpy as jnp
from jax import lax
from jax.experimental import pallas as pl
from jax.experimental.pallas import tpu as pltpu
from jax.sharding import PartitionSpec as P

EPS = 0.35
SCALE = math.sqrt(math.log2(math.e) / (2.0 * EPS * EPS))
GRID = 4.0
TINY = 1e-30
GROUP = 16
DISTANCE_ROWS = 96
DRIFT_ROWS = 64
bf16, f32 = jnp.bfloat16, jnp.float32


def round_bf16(value):
    return value.astype(bf16).astype(f32)


def pieces(value, count):
    parts = []
    for _ in range(count):
        part = round_bf16(value)
        parts.append(part)
        value = value - part
    return parts


def row_of(value):
    return lax.broadcasted_iota(jnp.int32, value.shape, 0)


def rows_sum(value):
    return jnp.sum(value, axis=0, keepdims=True)


def stacked(groups):
    if len(groups) % 2:
        groups = groups + [jnp.zeros_like(groups[0])]
    return jnp.concatenate(groups, axis=0).astype(bf16)


def scalar_groups(value, like):
    row = row_of(like)
    first, second, third = pieces(value, 3)
    low = jnp.where(row == 0, first, jnp.where(row == 1, second, jnp.where(row == 2, third, 0.0)))
    high = jnp.where(row == 3, first, jnp.where(row == 4, second, jnp.where(row == 5, third, 0.0)))
    ones_low, ones_high = row < 3, (row >= 3) & (row < 6)
    return jnp.where(ones_high, 1.0, low), jnp.where(ones_low, 1.0, high)


def grid_parts(place):
    coarse = jnp.floor(place * GRID + 0.5) * (1.0 / GRID)
    return [coarse] + pieces(place - coarse, 2)


def distance_features(parts):
    coarse, fine, rest = parts
    minor = fine + rest
    query_norm, key_norm = scalar_groups(-rows_sum(coarse * coarse), coarse)
    query_less, key_less = scalar_groups(-rows_sum(minor * (2.0 * coarse + minor)), coarse)
    key = [coarse, key_norm, coarse, coarse, fine, rest, key_less, fine, fine, rest, rest]
    coarse, fine, rest = coarse * 2.0, fine * 2.0, rest * 2.0
    query = [coarse, query_norm, fine, rest, coarse, coarse, query_less, fine, rest, fine, rest]
    return stacked(key), stacked(query)


def weighted_rows(weight, value):
    row = row_of(value)
    whole = jnp.where(row < 3, value, jnp.where(row == 3, 1.0, 0.0)) * weight
    first, second, third = pieces(whole, 3)
    return stacked([first, second + pltpu.roll(third, 4, 0)])


def product(left, right):
    return jnp.dot(left, right, preferred_element_type=f32)


def store_split(ref, rows, matrix):
    half = ref.shape[0] // 2
    upper = matrix.astype(bf16)
    ref[rows, :] = upper
    ref[pl.ds(half + rows.start, rows.size), :] = (matrix - upper.astype(f32)).astype(bf16)


def sum_rows(left, ref):
    return product(jnp.concatenate([left, left], axis=1), ref[...])


def sum_columns(left, ref):
    both = lax.dot_general(left, ref[...], (((1,), (1,)), ((), ())), preferred_element_type=f32)
    half = ref.shape[0] // 2
    return both[:, :half] + both[:, half:]


def sum_rows_less(left, ref):
    half = ref.shape[0] // 2
    both = product(left, ref[:half, :])
    few = left.shape[0] // 2
    return both[:few] + product(left[:few], ref[half:, :]), both[few:]


def sum_columns_less(left, ref):
    half, few = ref.shape[0] // 2, left.shape[0] // 2
    turned = (((1,), (1,)), ((), ()))
    both = lax.dot_general(left, ref[:half, :], turned, preferred_element_type=f32)
    less = lax.dot_general(left[:few], ref[half:, :], turned, preferred_element_type=f32)
    return both[:few] + less, both[few:]


def joined(total):
    upper, lower = total[0:8], total[8:16]
    return upper + lower + pltpu.roll(lower, 4, 0)


def drift_rows(weight, place, score):
    row = row_of(place)
    base = place + jnp.where(row == 3, 1.0, 0.0) + pltpu.roll(score, 4, 0)
    cubic = rows_sum(place * place) * score - rows_sum(place * score) * place
    groups = [weight * base]
    for i in range(3):
        here = slice(i, i + 1)
        groups.append(weight * jnp.where(row == 3, cubic[here], place[here] * base))
    return stacked(sum(map(list, zip(*[pieces(group, 2) for group in groups])), []))


def drift_sum(total, place, score):
    row = row_of(place)
    first, *rest = [total[8 * i : 8 * i + 8] for i in range(4)]
    turned = [pltpu.roll(group, 4, 0) for group in rest]
    count, scores = first[3:4], pltpu.roll(first, 4, 0)
    square, both = rows_sum(place * place), rows_sum(place * score)
    trace = rest[0][0:1] + rest[1][1:2] + rest[2][2:3]
    cross = turned[0][0:1] + turned[1][1:2] + turned[2][2:3]
    drift = score * (square * count - 2.0 * rows_sum(place * first) + trace) - square * scores
    drift += both * first + place * (
        rows_sum(place * scores) + rows_sum(score * first) - both * count - cross
    )
    ends = []
    for i in range(3):
        here = slice(i, i + 1)
        drift += 2.0 * place[here] * turned[i] - score[here] * rest[i]
        ends.append(rows_sum(place * turned[i]) + rest[i][3:4])
    return drift - jnp.where(row == 0, ends[0], jnp.where(row == 1, ends[1], ends[2]))


def widened(block):
    return jnp.concatenate([block[0], jnp.zeros_like(block[0])], axis=0)


def prepared(whole, live):
    weight = jnp.where(live, whole[3:4], 0.0)
    parts = grid_parts(jnp.where(row_of(whole) < 3, whole * SCALE, 0.0))
    place = parts[0] + parts[1] + parts[2]
    key, query = distance_features(parts)
    return weight, place, key.T, query, weighted_rows(weight, place)


def split_both(exponent, blobs, distances, rows):
    values = exponent[rows, :]
    if blobs is not None:
        store_split(blobs, rows, jnp.exp2(values))
    if distances is not None:
        negative = jnp.minimum(values, -TINY)
        store_split(distances, rows, negative * lax.rsqrt(-negative))


def diagonal_tiles(start, width):
    half = width // 2
    return [(start, half, start, half, 0), (start + half, half, start, width, half)]


def add_blobs(tile, split, moments, sums_ref):
    key, keys, query, queries, turned = tile

    def rows():
        sums_ref[:, pl.ds(query, queries)] += sum_rows(moments(key, keys), split)

    def columns():
        left, right = moments(query, turned), split.at[:, 0:turned]
        sums_ref[:, pl.ds(key, keys)] += sum_columns(left, right)

    return [rows, columns] if turned else [rows]


def add_distances(tile, split, fluxes, totals_ref):
    key, keys, query, queries, turned = tile
    upper, lower = sum_rows_less(fluxes(key, keys), split)
    totals_ref[:, pl.ds(query, queries)] += upper + lower
    if turned:
        upper, lower = sum_columns_less(fluxes(query, turned), split.at[:, 0:turned])
        totals_ref[:, pl.ds(key, keys)] += upper + lower


def stage(tiles, exponent, moments, sums_ref, exponent_refs, split_refs, distance_refs):
    def buffer(index):
        _, keys, _, queries, _ = tiles[index]
        return exponent_refs[index % 2].at[0:keys, 0:queries]

    def split(index):
        _, keys, _, queries, _ = tiles[index]
        return split_refs[index % 2].at[0 : 2 * keys, 0:queries]

    def fill(index):
        buffer(index)[...] = exponent(tiles[index])

    fill(0)
    sums = []
    for index, tile in enumerate(tiles):
        jobs = [functools.partial(fill, index + 1)] if index + 1 < len(tiles) else []
        jobs += sums
        groups = list(range(0, tile[1], GROUP))
        for at, group in enumerate(groups):
            if jobs and at * 4 % len(groups) == 0:
                jobs.pop(0)()
            split_both(buffer(index), split(index), distance_refs[index], pl.ds(group, GROUP))
        for job in jobs:
            job()
        sums = add_blobs(tile, split(index), moments, sums_ref)
    for job in sums:
        job()


def looked_up(refs, width, axis):
    def read(start, size):
        at = pl.ds(start % width, size)
        ref = refs[start // width]
        return ref[at, :] if axis == 0 else ref[:, at]

    return read


def exponent_of(keys, queries):
    return lambda tile: product(keys(tile[0], tile[1]), queries(tile[2], tile[3]))


def lanes_of(source, width):
    return lax.broadcasted_iota(jnp.int32, (1, width), 1) + source * width


def owner_of(sources):
    here = lax.axis_index("sharers")
    return sum(jnp.where(here == i, source, 0) for i, source in enumerate(sources))


def own_kernel(filled, block, key_out, query_out, moment_out, sums_out, first_out, second_out,
               *scratch):
    width = block.shape[2]
    live = lanes_of(lax.axis_index("sharers"), width) < filled[...]
    _, _, key, query, moment = prepared(widened(block), live)
    key_out[...] = key
    query_out[...] = query
    moment_out[...] = moment
    sums_out[...] = jnp.zeros_like(sums_out)
    exponent = exponent_of(looked_up([key_out], width, 0), looked_up([query_out], width, 1))
    moments = looked_up([moment_out], width, 1)
    tiles = diagonal_tiles(0, width)
    stage(tiles, exponent, moments, sums_out, scratch[:2], scratch[2:], (first_out, second_out))


def next_kernel(sources, filled, block, own_key, own_query, own_moment, own_sums, key_out,
                query_out, moment_out, sums_out, *refs):
    width = block.shape[2]
    live = lanes_of(owner_of(sources), width) < filled[...]
    _, _, key, query, moment = prepared(widened(block), live)
    key_out[...] = key
    query_out[...] = query
    moment_out[...] = moment
    sums_out[:, 0:width] = own_sums[...]
    sums_out[:, width:] = jnp.zeros_like(own_sums)
    exponent = exponent_of(
        looked_up([own_key, key_out], width, 0), looked_up([own_query, query_out], width, 1)
    )
    moments = looked_up([own_moment, moment_out], width, 1)
    tiles = square_tiles(width, 0, width) + diagonal_tiles(width, width)
    distances, scratch = refs[: len(tiles)], refs[len(tiles) :]
    stage(tiles, exponent, moments, sums_out, scratch[:2], scratch[2:], distances)


def feature_shapes(width):
    return [
        jax.ShapeDtypeStruct((width, DISTANCE_ROWS), bf16),
        jax.ShapeDtypeStruct((DISTANCE_ROWS, width), bf16),
        jax.ShapeDtypeStruct((16, width), bf16),
    ]


def diagonal_shapes(width):
    half = width // 2
    return [
        jax.ShapeDtypeStruct((2 * half, half), bf16),
        jax.ShapeDtypeStruct((2 * half, width), bf16),
    ]


def stage_scratch(width):
    half = width // 2
    return [pltpu.VMEM((half, width), f32)] * 2 + [pltpu.VMEM((width, width), bf16)] * 2


def own_part(filled, block):
    width = block.shape[2]
    vector = pl.BlockSpec(memory_space=pltpu.VMEM)
    shapes = feature_shapes(width) + [jax.ShapeDtypeStruct((16, width), f32)] + diagonal_shapes(width)
    return pl.pallas_call(
        own_kernel,
        out_shape=shapes,
        in_specs=[vector] * 2,
        out_specs=[vector] * len(shapes),
        scratch_shapes=stage_scratch(width),
        compiler_params=pltpu.CompilerParams(vmem_limit_bytes=16 << 20),
        name="own",
    )(filled, block)


def next_part(filled, block, features, sums, sources):
    width = block.shape[2]
    vector = pl.BlockSpec(memory_space=pltpu.VMEM)
    shapes = feature_shapes(width) + [jax.ShapeDtypeStruct((16, 2 * width), f32)]
    shapes += [jax.ShapeDtypeStruct((width, width), bf16)] * 2 + diagonal_shapes(width)
    return pl.pallas_call(
        functools.partial(next_kernel, sources),
        out_shape=shapes,
        in_specs=[vector] * 6,
        out_specs=[vector] * len(shapes),
        scratch_shapes=stage_scratch(width),
        compiler_params=pltpu.CompilerParams(vmem_limit_bytes=20 << 20),
        name="next",
    )(filled, block, *features, sums)


def square_tiles(key, query, width):
    half = width // 2
    return [(key + part, half, query, width, width) for part in (0, half)]


def late_tiles(count, width):
    tiles = []
    for query in range(count):
        first = max(query + 1, 2)
        tiles += diagonal_tiles(query * width, width) if query >= 2 else []
        for key in range(first, count):
            tiles += square_tiles(key * width, query * width, width)
    return tiles


def scored(weight, place, sums):
    vector, live = row_of(place) < 3, weight > 0.0
    density_sum = jnp.where(live, sums[3:4], 1.0)
    pull = place * density_sum - sums
    return jnp.where(vector & live, pull / (-SCALE * EPS * EPS * density_sum), 0.0)


def whole_cell(blocks, live):
    weight = jnp.concatenate(
        [jnp.where(on, block[0, 3:4], 0.0) for on, block in zip(live, blocks)], axis=1
    )
    whole = jnp.concatenate([widened(block) for block in blocks], axis=1)
    vector = row_of(whole) < 3
    parts = grid_parts(jnp.where(vector, whole * SCALE, 0.0))
    place = parts[0] + parts[1] + parts[2]
    middle = jnp.sum(place * weight, axis=1, keepdims=True)
    middle = middle / jnp.sum(weight, axis=1, keepdims=True)
    return weight, place, jnp.where(vector, place - middle, 0.0)


def finish(blocks, total_slots, weight, centred, score, totals, outs):
    scores_out, drift_out, start_out, speed_out = outs
    width = blocks[0].shape[2]
    spread = totals.shape[1]
    drift = drift_sum(totals, centred[:, 0:spread], score[:, 0:spread])
    factor = 1.0 / (SCALE * SCALE * SCALE * total_slots)
    live = (row_of(drift) < 3) & (weight[:, 0:spread] > 0.0)
    drift = jnp.where(live, drift * factor, 0.0)
    largest = jnp.max(rows_sum(drift * drift), axis=1, keepdims=True)
    speed_out[...] = jnp.broadcast_to(jnp.sqrt(largest), speed_out.shape)
    scores_out[...] = score[:, 0:width]
    for part in range(width // 128):
        lanes = slice(part * 128, part * 128 + 128)
        for axis in range(3):
            drift_out[axis, part : part + 1, :] = drift[axis : axis + 1, lanes]
            start_out[axis, part : part + 1, :] = blocks[0][0, axis : axis + 1, lanes]


def sweep_kernel(sources, *refs):
    count = len(sources)
    filled, blocks, refs = refs[0], refs[1 : count + 1], list(refs[count + 1 :])
    own, following, refs = refs[:5], refs[5:13], refs[13:]
    outs, (key_ref, query_ref, moment_ref, flux_ref, sums_ref, totals_ref), refs = (
        refs[:4], refs[4:10], refs[10:]
    )
    width = blocks[0].shape[2]
    half = 2 * width
    scratch, distance_refs = refs[:4], refs[4:]

    live = [lanes_of(owner_of(source), width) < filled[...] for source in sources]
    late = range(2, count)
    for index in late:
        _, _, key, query, moment = prepared(widened(blocks[index]), live[index])
        lanes = pl.ds((index - 2) * width, width)
        key_ref[lanes, :] = key
        query_ref[:, lanes] = query
        moment_ref[:, lanes] = moment
    weight, place, centred = whole_cell(blocks, live)
    lanes = [pl.ds((index - 2) * width, width) for index in late]
    keys = [own[0], following[0]] + [key_ref.at[lane, :] for lane in lanes]
    queries = [own[1], following[1]] + [query_ref.at[:, lane] for lane in lanes]
    moments = [own[2], following[2]] + [moment_ref.at[:, lane] for lane in lanes]
    exponent = exponent_of(looked_up(keys, width, 0), looked_up(queries, width, 1))

    sums_ref[:, 0:half] = following[3][...]
    sums_ref[:, half:] = jnp.zeros_like(sums_ref[:, half:])
    tiles = late_tiles(count, width)
    stage(
        tiles, exponent, looked_up(moments, width, 1), sums_ref, scratch[:2], scratch[2:],
        distance_refs,
    )
    score = scored(weight, place, joined(sums_ref[...]))
    flux_ref[...] = drift_rows(weight, centred, score)
    totals_ref[...] = jnp.zeros_like(totals_ref)

    def fluxes(start, size):
        return flux_ref[:, pl.ds(start, size)]

    early = diagonal_tiles(0, width) + square_tiles(width, 0, width)
    early += diagonal_tiles(width, width)
    for tile, split in zip(early + tiles, own[3:5] + following[4:8] + distance_refs):
        add_distances(tile, split, fluxes, totals_ref)
    finish(blocks, count * width, weight, centred, score, totals_ref[...], outs)


def sweep_shapes(width, copies):
    parts = jax.ShapeDtypeStruct((3, width // 128, 128), f32)
    speeds = jax.ShapeDtypeStruct((copies, 128), f32)
    return [jax.ShapeDtypeStruct((8, width), f32), parts, parts, speeds]


def sweep(filled, blocks, sources):
    count, width = len(blocks), blocks[0].shape[2]
    slots, late = count * width, (count - 2) * width
    own = own_part(filled, blocks[0])
    following = next_part(filled, blocks[1], own[:3], own[3], sources[1])
    early = [*own[:3], *own[4:], *following]
    vector = pl.BlockSpec(memory_space=pltpu.VMEM)
    distances = [pltpu.VMEM((2 * tile[1], tile[3]), bf16) for tile in late_tiles(count, width)]
    return pl.pallas_call(
        functools.partial(sweep_kernel, sources),
        out_shape=sweep_shapes(width, 1),
        in_specs=[vector] * (1 + count + len(early)),
        out_specs=[vector] * 4,
        scratch_shapes=[
            pltpu.VMEM((late, DISTANCE_ROWS), bf16),
            pltpu.VMEM((DISTANCE_ROWS, late), bf16),
            pltpu.VMEM((16, late), bf16),
            pltpu.VMEM((DRIFT_ROWS, slots), bf16),
            pltpu.VMEM((16, slots), f32),
            pltpu.VMEM((DRIFT_ROWS // 2, slots), f32),
        ]
        + stage_scratch(width)
        + distances,
        compiler_params=pltpu.CompilerParams(vmem_limit_bytes=24 << 20),
        name="sweep",
    )(filled, *blocks, *early)


def long_kernel(sources, filled, *refs):
    count = len(sources)
    blocks, outs, refs = refs[:count], refs[count : count + 4], refs[count + 4 :]
    key_ref, query_ref, moment_ref, flux_ref, sums_ref, totals_ref, exponent_ref, split_ref = refs
    width = blocks[0].shape[2]
    live = [lanes_of(owner_of(source), width) < filled[...] for source in sources]
    for index, (block, on) in enumerate(zip(blocks, live)):
        _, _, key, query, moment = prepared(widened(block), on)
        lanes = pl.ds(index * width, width)
        key_ref[lanes, :] = key
        query_ref[:, lanes] = query
        moment_ref[:, lanes] = moment
    weight, place, centred = whole_cell(blocks, live)
    sums_ref[...] = jnp.zeros_like(sums_ref)
    totals_ref[...] = jnp.zeros_like(totals_ref)

    def block_tile(key, query, both):
        start, first = (pl.multiple_of(block * width, width) for block in (key, query))
        return (start, width, first, width, width if both else 0)

    def fill(tile):
        key, keys, query, queries, _ = tile
        exponent_ref[...] = product(key_ref[pl.ds(key, keys), :], query_ref[:, pl.ds(query, queries)])

    def blobs(key, query, both):
        tile = block_tile(key, query, both)
        fill(tile)
        for group in range(0, width, GROUP):
            split_both(exponent_ref, split_ref, None, pl.ds(group, GROUP))
        for job in add_blobs(
            tile, split_ref, lambda at, size: moment_ref[:, pl.ds(at, size)], sums_ref
        ):
            job()

    @pl.loop(0, count)
    def _(query):
        blobs(query, query, False)

        @pl.loop(query + 1, count)
        def _(key):
            blobs(key, query, True)

    score = scored(weight, place, joined(sums_ref[...]))
    flux_ref[...] = drift_rows(weight, centred, score)

    @pl.loop(0, count)
    def _(key):
        tile = block_tile(key, 0, False)
        fill(tile)
        for group in range(0, width, GROUP):
            split_both(exponent_ref, None, split_ref, pl.ds(group, GROUP))
        add_distances(tile, split_ref, lambda at, size: flux_ref[:, pl.ds(at, size)], totals_ref)

    finish(blocks, count * width, weight, centred, score, totals_ref[...], outs)


def long_sweep(filled, blocks, sources, copies):
    count, width = len(blocks), blocks[0].shape[2]
    slots = count * width
    vector = pl.BlockSpec(memory_space=pltpu.VMEM)
    return pl.pallas_call(
        functools.partial(long_kernel, sources),
        out_shape=sweep_shapes(width, copies),
        in_specs=[vector] * (1 + count),
        out_specs=[vector] * 4,
        scratch_shapes=[
            pltpu.VMEM((slots, DISTANCE_ROWS), bf16),
            pltpu.VMEM((DISTANCE_ROWS, slots), bf16),
            pltpu.VMEM((16, slots), bf16),
            pltpu.VMEM((DRIFT_ROWS, slots), bf16),
            pltpu.VMEM((16, slots), f32),
            pltpu.VMEM((DRIFT_ROWS // 2, width), f32),
            pltpu.VMEM((width, width), f32),
            pltpu.VMEM((2 * width, width), bf16),
        ],
        compiler_params=pltpu.CompilerParams(vmem_limit_bytes=(16 << 20) + slots * 2688),
        name="sweep",
    )(filled, *blocks)


def swapped(value, axis, step):
    pairs = [(i, i ^ step) for i in range(lax.axis_size(axis))]
    return lax.ppermute(value, axis, pairs)


def bits(size):
    return [1 << bit for bit in range(size.bit_length() - 1)]


ROUNDS = ((2, 3, 1, 0), (3, 2, 0, 1), (1, 0, 3, 2))


def gathered(block):
    size = lax.axis_size("sharers")
    if size == len(ROUNDS) + 1:
        blocks, sources = [block], [tuple(range(size))]
        for targets in ROUNDS:
            blocks.append(lax.ppermute(block, "sharers", list(enumerate(targets))))
            sources.append(tuple(targets.index(i) for i in range(size)))
        return blocks, sources
    for step in bits(size):
        block = jnp.concatenate([block, swapped(block, "sharers", step)], axis=0)
    sources = [tuple(i ^ step for i in range(size)) for step in range(size)]
    return [block[i : i + 1] for i in range(size)], sources


def local(velocities, weights, counts):
    filled = counts.reshape(1, 1)
    blocks, sources = gathered(jnp.concatenate([velocities, weights[:, None]], axis=1))
    if len(blocks) == len(ROUNDS) + 1:
        scores, drift, start, speeds = sweep(filled, blocks, sources)
        for step in reversed(bits(lax.axis_size("cells"))):
            speeds = jnp.maximum(speeds, swapped(speeds, "cells", 2 * step - 1))
        largest = speeds
    else:
        axes = ("cells", "sharers")
        scores, drift, start, speeds = long_sweep(filled, blocks, sources, lax.axis_size(axes))
        largest = jnp.max(lax.all_to_all(speeds[:, None], axes, 0, 0, tiled=True), axis=0)
    time_step = 0.5 / (largest + 1e-06)
    moved = start + time_step[None] * drift
    return moved.reshape(velocities.shape), scores[None, 0:3]


def solution(mesh):
    in_specs = (
        P(("groups", "cells"), None, "sharers"),
        P(("groups", "cells"), "sharers"),
        P(("groups", "cells")),
    )
    out_specs = (P(("groups", "cells"), None, "sharers"), P(("groups", "cells"), None, "sharers"))
    return jax.shard_map(local, mesh=mesh, in_specs=in_specs, out_specs=out_specs, check_vma=False)
```

```python
import functools
import functools
import math

import jax
import jax.numpy as jnp
from jax import lax
from jax.experimental import pallas as pl
from jax.experimental.pallas import tpu as pltpu
from jax.sharding import PartitionSpec as P

EPS = 0.35
SCALE = math.sqrt(math.log2(math.e) / (2.0 * EPS * EPS))
GRID = 4.0
TINY = 1e-30
GROUP = 32
DISTANCE_ROWS = 96
DRIFT_ROWS = 64
bf16, f32 = jnp.bfloat16, jnp.float32


def round_bf16(value):
    return value.astype(bf16).astype(f32)


def pieces(value, count):
    parts = []
    for _ in range(count):
        part = round_bf16(value)
        parts.append(part)
        value = value - part
    return parts


def row_of(value):
    return lax.broadcasted_iota(jnp.int32, value.shape, 0)


def rows_sum(value):
    return jnp.sum(value, axis=0, keepdims=True)


def stacked(groups):
    if len(groups) % 2:
        groups = groups + [jnp.zeros_like(groups[0])]
    return jnp.concatenate(groups, axis=0).astype(bf16)


def scalar_groups(value, like):
    row = row_of(like)
    first, second, third = pieces(value, 3)
    low = jnp.where(row == 0, first, jnp.where(row == 1, second, jnp.where(row == 2, third, 0.0)))
    high = jnp.where(row == 3, first, jnp.where(row == 4, second, jnp.where(row == 5, third, 0.0)))
    ones_low, ones_high = row < 3, (row >= 3) & (row < 6)
    return jnp.where(ones_high, 1.0, low), jnp.where(ones_low, 1.0, high)


def grid_parts(place):
    coarse = jnp.floor(place * GRID + 0.5) * (1.0 / GRID)
    return [coarse] + pieces(place - coarse, 2)


def distance_features(parts):
    coarse, fine, rest = parts
    minor = fine + rest
    query_norm, key_norm = scalar_groups(-rows_sum(coarse * coarse), coarse)
    query_less, key_less = scalar_groups(-rows_sum(minor * (2.0 * coarse + minor)), coarse)
    key = [coarse, key_norm, coarse, coarse, fine, rest, key_less, fine, fine, rest, rest]
    coarse, fine, rest = coarse * 2.0, fine * 2.0, rest * 2.0
    query = [coarse, query_norm, fine, rest, coarse, coarse, query_less, fine, rest, fine, rest]
    return stacked(key), stacked(query)


def weighted_rows(weight, value):
    row = row_of(value)
    whole = jnp.where(row < 3, value, jnp.where(row == 3, 1.0, 0.0)) * weight
    first, second, third = pieces(whole, 3)
    return stacked([first, second + pltpu.roll(third, 4, 0)])


def product(left, right):
    return jnp.dot(left, right, preferred_element_type=f32)


def store_split(ref, rows, matrix):
    half = ref.shape[0] // 2
    upper = matrix.astype(bf16)
    ref[rows, :] = upper
    ref[pl.ds(half + rows.start, rows.size), :] = (matrix - upper.astype(f32)).astype(bf16)


def sum_rows(left, ref):
    return product(jnp.concatenate([left, left], axis=1), ref[...])


def sum_columns(left, ref):
    both = lax.dot_general(left, ref[...], (((1,), (1,)), ((), ())), preferred_element_type=f32)
    half = ref.shape[0] // 2
    return both[:, :half] + both[:, half:]


def sum_rows_less(left, ref):
    half = ref.shape[0] // 2
    both = product(left, ref[:half, :])
    few = left.shape[0] // 2
    return both[:few] + product(left[:few], ref[half:, :]), both[few:]


def sum_columns_less(left, ref):
    half, few = ref.shape[0] // 2, left.shape[0] // 2
    turned = (((1,), (1,)), ((), ()))
    both = lax.dot_general(left, ref[:half, :], turned, preferred_element_type=f32)
    less = lax.dot_general(left[:few], ref[half:, :], turned, preferred_element_type=f32)
    return both[:few] + less, both[few:]


def joined(total):
    upper, lower = total[0:8], total[8:16]
    return upper + lower + pltpu.roll(lower, 4, 0)


def drift_rows(weight, place, score):
    row = row_of(place)
    base = place + jnp.where(row == 3, 1.0, 0.0) + pltpu.roll(score, 4, 0)
    cubic = rows_sum(place * place) * score - rows_sum(place * score) * place
    groups = [weight * base]
    for i in range(3):
        here = slice(i, i + 1)
        groups.append(weight * jnp.where(row == 3, cubic[here], place[here] * base))
    return stacked(sum(map(list, zip(*[pieces(group, 2) for group in groups])), []))


def drift_sum(total, place, score):
    row = row_of(place)
    first, *rest = [total[8 * i : 8 * i + 8] for i in range(4)]
    turned = [pltpu.roll(group, 4, 0) for group in rest]
    count, scores = first[3:4], pltpu.roll(first, 4, 0)
    square, both = rows_sum(place * place), rows_sum(place * score)
    trace = rest[0][0:1] + rest[1][1:2] + rest[2][2:3]
    cross = turned[0][0:1] + turned[1][1:2] + turned[2][2:3]
    drift = score * (square * count - 2.0 * rows_sum(place * first) + trace) - square * scores
    drift += both * first + place * (
        rows_sum(place * scores) + rows_sum(score * first) - both * count - cross
    )
    ends = []
    for i in range(3):
        here = slice(i, i + 1)
        drift += 2.0 * place[here] * turned[i] - score[here] * rest[i]
        ends.append(rows_sum(place * turned[i]) + rest[i][3:4])
    return drift - jnp.where(row == 0, ends[0], jnp.where(row == 1, ends[1], ends[2]))


def widened(block):
    return jnp.concatenate([block[0], jnp.zeros_like(block[0])], axis=0)


def prepared(whole, live):
    weight = jnp.where(live, whole[3:4], 0.0)
    parts = grid_parts(jnp.where(row_of(whole) < 3, whole * SCALE, 0.0))
    place = parts[0] + parts[1] + parts[2]
    key, query = distance_features(parts)
    return weight, place, key.T, query, weighted_rows(weight, place)


def split_blobs(exponent, split):
    for group in range(0, exponent.shape[0], GROUP):
        rows = pl.ds(group, GROUP)
        store_split(split, rows, jnp.exp2(exponent[rows, :]))


def split_distances(exponent, split):
    for group in range(0, exponent.shape[0], GROUP):
        rows = pl.ds(group, GROUP)
        negative = jnp.minimum(exponent[rows, :], -TINY)
        store_split(split, rows, negative * lax.rsqrt(-negative))


def diagonal_tiles(start, width):
    half = width // 2
    return [(start, half, start, half, 0), (start + half, half, start, width, half)]


def add_blobs(tile, split, moments, sums_ref):
    key, keys, query, queries, turned = tile
    sums_ref[:, pl.ds(query, queries)] += sum_rows(moments(key, keys), split)
    if turned:
        sums_ref[:, pl.ds(key, keys)] += sum_columns(moments(query, turned), split.at[:, 0:turned])


def add_distances(tile, split, fluxes, totals_ref):
    key, keys, query, queries, turned = tile
    upper, lower = sum_rows_less(fluxes(key, keys), split)
    totals_ref[:, pl.ds(query, queries)] += upper + lower
    if turned:
        upper, lower = sum_columns_less(fluxes(query, turned), split.at[:, 0:turned])
        totals_ref[:, pl.ds(key, keys)] += upper + lower


def stage(tiles, exponent, moments, sums_ref, exponent_refs, split_refs, distance_refs):
    def buffer(index):
        _, keys, _, queries, _ = tiles[index]
        return exponent_refs[index % 2].at[0:keys, 0:queries]

    buffer(0)[...] = exponent(tiles[0])
    for index, tile in enumerate(tiles):
        if index + 1 < len(tiles):
            buffer(index + 1)[...] = exponent(tiles[index + 1])
        split = split_refs[index % 2].at[0 : 2 * tile[1], 0 : tile[3]]
        split_blobs(buffer(index), split)
        add_blobs(tile, split, moments, sums_ref)
        split_distances(buffer(index), distance_refs[index])


def looked_up(refs, width, axis):
    def read(start, size):
        at = pl.ds(start % width, size)
        ref = refs[start // width]
        return ref[at, :] if axis == 0 else ref[:, at]

    return read


def exponent_of(keys, queries):
    return lambda tile: product(keys(tile[0], tile[1]), queries(tile[2], tile[3]))


def lanes_of(source, width):
    return lax.broadcasted_iota(jnp.int32, (1, width), 1) + source * width


def owner_of(sources):
    here = lax.axis_index("sharers")
    return sum(jnp.where(here == i, source, 0) for i, source in enumerate(sources))


def own_kernel(filled, block, key_out, query_out, moment_out, sums_out, first_out, second_out,
               *scratch):
    width = block.shape[2]
    live = lanes_of(lax.axis_index("sharers"), width) < filled[...]
    _, _, key, query, moment = prepared(widened(block), live)
    key_out[...] = key
    query_out[...] = query
    moment_out[...] = moment
    sums_out[...] = jnp.zeros_like(sums_out)
    exponent = exponent_of(looked_up([key_out], width, 0), looked_up([query_out], width, 1))
    moments = looked_up([moment_out], width, 1)
    tiles = diagonal_tiles(0, width)
    stage(tiles, exponent, moments, sums_out, scratch[:2], scratch[2:], (first_out, second_out))


def next_kernel(sources, filled, block, own_key, own_query, own_moment, own_sums, key_out,
                query_out, moment_out, sums_out, *refs):
    width = block.shape[2]
    live = lanes_of(owner_of(sources), width) < filled[...]
    _, _, key, query, moment = prepared(widened(block), live)
    key_out[...] = key
    query_out[...] = query
    moment_out[...] = moment
    sums_out[:, 0:width] = own_sums[...]
    sums_out[:, width:] = jnp.zeros_like(own_sums)
    exponent = exponent_of(
        looked_up([own_key, key_out], width, 0), looked_up([own_query, query_out], width, 1)
    )
    moments = looked_up([own_moment, moment_out], width, 1)
    tiles = square_tiles(width, 0, width) + diagonal_tiles(width, width)
    distances, scratch = refs[: len(tiles)], refs[len(tiles) :]
    stage(tiles, exponent, moments, sums_out, scratch[:2], scratch[2:], distances)


def feature_shapes(width):
    return [
        jax.ShapeDtypeStruct((width, DISTANCE_ROWS), bf16),
        jax.ShapeDtypeStruct((DISTANCE_ROWS, width), bf16),
        jax.ShapeDtypeStruct((16, width), bf16),
    ]


def diagonal_shapes(width):
    half = width // 2
    return [
        jax.ShapeDtypeStruct((2 * half, half), bf16),
        jax.ShapeDtypeStruct((2 * half, width), bf16),
    ]


def stage_scratch(width):
    half = width // 2
    return [pltpu.VMEM((half, width), f32)] * 2 + [pltpu.VMEM((width, width), bf16)] * 2


def own_part(filled, block):
    width = block.shape[2]
    vector = pl.BlockSpec(memory_space=pltpu.VMEM)
    shapes = feature_shapes(width) + [jax.ShapeDtypeStruct((16, width), f32)] + diagonal_shapes(width)
    return pl.pallas_call(
        own_kernel,
        out_shape=shapes,
        in_specs=[vector] * 2,
        out_specs=[vector] * len(shapes),
        scratch_shapes=stage_scratch(width),
        compiler_params=pltpu.CompilerParams(vmem_limit_bytes=16 << 20),
        name="own",
    )(filled, block)


def next_part(filled, block, features, sums, sources):
    width = block.shape[2]
    vector = pl.BlockSpec(memory_space=pltpu.VMEM)
    shapes = feature_shapes(width) + [jax.ShapeDtypeStruct((16, 2 * width), f32)]
    shapes += [jax.ShapeDtypeStruct((width, width), bf16)] * 2 + diagonal_shapes(width)
    return pl.pallas_call(
        functools.partial(next_kernel, sources),
        out_shape=shapes,
        in_specs=[vector] * 6,
        out_specs=[vector] * len(shapes),
        scratch_shapes=stage_scratch(width),
        compiler_params=pltpu.CompilerParams(vmem_limit_bytes=20 << 20),
        name="next",
    )(filled, block, *features, sums)


def square_tiles(key, query, width):
    half = width // 2
    return [(key + part, half, query, width, width) for part in (0, half)]


def scored(weight, place, sums):
    vector, live = row_of(place) < 3, weight > 0.0
    density_sum = jnp.where(live, sums[3:4], 1.0)
    pull = place * density_sum - sums
    return jnp.where(vector & live, pull / (-SCALE * EPS * EPS * density_sum), 0.0)


def whole_cell(blocks, live):
    weight = jnp.concatenate(
        [jnp.where(on, block[0, 3:4], 0.0) for on, block in zip(live, blocks)], axis=1
    )
    whole = jnp.concatenate([widened(block) for block in blocks], axis=1)
    vector = row_of(whole) < 3
    parts = grid_parts(jnp.where(vector, whole * SCALE, 0.0))
    place = parts[0] + parts[1] + parts[2]
    middle = jnp.sum(place * weight, axis=1, keepdims=True)
    middle = middle / jnp.sum(weight, axis=1, keepdims=True)
    return weight, place, jnp.where(vector, place - middle, 0.0)


def finish(blocks, total_slots, weight, centred, score, totals, outs):
    scores_out, drift_out, start_out, speed_out = outs
    width = blocks[0].shape[2]
    spread = totals.shape[1]
    drift = drift_sum(totals, centred[:, 0:spread], score[:, 0:spread])
    factor = 1.0 / (SCALE * SCALE * SCALE * total_slots)
    live = (row_of(drift) < 3) & (weight[:, 0:spread] > 0.0)
    drift = jnp.where(live, drift * factor, 0.0)
    largest = jnp.max(rows_sum(drift * drift), axis=1, keepdims=True)
    speed_out[...] = jnp.broadcast_to(jnp.sqrt(largest), speed_out.shape)
    scores_out[...] = score[:, 0:width]
    for part in range(width // 128):
        lanes = slice(part * 128, part * 128 + 128)
        for axis in range(3):
            drift_out[axis, part : part + 1, :] = drift[axis : axis + 1, lanes]
            start_out[axis, part : part + 1, :] = blocks[0][0, axis : axis + 1, lanes]


def pair_of(step):
    return 2 + ((step & 1) | (step >> 2)), step >> 1


LATE_PAIRS = 5


def sweep_kernel(sources, *refs):
    count = len(sources)
    filled, blocks, refs = refs[0], refs[1 : count + 1], list(refs[count + 1 :])
    own, following, refs = refs[:5], refs[5:13], refs[13:]
    outs, (key_ref, query_ref, moment_ref, flux_ref, sums_ref, totals_ref), refs = (
        refs[:4], refs[4:10], refs[10:]
    )
    width = blocks[0].shape[2]
    half = width // 2
    exponent_refs, split_refs, pair_ref, diagonal_refs = refs[:2], refs[2:4], refs[4], refs[5:]

    live = [lanes_of(owner_of(source), width) < filled[...] for source in sources]
    for index, early in enumerate((own, following)):
        lanes = pl.ds(index * width, width)
        query_ref[:, lanes] = early[1][...]
        moment_ref[:, lanes] = early[2][...]
    for index in range(2, count):
        _, _, key, query, moment = prepared(widened(blocks[index]), live[index])
        lanes = pl.ds(index * width, width)
        key_ref[pl.ds((index - 2) * width, width), :] = key
        query_ref[:, lanes] = query
        moment_ref[:, lanes] = moment
    weight, place, centred = whole_cell(blocks, live)

    def exponent(key, keys, query, queries):
        return product(key_ref[pl.ds(key - 2 * width, keys), :], query_ref[:, pl.ds(query, queries)])

    def moments(start, size):
        return moment_ref[:, pl.ds(start, size)]

    sums_ref[:, 0 : 2 * width] = following[3][...]
    sums_ref[:, 2 * width :] = jnp.zeros_like(sums_ref[:, 2 * width :])

    def half_tile(step, part):
        key, query = pair_of(step)
        key = pl.multiple_of(key * width + part * half, half)
        return (key, half, pl.multiple_of(query * width, width), width, width)

    def work(tile, exponents, split, distances):
        split_blobs(exponents, split)
        add_blobs(tile, split, moments, sums_ref)
        split_distances(exponents, distances)

    exponent_refs[0][...] = exponent(*half_tile(0, 0)[:4])

    @pl.loop(0, LATE_PAIRS)
    def _(step):
        exponent_refs[1][...] = exponent(*half_tile(step, 1)[:4])
        work(half_tile(step, 0), exponent_refs[0], split_refs[0], pair_ref.at[2 * step])
        following_step = jnp.minimum(step + 1, LATE_PAIRS - 1)
        exponent_refs[0][...] = exponent(*half_tile(following_step, 0)[:4])
        work(half_tile(step, 1), exponent_refs[1], split_refs[1], pair_ref.at[2 * step + 1])

    diagonal = diagonal_tiles(2 * width, width) + diagonal_tiles(3 * width, width)
    stage(
        diagonal, lambda tile: exponent(*tile[:4]), moments, sums_ref, exponent_refs, split_refs,
        diagonal_refs,
    )
    score = scored(weight, place, joined(sums_ref[...]))
    flux_ref[...] = drift_rows(weight, centred, score)
    totals_ref[...] = jnp.zeros_like(totals_ref)

    def fluxes(start, size):
        return flux_ref[:, pl.ds(start, size)]

    early = diagonal_tiles(0, width) + square_tiles(width, 0, width)
    early += diagonal_tiles(width, width)
    for tile, split in zip(early + diagonal, own[3:5] + following[4:8] + diagonal_refs):
        add_distances(tile, split, fluxes, totals_ref)

    @pl.loop(0, LATE_PAIRS)
    def _(step):
        for part in range(2):
            add_distances(half_tile(step, part), pair_ref.at[2 * step + part], fluxes, totals_ref)

    finish(blocks, count * width, weight, centred, score, totals_ref[...], outs)


def sweep_shapes(width, copies):
    parts = jax.ShapeDtypeStruct((3, width // 128, 128), f32)
    speeds = jax.ShapeDtypeStruct((copies, 128), f32)
    return [jax.ShapeDtypeStruct((8, width), f32), parts, parts, speeds]


def sweep(filled, blocks, sources):
    count, width = len(blocks), blocks[0].shape[2]
    slots = count * width
    own = own_part(filled, blocks[0])
    following = next_part(filled, blocks[1], own[:3], own[3], sources[1])
    early = [*own[:3], *own[4:], *following]
    vector = pl.BlockSpec(memory_space=pltpu.VMEM)
    diagonal = diagonal_tiles(0, width) * 2
    return pl.pallas_call(
        functools.partial(sweep_kernel, sources),
        out_shape=sweep_shapes(width, 1),
        in_specs=[vector] * (1 + count + len(early)),
        out_specs=[vector] * 4,
        scratch_shapes=[
            pltpu.VMEM((slots - 2 * width, DISTANCE_ROWS), bf16),
            pltpu.VMEM((DISTANCE_ROWS, slots), bf16),
            pltpu.VMEM((16, slots), bf16),
            pltpu.VMEM((DRIFT_ROWS, slots), bf16),
            pltpu.VMEM((16, slots), f32),
            pltpu.VMEM((DRIFT_ROWS // 2, slots), f32),
        ]
        + stage_scratch(width)
        + [pltpu.VMEM((2 * LATE_PAIRS, width, width), bf16)]
        + [pltpu.VMEM((2 * tile[1], tile[3]), bf16) for tile in diagonal],
        compiler_params=pltpu.CompilerParams(vmem_limit_bytes=24 << 20),
        name="sweep",
    )(filled, *blocks, *early)


def long_kernel(sources, filled, *refs):
    count = len(sources)
    blocks, outs, refs = refs[:count], refs[count : count + 4], refs[count + 4 :]
    key_ref, query_ref, moment_ref, flux_ref, sums_ref, totals_ref, exponent_ref, split_ref = refs
    width = blocks[0].shape[2]
    live = [lanes_of(owner_of(source), width) < filled[...] for source in sources]
    for index, (block, on) in enumerate(zip(blocks, live)):
        _, _, key, query, moment = prepared(widened(block), on)
        lanes = pl.ds(index * width, width)
        key_ref[lanes, :] = key
        query_ref[:, lanes] = query
        moment_ref[:, lanes] = moment
    weight, place, centred = whole_cell(blocks, live)
    sums_ref[...] = jnp.zeros_like(sums_ref)
    totals_ref[...] = jnp.zeros_like(totals_ref)

    def block_tile(key, query, both):
        start, first = (pl.multiple_of(block * width, width) for block in (key, query))
        return (start, width, first, width, width if both else 0)

    def fill(tile):
        key, keys, query, queries, _ = tile
        exponent_ref[...] = product(key_ref[pl.ds(key, keys), :], query_ref[:, pl.ds(query, queries)])

    def blobs(key, query, both):
        tile = block_tile(key, query, both)
        fill(tile)
        split_blobs(exponent_ref, split_ref)
        add_blobs(tile, split_ref, lambda at, size: moment_ref[:, pl.ds(at, size)], sums_ref)

    @pl.loop(0, count)
    def _(query):
        blobs(query, query, False)

        @pl.loop(query + 1, count)
        def _(key):
            blobs(key, query, True)

    score = scored(weight, place, joined(sums_ref[...]))
    flux_ref[...] = drift_rows(weight, centred, score)

    @pl.loop(0, count)
    def _(key):
        tile = block_tile(key, 0, False)
        fill(tile)
        split_distances(exponent_ref, split_ref)
        add_distances(tile, split_ref, lambda at, size: flux_ref[:, pl.ds(at, size)], totals_ref)

    finish(blocks, count * width, weight, centred, score, totals_ref[...], outs)


def long_sweep(filled, blocks, sources, copies):
    count, width = len(blocks), blocks[0].shape[2]
    slots = count * width
    vector = pl.BlockSpec(memory_space=pltpu.VMEM)
    return pl.pallas_call(
        functools.partial(long_kernel, sources),
        out_shape=sweep_shapes(width, copies),
        in_specs=[vector] * (1 + count),
        out_specs=[vector] * 4,
        scratch_shapes=[
            pltpu.VMEM((slots, DISTANCE_ROWS), bf16),
            pltpu.VMEM((DISTANCE_ROWS, slots), bf16),
            pltpu.VMEM((16, slots), bf16),
            pltpu.VMEM((DRIFT_ROWS, slots), bf16),
            pltpu.VMEM((16, slots), f32),
            pltpu.VMEM((DRIFT_ROWS // 2, width), f32),
            pltpu.VMEM((width, width), f32),
            pltpu.VMEM((2 * width, width), bf16),
        ],
        compiler_params=pltpu.CompilerParams(vmem_limit_bytes=(16 << 20) + slots * 2688),
        name="sweep",
    )(filled, *blocks)


def swapped(value, axis, step):
    pairs = [(i, i ^ step) for i in range(lax.axis_size(axis))]
    return lax.ppermute(value, axis, pairs)


def bits(size):
    return [1 << bit for bit in range(size.bit_length() - 1)]


ROUNDS = ((2, 3, 1, 0), (3, 2, 0, 1), (1, 0, 3, 2))


def gathered(block):
    size = lax.axis_size("sharers")
    if size == len(ROUNDS) + 1:
        blocks, sources = [block], [tuple(range(size))]
        for targets in ROUNDS:
            blocks.append(lax.ppermute(block, "sharers", list(enumerate(targets))))
            sources.append(tuple(targets.index(i) for i in range(size)))
        return blocks, sources
    for step in bits(size):
        block = jnp.concatenate([block, swapped(block, "sharers", step)], axis=0)
    sources = [tuple(i ^ step for i in range(size)) for step in range(size)]
    return [block[i : i + 1] for i in range(size)], sources


def local(velocities, weights, counts):
    filled = counts.reshape(1, 1)
    blocks, sources = gathered(jnp.concatenate([velocities, weights[:, None]], axis=1))
    if len(blocks) == len(ROUNDS) + 1:
        scores, drift, start, speeds = sweep(filled, blocks, sources)
        for step in bits(lax.axis_size("cells")):
            speeds = jnp.maximum(speeds, swapped(speeds, "cells", 2 * step - 1))
        largest = speeds
    else:
        axes = ("cells", "sharers")
        scores, drift, start, speeds = long_sweep(filled, blocks, sources, lax.axis_size(axes))
        largest = jnp.max(lax.all_to_all(speeds[:, None], axes, 0, 0, tiled=True), axis=0)
    time_step = 0.5 / (largest + 1e-06)
    moved = start + time_step[None] * drift
    return moved.reshape(velocities.shape), scores[None, 0:3]


def solution(mesh):
    in_specs = (
        P(("groups", "cells"), None, "sharers"),
        P(("groups", "cells"), "sharers"),
        P(("groups", "cells")),
    )
    out_specs = (P(("groups", "cells"), None, "sharers"), P(("groups", "cells"), None, "sharers"))
    return jax.shard_map(local, mesh=mesh, in_specs=in_specs, out_specs=out_specs, check_vma=False)
```

```python
import functools
import functools
import math

import jax
import jax.numpy as jnp
from jax import lax
from jax.experimental import pallas as pl
from jax.experimental.pallas import tpu as pltpu
from jax.sharding import PartitionSpec as P

EPS = 0.35
SCALE = math.sqrt(math.log2(math.e) / (2.0 * EPS * EPS))
GRID = 4.0
TINY = 1e-30
GROUP = 32
DISTANCE_ROWS = 96
DRIFT_ROWS = 64
bf16, f32 = jnp.bfloat16, jnp.float32


def round_bf16(value):
    return value.astype(bf16).astype(f32)


def pieces(value, count):
    parts = []
    for _ in range(count):
        part = round_bf16(value)
        parts.append(part)
        value = value - part
    return parts


def row_of(value):
    return lax.broadcasted_iota(jnp.int32, value.shape, 0)


def rows_sum(value):
    return jnp.sum(value, axis=0, keepdims=True)


def stacked(groups):
    if len(groups) % 2:
        groups = groups + [jnp.zeros_like(groups[0])]
    return jnp.concatenate(groups, axis=0).astype(bf16)


def scalar_groups(value, like):
    row = row_of(like)
    first, second, third = pieces(value, 3)
    low = jnp.where(row == 0, first, jnp.where(row == 1, second, jnp.where(row == 2, third, 0.0)))
    high = jnp.where(row == 3, first, jnp.where(row == 4, second, jnp.where(row == 5, third, 0.0)))
    ones_low, ones_high = row < 3, (row >= 3) & (row < 6)
    return jnp.where(ones_high, 1.0, low), jnp.where(ones_low, 1.0, high)


def grid_parts(place):
    coarse = jnp.floor(place * GRID + 0.5) * (1.0 / GRID)
    return [coarse] + pieces(place - coarse, 2)


def distance_features(parts):
    coarse, fine, rest = parts
    minor = fine + rest
    query_norm, key_norm = scalar_groups(-rows_sum(coarse * coarse), coarse)
    query_less, key_less = scalar_groups(-rows_sum(minor * (2.0 * coarse + minor)), coarse)
    key = [coarse, key_norm, coarse, coarse, fine, rest, key_less, fine, fine, rest, rest]
    coarse, fine, rest = coarse * 2.0, fine * 2.0, rest * 2.0
    query = [coarse, query_norm, fine, rest, coarse, coarse, query_less, fine, rest, fine, rest]
    return stacked(key), stacked(query)


def weighted_rows(weight, value):
    row = row_of(value)
    whole = jnp.where(row < 3, value, jnp.where(row == 3, 1.0, 0.0)) * weight
    first, second, third = pieces(whole, 3)
    return stacked([first, second + pltpu.roll(third, 4, 0)])


def product(left, right):
    return jnp.dot(left, right, preferred_element_type=f32)


def store_split(ref, rows, matrix):
    half = ref.shape[0] // 2
    upper = matrix.astype(bf16)
    ref[rows, :] = upper
    ref[pl.ds(half + rows.start, rows.size), :] = (matrix - upper.astype(f32)).astype(bf16)


def sum_rows(left, ref):
    return product(jnp.concatenate([left, left], axis=1), ref[...])


def sum_columns(left, ref):
    both = lax.dot_general(left, ref[...], (((1,), (1,)), ((), ())), preferred_element_type=f32)
    half = ref.shape[0] // 2
    return both[:, :half] + both[:, half:]


def sum_rows_less(left, ref):
    half = ref.shape[0] // 2
    both = product(left, ref[:half, :])
    few = left.shape[0] // 2
    return both[:few] + product(left[:few], ref[half:, :]), both[few:]


def sum_columns_less(left, ref):
    half, few = ref.shape[0] // 2, left.shape[0] // 2
    turned = (((1,), (1,)), ((), ()))
    both = lax.dot_general(left, ref[:half, :], turned, preferred_element_type=f32)
    less = lax.dot_general(left[:few], ref[half:, :], turned, preferred_element_type=f32)
    return both[:few] + less, both[few:]


def joined(total):
    upper, lower = total[0:8], total[8:16]
    return upper + lower + pltpu.roll(lower, 4, 0)


def drift_rows(weight, place, score):
    row = row_of(place)
    base = place + jnp.where(row == 3, 1.0, 0.0) + pltpu.roll(score, 4, 0)
    cubic = rows_sum(place * place) * score - rows_sum(place * score) * place
    groups = [weight * base]
    for i in range(3):
        here = slice(i, i + 1)
        groups.append(weight * jnp.where(row == 3, cubic[here], place[here] * base))
    return stacked(sum(map(list, zip(*[pieces(group, 2) for group in groups])), []))


def drift_sum(total, place, score):
    row = row_of(place)
    first, *rest = [total[8 * i : 8 * i + 8] for i in range(4)]
    turned = [pltpu.roll(group, 4, 0) for group in rest]
    count, scores = first[3:4], pltpu.roll(first, 4, 0)
    square, both = rows_sum(place * place), rows_sum(place * score)
    trace = rest[0][0:1] + rest[1][1:2] + rest[2][2:3]
    cross = turned[0][0:1] + turned[1][1:2] + turned[2][2:3]
    drift = score * (square * count - 2.0 * rows_sum(place * first) + trace) - square * scores
    drift += both * first + place * (
        rows_sum(place * scores) + rows_sum(score * first) - both * count - cross
    )
    ends = []
    for i in range(3):
        here = slice(i, i + 1)
        drift += 2.0 * place[here] * turned[i] - score[here] * rest[i]
        ends.append(rows_sum(place * turned[i]) + rest[i][3:4])
    return drift - jnp.where(row == 0, ends[0], jnp.where(row == 1, ends[1], ends[2]))


def widened(block):
    return jnp.concatenate([block[0], jnp.zeros_like(block[0])], axis=0)


def prepared(whole, live):
    weight = jnp.where(live, whole[3:4], 0.0)
    parts = grid_parts(jnp.where(row_of(whole) < 3, whole * SCALE, 0.0))
    place = parts[0] + parts[1] + parts[2]
    key, query = distance_features(parts)
    return weight, place, key.T, query, weighted_rows(weight, place)


def split_blobs(exponent, split):
    for group in range(0, exponent.shape[0], GROUP):
        rows = pl.ds(group, GROUP)
        store_split(split, rows, jnp.exp2(exponent[rows, :]))


def split_distances(exponent, split):
    for group in range(0, exponent.shape[0], GROUP):
        rows = pl.ds(group, GROUP)
        negative = jnp.minimum(exponent[rows, :], -TINY)
        store_split(split, rows, negative * lax.rsqrt(-negative))


def diagonal_tiles(start, width):
    half = width // 2
    return [(start, half, start, half, 0), (start + half, half, start, width, half)]


def add_blobs(tile, split, moments, sums_ref):
    key, keys, query, queries, turned = tile
    sums_ref[:, pl.ds(query, queries)] += sum_rows(moments(key, keys), split)
    if turned:
        sums_ref[:, pl.ds(key, keys)] += sum_columns(moments(query, turned), split.at[:, 0:turned])


def add_distances(tile, split, fluxes, totals_ref):
    key, keys, query, queries, turned = tile
    upper, lower = sum_rows_less(fluxes(key, keys), split)
    totals_ref[:, pl.ds(query, queries)] += upper + lower
    if turned:
        upper, lower = sum_columns_less(fluxes(query, turned), split.at[:, 0:turned])
        totals_ref[:, pl.ds(key, keys)] += upper + lower


def stage(tiles, exponent, moments, sums_ref, exponent_refs, split_refs, distance_refs):
    def buffer(index):
        _, keys, _, queries, _ = tiles[index]
        return exponent_refs[index % len(exponent_refs)].at[0:keys, 0:queries]

    buffer(0)[...] = exponent(tiles[0])
    for index, tile in enumerate(tiles):
        if index + 1 < len(tiles):
            buffer(index + 1)[...] = exponent(tiles[index + 1])
        split = split_refs[index % 2].at[0 : 2 * tile[1], 0 : tile[3]]
        split_blobs(buffer(index), split)
        add_blobs(tile, split, moments, sums_ref)
        if distance_refs is not None:
            split_distances(buffer(index), distance_refs[index])


def looked_up(refs, width, axis):
    def read(start, size):
        at = pl.ds(start % width, size)
        ref = refs[start // width]
        return ref[at, :] if axis == 0 else ref[:, at]

    return read


def exponent_of(keys, queries):
    return lambda tile: product(keys(tile[0], tile[1]), queries(tile[2], tile[3]))


def lanes_of(source, width):
    return lax.broadcasted_iota(jnp.int32, (1, width), 1) + source * width


def owner_of(sources):
    here = lax.axis_index("sharers")
    return sum(jnp.where(here == i, source, 0) for i, source in enumerate(sources))


def own_kernel(filled, block, key_out, query_out, moment_out, sums_out, first_out, second_out,
               *scratch):
    width = block.shape[2]
    live = lanes_of(lax.axis_index("sharers"), width) < filled[...]
    _, _, key, query, moment = prepared(widened(block), live)
    key_out[...] = key
    query_out[...] = query
    moment_out[...] = moment
    sums_out[...] = jnp.zeros_like(sums_out)
    exponent = exponent_of(looked_up([key_out], width, 0), looked_up([query_out], width, 1))
    moments = looked_up([moment_out], width, 1)
    tiles = diagonal_tiles(0, width)
    stage(tiles, exponent, moments, sums_out, scratch[:2], scratch[2:], (first_out, second_out))


def next_kernel(sources, filled, block, own_key, own_query, own_moment, own_sums, key_out,
                query_out, moment_out, sums_out, *refs):
    width = block.shape[2]
    live = lanes_of(owner_of(sources), width) < filled[...]
    _, _, key, query, moment = prepared(widened(block), live)
    key_out[...] = key
    query_out[...] = query
    moment_out[...] = moment
    sums_out[:, 0:width] = own_sums[...]
    sums_out[:, width:] = jnp.zeros_like(own_sums)
    exponent = exponent_of(
        looked_up([own_key, key_out], width, 0), looked_up([own_query, query_out], width, 1)
    )
    moments = looked_up([own_moment, moment_out], width, 1)
    tiles = square_tiles(width, 0, width) + diagonal_tiles(width, width)
    distances, scratch = refs[: len(tiles)], refs[len(tiles) :]
    stage(tiles, exponent, moments, sums_out, scratch[:2], scratch[2:], distances)


def feature_shapes(width):
    return [
        jax.ShapeDtypeStruct((width, DISTANCE_ROWS), bf16),
        jax.ShapeDtypeStruct((DISTANCE_ROWS, width), bf16),
        jax.ShapeDtypeStruct((16, width), bf16),
    ]


def diagonal_shapes(width):
    half = width // 2
    return [
        jax.ShapeDtypeStruct((2 * half, half), bf16),
        jax.ShapeDtypeStruct((2 * half, width), bf16),
    ]


def stage_scratch(width):
    half = width // 2
    return [pltpu.VMEM((half, width), f32)] * 2 + [pltpu.VMEM((width, width), bf16)] * 2


def own_part(filled, block):
    width = block.shape[2]
    vector = pl.BlockSpec(memory_space=pltpu.VMEM)
    shapes = feature_shapes(width) + [jax.ShapeDtypeStruct((16, width), f32)] + diagonal_shapes(width)
    return pl.pallas_call(
        own_kernel,
        out_shape=shapes,
        in_specs=[vector] * 2,
        out_specs=[vector] * len(shapes),
        scratch_shapes=stage_scratch(width),
        compiler_params=pltpu.CompilerParams(vmem_limit_bytes=16 << 20),
        name="own",
    )(filled, block)


def next_part(filled, block, features, sums, sources):
    width = block.shape[2]
    vector = pl.BlockSpec(memory_space=pltpu.VMEM)
    shapes = feature_shapes(width) + [jax.ShapeDtypeStruct((16, 2 * width), f32)]
    shapes += [jax.ShapeDtypeStruct((width, width), bf16)] * 2 + diagonal_shapes(width)
    return pl.pallas_call(
        functools.partial(next_kernel, sources),
        out_shape=shapes,
        in_specs=[vector] * 6,
        out_specs=[vector] * len(shapes),
        scratch_shapes=stage_scratch(width),
        compiler_params=pltpu.CompilerParams(vmem_limit_bytes=20 << 20),
        name="next",
    )(filled, block, *features, sums)


def square_tiles(key, query, width):
    half = width // 2
    return [(key + part, half, query, width, width) for part in (0, half)]


def late_tiles(count, width):
    tiles = []
    for query in range(count):
        first = max(query + 1, 2)
        tiles += diagonal_tiles(query * width, width) if query >= 2 else []
        for key in range(first, count):
            tiles += square_tiles(key * width, query * width, width)
    return tiles


def scored(weight, place, sums):
    vector, live = row_of(place) < 3, weight > 0.0
    density_sum = jnp.where(live, sums[3:4], 1.0)
    pull = place * density_sum - sums
    return jnp.where(vector & live, pull / (-SCALE * EPS * EPS * density_sum), 0.0)


def whole_cell(blocks, live):
    weight = jnp.concatenate(
        [jnp.where(on, block[0, 3:4], 0.0) for on, block in zip(live, blocks)], axis=1
    )
    whole = jnp.concatenate([widened(block) for block in blocks], axis=1)
    vector = row_of(whole) < 3
    parts = grid_parts(jnp.where(vector, whole * SCALE, 0.0))
    place = parts[0] + parts[1] + parts[2]
    middle = jnp.sum(place * weight, axis=1, keepdims=True)
    middle = middle / jnp.sum(weight, axis=1, keepdims=True)
    return weight, place, jnp.where(vector, place - middle, 0.0)


def finish(blocks, total_slots, weight, centred, score, totals, outs):
    scores_out, drift_out, start_out, speed_out = outs
    width = blocks[0].shape[2]
    spread = totals.shape[1]
    drift = drift_sum(totals, centred[:, 0:spread], score[:, 0:spread])
    factor = 1.0 / (SCALE * SCALE * SCALE * total_slots)
    live = (row_of(drift) < 3) & (weight[:, 0:spread] > 0.0)
    drift = jnp.where(live, drift * factor, 0.0)
    largest = jnp.max(rows_sum(drift * drift), axis=1, keepdims=True)
    speed_out[...] = jnp.broadcast_to(jnp.sqrt(largest), speed_out.shape)
    scores_out[...] = score[:, 0:width]
    for part in range(width // 128):
        lanes = slice(part * 128, part * 128 + 128)
        for axis in range(3):
            drift_out[axis, part : part + 1, :] = drift[axis : axis + 1, lanes]
            start_out[axis, part : part + 1, :] = blocks[0][0, axis : axis + 1, lanes]


def sweep_kernel(sources, *refs):
    count = len(sources)
    filled, blocks, refs = refs[0], refs[1 : count + 1], list(refs[count + 1 :])
    own, following, refs = refs[:5], refs[5:13], refs[13:]
    outs, (key_ref, query_ref, moment_ref, flux_ref, sums_ref, totals_ref), refs = (
        refs[:4], refs[4:10], refs[10:]
    )
    width = blocks[0].shape[2]
    half = 2 * width
    split_refs, refs = refs[:2], refs[2:]
    exponent_refs, distance_refs = refs[: len(refs) // 2], refs[len(refs) // 2 :]

    live = [lanes_of(owner_of(source), width) < filled[...] for source in sources]
    late = range(2, count)
    for index in late:
        _, _, key, query, moment = prepared(widened(blocks[index]), live[index])
        lanes = pl.ds((index - 2) * width, width)
        key_ref[lanes, :] = key
        query_ref[:, lanes] = query
        moment_ref[:, lanes] = moment
    weight, place, centred = whole_cell(blocks, live)
    lanes = [pl.ds((index - 2) * width, width) for index in late]
    keys = [own[0], following[0]] + [key_ref.at[lane, :] for lane in lanes]
    queries = [own[1], following[1]] + [query_ref.at[:, lane] for lane in lanes]
    moments = [own[2], following[2]] + [moment_ref.at[:, lane] for lane in lanes]
    exponent = exponent_of(looked_up(keys, width, 0), looked_up(queries, width, 1))

    sums_ref[:, 0:half] = following[3][...]
    sums_ref[:, half:] = jnp.zeros_like(sums_ref[:, half:])
    tiles = late_tiles(count, width)
    stage(
        tiles, exponent, looked_up(moments, width, 1), sums_ref, exponent_refs, split_refs, None
    )
    score = scored(weight, place, joined(sums_ref[...]))
    flux_ref[...] = drift_rows(weight, centred, score)
    totals_ref[...] = jnp.zeros_like(totals_ref)

    def fluxes(start, size):
        return flux_ref[:, pl.ds(start, size)]

    early = diagonal_tiles(0, width) + square_tiles(width, 0, width)
    early += diagonal_tiles(width, width)
    ready = list(zip(early, own[3:5] + following[4:8]))
    for tile, exponents, distances in zip(tiles, exponent_refs, distance_refs):
        split_distances(exponents, distances)
        add_distances(*ready.pop(0), fluxes, totals_ref)
        ready.append((tile, distances))
    for tile, distances in ready:
        add_distances(tile, distances, fluxes, totals_ref)
    finish(blocks, count * width, weight, centred, score, totals_ref[...], outs)


def sweep_shapes(width, copies):
    parts = jax.ShapeDtypeStruct((3, width // 128, 128), f32)
    speeds = jax.ShapeDtypeStruct((copies, 128), f32)
    return [jax.ShapeDtypeStruct((8, width), f32), parts, parts, speeds]


def sweep(filled, blocks, sources):
    count, width = len(blocks), blocks[0].shape[2]
    slots, late = count * width, (count - 2) * width
    own = own_part(filled, blocks[0])
    following = next_part(filled, blocks[1], own[:3], own[3], sources[1])
    early = [*own[:3], *own[4:], *following]
    vector = pl.BlockSpec(memory_space=pltpu.VMEM)
    distances = [pltpu.VMEM((2 * tile[1], tile[3]), bf16) for tile in late_tiles(count, width)]
    return pl.pallas_call(
        functools.partial(sweep_kernel, sources),
        out_shape=sweep_shapes(width, 1),
        in_specs=[vector] * (1 + count + len(early)),
        out_specs=[vector] * 4,
        scratch_shapes=[
            pltpu.VMEM((late, DISTANCE_ROWS), bf16),
            pltpu.VMEM((DISTANCE_ROWS, late), bf16),
            pltpu.VMEM((16, late), bf16),
            pltpu.VMEM((DRIFT_ROWS, slots), bf16),
            pltpu.VMEM((16, slots), f32),
            pltpu.VMEM((DRIFT_ROWS // 2, slots), f32),
        ]
        + [pltpu.VMEM((width, width), bf16)] * 2
        + [pltpu.VMEM((tile[1], tile[3]), f32) for tile in late_tiles(count, width)]
        + distances,
        compiler_params=pltpu.CompilerParams(vmem_limit_bytes=24 << 20),
        name="sweep",
    )(filled, *blocks, *early)


def long_kernel(sources, filled, *refs):
    count = len(sources)
    blocks, outs, refs = refs[:count], refs[count : count + 4], refs[count + 4 :]
    key_ref, query_ref, moment_ref, flux_ref, sums_ref, totals_ref, exponent_ref, split_ref = refs
    width = blocks[0].shape[2]
    live = [lanes_of(owner_of(source), width) < filled[...] for source in sources]
    for index, (block, on) in enumerate(zip(blocks, live)):
        _, _, key, query, moment = prepared(widened(block), on)
        lanes = pl.ds(index * width, width)
        key_ref[lanes, :] = key
        query_ref[:, lanes] = query
        moment_ref[:, lanes] = moment
    weight, place, centred = whole_cell(blocks, live)
    sums_ref[...] = jnp.zeros_like(sums_ref)
    totals_ref[...] = jnp.zeros_like(totals_ref)

    def block_tile(key, query, both):
        start, first = (pl.multiple_of(block * width, width) for block in (key, query))
        return (start, width, first, width, width if both else 0)

    def fill(tile):
        key, keys, query, queries, _ = tile
        exponent_ref[...] = product(key_ref[pl.ds(key, keys), :], query_ref[:, pl.ds(query, queries)])

    def blobs(key, query, both):
        tile = block_tile(key, query, both)
        fill(tile)
        split_blobs(exponent_ref, split_ref)
        add_blobs(tile, split_ref, lambda at, size: moment_ref[:, pl.ds(at, size)], sums_ref)

    @pl.loop(0, count)
    def _(query):
        blobs(query, query, False)

        @pl.loop(query + 1, count)
        def _(key):
            blobs(key, query, True)

    score = scored(weight, place, joined(sums_ref[...]))
    flux_ref[...] = drift_rows(weight, centred, score)

    @pl.loop(0, count)
    def _(key):
        tile = block_tile(key, 0, False)
        fill(tile)
        split_distances(exponent_ref, split_ref)
        add_distances(tile, split_ref, lambda at, size: flux_ref[:, pl.ds(at, size)], totals_ref)

    finish(blocks, count * width, weight, centred, score, totals_ref[...], outs)


def long_sweep(filled, blocks, sources, copies):
    count, width = len(blocks), blocks[0].shape[2]
    slots = count * width
    vector = pl.BlockSpec(memory_space=pltpu.VMEM)
    return pl.pallas_call(
        functools.partial(long_kernel, sources),
        out_shape=sweep_shapes(width, copies),
        in_specs=[vector] * (1 + count),
        out_specs=[vector] * 4,
        scratch_shapes=[
            pltpu.VMEM((slots, DISTANCE_ROWS), bf16),
            pltpu.VMEM((DISTANCE_ROWS, slots), bf16),
            pltpu.VMEM((16, slots), bf16),
            pltpu.VMEM((DRIFT_ROWS, slots), bf16),
            pltpu.VMEM((16, slots), f32),
            pltpu.VMEM((DRIFT_ROWS // 2, width), f32),
            pltpu.VMEM((width, width), f32),
            pltpu.VMEM((2 * width, width), bf16),
        ],
        compiler_params=pltpu.CompilerParams(vmem_limit_bytes=(16 << 20) + slots * 2688),
        name="sweep",
    )(filled, *blocks)


def swapped(value, axis, step):
    pairs = [(i, i ^ step) for i in range(lax.axis_size(axis))]
    return lax.ppermute(value, axis, pairs)


def bits(size):
    return [1 << bit for bit in range(size.bit_length() - 1)]


ROUNDS = ((2, 3, 1, 0), (3, 2, 0, 1), (1, 0, 3, 2))


def gathered(block):
    size = lax.axis_size("sharers")
    if size == len(ROUNDS) + 1:
        blocks, sources = [block], [tuple(range(size))]
        for targets in ROUNDS:
            blocks.append(lax.ppermute(block, "sharers", list(enumerate(targets))))
            sources.append(tuple(targets.index(i) for i in range(size)))
        return blocks, sources
    for step in bits(size):
        block = jnp.concatenate([block, swapped(block, "sharers", step)], axis=0)
    sources = [tuple(i ^ step for i in range(size)) for step in range(size)]
    return [block[i : i + 1] for i in range(size)], sources


def local(velocities, weights, counts):
    filled = counts.reshape(1, 1)
    blocks, sources = gathered(jnp.concatenate([velocities, weights[:, None]], axis=1))
    if len(blocks) == len(ROUNDS) + 1:
        scores, drift, start, speeds = sweep(filled, blocks, sources)
        for step in bits(lax.axis_size("cells")):
            speeds = jnp.maximum(speeds, swapped(speeds, "cells", 2 * step - 1))
        largest = speeds
    else:
        axes = ("cells", "sharers")
        scores, drift, start, speeds = long_sweep(filled, blocks, sources, lax.axis_size(axes))
        largest = jnp.max(lax.all_to_all(speeds[:, None], axes, 0, 0, tiled=True), axis=0)
    time_step = 0.5 / (largest + 1e-06)
    moved = start + time_step[None] * drift
    return moved.reshape(velocities.shape), scores[None, 0:3]


def solution(mesh):
    in_specs = (
        P(("groups", "cells"), None, "sharers"),
        P(("groups", "cells"), "sharers"),
        P(("groups", "cells")),
    )
    out_specs = (P(("groups", "cells"), None, "sharers"), P(("groups", "cells"), None, "sharers"))
    return jax.shard_map(local, mesh=mesh, in_specs=in_specs, out_specs=out_specs, check_vma=False)
```

```python
import functools
import functools
import math

import jax
import jax.numpy as jnp
from jax import lax
from jax.experimental import pallas as pl
from jax.experimental.pallas import tpu as pltpu
from jax.sharding import PartitionSpec as P

EPS = 0.35
SCALE = math.sqrt(math.log2(math.e) / (2.0 * EPS * EPS))
GRID = 4.0
TINY = 1e-30
GROUP = 32
DISTANCE_ROWS = 96
DRIFT_ROWS = 64
bf16, f32 = jnp.bfloat16, jnp.float32


def round_bf16(value):
    return value.astype(bf16).astype(f32)


def pieces(value, count):
    parts = []
    for _ in range(count):
        part = round_bf16(value)
        parts.append(part)
        value = value - part
    return parts


def row_of(value):
    return lax.broadcasted_iota(jnp.int32, value.shape, 0)


def rows_sum(value):
    return jnp.sum(value, axis=0, keepdims=True)


def stacked(groups):
    if len(groups) % 2:
        groups = groups + [jnp.zeros_like(groups[0])]
    return jnp.concatenate(groups, axis=0).astype(bf16)


def scalar_groups(value, like):
    row = row_of(like)
    first, second, third = pieces(value, 3)
    low = jnp.where(row == 0, first, jnp.where(row == 1, second, jnp.where(row == 2, third, 0.0)))
    high = jnp.where(row == 3, first, jnp.where(row == 4, second, jnp.where(row == 5, third, 0.0)))
    ones_low, ones_high = row < 3, (row >= 3) & (row < 6)
    return jnp.where(ones_high, 1.0, low), jnp.where(ones_low, 1.0, high)


def grid_parts(place):
    coarse = jnp.floor(place * GRID + 0.5) * (1.0 / GRID)
    return [coarse] + pieces(place - coarse, 2)


def distance_features(parts):
    coarse, fine, rest = parts
    minor = fine + rest
    query_norm, key_norm = scalar_groups(-rows_sum(coarse * coarse), coarse)
    query_less, key_less = scalar_groups(-rows_sum(minor * (2.0 * coarse + minor)), coarse)
    key = [coarse, key_norm, coarse, coarse, fine, rest, key_less, fine, fine, rest, rest]
    coarse, fine, rest = coarse * 2.0, fine * 2.0, rest * 2.0
    query = [coarse, query_norm, fine, rest, coarse, coarse, query_less, fine, rest, fine, rest]
    return stacked(key), stacked(query)


def weighted_rows(weight, value):
    row = row_of(value)
    whole = jnp.where(row < 3, value, jnp.where(row == 3, 1.0, 0.0)) * weight
    first, second, third = pieces(whole, 3)
    return stacked([first, second + pltpu.roll(third, 4, 0)])


def product(left, right):
    return jnp.dot(left, right, preferred_element_type=f32)


def store_split(ref, rows, matrix):
    half = ref.shape[0] // 2
    upper = matrix.astype(bf16)
    ref[rows, :] = upper
    ref[pl.ds(half + rows.start, rows.size), :] = (matrix - upper.astype(f32)).astype(bf16)


def sum_rows(left, ref):
    return product(jnp.concatenate([left, left], axis=1), ref[...])


def sum_columns(left, ref):
    both = lax.dot_general(left, ref[...], (((1,), (1,)), ((), ())), preferred_element_type=f32)
    half = ref.shape[0] // 2
    return both[:, :half] + both[:, half:]


def sum_rows_less(left, ref):
    half = ref.shape[0] // 2
    both = product(left, ref[:half, :])
    few = left.shape[0] // 2
    return both[:few] + product(left[:few], ref[half:, :]), both[few:]


def sum_columns_less(left, ref):
    half, few = ref.shape[0] // 2, left.shape[0] // 2
    turned = (((1,), (1,)), ((), ()))
    both = lax.dot_general(left, ref[:half, :], turned, preferred_element_type=f32)
    less = lax.dot_general(left[:few], ref[half:, :], turned, preferred_element_type=f32)
    return both[:few] + less, both[few:]


def joined(total):
    upper, lower = total[0:8], total[8:16]
    return upper + lower + pltpu.roll(lower, 4, 0)


def drift_rows(weight, place, score):
    row = row_of(place)
    base = place + jnp.where(row == 3, 1.0, 0.0) + pltpu.roll(score, 4, 0)
    cubic = rows_sum(place * place) * score - rows_sum(place * score) * place
    groups = [weight * base]
    for i in range(3):
        here = slice(i, i + 1)
        groups.append(weight * jnp.where(row == 3, cubic[here], place[here] * base))
    return stacked(sum(map(list, zip(*[pieces(group, 2) for group in groups])), []))


def drift_sum(total, place, score):
    row = row_of(place)
    first, *rest = [total[8 * i : 8 * i + 8] for i in range(4)]
    turned = [pltpu.roll(group, 4, 0) for group in rest]
    count, scores = first[3:4], pltpu.roll(first, 4, 0)
    square, both = rows_sum(place * place), rows_sum(place * score)
    trace = rest[0][0:1] + rest[1][1:2] + rest[2][2:3]
    cross = turned[0][0:1] + turned[1][1:2] + turned[2][2:3]
    drift = score * (square * count - 2.0 * rows_sum(place * first) + trace) - square * scores
    drift += both * first + place * (
        rows_sum(place * scores) + rows_sum(score * first) - both * count - cross
    )
    ends = []
    for i in range(3):
        here = slice(i, i + 1)
        drift += 2.0 * place[here] * turned[i] - score[here] * rest[i]
        ends.append(rows_sum(place * turned[i]) + rest[i][3:4])
    return drift - jnp.where(row == 0, ends[0], jnp.where(row == 1, ends[1], ends[2]))


def widened(block):
    return jnp.concatenate([block[0], jnp.zeros_like(block[0])], axis=0)


def prepared(whole, live):
    weight = jnp.where(live, whole[3:4], 0.0)
    parts = grid_parts(jnp.where(row_of(whole) < 3, whole * SCALE, 0.0))
    place = parts[0] + parts[1] + parts[2]
    key, query = distance_features(parts)
    return weight, place, key.T, query, weighted_rows(weight, place)


def split_blobs(exponent, split):
    for group in range(0, exponent.shape[0], GROUP):
        rows = pl.ds(group, GROUP)
        store_split(split, rows, jnp.exp2(exponent[rows, :]))


def split_distances(exponent, split):
    for group in range(0, exponent.shape[0], GROUP):
        rows = pl.ds(group, GROUP)
        negative = jnp.minimum(exponent[rows, :], -TINY)
        store_split(split, rows, negative * lax.rsqrt(-negative))


def diagonal_tiles(start, width):
    half = width // 2
    return [(start, half, start, half, 0), (start + half, half, start, width, half)]


def add_blobs(tile, split, moments, sums_ref):
    key, keys, query, queries, turned = tile
    sums_ref[:, pl.ds(query, queries)] += sum_rows(moments(key, keys), split)
    if turned:
        sums_ref[:, pl.ds(key, keys)] += sum_columns(moments(query, turned), split.at[:, 0:turned])


def add_distances(tile, split, fluxes, totals_ref):
    key, keys, query, queries, turned = tile
    upper, lower = sum_rows_less(fluxes(key, keys), split)
    totals_ref[:, pl.ds(query, queries)] += upper + lower
    if turned:
        upper, lower = sum_columns_less(fluxes(query, turned), split.at[:, 0:turned])
        totals_ref[:, pl.ds(key, keys)] += upper + lower


def stage(tiles, exponent, moments, sums_ref, exponent_refs, split_refs, distance_refs):
    def buffer(index):
        _, keys, _, queries, _ = tiles[index]
        return exponent_refs[index % len(exponent_refs)].at[0:keys, 0:queries]

    buffer(0)[...] = exponent(tiles[0])
    for index, tile in enumerate(tiles):
        if index + 1 < len(tiles):
            buffer(index + 1)[...] = exponent(tiles[index + 1])
        split = split_refs[index % 2].at[0 : 2 * tile[1], 0 : tile[3]]
        split_blobs(buffer(index), split)
        add_blobs(tile, split, moments, sums_ref)
        if distance_refs is not None:
            split_distances(buffer(index), distance_refs[index])


def looked_up(refs, width, axis):
    def read(start, size):
        at = pl.ds(start % width, size)
        ref = refs[start // width]
        return ref[at, :] if axis == 0 else ref[:, at]

    return read


def exponent_of(keys, queries):
    return lambda tile: product(keys(tile[0], tile[1]), queries(tile[2], tile[3]))


def lanes_of(source, width):
    return lax.broadcasted_iota(jnp.int32, (1, width), 1) + source * width


def owner_of(sources):
    here = lax.axis_index("sharers")
    return sum(jnp.where(here == i, source, 0) for i, source in enumerate(sources))


def own_kernel(filled, block, key_out, query_out, moment_out, sums_out, first_out, second_out,
               *scratch):
    width = block.shape[2]
    live = lanes_of(lax.axis_index("sharers"), width) < filled[...]
    _, _, key, query, moment = prepared(widened(block), live)
    key_out[...] = key
    query_out[...] = query
    moment_out[...] = moment
    sums_out[...] = jnp.zeros_like(sums_out)
    exponent = exponent_of(looked_up([key_out], width, 0), looked_up([query_out], width, 1))
    moments = looked_up([moment_out], width, 1)
    tiles = diagonal_tiles(0, width)
    stage(tiles, exponent, moments, sums_out, scratch[:2], scratch[2:], (first_out, second_out))


def next_kernel(sources, filled, block, own_key, own_query, own_moment, own_sums, key_out,
                query_out, moment_out, sums_out, *refs):
    width = block.shape[2]
    live = lanes_of(owner_of(sources), width) < filled[...]
    _, _, key, query, moment = prepared(widened(block), live)
    key_out[...] = key
    query_out[...] = query
    moment_out[...] = moment
    sums_out[:, 0:width] = own_sums[...]
    sums_out[:, width:] = jnp.zeros_like(own_sums)
    exponent = exponent_of(
        looked_up([own_key, key_out], width, 0), looked_up([own_query, query_out], width, 1)
    )
    moments = looked_up([own_moment, moment_out], width, 1)
    tiles = square_tiles(width, 0, width) + diagonal_tiles(width, width)
    distances, scratch = refs[: len(tiles)], refs[len(tiles) :]
    stage(tiles, exponent, moments, sums_out, scratch[:2], scratch[2:], distances)


def feature_shapes(width):
    return [
        jax.ShapeDtypeStruct((width, DISTANCE_ROWS), bf16),
        jax.ShapeDtypeStruct((DISTANCE_ROWS, width), bf16),
        jax.ShapeDtypeStruct((16, width), bf16),
    ]


def diagonal_shapes(width):
    half = width // 2
    return [
        jax.ShapeDtypeStruct((2 * half, half), bf16),
        jax.ShapeDtypeStruct((2 * half, width), bf16),
    ]


def stage_scratch(width):
    half = width // 2
    return [pltpu.VMEM((half, width), f32)] * 2 + [pltpu.VMEM((width, width), bf16)] * 2


def own_part(filled, block):
    width = block.shape[2]
    vector = pl.BlockSpec(memory_space=pltpu.VMEM)
    shapes = feature_shapes(width) + [jax.ShapeDtypeStruct((16, width), f32)] + diagonal_shapes(width)
    return pl.pallas_call(
        own_kernel,
        out_shape=shapes,
        in_specs=[vector] * 2,
        out_specs=[vector] * len(shapes),
        scratch_shapes=stage_scratch(width),
        compiler_params=pltpu.CompilerParams(vmem_limit_bytes=16 << 20),
        name="own",
    )(filled, block)


def next_part(filled, block, features, sums, sources):
    width = block.shape[2]
    vector = pl.BlockSpec(memory_space=pltpu.VMEM)
    shapes = feature_shapes(width) + [jax.ShapeDtypeStruct((16, 2 * width), f32)]
    shapes += [jax.ShapeDtypeStruct((width, width), bf16)] * 2 + diagonal_shapes(width)
    return pl.pallas_call(
        functools.partial(next_kernel, sources),
        out_shape=shapes,
        in_specs=[vector] * 6,
        out_specs=[vector] * len(shapes),
        scratch_shapes=stage_scratch(width),
        compiler_params=pltpu.CompilerParams(vmem_limit_bytes=20 << 20),
        name="next",
    )(filled, block, *features, sums)


def square_tiles(key, query, width):
    half = width // 2
    return [(key + part, half, query, width, width) for part in (0, half)]


def late_tiles(count, width):
    tiles, late = [], range(2, count)
    for query in late:
        for key in range(2):
            tiles += square_tiles(key * width, query * width, width)
    for query in late:
        for key in range(2, query):
            tiles += square_tiles(key * width, query * width, width)
    for query in late:
        tiles += diagonal_tiles(query * width, width)
    return tiles


def scored(weight, place, sums):
    vector, live = row_of(place) < 3, weight > 0.0
    density_sum = jnp.where(live, sums[3:4], 1.0)
    pull = place * density_sum - sums
    return jnp.where(vector & live, pull / (-SCALE * EPS * EPS * density_sum), 0.0)


def whole_cell(blocks, live):
    weight = jnp.concatenate(
        [jnp.where(on, block[0, 3:4], 0.0) for on, block in zip(live, blocks)], axis=1
    )
    whole = jnp.concatenate([widened(block) for block in blocks], axis=1)
    vector = row_of(whole) < 3
    parts = grid_parts(jnp.where(vector, whole * SCALE, 0.0))
    place = parts[0] + parts[1] + parts[2]
    middle = jnp.sum(place * weight, axis=1, keepdims=True)
    middle = middle / jnp.sum(weight, axis=1, keepdims=True)
    return weight, place, jnp.where(vector, place - middle, 0.0)


def finish(blocks, total_slots, weight, centred, score, totals, outs):
    scores_out, drift_out, start_out, speed_out = outs
    width = blocks[0].shape[2]
    spread = totals.shape[1]
    drift = drift_sum(totals, centred[:, 0:spread], score[:, 0:spread])
    factor = 1.0 / (SCALE * SCALE * SCALE * total_slots)
    live = (row_of(drift) < 3) & (weight[:, 0:spread] > 0.0)
    drift = jnp.where(live, drift * factor, 0.0)
    largest = jnp.max(rows_sum(drift * drift), axis=1, keepdims=True)
    speed_out[...] = jnp.broadcast_to(jnp.sqrt(largest), speed_out.shape)
    scores_out[...] = score[:, 0:width]
    for part in range(width // 128):
        lanes = slice(part * 128, part * 128 + 128)
        for axis in range(3):
            drift_out[axis, part : part + 1, :] = drift[axis : axis + 1, lanes]
            start_out[axis, part : part + 1, :] = blocks[0][0, axis : axis + 1, lanes]


def sweep_kernel(sources, *refs):
    count = len(sources)
    filled, blocks, refs = refs[0], refs[1 : count + 1], list(refs[count + 1 :])
    own, following, refs = refs[:5], refs[5:13], refs[13:]
    outs, (key_ref, query_ref, moment_ref, flux_ref, sums_ref, totals_ref), refs = (
        refs[:4], refs[4:10], refs[10:]
    )
    width = blocks[0].shape[2]
    half = 2 * width
    split_refs, refs = refs[:2], refs[2:]
    exponent_refs, distance_refs = refs[: len(refs) // 2], refs[len(refs) // 2 :]

    live = [lanes_of(owner_of(source), width) < filled[...] for source in sources]
    late = range(2, count)
    for index in late:
        _, _, key, query, moment = prepared(widened(blocks[index]), live[index])
        lanes = pl.ds((index - 2) * width, width)
        key_ref[lanes, :] = key
        query_ref[:, lanes] = query
        moment_ref[:, lanes] = moment
    weight, place, centred = whole_cell(blocks, live)
    lanes = [pl.ds((index - 2) * width, width) for index in late]
    keys = [own[0], following[0]] + [key_ref.at[lane, :] for lane in lanes]
    queries = [own[1], following[1]] + [query_ref.at[:, lane] for lane in lanes]
    moments = [own[2], following[2]] + [moment_ref.at[:, lane] for lane in lanes]
    exponent = exponent_of(looked_up(keys, width, 0), looked_up(queries, width, 1))

    sums_ref[:, 0:half] = following[3][...]
    sums_ref[:, half:] = jnp.zeros_like(sums_ref[:, half:])
    tiles = late_tiles(count, width)
    stage(
        tiles, exponent, looked_up(moments, width, 1), sums_ref, exponent_refs, split_refs, None
    )
    score = scored(weight, place, joined(sums_ref[...]))
    flux_ref[...] = drift_rows(weight, centred, score)
    totals_ref[...] = jnp.zeros_like(totals_ref)

    def fluxes(start, size):
        return flux_ref[:, pl.ds(start, size)]

    early = diagonal_tiles(0, width) + square_tiles(width, 0, width)
    early += diagonal_tiles(width, width)
    ready = list(zip(early, own[3:5] + following[4:8]))
    for tile, exponents, distances in zip(tiles, exponent_refs, distance_refs):
        split_distances(exponents, distances)
        add_distances(*ready.pop(0), fluxes, totals_ref)
        ready.append((tile, distances))
    for tile, distances in ready:
        add_distances(tile, distances, fluxes, totals_ref)
    finish(blocks, count * width, weight, centred, score, totals_ref[...], outs)


def sweep_shapes(width, copies):
    parts = jax.ShapeDtypeStruct((3, width // 128, 128), f32)
    speeds = jax.ShapeDtypeStruct((copies, 128), f32)
    return [jax.ShapeDtypeStruct((8, width), f32), parts, parts, speeds]


def sweep(filled, blocks, sources):
    count, width = len(blocks), blocks[0].shape[2]
    slots, late = count * width, (count - 2) * width
    own = own_part(filled, blocks[0])
    following = next_part(filled, blocks[1], own[:3], own[3], sources[1])
    early = [*own[:3], *own[4:], *following]
    vector = pl.BlockSpec(memory_space=pltpu.VMEM)
    distances = [pltpu.VMEM((2 * tile[1], tile[3]), bf16) for tile in late_tiles(count, width)]
    return pl.pallas_call(
        functools.partial(sweep_kernel, sources),
        out_shape=sweep_shapes(width, 1),
        in_specs=[vector] * (1 + count + len(early)),
        out_specs=[vector] * 4,
        scratch_shapes=[
            pltpu.VMEM((late, DISTANCE_ROWS), bf16),
            pltpu.VMEM((DISTANCE_ROWS, late), bf16),
            pltpu.VMEM((16, late), bf16),
            pltpu.VMEM((DRIFT_ROWS, slots), bf16),
            pltpu.VMEM((16, slots), f32),
            pltpu.VMEM((DRIFT_ROWS // 2, slots), f32),
        ]
        + [pltpu.VMEM((width, width), bf16)] * 2
        + [pltpu.VMEM((tile[1], tile[3]), f32) for tile in late_tiles(count, width)]
        + distances,
        compiler_params=pltpu.CompilerParams(vmem_limit_bytes=24 << 20),
        name="sweep",
    )(filled, *blocks, *early)


def long_kernel(sources, filled, *refs):
    count = len(sources)
    blocks, outs, refs = refs[:count], refs[count : count + 4], refs[count + 4 :]
    key_ref, query_ref, moment_ref, flux_ref, sums_ref, totals_ref, exponent_ref, split_ref = refs
    width = blocks[0].shape[2]
    live = [lanes_of(owner_of(source), width) < filled[...] for source in sources]
    for index, (block, on) in enumerate(zip(blocks, live)):
        _, _, key, query, moment = prepared(widened(block), on)
        lanes = pl.ds(index * width, width)
        key_ref[lanes, :] = key
        query_ref[:, lanes] = query
        moment_ref[:, lanes] = moment
    weight, place, centred = whole_cell(blocks, live)
    sums_ref[...] = jnp.zeros_like(sums_ref)
    totals_ref[...] = jnp.zeros_like(totals_ref)

    def block_tile(key, query, both):
        start, first = (pl.multiple_of(block * width, width) for block in (key, query))
        return (start, width, first, width, width if both else 0)

    def fill(tile):
        key, keys, query, queries, _ = tile
        exponent_ref[...] = product(key_ref[pl.ds(key, keys), :], query_ref[:, pl.ds(query, queries)])

    def blobs(key, query, both):
        tile = block_tile(key, query, both)
        fill(tile)
        split_blobs(exponent_ref, split_ref)
        add_blobs(tile, split_ref, lambda at, size: moment_ref[:, pl.ds(at, size)], sums_ref)

    @pl.loop(0, count)
    def _(query):
        blobs(query, query, False)

        @pl.loop(query + 1, count)
        def _(key):
            blobs(key, query, True)

    score = scored(weight, place, joined(sums_ref[...]))
    flux_ref[...] = drift_rows(weight, centred, score)

    @pl.loop(0, count)
    def _(key):
        tile = block_tile(key, 0, False)
        fill(tile)
        split_distances(exponent_ref, split_ref)
        add_distances(tile, split_ref, lambda at, size: flux_ref[:, pl.ds(at, size)], totals_ref)

    finish(blocks, count * width, weight, centred, score, totals_ref[...], outs)


def long_sweep(filled, blocks, sources, copies):
    count, width = len(blocks), blocks[0].shape[2]
    slots = count * width
    vector = pl.BlockSpec(memory_space=pltpu.VMEM)
    return pl.pallas_call(
        functools.partial(long_kernel, sources),
        out_shape=sweep_shapes(width, copies),
        in_specs=[vector] * (1 + count),
        out_specs=[vector] * 4,
        scratch_shapes=[
            pltpu.VMEM((slots, DISTANCE_ROWS), bf16),
            pltpu.VMEM((DISTANCE_ROWS, slots), bf16),
            pltpu.VMEM((16, slots), bf16),
            pltpu.VMEM((DRIFT_ROWS, slots), bf16),
            pltpu.VMEM((16, slots), f32),
            pltpu.VMEM((DRIFT_ROWS // 2, width), f32),
            pltpu.VMEM((width, width), f32),
            pltpu.VMEM((2 * width, width), bf16),
        ],
        compiler_params=pltpu.CompilerParams(vmem_limit_bytes=(16 << 20) + slots * 2688),
        name="sweep",
    )(filled, *blocks)


def swapped(value, axis, step):
    pairs = [(i, i ^ step) for i in range(lax.axis_size(axis))]
    return lax.ppermute(value, axis, pairs)


def bits(size):
    return [1 << bit for bit in range(size.bit_length() - 1)]


ROUNDS = ((2, 3, 1, 0), (3, 2, 0, 1), (1, 0, 3, 2))


def gathered(block):
    size = lax.axis_size("sharers")
    if size == len(ROUNDS) + 1:
        blocks, sources = [block], [tuple(range(size))]
        for targets in ROUNDS:
            blocks.append(lax.ppermute(block, "sharers", list(enumerate(targets))))
            sources.append(tuple(targets.index(i) for i in range(size)))
        return blocks, sources
    for step in bits(size):
        block = jnp.concatenate([block, swapped(block, "sharers", step)], axis=0)
    sources = [tuple(i ^ step for i in range(size)) for step in range(size)]
    return [block[i : i + 1] for i in range(size)], sources


def local(velocities, weights, counts):
    filled = counts.reshape(1, 1)
    blocks, sources = gathered(jnp.concatenate([velocities, weights[:, None]], axis=1))
    if len(blocks) == len(ROUNDS) + 1:
        scores, drift, start, speeds = sweep(filled, blocks, sources)
        for step in bits(lax.axis_size("cells")):
            speeds = jnp.maximum(speeds, swapped(speeds, "cells", 2 * step - 1))
        largest = speeds
    else:
        axes = ("cells", "sharers")
        scores, drift, start, speeds = long_sweep(filled, blocks, sources, lax.axis_size(axes))
        largest = jnp.max(lax.all_to_all(speeds[:, None], axes, 0, 0, tiled=True), axis=0)
    time_step = 0.5 / (largest + 1e-06)
    moved = start + time_step[None] * drift
    return moved.reshape(velocities.shape), scores[None, 0:3]


def solution(mesh):
    in_specs = (
        P(("groups", "cells"), None, "sharers"),
        P(("groups", "cells"), "sharers"),
        P(("groups", "cells")),
    )
    out_specs = (P(("groups", "cells"), None, "sharers"), P(("groups", "cells"), None, "sharers"))
    return jax.shard_map(local, mesh=mesh, in_specs=in_specs, out_specs=out_specs, check_vma=False)
```

```python
import functools
import functools
import math

import jax
import jax.numpy as jnp
from jax import lax
from jax.experimental import pallas as pl
from jax.experimental.pallas import tpu as pltpu
from jax.sharding import PartitionSpec as P

EPS = 0.35
SCALE = math.sqrt(math.log2(math.e) / (2.0 * EPS * EPS))
GRID = 4.0
TINY = 1e-30
GROUP = 32
DISTANCE_ROWS = 96
DRIFT_ROWS = 64
bf16, f32 = jnp.bfloat16, jnp.float32


def round_bf16(value):
    return value.astype(bf16).astype(f32)


def pieces(value, count):
    parts = []
    for _ in range(count):
        part = round_bf16(value)
        parts.append(part)
        value = value - part
    return parts


def row_of(value):
    return lax.broadcasted_iota(jnp.int32, value.shape, 0)


def rows_sum(value):
    return jnp.sum(value, axis=0, keepdims=True)


def stacked(groups):
    if len(groups) % 2:
        groups = groups + [jnp.zeros_like(groups[0])]
    return jnp.concatenate(groups, axis=0).astype(bf16)


def scalar_groups(value, like):
    row = row_of(like)
    first, second, third = pieces(value, 3)
    low = jnp.where(row == 0, first, jnp.where(row == 1, second, jnp.where(row == 2, third, 0.0)))
    high = jnp.where(row == 3, first, jnp.where(row == 4, second, jnp.where(row == 5, third, 0.0)))
    ones_low, ones_high = row < 3, (row >= 3) & (row < 6)
    return jnp.where(ones_high, 1.0, low), jnp.where(ones_low, 1.0, high)


def grid_parts(place):
    coarse = jnp.floor(place * GRID + 0.5) * (1.0 / GRID)
    return [coarse] + pieces(place - coarse, 2)


def distance_features(parts):
    coarse, fine, rest = parts
    minor = fine + rest
    query_norm, key_norm = scalar_groups(-rows_sum(coarse * coarse), coarse)
    query_less, key_less = scalar_groups(-rows_sum(minor * (2.0 * coarse + minor)), coarse)
    key = [coarse, key_norm, coarse, coarse, fine, rest, key_less, fine, fine, rest, rest]
    coarse, fine, rest = coarse * 2.0, fine * 2.0, rest * 2.0
    query = [coarse, query_norm, fine, rest, coarse, coarse, query_less, fine, rest, fine, rest]
    return stacked(key), stacked(query)


def weighted_rows(weight, value):
    row = row_of(value)
    whole = jnp.where(row < 3, value, jnp.where(row == 3, 1.0, 0.0)) * weight
    first, second, third = pieces(whole, 3)
    return stacked([first, second + pltpu.roll(third, 4, 0)])


def product(left, right):
    return jnp.dot(left, right, preferred_element_type=f32)


def store_split(ref, rows, matrix):
    half = ref.shape[0] // 2
    upper = matrix.astype(bf16)
    ref[rows, :] = upper
    ref[pl.ds(half + rows.start, rows.size), :] = (matrix - upper.astype(f32)).astype(bf16)


def sum_rows(left, ref):
    return product(jnp.concatenate([left, left], axis=1), ref[...])


def sum_columns(left, ref):
    both = lax.dot_general(left, ref[...], (((1,), (1,)), ((), ())), preferred_element_type=f32)
    half = ref.shape[0] // 2
    return both[:, :half] + both[:, half:]


def sum_rows_less(left, ref):
    half = ref.shape[0] // 2
    both = product(left, ref[:half, :])
    few = left.shape[0] // 2
    return both[:few] + product(left[:few], ref[half:, :]), both[few:]


def sum_columns_less(left, ref):
    half, few = ref.shape[0] // 2, left.shape[0] // 2
    turned = (((1,), (1,)), ((), ()))
    both = lax.dot_general(left, ref[:half, :], turned, preferred_element_type=f32)
    less = lax.dot_general(left[:few], ref[half:, :], turned, preferred_element_type=f32)
    return both[:few] + less, both[few:]


def joined(total):
    upper, lower = total[0:8], total[8:16]
    return upper + lower + pltpu.roll(lower, 4, 0)


def drift_rows(weight, place, score):
    row = row_of(place)
    base = place + jnp.where(row == 3, 1.0, 0.0) + pltpu.roll(score, 4, 0)
    cubic = rows_sum(place * place) * score - rows_sum(place * score) * place
    groups = [weight * base]
    for i in range(3):
        here = slice(i, i + 1)
        groups.append(weight * jnp.where(row == 3, cubic[here], place[here] * base))
    return stacked(sum(map(list, zip(*[pieces(group, 2) for group in groups])), []))


def drift_sum(total, place, score):
    row = row_of(place)
    first, *rest = [total[8 * i : 8 * i + 8] for i in range(4)]
    turned = [pltpu.roll(group, 4, 0) for group in rest]
    count, scores = first[3:4], pltpu.roll(first, 4, 0)
    square, both = rows_sum(place * place), rows_sum(place * score)
    trace = rest[0][0:1] + rest[1][1:2] + rest[2][2:3]
    cross = turned[0][0:1] + turned[1][1:2] + turned[2][2:3]
    drift = score * (square * count - 2.0 * rows_sum(place * first) + trace) - square * scores
    drift += both * first + place * (
        rows_sum(place * scores) + rows_sum(score * first) - both * count - cross
    )
    ends = []
    for i in range(3):
        here = slice(i, i + 1)
        drift += 2.0 * place[here] * turned[i] - score[here] * rest[i]
        ends.append(rows_sum(place * turned[i]) + rest[i][3:4])
    return drift - jnp.where(row == 0, ends[0], jnp.where(row == 1, ends[1], ends[2]))


def widened(block):
    return jnp.concatenate([block[0], jnp.zeros_like(block[0])], axis=0)


def prepared(whole, live):
    weight = jnp.where(live, whole[3:4], 0.0)
    parts = grid_parts(jnp.where(row_of(whole) < 3, whole * SCALE, 0.0))
    place = parts[0] + parts[1] + parts[2]
    key, query = distance_features(parts)
    return weight, place, key.T, query, weighted_rows(weight, place)


def split_blobs(exponent, split):
    for group in range(0, exponent.shape[0], GROUP):
        rows = pl.ds(group, GROUP)
        store_split(split, rows, jnp.exp2(exponent[rows, :]))


def split_distances(exponent, split):
    for group in range(0, exponent.shape[0], GROUP):
        rows = pl.ds(group, GROUP)
        negative = jnp.minimum(exponent[rows, :], -TINY)
        store_split(split, rows, negative * lax.rsqrt(-negative))


def diagonal_tiles(start, width):
    half = width // 2
    return [(start, half, start, half, 0), (start + half, half, start, width, half)]


def add_blobs(tile, split, moments, sums_ref):
    key, keys, query, queries, turned = tile
    sums_ref[:, pl.ds(query, queries)] += sum_rows(moments(key, keys), split)
    if turned:
        sums_ref[:, pl.ds(key, keys)] += sum_columns(moments(query, turned), split.at[:, 0:turned])


def add_distances(tile, split, fluxes, totals_ref):
    key, keys, query, queries, turned = tile

    def rows():
        upper, lower = sum_rows_less(fluxes(key, keys), split)
        totals_ref[:, pl.ds(query, queries)] += upper + lower

    def columns():
        upper, lower = sum_columns_less(fluxes(query, turned), split.at[:, 0:turned])
        totals_ref[:, pl.ds(key, keys)] += upper + lower

    return rows, columns if turned else lambda: None


def stage(tiles, exponent, moments, sums_ref, exponent_refs, split_refs, distance_refs,
          after=lambda index: None):
    def buffer(index):
        _, keys, _, queries, _ = tiles[index]
        return exponent_refs[index % len(exponent_refs)].at[0:keys, 0:queries]

    buffer(0)[...] = exponent(tiles[0])
    for index, tile in enumerate(tiles):
        if index + 1 < len(tiles):
            buffer(index + 1)[...] = exponent(tiles[index + 1])
        split = split_refs[index % 2].at[0 : 2 * tile[1], 0 : tile[3]]
        split_blobs(buffer(index), split)
        add_blobs(tile, split, moments, sums_ref)
        if distance_refs is not None:
            split_distances(buffer(index), distance_refs[index])
        after(index)


def looked_up(refs, width, axis):
    def read(start, size):
        at = pl.ds(start % width, size)
        ref = refs[start // width]
        return ref[at, :] if axis == 0 else ref[:, at]

    return read


def exponent_of(keys, queries):
    return lambda tile: product(keys(tile[0], tile[1]), queries(tile[2], tile[3]))


def lanes_of(source, width):
    return lax.broadcasted_iota(jnp.int32, (1, width), 1) + source * width


def owner_of(sources):
    here = lax.axis_index("sharers")
    return sum(jnp.where(here == i, source, 0) for i, source in enumerate(sources))


def own_kernel(filled, block, key_out, query_out, moment_out, sums_out, first_out, second_out,
               *scratch):
    width = block.shape[2]
    live = lanes_of(lax.axis_index("sharers"), width) < filled[...]
    _, _, key, query, moment = prepared(widened(block), live)
    key_out[...] = key
    query_out[...] = query
    moment_out[...] = moment
    sums_out[...] = jnp.zeros_like(sums_out)
    exponent = exponent_of(looked_up([key_out], width, 0), looked_up([query_out], width, 1))
    moments = looked_up([moment_out], width, 1)
    tiles = diagonal_tiles(0, width)
    stage(tiles, exponent, moments, sums_out, scratch[:2], scratch[2:], (first_out, second_out))


def next_kernel(sources, filled, block, own_key, own_query, own_moment, own_sums, key_out,
                query_out, moment_out, sums_out, *refs):
    width = block.shape[2]
    live = lanes_of(owner_of(sources), width) < filled[...]
    _, _, key, query, moment = prepared(widened(block), live)
    key_out[...] = key
    query_out[...] = query
    moment_out[...] = moment
    sums_out[:, 0:width] = own_sums[...]
    sums_out[:, width:] = jnp.zeros_like(own_sums)
    exponent = exponent_of(
        looked_up([own_key, key_out], width, 0), looked_up([own_query, query_out], width, 1)
    )
    moments = looked_up([own_moment, moment_out], width, 1)
    tiles = square_tiles(width, 0, width) + diagonal_tiles(width, width)
    distances, scratch = refs[: len(tiles)], refs[len(tiles) :]
    stage(tiles, exponent, moments, sums_out, scratch[:2], scratch[2:], distances)


def feature_shapes(width):
    return [
        jax.ShapeDtypeStruct((width, DISTANCE_ROWS), bf16),
        jax.ShapeDtypeStruct((DISTANCE_ROWS, width), bf16),
        jax.ShapeDtypeStruct((16, width), bf16),
    ]


def diagonal_shapes(width):
    half = width // 2
    return [
        jax.ShapeDtypeStruct((2 * half, half), bf16),
        jax.ShapeDtypeStruct((2 * half, width), bf16),
    ]


def stage_scratch(width):
    half = width // 2
    return [pltpu.VMEM((half, width), f32)] * 2 + [pltpu.VMEM((width, width), bf16)] * 2


def own_part(filled, block):
    width = block.shape[2]
    vector = pl.BlockSpec(memory_space=pltpu.VMEM)
    shapes = feature_shapes(width) + [jax.ShapeDtypeStruct((16, width), f32)] + diagonal_shapes(width)
    return pl.pallas_call(
        own_kernel,
        out_shape=shapes,
        in_specs=[vector] * 2,
        out_specs=[vector] * len(shapes),
        scratch_shapes=stage_scratch(width),
        compiler_params=pltpu.CompilerParams(vmem_limit_bytes=16 << 20),
        name="own",
    )(filled, block)


def next_part(filled, block, features, sums, sources):
    width = block.shape[2]
    vector = pl.BlockSpec(memory_space=pltpu.VMEM)
    shapes = feature_shapes(width) + [jax.ShapeDtypeStruct((16, 2 * width), f32)]
    shapes += [jax.ShapeDtypeStruct((width, width), bf16)] * 2 + diagonal_shapes(width)
    return pl.pallas_call(
        functools.partial(next_kernel, sources),
        out_shape=shapes,
        in_specs=[vector] * 6,
        out_specs=[vector] * len(shapes),
        scratch_shapes=stage_scratch(width),
        compiler_params=pltpu.CompilerParams(vmem_limit_bytes=20 << 20),
        name="next",
    )(filled, block, *features, sums)


def square_tiles(key, query, width):
    half = width // 2
    return [(key + part, half, query, width, width) for part in (0, half)]


def late_tiles(count, width):
    tiles, late = [], range(2, count)
    for query in late:
        for key in range(2):
            tiles += square_tiles(key * width, query * width, width)
    for query in late:
        for key in range(2, query):
            tiles += square_tiles(key * width, query * width, width)
    for query in late:
        tiles += diagonal_tiles(query * width, width)
    return tiles


def scored(weight, place, sums):
    vector, live = row_of(place) < 3, weight > 0.0
    density_sum = jnp.where(live, sums[3:4], 1.0)
    pull = place * density_sum - sums
    return jnp.where(vector & live, pull / (-SCALE * EPS * EPS * density_sum), 0.0)


def whole_cell(blocks, live):
    weight = jnp.concatenate(
        [jnp.where(on, block[0, 3:4], 0.0) for on, block in zip(live, blocks)], axis=1
    )
    whole = jnp.concatenate([widened(block) for block in blocks], axis=1)
    vector = row_of(whole) < 3
    parts = grid_parts(jnp.where(vector, whole * SCALE, 0.0))
    place = parts[0] + parts[1] + parts[2]
    middle = jnp.sum(place * weight, axis=1, keepdims=True)
    middle = middle / jnp.sum(weight, axis=1, keepdims=True)
    return weight, place, jnp.where(vector, place - middle, 0.0)


def drift_of(total, centred, score, weight, total_slots):
    drift = drift_sum(total, centred, score)
    live = (row_of(drift) < 3) & (weight > 0.0)
    return jnp.where(live, drift * (1.0 / (SCALE * SCALE * SCALE * total_slots)), 0.0)


def finish(blocks, score, drifts, outs):
    scores_out, drift_out, start_out, speed_out = outs
    width = blocks[0].shape[2]
    square = functools.reduce(jnp.maximum, [rows_sum(drift * drift) for drift in drifts])
    largest = jnp.max(square, axis=1, keepdims=True)
    speed_out[...] = jnp.broadcast_to(jnp.sqrt(largest), speed_out.shape)
    scores_out[...] = score
    for part in range(width // 128):
        lanes = slice(part * 128, part * 128 + 128)
        for axis in range(3):
            drift_out[axis, part : part + 1, :] = drifts[0][axis : axis + 1, lanes]
            start_out[axis, part : part + 1, :] = blocks[0][0, axis : axis + 1, lanes]


def sweep_kernel(sources, *refs):
    count = len(sources)
    filled, blocks, refs = refs[0], refs[1 : count + 1], list(refs[count + 1 :])
    own, following, refs = refs[:5], refs[5:13], refs[13:]
    outs, (key_ref, query_ref, moment_ref, sums_ref, totals_ref), refs = (
        refs[:4], refs[4:9], refs[9:]
    )
    flux_refs, refs = refs[:count], refs[count:]
    width = blocks[0].shape[2]
    half = 2 * width
    split_refs, refs = refs[:2], refs[2:]
    exponent_refs, distance_refs = refs[: len(refs) // 2], refs[len(refs) // 2 :]

    live = [lanes_of(owner_of(source), width) < filled[...] for source in sources]
    late = range(2, count)
    for index in late:
        _, _, key, query, moment = prepared(widened(blocks[index]), live[index])
        lanes = pl.ds((index - 2) * width, width)
        key_ref[lanes, :] = key
        query_ref[:, lanes] = query
        moment_ref[:, lanes] = moment
    weight, place, centred = whole_cell(blocks, live)
    lanes = [pl.ds((index - 2) * width, width) for index in late]
    keys = [own[0], following[0]] + [key_ref.at[lane, :] for lane in lanes]
    queries = [own[1], following[1]] + [query_ref.at[:, lane] for lane in lanes]
    moments = [own[2], following[2]] + [moment_ref.at[:, lane] for lane in lanes]
    exponent = exponent_of(looked_up(keys, width, 0), looked_up(queries, width, 1))

    sums_ref[:, 0:half] = following[3][...]
    sums_ref[:, half:] = jnp.zeros_like(sums_ref[:, half:])
    tiles = late_tiles(count, width)
    totals_ref[...] = jnp.zeros_like(totals_ref)
    lanes = [slice(index * width, index * width + width) for index in range(count)]
    scores = [None] * count
    fluxes = looked_up(flux_refs, width, 1)

    def score_blocks(*indices):
        for index in indices:
            at = lanes[index]
            scores[index] = scored(weight[:, at], place[:, at], joined(sums_ref[:, at]))
            flux_refs[index][...] = drift_rows(weight[:, at], centred[:, at], scores[index])

    mixed = sum(tile[0] < half for tile in tiles)

    def after(index):
        if index == mixed - 1:
            score_blocks(0, 1)

    stage(
        tiles, exponent, looked_up(moments, width, 1), sums_ref, exponent_refs, split_refs, None,
        after,
    )
    early = diagonal_tiles(0, width) + square_tiles(width, 0, width)
    early += diagonal_tiles(width, width)
    for tile, distances in zip(early, own[3:5] + following[4:8]):
        for job in add_distances(tile, distances, fluxes, totals_ref):
            job()
    score_blocks(*range(2, count))

    total_slots = count * width
    drifts = [None] * count

    def drift_block(index):
        at = lanes[index]
        drifts[index] = drift_of(
            totals_ref[:, at], centred[:, at], scores[index], weight[:, at], total_slots
        )

    turns = []
    for index in range(mixed):
        split_distances(exponent_refs[index], distance_refs[index])
        rows, columns = add_distances(tiles[index], distance_refs[index], fluxes, totals_ref)
        rows()
        turns.append((tiles[index][0], columns))
    for index in range(2):
        for key, columns in turns:
            if key // width == index:
                columns()
        drift_block(index)
    for index in range(mixed, len(tiles)):
        split_distances(exponent_refs[index], distance_refs[index])
        for job in add_distances(tiles[index], distance_refs[index], fluxes, totals_ref):
            job()
    for index in range(2, count):
        drift_block(index)
    finish(blocks, scores[0], drifts, outs)


def sweep_shapes(width, copies):
    parts = jax.ShapeDtypeStruct((3, width // 128, 128), f32)
    speeds = jax.ShapeDtypeStruct((copies, 128), f32)
    return [jax.ShapeDtypeStruct((8, width), f32), parts, parts, speeds]


def sweep(filled, blocks, sources):
    count, width = len(blocks), blocks[0].shape[2]
    slots, late = count * width, (count - 2) * width
    own = own_part(filled, blocks[0])
    following = next_part(filled, blocks[1], own[:3], own[3], sources[1])
    early = [*own[:3], *own[4:], *following]
    vector = pl.BlockSpec(memory_space=pltpu.VMEM)
    distances = [pltpu.VMEM((2 * tile[1], tile[3]), bf16) for tile in late_tiles(count, width)]
    return pl.pallas_call(
        functools.partial(sweep_kernel, sources),
        out_shape=sweep_shapes(width, 1),
        in_specs=[vector] * (1 + count + len(early)),
        out_specs=[vector] * 4,
        scratch_shapes=[
            pltpu.VMEM((late, DISTANCE_ROWS), bf16),
            pltpu.VMEM((DISTANCE_ROWS, late), bf16),
            pltpu.VMEM((16, late), bf16),
            pltpu.VMEM((16, slots), f32),
            pltpu.VMEM((DRIFT_ROWS // 2, slots), f32),
        ]
        + [pltpu.VMEM((DRIFT_ROWS, width), bf16)] * count
        + [pltpu.VMEM((width, width), bf16)] * 2
        + [pltpu.VMEM((tile[1], tile[3]), f32) for tile in late_tiles(count, width)]
        + distances,
        compiler_params=pltpu.CompilerParams(vmem_limit_bytes=24 << 20),
        name="sweep",
    )(filled, *blocks, *early)


def long_kernel(sources, filled, *refs):
    count = len(sources)
    blocks, outs, refs = refs[:count], refs[count : count + 4], refs[count + 4 :]
    key_ref, query_ref, moment_ref, flux_ref, sums_ref, totals_ref, exponent_ref, split_ref = refs
    width = blocks[0].shape[2]
    live = [lanes_of(owner_of(source), width) < filled[...] for source in sources]
    for index, (block, on) in enumerate(zip(blocks, live)):
        _, _, key, query, moment = prepared(widened(block), on)
        lanes = pl.ds(index * width, width)
        key_ref[lanes, :] = key
        query_ref[:, lanes] = query
        moment_ref[:, lanes] = moment
    weight, place, centred = whole_cell(blocks, live)
    sums_ref[...] = jnp.zeros_like(sums_ref)
    totals_ref[...] = jnp.zeros_like(totals_ref)

    def block_tile(key, query, both):
        start, first = (pl.multiple_of(block * width, width) for block in (key, query))
        return (start, width, first, width, width if both else 0)

    def fill(tile):
        key, keys, query, queries, _ = tile
        exponent_ref[...] = product(key_ref[pl.ds(key, keys), :], query_ref[:, pl.ds(query, queries)])

    def blobs(key, query, both):
        tile = block_tile(key, query, both)
        fill(tile)
        split_blobs(exponent_ref, split_ref)
        add_blobs(tile, split_ref, lambda at, size: moment_ref[:, pl.ds(at, size)], sums_ref)

    @pl.loop(0, count)
    def _(query):
        blobs(query, query, False)

        @pl.loop(query + 1, count)
        def _(key):
            blobs(key, query, True)

    score = scored(weight, place, joined(sums_ref[...]))
    flux_ref[...] = drift_rows(weight, centred, score)

    @pl.loop(0, count)
    def _(key):
        tile = block_tile(key, 0, False)
        fill(tile)
        split_distances(exponent_ref, split_ref)
        for job in add_distances(
            tile, split_ref, lambda at, size: flux_ref[:, pl.ds(at, size)], totals_ref
        ):
            job()

    own = slice(0, width)
    drift = drift_of(
        totals_ref[...], centred[:, own], score[:, own], weight[:, own], count * width
    )
    finish(blocks, score[:, own], [drift], outs)


def long_sweep(filled, blocks, sources, copies):
    count, width = len(blocks), blocks[0].shape[2]
    slots = count * width
    vector = pl.BlockSpec(memory_space=pltpu.VMEM)
    return pl.pallas_call(
        functools.partial(long_kernel, sources),
        out_shape=sweep_shapes(width, copies),
        in_specs=[vector] * (1 + count),
        out_specs=[vector] * 4,
        scratch_shapes=[
            pltpu.VMEM((slots, DISTANCE_ROWS), bf16),
            pltpu.VMEM((DISTANCE_ROWS, slots), bf16),
            pltpu.VMEM((16, slots), bf16),
            pltpu.VMEM((DRIFT_ROWS, slots), bf16),
            pltpu.VMEM((16, slots), f32),
            pltpu.VMEM((DRIFT_ROWS // 2, width), f32),
            pltpu.VMEM((width, width), f32),
            pltpu.VMEM((2 * width, width), bf16),
        ],
        compiler_params=pltpu.CompilerParams(vmem_limit_bytes=(16 << 20) + slots * 2688),
        name="sweep",
    )(filled, *blocks)


def swapped(value, axis, step):
    pairs = [(i, i ^ step) for i in range(lax.axis_size(axis))]
    return lax.ppermute(value, axis, pairs)


def bits(size):
    return [1 << bit for bit in range(size.bit_length() - 1)]


ROUNDS = ((2, 3, 1, 0), (3, 2, 0, 1), (1, 0, 3, 2))


def gathered(block):
    size = lax.axis_size("sharers")
    if size == len(ROUNDS) + 1:
        blocks, sources = [block], [tuple(range(size))]
        for targets in ROUNDS:
            blocks.append(lax.ppermute(block, "sharers", list(enumerate(targets))))
            sources.append(tuple(targets.index(i) for i in range(size)))
        return blocks, sources
    for step in bits(size):
        block = jnp.concatenate([block, swapped(block, "sharers", step)], axis=0)
    sources = [tuple(i ^ step for i in range(size)) for step in range(size)]
    return [block[i : i + 1] for i in range(size)], sources


def local(velocities, weights, counts):
    filled = counts.reshape(1, 1)
    blocks, sources = gathered(jnp.concatenate([velocities, weights[:, None]], axis=1))
    if len(blocks) == len(ROUNDS) + 1:
        scores, drift, start, speeds = sweep(filled, blocks, sources)
        for step in bits(lax.axis_size("cells")):
            speeds = jnp.maximum(speeds, swapped(speeds, "cells", 2 * step - 1))
        largest = speeds
    else:
        axes = ("cells", "sharers")
        scores, drift, start, speeds = long_sweep(filled, blocks, sources, lax.axis_size(axes))
        largest = jnp.max(lax.all_to_all(speeds[:, None], axes, 0, 0, tiled=True), axis=0)
    time_step = 0.5 / (largest + 1e-06)
    moved = start + time_step[None] * drift
    return moved.reshape(velocities.shape), scores[None, 0:3]


def solution(mesh):
    in_specs = (
        P(("groups", "cells"), None, "sharers"),
        P(("groups", "cells"), "sharers"),
        P(("groups", "cells")),
    )
    out_specs = (P(("groups", "cells"), None, "sharers"), P(("groups", "cells"), None, "sharers"))
    return jax.shard_map(local, mesh=mesh, in_specs=in_specs, out_specs=out_specs, check_vma=False)
```

```python
import functools
import functools
import math

import jax
import jax.numpy as jnp
from jax import lax
from jax.experimental import pallas as pl
from jax.experimental.pallas import tpu as pltpu
from jax.sharding import PartitionSpec as P

EPS = 0.35
SCALE = math.sqrt(math.log2(math.e) / (2.0 * EPS * EPS))
GRID = 4.0
TINY = 1e-30
GROUP = 32
DISTANCE_ROWS = 96
DRIFT_ROWS = 64
bf16, f32 = jnp.bfloat16, jnp.float32


def round_bf16(value):
    return value.astype(bf16).astype(f32)


def pieces(value, count):
    parts = []
    for _ in range(count):
        part = round_bf16(value)
        parts.append(part)
        value = value - part
    return parts


def row_of(value):
    return lax.broadcasted_iota(jnp.int32, value.shape, 0)


def rows_sum(value):
    return jnp.sum(value, axis=0, keepdims=True)


def stacked(groups):
    if len(groups) % 2:
        groups = groups + [jnp.zeros_like(groups[0])]
    return jnp.concatenate(groups, axis=0).astype(bf16)


def scalar_groups(value, like):
    row = row_of(like)
    first, second, third = pieces(value, 3)
    low = jnp.where(row == 0, first, jnp.where(row == 1, second, jnp.where(row == 2, third, 0.0)))
    high = jnp.where(row == 3, first, jnp.where(row == 4, second, jnp.where(row == 5, third, 0.0)))
    ones_low, ones_high = row < 3, (row >= 3) & (row < 6)
    return jnp.where(ones_high, 1.0, low), jnp.where(ones_low, 1.0, high)


def grid_parts(place):
    coarse = jnp.floor(place * GRID + 0.5) * (1.0 / GRID)
    return [coarse] + pieces(place - coarse, 2)


def distance_features(parts):
    coarse, fine, rest = parts
    minor = fine + rest
    query_norm, key_norm = scalar_groups(-rows_sum(coarse * coarse), coarse)
    query_less, key_less = scalar_groups(-rows_sum(minor * (2.0 * coarse + minor)), coarse)
    key = [coarse, key_norm, coarse, coarse, fine, rest, key_less, fine, fine, rest, rest]
    coarse, fine, rest = coarse * 2.0, fine * 2.0, rest * 2.0
    query = [coarse, query_norm, fine, rest, coarse, coarse, query_less, fine, rest, fine, rest]
    return stacked(key), stacked(query)


def weighted_rows(weight, value):
    row = row_of(value)
    whole = jnp.where(row < 3, value, jnp.where(row == 3, 1.0, 0.0)) * weight
    first, second, third = pieces(whole, 3)
    return stacked([first, second + pltpu.roll(third, 4, 0)])


def product(left, right):
    return jnp.dot(left, right, preferred_element_type=f32)


def store_split(ref, rows, matrix):
    half = ref.shape[0] // 2
    upper = matrix.astype(bf16)
    ref[rows, :] = upper
    ref[pl.ds(half + rows.start, rows.size), :] = (matrix - upper.astype(f32)).astype(bf16)


def sum_rows(left, ref):
    return product(jnp.concatenate([left, left], axis=1), ref[...])


TURNED = (((1,), (1,)), ((), ()))


def sum_columns(left, ref):
    both = lax.dot_general(ref[...], left, TURNED, preferred_element_type=f32)
    half = ref.shape[0] // 2
    return (both[:half] + both[half:]).T


def sum_rows_less(left, ref):
    half = ref.shape[0] // 2
    both = product(left, ref[:half, :])
    few = left.shape[0] // 2
    return both[:few] + product(left[:few], ref[half:, :]), both[few:]


def sum_columns_less(left, ref):
    half, few = ref.shape[0] // 2, left.shape[0] // 2
    both = lax.dot_general(ref[:half, :], left, TURNED, preferred_element_type=f32).T
    less = lax.dot_general(ref[half:, :], left[:few], TURNED, preferred_element_type=f32).T
    return both[:few] + less, both[few:]


def joined(total):
    upper, lower = total[0:8], total[8:16]
    return upper + lower + pltpu.roll(lower, 4, 0)


def drift_rows(weight, place, score):
    row = row_of(place)
    base = place + jnp.where(row == 3, 1.0, 0.0) + pltpu.roll(score, 4, 0)
    cubic = rows_sum(place * place) * score - rows_sum(place * score) * place
    groups = [weight * base]
    for i in range(3):
        here = slice(i, i + 1)
        groups.append(weight * jnp.where(row == 3, cubic[here], place[here] * base))
    return stacked(sum(map(list, zip(*[pieces(group, 2) for group in groups])), []))


def drift_sum(total, place, score):
    row = row_of(place)
    first, *rest = [total[8 * i : 8 * i + 8] for i in range(4)]
    turned = [pltpu.roll(group, 4, 0) for group in rest]
    count, scores = first[3:4], pltpu.roll(first, 4, 0)
    square, both = rows_sum(place * place), rows_sum(place * score)
    trace = rest[0][0:1] + rest[1][1:2] + rest[2][2:3]
    cross = turned[0][0:1] + turned[1][1:2] + turned[2][2:3]
    drift = score * (square * count - 2.0 * rows_sum(place * first) + trace) - square * scores
    drift += both * first + place * (
        rows_sum(place * scores) + rows_sum(score * first) - both * count - cross
    )
    ends = []
    for i in range(3):
        here = slice(i, i + 1)
        drift += 2.0 * place[here] * turned[i] - score[here] * rest[i]
        ends.append(rows_sum(place * turned[i]) + rest[i][3:4])
    return drift - jnp.where(row == 0, ends[0], jnp.where(row == 1, ends[1], ends[2]))


def widened(block):
    return jnp.concatenate([block[0], jnp.zeros_like(block[0])], axis=0)


def prepared(whole, live):
    weight = jnp.where(live, whole[3:4], 0.0)
    parts = grid_parts(jnp.where(row_of(whole) < 3, whole * SCALE, 0.0))
    place = parts[0] + parts[1] + parts[2]
    key, query = distance_features(parts)
    return weight, place, key.T, query, weighted_rows(weight, place)


def split_blobs(exponent, split):
    for group in range(0, exponent.shape[0], GROUP):
        rows = pl.ds(group, GROUP)
        store_split(split, rows, jnp.exp2(exponent[rows, :]))


def split_distances(exponent, split):
    for group in range(0, exponent.shape[0], GROUP):
        rows = pl.ds(group, GROUP)
        negative = jnp.minimum(exponent[rows, :], -TINY)
        store_split(split, rows, negative * lax.rsqrt(-negative))


def diagonal_tiles(start, width):
    half = width // 2
    return [(start, half, start, half, 0), (start + half, half, start, width, half)]


def add_blobs(tile, split, moments, sums_ref):
    key, keys, query, queries, turned = tile
    sums_ref[:, pl.ds(query, queries)] += sum_rows(moments(key, keys), split)
    if turned:
        sums_ref[:, pl.ds(key, keys)] += sum_columns(moments(query, turned), split.at[:, 0:turned])


def add_distances(tile, split, fluxes, totals_ref):
    key, keys, query, queries, turned = tile

    def rows():
        upper, lower = sum_rows_less(fluxes(key, keys), split)
        totals_ref[:, pl.ds(query, queries)] += upper + lower

    def columns():
        upper, lower = sum_columns_less(fluxes(query, turned), split.at[:, 0:turned])
        totals_ref[:, pl.ds(key, keys)] += upper + lower

    return rows, columns if turned else lambda: None


def stage(tiles, exponent, moments, sums_ref, exponent_refs, split_refs, distance_refs,
          after=lambda index: None):
    def buffer(index):
        _, keys, _, queries, _ = tiles[index]
        return exponent_refs[index % len(exponent_refs)].at[0:keys, 0:queries]

    buffer(0)[...] = exponent(tiles[0])
    for index, tile in enumerate(tiles):
        if index + 1 < len(tiles):
            buffer(index + 1)[...] = exponent(tiles[index + 1])
        split = split_refs[index % 2].at[0 : 2 * tile[1], 0 : tile[3]]
        split_blobs(buffer(index), split)
        add_blobs(tile, split, moments, sums_ref)
        if distance_refs is not None:
            split_distances(buffer(index), distance_refs[index])
        after(index)


def looked_up(refs, width, axis):
    def read(start, size):
        at = pl.ds(start % width, size)
        ref = refs[start // width]
        return ref[at, :] if axis == 0 else ref[:, at]

    return read


def exponent_of(keys, queries):
    return lambda tile: product(keys(tile[0], tile[1]), queries(tile[2], tile[3]))


def lanes_of(source, width):
    return lax.broadcasted_iota(jnp.int32, (1, width), 1) + source * width


def owner_of(sources):
    here = lax.axis_index("sharers")
    return sum(jnp.where(here == i, source, 0) for i, source in enumerate(sources))


def own_kernel(filled, block, key_out, query_out, moment_out, sums_out, first_out, second_out,
               *scratch):
    width = block.shape[2]
    live = lanes_of(lax.axis_index("sharers"), width) < filled[...]
    _, _, key, query, moment = prepared(widened(block), live)
    key_out[...] = key
    query_out[...] = query
    moment_out[...] = moment
    sums_out[...] = jnp.zeros_like(sums_out)
    exponent = exponent_of(looked_up([key_out], width, 0), looked_up([query_out], width, 1))
    moments = looked_up([moment_out], width, 1)
    tiles = diagonal_tiles(0, width)
    stage(tiles, exponent, moments, sums_out, scratch[:2], scratch[2:], (first_out, second_out))


def next_kernel(sources, filled, block, own_key, own_query, own_moment, own_sums, key_out,
                query_out, moment_out, sums_out, *refs):
    width = block.shape[2]
    live = lanes_of(owner_of(sources), width) < filled[...]
    _, _, key, query, moment = prepared(widened(block), live)
    key_out[...] = key
    query_out[...] = query
    moment_out[...] = moment
    sums_out[:, 0:width] = own_sums[...]
    sums_out[:, width:] = jnp.zeros_like(own_sums)
    exponent = exponent_of(
        looked_up([own_key, key_out], width, 0), looked_up([own_query, query_out], width, 1)
    )
    moments = looked_up([own_moment, moment_out], width, 1)
    tiles = square_tiles(width, 0, width) + diagonal_tiles(width, width)
    distances, scratch = refs[: len(tiles)], refs[len(tiles) :]
    stage(tiles, exponent, moments, sums_out, scratch[:2], scratch[2:], distances)


def feature_shapes(width):
    return [
        jax.ShapeDtypeStruct((width, DISTANCE_ROWS), bf16),
        jax.ShapeDtypeStruct((DISTANCE_ROWS, width), bf16),
        jax.ShapeDtypeStruct((16, width), bf16),
    ]


def diagonal_shapes(width):
    half = width // 2
    return [
        jax.ShapeDtypeStruct((2 * half, half), bf16),
        jax.ShapeDtypeStruct((2 * half, width), bf16),
    ]


def stage_scratch(width):
    half = width // 2
    return [pltpu.VMEM((half, width), f32)] * 2 + [pltpu.VMEM((width, width), bf16)] * 2


def own_part(filled, block):
    width = block.shape[2]
    vector = pl.BlockSpec(memory_space=pltpu.VMEM)
    shapes = feature_shapes(width) + [jax.ShapeDtypeStruct((16, width), f32)] + diagonal_shapes(width)
    return pl.pallas_call(
        own_kernel,
        out_shape=shapes,
        in_specs=[vector] * 2,
        out_specs=[vector] * len(shapes),
        scratch_shapes=stage_scratch(width),
        compiler_params=pltpu.CompilerParams(vmem_limit_bytes=16 << 20),
        name="own",
    )(filled, block)


def next_part(filled, block, features, sums, sources):
    width = block.shape[2]
    vector = pl.BlockSpec(memory_space=pltpu.VMEM)
    shapes = feature_shapes(width) + [jax.ShapeDtypeStruct((16, 2 * width), f32)]
    shapes += [jax.ShapeDtypeStruct((width, width), bf16)] * 2 + diagonal_shapes(width)
    return pl.pallas_call(
        functools.partial(next_kernel, sources),
        out_shape=shapes,
        in_specs=[vector] * 6,
        out_specs=[vector] * len(shapes),
        scratch_shapes=stage_scratch(width),
        compiler_params=pltpu.CompilerParams(vmem_limit_bytes=20 << 20),
        name="next",
    )(filled, block, *features, sums)


def square_tiles(key, query, width):
    half = width // 2
    return [(key + part, half, query, width, width) for part in (0, half)]


def late_tiles(count, width):
    tiles, late = [], range(2, count)
    for query in late:
        for key in range(2):
            tiles += square_tiles(key * width, query * width, width)
    for query in late:
        for key in range(2, query):
            tiles += square_tiles(key * width, query * width, width)
    for query in late:
        tiles += diagonal_tiles(query * width, width)
    return tiles


def scored(weight, place, sums):
    vector, live = row_of(place) < 3, weight > 0.0
    density_sum = jnp.where(live, sums[3:4], 1.0)
    pull = place * density_sum - sums
    return jnp.where(vector & live, pull / (-SCALE * EPS * EPS * density_sum), 0.0)


def whole_cell(blocks, live):
    weight = jnp.concatenate(
        [jnp.where(on, block[0, 3:4], 0.0) for on, block in zip(live, blocks)], axis=1
    )
    whole = jnp.concatenate([widened(block) for block in blocks], axis=1)
    vector = row_of(whole) < 3
    parts = grid_parts(jnp.where(vector, whole * SCALE, 0.0))
    place = parts[0] + parts[1] + parts[2]
    middle = jnp.sum(place * weight, axis=1, keepdims=True)
    middle = middle / jnp.sum(weight, axis=1, keepdims=True)
    return weight, place, jnp.where(vector, place - middle, 0.0)


def drift_of(total, centred, score, weight, total_slots):
    drift = drift_sum(total, centred, score)
    live = (row_of(drift) < 3) & (weight > 0.0)
    return jnp.where(live, drift * (1.0 / (SCALE * SCALE * SCALE * total_slots)), 0.0)


def finish(blocks, score, drifts, outs):
    scores_out, drift_out, start_out, speed_out = outs
    width = blocks[0].shape[2]
    square = functools.reduce(jnp.maximum, [rows_sum(drift * drift) for drift in drifts])
    largest = jnp.max(square, axis=1, keepdims=True)
    speed_out[...] = jnp.broadcast_to(jnp.sqrt(largest), speed_out.shape)
    scores_out[...] = score
    for part in range(width // 128):
        lanes = slice(part * 128, part * 128 + 128)
        for axis in range(3):
            drift_out[axis, part : part + 1, :] = drifts[0][axis : axis + 1, lanes]
            start_out[axis, part : part + 1, :] = blocks[0][0, axis : axis + 1, lanes]


def sweep_kernel(sources, *refs):
    count = len(sources)
    filled, blocks, refs = refs[0], refs[1 : count + 1], list(refs[count + 1 :])
    own, following, refs = refs[:5], refs[5:13], refs[13:]
    outs, (key_ref, query_ref, moment_ref, sums_ref, totals_ref), refs = (
        refs[:4], refs[4:9], refs[9:]
    )
    flux_refs, refs = refs[:count], refs[count:]
    width = blocks[0].shape[2]
    half = 2 * width
    split_refs, refs = refs[:2], refs[2:]
    exponent_refs, distance_refs = refs[: len(refs) // 2], refs[len(refs) // 2 :]

    live = [lanes_of(owner_of(source), width) < filled[...] for source in sources]
    late = range(2, count)
    for index in late:
        _, _, key, query, moment = prepared(widened(blocks[index]), live[index])
        lanes = pl.ds((index - 2) * width, width)
        key_ref[lanes, :] = key
        query_ref[:, lanes] = query
        moment_ref[:, lanes] = moment
    weight, place, centred = whole_cell(blocks, live)
    lanes = [pl.ds((index - 2) * width, width) for index in late]
    keys = [own[0], following[0]] + [key_ref.at[lane, :] for lane in lanes]
    queries = [own[1], following[1]] + [query_ref.at[:, lane] for lane in lanes]
    moments = [own[2], following[2]] + [moment_ref.at[:, lane] for lane in lanes]
    exponent = exponent_of(looked_up(keys, width, 0), looked_up(queries, width, 1))

    sums_ref[:, 0:half] = following[3][...]
    sums_ref[:, half:] = jnp.zeros_like(sums_ref[:, half:])
    tiles = late_tiles(count, width)
    totals_ref[...] = jnp.zeros_like(totals_ref)
    lanes = [slice(index * width, index * width + width) for index in range(count)]
    scores = [None] * count
    fluxes = looked_up(flux_refs, width, 1)

    def score_blocks(*indices):
        for index in indices:
            at = lanes[index]
            scores[index] = scored(weight[:, at], place[:, at], joined(sums_ref[:, at]))
            flux_refs[index][...] = drift_rows(weight[:, at], centred[:, at], scores[index])

    mixed = sum(tile[0] < half for tile in tiles)

    def after(index):
        if index == mixed - 1:
            score_blocks(0, 1)

    stage(
        tiles, exponent, looked_up(moments, width, 1), sums_ref, exponent_refs, split_refs, None,
        after,
    )
    early = diagonal_tiles(0, width) + square_tiles(width, 0, width)
    early += diagonal_tiles(width, width)
    for tile, distances in zip(early, own[3:5] + following[4:8]):
        for job in add_distances(tile, distances, fluxes, totals_ref):
            job()
    score_blocks(*range(2, count))

    total_slots = count * width
    drifts = [None] * count

    def drift_block(index):
        at = lanes[index]
        drifts[index] = drift_of(
            totals_ref[:, at], centred[:, at], scores[index], weight[:, at], total_slots
        )

    turns = []
    for index in range(mixed):
        split_distances(exponent_refs[index], distance_refs[index])
        rows, columns = add_distances(tiles[index], distance_refs[index], fluxes, totals_ref)
        rows()
        turns.append((tiles[index][0], columns))
    for index in range(2):
        for key, columns in turns:
            if key // width == index:
                columns()
        drift_block(index)
    for index in range(mixed, len(tiles)):
        split_distances(exponent_refs[index], distance_refs[index])
        for job in add_distances(tiles[index], distance_refs[index], fluxes, totals_ref):
            job()
    for index in range(2, count):
        drift_block(index)
    finish(blocks, scores[0], drifts, outs)


def sweep_shapes(width, copies):
    parts = jax.ShapeDtypeStruct((3, width // 128, 128), f32)
    speeds = jax.ShapeDtypeStruct((copies, 128), f32)
    return [jax.ShapeDtypeStruct((8, width), f32), parts, parts, speeds]


def sweep(filled, blocks, sources):
    count, width = len(blocks), blocks[0].shape[2]
    slots, late = count * width, (count - 2) * width
    own = own_part(filled, blocks[0])
    following = next_part(filled, blocks[1], own[:3], own[3], sources[1])
    early = [*own[:3], *own[4:], *following]
    vector = pl.BlockSpec(memory_space=pltpu.VMEM)
    distances = [pltpu.VMEM((2 * tile[1], tile[3]), bf16) for tile in late_tiles(count, width)]
    return pl.pallas_call(
        functools.partial(sweep_kernel, sources),
        out_shape=sweep_shapes(width, 1),
        in_specs=[vector] * (1 + count + len(early)),
        out_specs=[vector] * 4,
        scratch_shapes=[
            pltpu.VMEM((late, DISTANCE_ROWS), bf16),
            pltpu.VMEM((DISTANCE_ROWS, late), bf16),
            pltpu.VMEM((16, late), bf16),
            pltpu.VMEM((16, slots), f32),
            pltpu.VMEM((DRIFT_ROWS // 2, slots), f32),
        ]
        + [pltpu.VMEM((DRIFT_ROWS, width), bf16)] * count
        + [pltpu.VMEM((width, width), bf16)] * 2
        + [pltpu.VMEM((tile[1], tile[3]), f32) for tile in late_tiles(count, width)]
        + distances,
        compiler_params=pltpu.CompilerParams(vmem_limit_bytes=24 << 20),
        name="sweep",
    )(filled, *blocks, *early)


def long_kernel(sources, filled, *refs):
    count = len(sources)
    blocks, outs, refs = refs[:count], refs[count : count + 4], refs[count + 4 :]
    key_ref, query_ref, moment_ref, flux_ref, sums_ref, totals_ref, exponent_ref, split_ref = refs
    width = blocks[0].shape[2]
    live = [lanes_of(owner_of(source), width) < filled[...] for source in sources]
    for index, (block, on) in enumerate(zip(blocks, live)):
        _, _, key, query, moment = prepared(widened(block), on)
        lanes = pl.ds(index * width, width)
        key_ref[lanes, :] = key
        query_ref[:, lanes] = query
        moment_ref[:, lanes] = moment
    weight, place, centred = whole_cell(blocks, live)
    sums_ref[...] = jnp.zeros_like(sums_ref)
    totals_ref[...] = jnp.zeros_like(totals_ref)

    def block_tile(key, query, both):
        start, first = (pl.multiple_of(block * width, width) for block in (key, query))
        return (start, width, first, width, width if both else 0)

    def fill(tile):
        key, keys, query, queries, _ = tile
        exponent_ref[...] = product(key_ref[pl.ds(key, keys), :], query_ref[:, pl.ds(query, queries)])

    def blobs(key, query, both):
        tile = block_tile(key, query, both)
        fill(tile)
        split_blobs(exponent_ref, split_ref)
        add_blobs(tile, split_ref, lambda at, size: moment_ref[:, pl.ds(at, size)], sums_ref)

    @pl.loop(0, count)
    def _(query):
        blobs(query, query, False)

        @pl.loop(query + 1, count)
        def _(key):
            blobs(key, query, True)

    score = scored(weight, place, joined(sums_ref[...]))
    flux_ref[...] = drift_rows(weight, centred, score)

    @pl.loop(0, count)
    def _(key):
        tile = block_tile(key, 0, False)
        fill(tile)
        split_distances(exponent_ref, split_ref)
        for job in add_distances(
            tile, split_ref, lambda at, size: flux_ref[:, pl.ds(at, size)], totals_ref
        ):
            job()

    own = slice(0, width)
    drift = drift_of(
        totals_ref[...], centred[:, own], score[:, own], weight[:, own], count * width
    )
    finish(blocks, score[:, own], [drift], outs)


def long_sweep(filled, blocks, sources, copies):
    count, width = len(blocks), blocks[0].shape[2]
    slots = count * width
    vector = pl.BlockSpec(memory_space=pltpu.VMEM)
    return pl.pallas_call(
        functools.partial(long_kernel, sources),
        out_shape=sweep_shapes(width, copies),
        in_specs=[vector] * (1 + count),
        out_specs=[vector] * 4,
        scratch_shapes=[
            pltpu.VMEM((slots, DISTANCE_ROWS), bf16),
            pltpu.VMEM((DISTANCE_ROWS, slots), bf16),
            pltpu.VMEM((16, slots), bf16),
            pltpu.VMEM((DRIFT_ROWS, slots), bf16),
            pltpu.VMEM((16, slots), f32),
            pltpu.VMEM((DRIFT_ROWS // 2, width), f32),
            pltpu.VMEM((width, width), f32),
            pltpu.VMEM((2 * width, width), bf16),
        ],
        compiler_params=pltpu.CompilerParams(vmem_limit_bytes=(16 << 20) + slots * 2688),
        name="sweep",
    )(filled, *blocks)


def swapped(value, axis, step):
    pairs = [(i, i ^ step) for i in range(lax.axis_size(axis))]
    return lax.ppermute(value, axis, pairs)


def bits(size):
    return [1 << bit for bit in range(size.bit_length() - 1)]


ROUNDS = ((2, 3, 1, 0), (3, 2, 0, 1), (1, 0, 3, 2))


def gathered(block):
    size = lax.axis_size("sharers")
    if size == len(ROUNDS) + 1:
        blocks, sources = [block], [tuple(range(size))]
        for targets in ROUNDS:
            blocks.append(lax.ppermute(block, "sharers", list(enumerate(targets))))
            sources.append(tuple(targets.index(i) for i in range(size)))
        return blocks, sources
    for step in bits(size):
        block = jnp.concatenate([block, swapped(block, "sharers", step)], axis=0)
    sources = [tuple(i ^ step for i in range(size)) for step in range(size)]
    return [block[i : i + 1] for i in range(size)], sources


def local(velocities, weights, counts):
    filled = counts.reshape(1, 1)
    blocks, sources = gathered(jnp.concatenate([velocities, weights[:, None]], axis=1))
    if len(blocks) == len(ROUNDS) + 1:
        scores, drift, start, speeds = sweep(filled, blocks, sources)
        for step in bits(lax.axis_size("cells")):
            speeds = jnp.maximum(speeds, swapped(speeds, "cells", 2 * step - 1))
        largest = speeds
    else:
        axes = ("cells", "sharers")
        scores, drift, start, speeds = long_sweep(filled, blocks, sources, lax.axis_size(axes))
        largest = jnp.max(lax.all_to_all(speeds[:, None], axes, 0, 0, tiled=True), axis=0)
    time_step = 0.5 / (largest + 1e-06)
    moved = start + time_step[None] * drift
    return moved.reshape(velocities.shape), scores[None, 0:3]


def solution(mesh):
    in_specs = (
        P(("groups", "cells"), None, "sharers"),
        P(("groups", "cells"), "sharers"),
        P(("groups", "cells")),
    )
    out_specs = (P(("groups", "cells"), None, "sharers"), P(("groups", "cells"), None, "sharers"))
    return jax.shard_map(local, mesh=mesh, in_specs=in_specs, out_specs=out_specs, check_vma=False)
```

```python
import functools
import functools
import math

import jax
import jax.numpy as jnp
from jax import lax
from jax.experimental import pallas as pl
from jax.experimental.pallas import tpu as pltpu
from jax.sharding import PartitionSpec as P

EPS = 0.35
SCALE = math.sqrt(math.log2(math.e) / (2.0 * EPS * EPS))
GRID = 4.0
TINY = 1e-30
GROUP = 16
DISTANCE_ROWS = 96
DRIFT_ROWS = 64
bf16, f32 = jnp.bfloat16, jnp.float32


def round_bf16(value):
    return value.astype(bf16).astype(f32)


def pieces(value, count):
    parts = []
    for _ in range(count):
        part = round_bf16(value)
        parts.append(part)
        value = value - part
    return parts


def row_of(value):
    return lax.broadcasted_iota(jnp.int32, value.shape, 0)


def rows_sum(value):
    return jnp.sum(value, axis=0, keepdims=True)


def stacked(groups):
    if len(groups) % 2:
        groups = groups + [jnp.zeros_like(groups[0])]
    return jnp.concatenate(groups, axis=0).astype(bf16)


def scalar_groups(value, like):
    row = row_of(like)
    first, second, third = pieces(value, 3)
    low = jnp.where(row == 0, first, jnp.where(row == 1, second, jnp.where(row == 2, third, 0.0)))
    high = jnp.where(row == 3, first, jnp.where(row == 4, second, jnp.where(row == 5, third, 0.0)))
    ones_low, ones_high = row < 3, (row >= 3) & (row < 6)
    return jnp.where(ones_high, 1.0, low), jnp.where(ones_low, 1.0, high)


def grid_parts(place):
    coarse = jnp.floor(place * GRID + 0.5) * (1.0 / GRID)
    return [coarse] + pieces(place - coarse, 2)


def distance_features(parts):
    coarse, fine, rest = parts
    minor = fine + rest
    query_norm, key_norm = scalar_groups(-rows_sum(coarse * coarse), coarse)
    query_less, key_less = scalar_groups(-rows_sum(minor * (2.0 * coarse + minor)), coarse)
    key = [coarse, key_norm, coarse, coarse, fine, rest, key_less, fine, fine, rest, rest]
    coarse, fine, rest = coarse * 2.0, fine * 2.0, rest * 2.0
    query = [coarse, query_norm, fine, rest, coarse, coarse, query_less, fine, rest, fine, rest]
    return stacked(key), stacked(query)


def weighted_rows(weight, value):
    row = row_of(value)
    whole = jnp.where(row < 3, value, jnp.where(row == 3, 1.0, 0.0)) * weight
    first, second, third = pieces(whole, 3)
    return stacked([first, second + pltpu.roll(third, 4, 0)])


def product(left, right):
    return jnp.dot(left, right, preferred_element_type=f32)


def store_split(ref, rows, matrix):
    half = ref.shape[0] // 2
    upper = matrix.astype(bf16)
    ref[rows, :] = upper
    ref[pl.ds(half + rows.start, rows.size), :] = (matrix - upper.astype(f32)).astype(bf16)


def sum_rows(left, ref):
    return product(jnp.concatenate([left, left], axis=1), ref[...])


def sum_columns(left, ref):
    both = lax.dot_general(left, ref[...], (((1,), (1,)), ((), ())), preferred_element_type=f32)
    half = ref.shape[0] // 2
    return both[:, :half] + both[:, half:]


def sum_rows_less(left, ref):
    half = ref.shape[0] // 2
    both = product(left, ref[:half, :])
    few = left.shape[0] // 2
    return both[:few] + product(left[:few], ref[half:, :]), both[few:]


def sum_columns_less(left, ref):
    half, few = ref.shape[0] // 2, left.shape[0] // 2
    turned = (((1,), (1,)), ((), ()))
    both = lax.dot_general(left, ref[:half, :], turned, preferred_element_type=f32)
    less = lax.dot_general(left[:few], ref[half:, :], turned, preferred_element_type=f32)
    return both[:few] + less, both[few:]


def joined(total):
    upper, lower = total[0:8], total[8:16]
    return upper + lower + pltpu.roll(lower, 4, 0)


def drift_rows(weight, place, score):
    row = row_of(place)
    base = place + jnp.where(row == 3, 1.0, 0.0) + pltpu.roll(score, 4, 0)
    cubic = rows_sum(place * place) * score - rows_sum(place * score) * place
    groups = [weight * base]
    for i in range(3):
        here = slice(i, i + 1)
        groups.append(weight * jnp.where(row == 3, cubic[here], place[here] * base))
    return stacked(sum(map(list, zip(*[pieces(group, 2) for group in groups])), []))


def drift_sum(total, place, score):
    row = row_of(place)
    first, *rest = [total[8 * i : 8 * i + 8] for i in range(4)]
    turned = [pltpu.roll(group, 4, 0) for group in rest]
    count, scores = first[3:4], pltpu.roll(first, 4, 0)
    square, both = rows_sum(place * place), rows_sum(place * score)
    trace = rest[0][0:1] + rest[1][1:2] + rest[2][2:3]
    cross = turned[0][0:1] + turned[1][1:2] + turned[2][2:3]
    drift = score * (square * count - 2.0 * rows_sum(place * first) + trace) - square * scores
    drift += both * first + place * (
        rows_sum(place * scores) + rows_sum(score * first) - both * count - cross
    )
    ends = []
    for i in range(3):
        here = slice(i, i + 1)
        drift += 2.0 * place[here] * turned[i] - score[here] * rest[i]
        ends.append(rows_sum(place * turned[i]) + rest[i][3:4])
    return drift - jnp.where(row == 0, ends[0], jnp.where(row == 1, ends[1], ends[2]))


def widened(block):
    return jnp.concatenate([block[0], jnp.zeros_like(block[0])], axis=0)


def prepared(whole, live):
    weight = jnp.where(live, whole[3:4], 0.0)
    parts = grid_parts(jnp.where(row_of(whole) < 3, whole * SCALE, 0.0))
    place = parts[0] + parts[1] + parts[2]
    key, query = distance_features(parts)
    return weight, place, key.T, query, weighted_rows(weight, place)


def split_blobs(exponent, split):
    for group in range(0, exponent.shape[0], GROUP):
        rows = pl.ds(group, GROUP)
        store_split(split, rows, jnp.exp2(exponent[rows, :]))


def negative_distance(exponent):
    negative = jnp.minimum(exponent, -TINY)
    return negative * lax.rsqrt(-negative)


def split_distances(exponent, split):
    for group in range(0, exponent.shape[0], GROUP):
        rows = pl.ds(group, GROUP)
        store_split(split, rows, negative_distance(exponent[rows, :]))


def diagonal_tiles(start, width):
    half = width // 2
    return [(start, half, start, half, 0), (start + half, half, start, width, half)]


def add_blobs(tile, split, moments, sums_ref):
    key, keys, query, queries, turned = tile
    sums_ref[:, pl.ds(query, queries)] += sum_rows(moments(key, keys), split)
    if turned:
        sums_ref[:, pl.ds(key, keys)] += sum_columns(moments(query, turned), split.at[:, 0:turned])


def add_distances(tile, split, fluxes, totals_ref):
    key, keys, query, queries, turned = tile

    def rows():
        upper, lower = sum_rows_less(fluxes(key, keys), split)
        totals_ref[:, pl.ds(query, queries)] += upper + lower

    def columns():
        upper, lower = sum_columns_less(fluxes(query, turned), split.at[:, 0:turned])
        totals_ref[:, pl.ds(key, keys)] += upper + lower

    return rows, columns if turned else lambda: None


def stage(tiles, exponent, moments, sums_ref, split_refs, distance_refs, after=lambda index: None):
    for index, tile in enumerate(tiles):
        split = split_refs[index % 2].at[0 : 2 * tile[1], 0 : tile[3]]
        values = exponent(tile)
        for group in range(0, tile[1], GROUP):
            rows, part = pl.ds(group, GROUP), values[group : group + GROUP]
            store_split(split, rows, jnp.exp2(part))
            store_split(distance_refs[index], rows, negative_distance(part))
        add_blobs(tile, split, moments, sums_ref)
        after(index)


def looked_up(refs, width, axis):
    def read(start, size):
        at = pl.ds(start % width, size)
        ref = refs[start // width]
        return ref[at, :] if axis == 0 else ref[:, at]

    return read


def exponent_of(keys, queries):
    return lambda tile: product(keys(tile[0], tile[1]), queries(tile[2], tile[3]))


def lanes_of(source, width):
    return lax.broadcasted_iota(jnp.int32, (1, width), 1) + source * width


def owner_of(sources):
    here = lax.axis_index("sharers")
    return sum(jnp.where(here == i, source, 0) for i, source in enumerate(sources))


def own_kernel(filled, block, key_out, query_out, moment_out, sums_out, first_out, second_out,
               *scratch):
    width = block.shape[2]
    live = lanes_of(lax.axis_index("sharers"), width) < filled[...]
    _, _, key, query, moment = prepared(widened(block), live)
    key_out[...] = key
    query_out[...] = query
    moment_out[...] = moment
    sums_out[...] = jnp.zeros_like(sums_out)
    exponent = exponent_of(looked_up([key_out], width, 0), looked_up([query_out], width, 1))
    moments = looked_up([moment_out], width, 1)
    tiles = diagonal_tiles(0, width)
    stage(tiles, exponent, moments, sums_out, scratch, (first_out, second_out))


def next_kernel(sources, filled, block, own_key, own_query, own_moment, own_sums, key_out,
                query_out, moment_out, sums_out, *refs):
    width = block.shape[2]
    live = lanes_of(owner_of(sources), width) < filled[...]
    _, _, key, query, moment = prepared(widened(block), live)
    key_out[...] = key
    query_out[...] = query
    moment_out[...] = moment
    sums_out[:, 0:width] = own_sums[...]
    sums_out[:, width:] = jnp.zeros_like(own_sums)
    exponent = exponent_of(
        looked_up([own_key, key_out], width, 0), looked_up([own_query, query_out], width, 1)
    )
    moments = looked_up([own_moment, moment_out], width, 1)
    tiles = square_tiles(width, 0, width) + diagonal_tiles(width, width)
    distances, scratch = refs[: len(tiles)], refs[len(tiles) :]
    stage(tiles, exponent, moments, sums_out, scratch, distances)


def feature_shapes(width):
    return [
        jax.ShapeDtypeStruct((width, DISTANCE_ROWS), bf16),
        jax.ShapeDtypeStruct((DISTANCE_ROWS, width), bf16),
        jax.ShapeDtypeStruct((16, width), bf16),
    ]


def diagonal_shapes(width):
    half = width // 2
    return [
        jax.ShapeDtypeStruct((2 * half, half), bf16),
        jax.ShapeDtypeStruct((2 * half, width), bf16),
    ]


def stage_scratch(width):
    return [pltpu.VMEM((width, width), bf16)] * 2


def own_part(filled, block):
    width = block.shape[2]
    vector = pl.BlockSpec(memory_space=pltpu.VMEM)
    shapes = feature_shapes(width) + [jax.ShapeDtypeStruct((16, width), f32)] + diagonal_shapes(width)
    return pl.pallas_call(
        own_kernel,
        out_shape=shapes,
        in_specs=[vector] * 2,
        out_specs=[vector] * len(shapes),
        scratch_shapes=stage_scratch(width),
        compiler_params=pltpu.CompilerParams(vmem_limit_bytes=16 << 20),
        name="own",
    )(filled, block)


def next_part(filled, block, features, sums, sources):
    width = block.shape[2]
    vector = pl.BlockSpec(memory_space=pltpu.VMEM)
    shapes = feature_shapes(width) + [jax.ShapeDtypeStruct((16, 2 * width), f32)]
    shapes += [jax.ShapeDtypeStruct((width, width), bf16)] * 2 + diagonal_shapes(width)
    return pl.pallas_call(
        functools.partial(next_kernel, sources),
        out_shape=shapes,
        in_specs=[vector] * 6,
        out_specs=[vector] * len(shapes),
        scratch_shapes=stage_scratch(width),
        compiler_params=pltpu.CompilerParams(vmem_limit_bytes=20 << 20),
        name="next",
    )(filled, block, *features, sums)


def square_tiles(key, query, width):
    half = width // 2
    return [(key + part, half, query, width, width) for part in (0, half)]


def late_tiles(count, width):
    tiles, late = [], range(2, count)
    for query in late:
        for key in range(2):
            tiles += square_tiles(key * width, query * width, width)
    for query in late:
        for key in range(2, query):
            tiles += square_tiles(key * width, query * width, width)
    for query in late:
        tiles += diagonal_tiles(query * width, width)
    return tiles


def scored(weight, place, sums):
    vector, live = row_of(place) < 3, weight > 0.0
    density_sum = jnp.where(live, sums[3:4], 1.0)
    pull = place * density_sum - sums
    return jnp.where(vector & live, pull / (-SCALE * EPS * EPS * density_sum), 0.0)


def whole_cell(blocks, live):
    weight = jnp.concatenate(
        [jnp.where(on, block[0, 3:4], 0.0) for on, block in zip(live, blocks)], axis=1
    )
    whole = jnp.concatenate([widened(block) for block in blocks], axis=1)
    vector = row_of(whole) < 3
    parts = grid_parts(jnp.where(vector, whole * SCALE, 0.0))
    place = parts[0] + parts[1] + parts[2]
    middle = jnp.sum(place * weight, axis=1, keepdims=True)
    middle = middle / jnp.sum(weight, axis=1, keepdims=True)
    return weight, place, jnp.where(vector, place - middle, 0.0)


def drift_of(total, centred, score, weight, total_slots):
    drift = drift_sum(total, centred, score)
    live = (row_of(drift) < 3) & (weight > 0.0)
    return jnp.where(live, drift * (1.0 / (SCALE * SCALE * SCALE * total_slots)), 0.0)


def finish(blocks, score, drifts, outs):
    scores_out, drift_out, start_out, speed_out = outs
    width = blocks[0].shape[2]
    square = functools.reduce(jnp.maximum, [rows_sum(drift * drift) for drift in drifts])
    largest = jnp.max(square, axis=1, keepdims=True)
    speed_out[...] = jnp.broadcast_to(jnp.sqrt(largest), speed_out.shape)
    scores_out[...] = score
    for part in range(width // 128):
        lanes = slice(part * 128, part * 128 + 128)
        for axis in range(3):
            drift_out[axis, part : part + 1, :] = drifts[0][axis : axis + 1, lanes]
            start_out[axis, part : part + 1, :] = blocks[0][0, axis : axis + 1, lanes]


def sweep_kernel(sources, *refs):
    count = len(sources)
    filled, blocks, refs = refs[0], refs[1 : count + 1], list(refs[count + 1 :])
    own, following, refs = refs[:5], refs[5:13], refs[13:]
    outs, (key_ref, query_ref, moment_ref, sums_ref, totals_ref), refs = (
        refs[:4], refs[4:9], refs[9:]
    )
    flux_refs, refs = refs[:count], refs[count:]
    width = blocks[0].shape[2]
    half = 2 * width
    split_refs, distance_refs = refs[:2], refs[2:]

    live = [lanes_of(owner_of(source), width) < filled[...] for source in sources]
    late = range(2, count)
    for index in late:
        _, _, key, query, moment = prepared(widened(blocks[index]), live[index])
        lanes = pl.ds((index - 2) * width, width)
        key_ref[lanes, :] = key
        query_ref[:, lanes] = query
        moment_ref[:, lanes] = moment
    weight, place, centred = whole_cell(blocks, live)
    lanes = [pl.ds((index - 2) * width, width) for index in late]
    keys = [own[0], following[0]] + [key_ref.at[lane, :] for lane in lanes]
    queries = [own[1], following[1]] + [query_ref.at[:, lane] for lane in lanes]
    moments = [own[2], following[2]] + [moment_ref.at[:, lane] for lane in lanes]
    exponent = exponent_of(looked_up(keys, width, 0), looked_up(queries, width, 1))

    sums_ref[:, 0:half] = following[3][...]
    sums_ref[:, half:] = jnp.zeros_like(sums_ref[:, half:])
    tiles = late_tiles(count, width)
    totals_ref[...] = jnp.zeros_like(totals_ref)
    lanes = [slice(index * width, index * width + width) for index in range(count)]
    scores = [None] * count
    fluxes = looked_up(flux_refs, width, 1)

    def score_blocks(*indices):
        for index in indices:
            at = lanes[index]
            scores[index] = scored(weight[:, at], place[:, at], joined(sums_ref[:, at]))
            flux_refs[index][...] = drift_rows(weight[:, at], centred[:, at], scores[index])

    mixed = sum(tile[0] < half for tile in tiles)

    def after(index):
        if index == mixed - 1:
            score_blocks(0, 1)

    moments = looked_up(moments, width, 1)
    stage(tiles, exponent, moments, sums_ref, split_refs, distance_refs, after)
    early = diagonal_tiles(0, width) + square_tiles(width, 0, width)
    early += diagonal_tiles(width, width)
    for tile, distances in zip(early, own[3:5] + following[4:8]):
        for job in add_distances(tile, distances, fluxes, totals_ref):
            job()
    score_blocks(*range(2, count))

    total_slots = count * width
    drifts = [None] * count

    def drift_block(index):
        at = lanes[index]
        drifts[index] = drift_of(
            totals_ref[:, at], centred[:, at], scores[index], weight[:, at], total_slots
        )

    turns = []
    for index in range(mixed):
        rows, columns = add_distances(tiles[index], distance_refs[index], fluxes, totals_ref)
        rows()
        turns.append((tiles[index][0], columns))
    for index in range(2):
        for key, columns in turns:
            if key // width == index:
                columns()
        drift_block(index)
    for index in range(mixed, len(tiles)):
        for job in add_distances(tiles[index], distance_refs[index], fluxes, totals_ref):
            job()
    for index in range(2, count):
        drift_block(index)
    finish(blocks, scores[0], drifts, outs)


def sweep_shapes(width, copies):
    parts = jax.ShapeDtypeStruct((3, width // 128, 128), f32)
    speeds = jax.ShapeDtypeStruct((copies, 128), f32)
    return [jax.ShapeDtypeStruct((8, width), f32), parts, parts, speeds]


def sweep(filled, blocks, sources):
    count, width = len(blocks), blocks[0].shape[2]
    slots, late = count * width, (count - 2) * width
    own = own_part(filled, blocks[0])
    following = next_part(filled, blocks[1], own[:3], own[3], sources[1])
    early = [*own[:3], *own[4:], *following]
    vector = pl.BlockSpec(memory_space=pltpu.VMEM)
    distances = [pltpu.VMEM((2 * tile[1], tile[3]), bf16) for tile in late_tiles(count, width)]
    return pl.pallas_call(
        functools.partial(sweep_kernel, sources),
        out_shape=sweep_shapes(width, 1),
        in_specs=[vector] * (1 + count + len(early)),
        out_specs=[vector] * 4,
        scratch_shapes=[
            pltpu.VMEM((late, DISTANCE_ROWS), bf16),
            pltpu.VMEM((DISTANCE_ROWS, late), bf16),
            pltpu.VMEM((16, late), bf16),
            pltpu.VMEM((16, slots), f32),
            pltpu.VMEM((DRIFT_ROWS // 2, slots), f32),
        ]
        + [pltpu.VMEM((DRIFT_ROWS, width), bf16)] * count
        + [pltpu.VMEM((width, width), bf16)] * 2
        + distances,
        compiler_params=pltpu.CompilerParams(vmem_limit_bytes=24 << 20),
        name="sweep",
    )(filled, *blocks, *early)


def long_kernel(sources, filled, *refs):
    count = len(sources)
    blocks, outs, refs = refs[:count], refs[count : count + 4], refs[count + 4 :]
    key_ref, query_ref, moment_ref, flux_ref, sums_ref, totals_ref, exponent_ref, split_ref = refs
    width = blocks[0].shape[2]
    live = [lanes_of(owner_of(source), width) < filled[...] for source in sources]
    for index, (block, on) in enumerate(zip(blocks, live)):
        _, _, key, query, moment = prepared(widened(block), on)
        lanes = pl.ds(index * width, width)
        key_ref[lanes, :] = key
        query_ref[:, lanes] = query
        moment_ref[:, lanes] = moment
    weight, place, centred = whole_cell(blocks, live)
    sums_ref[...] = jnp.zeros_like(sums_ref)
    totals_ref[...] = jnp.zeros_like(totals_ref)

    def block_tile(key, query, both):
        start, first = (pl.multiple_of(block * width, width) for block in (key, query))
        return (start, width, first, width, width if both else 0)

    def fill(tile):
        key, keys, query, queries, _ = tile
        exponent_ref[...] = product(key_ref[pl.ds(key, keys), :], query_ref[:, pl.ds(query, queries)])

    def blobs(key, query, both):
        tile = block_tile(key, query, both)
        fill(tile)
        split_blobs(exponent_ref, split_ref)
        add_blobs(tile, split_ref, lambda at, size: moment_ref[:, pl.ds(at, size)], sums_ref)

    @pl.loop(0, count)
    def _(query):
        blobs(query, query, False)

        @pl.loop(query + 1, count)
        def _(key):
            blobs(key, query, True)

    score = scored(weight, place, joined(sums_ref[...]))
    flux_ref[...] = drift_rows(weight, centred, score)

    @pl.loop(0, count)
    def _(key):
        tile = block_tile(key, 0, False)
        fill(tile)
        split_distances(exponent_ref, split_ref)
        for job in add_distances(
            tile, split_ref, lambda at, size: flux_ref[:, pl.ds(at, size)], totals_ref
        ):
            job()

    own = slice(0, width)
    drift = drift_of(
        totals_ref[...], centred[:, own], score[:, own], weight[:, own], count * width
    )
    finish(blocks, score[:, own], [drift], outs)


def long_sweep(filled, blocks, sources, copies):
    count, width = len(blocks), blocks[0].shape[2]
    slots = count * width
    vector = pl.BlockSpec(memory_space=pltpu.VMEM)
    return pl.pallas_call(
        functools.partial(long_kernel, sources),
        out_shape=sweep_shapes(width, copies),
        in_specs=[vector] * (1 + count),
        out_specs=[vector] * 4,
        scratch_shapes=[
            pltpu.VMEM((slots, DISTANCE_ROWS), bf16),
            pltpu.VMEM((DISTANCE_ROWS, slots), bf16),
            pltpu.VMEM((16, slots), bf16),
            pltpu.VMEM((DRIFT_ROWS, slots), bf16),
            pltpu.VMEM((16, slots), f32),
            pltpu.VMEM((DRIFT_ROWS // 2, width), f32),
            pltpu.VMEM((width, width), f32),
            pltpu.VMEM((2 * width, width), bf16),
        ],
        compiler_params=pltpu.CompilerParams(vmem_limit_bytes=(16 << 20) + slots * 2688),
        name="sweep",
    )(filled, *blocks)


def swapped(value, axis, step):
    pairs = [(i, i ^ step) for i in range(lax.axis_size(axis))]
    return lax.ppermute(value, axis, pairs)


def bits(size):
    return [1 << bit for bit in range(size.bit_length() - 1)]


ROUNDS = ((2, 3, 1, 0), (3, 2, 0, 1), (1, 0, 3, 2))


def gathered(block):
    size = lax.axis_size("sharers")
    if size == len(ROUNDS) + 1:
        blocks, sources = [block], [tuple(range(size))]
        for targets in ROUNDS:
            blocks.append(lax.ppermute(block, "sharers", list(enumerate(targets))))
            sources.append(tuple(targets.index(i) for i in range(size)))
        return blocks, sources
    for step in bits(size):
        block = jnp.concatenate([block, swapped(block, "sharers", step)], axis=0)
    sources = [tuple(i ^ step for i in range(size)) for step in range(size)]
    return [block[i : i + 1] for i in range(size)], sources


def local(velocities, weights, counts):
    filled = counts.reshape(1, 1)
    blocks, sources = gathered(jnp.concatenate([velocities, weights[:, None]], axis=1))
    if len(blocks) == len(ROUNDS) + 1:
        scores, drift, start, speeds = sweep(filled, blocks, sources)
        for step in bits(lax.axis_size("cells")):
            speeds = jnp.maximum(speeds, swapped(speeds, "cells", 2 * step - 1))
        largest = speeds
    else:
        axes = ("cells", "sharers")
        scores, drift, start, speeds = long_sweep(filled, blocks, sources, lax.axis_size(axes))
        largest = jnp.max(lax.all_to_all(speeds[:, None], axes, 0, 0, tiled=True), axis=0)
    time_step = 0.5 / (largest + 1e-06)
    moved = start + time_step[None] * drift
    return moved.reshape(velocities.shape), scores[None, 0:3]


def solution(mesh):
    in_specs = (
        P(("groups", "cells"), None, "sharers"),
        P(("groups", "cells"), "sharers"),
        P(("groups", "cells")),
    )
    out_specs = (P(("groups", "cells"), None, "sharers"), P(("groups", "cells"), None, "sharers"))
    return jax.shard_map(local, mesh=mesh, in_specs=in_specs, out_specs=out_specs, check_vma=False)
```

```python
import functools
import functools
import math

import jax
import jax.numpy as jnp
from jax import lax
from jax.experimental import pallas as pl
from jax.experimental.pallas import tpu as pltpu
from jax.sharding import PartitionSpec as P

EPS = 0.35
SCALE = math.sqrt(math.log2(math.e) / (2.0 * EPS * EPS))
GRID = 4.0
TINY = 1e-30
GROUP = 32
DISTANCE_ROWS = 96
DRIFT_ROWS = 64
bf16, f32 = jnp.bfloat16, jnp.float32


def round_bf16(value):
    return value.astype(bf16).astype(f32)


def pieces(value, count):
    parts = []
    for _ in range(count):
        part = round_bf16(value)
        parts.append(part)
        value = value - part
    return parts


def row_of(value):
    return lax.broadcasted_iota(jnp.int32, value.shape, 0)


def rows_sum(value):
    return jnp.sum(value, axis=0, keepdims=True)


def stacked(groups):
    if len(groups) % 2:
        groups = groups + [jnp.zeros_like(groups[0])]
    return jnp.concatenate(groups, axis=0).astype(bf16)


def scalar_groups(value, like):
    row = row_of(like)
    first, second, third = pieces(value, 3)
    low = jnp.where(row == 0, first, jnp.where(row == 1, second, jnp.where(row == 2, third, 0.0)))
    high = jnp.where(row == 3, first, jnp.where(row == 4, second, jnp.where(row == 5, third, 0.0)))
    ones_low, ones_high = row < 3, (row >= 3) & (row < 6)
    return jnp.where(ones_high, 1.0, low), jnp.where(ones_low, 1.0, high)


def grid_parts(place):
    coarse = jnp.floor(place * GRID + 0.5) * (1.0 / GRID)
    return [coarse] + pieces(place - coarse, 2)


def distance_features(parts):
    coarse, fine, rest = parts
    minor = fine + rest
    query_norm, key_norm = scalar_groups(-rows_sum(coarse * coarse), coarse)
    query_less, key_less = scalar_groups(-rows_sum(minor * (2.0 * coarse + minor)), coarse)
    key = [coarse, key_norm, coarse, coarse, fine, rest, key_less, fine, fine, rest, rest]
    coarse, fine, rest = coarse * 2.0, fine * 2.0, rest * 2.0
    query = [coarse, query_norm, fine, rest, coarse, coarse, query_less, fine, rest, fine, rest]
    return stacked(key), stacked(query)


def weighted_rows(weight, value):
    row = row_of(value)
    whole = jnp.where(row < 3, value, jnp.where(row == 3, 1.0, 0.0)) * weight
    first, second, third = pieces(whole, 3)
    return stacked([first, second + pltpu.roll(third, 4, 0)])


def product(left, right):
    return jnp.dot(left, right, preferred_element_type=f32)


def store_split(ref, rows, matrix):
    half = ref.shape[0] // 2
    spread = matrix * 65537.0
    upper = spread - (spread - matrix)
    ref[rows, :] = upper.astype(bf16)
    ref[pl.ds(half + rows.start, rows.size), :] = (matrix - upper).astype(bf16)


def sum_rows(left, ref):
    return product(jnp.concatenate([left, left], axis=1), ref[...])


def sum_columns(left, ref):
    both = lax.dot_general(left, ref[...], (((1,), (1,)), ((), ())), preferred_element_type=f32)
    half = ref.shape[0] // 2
    return both[:, :half] + both[:, half:]


def sum_rows_less(left, ref):
    half = ref.shape[0] // 2
    both = product(left, ref[:half, :])
    few = left.shape[0] // 2
    return both[:few] + product(left[:few], ref[half:, :]), both[few:]


def sum_columns_less(left, ref):
    half, few = ref.shape[0] // 2, left.shape[0] // 2
    turned = (((1,), (1,)), ((), ()))
    both = lax.dot_general(left, ref[:half, :], turned, preferred_element_type=f32)
    less = lax.dot_general(left[:few], ref[half:, :], turned, preferred_element_type=f32)
    return both[:few] + less, both[few:]


def joined(total):
    upper, lower = total[0:8], total[8:16]
    return upper + lower + pltpu.roll(lower, 4, 0)


def drift_rows(weight, place, score):
    row = row_of(place)
    base = place + jnp.where(row == 3, 1.0, 0.0) + pltpu.roll(score, 4, 0)
    cubic = rows_sum(place * place) * score - rows_sum(place * score) * place
    groups = [weight * base]
    for i in range(3):
        here = slice(i, i + 1)
        groups.append(weight * jnp.where(row == 3, cubic[here], place[here] * base))
    return stacked(sum(map(list, zip(*[pieces(group, 2) for group in groups])), []))


def drift_sum(total, place, score):
    row = row_of(place)
    first, *rest = [total[8 * i : 8 * i + 8] for i in range(4)]
    turned = [pltpu.roll(group, 4, 0) for group in rest]
    count, scores = first[3:4], pltpu.roll(first, 4, 0)
    square, both = rows_sum(place * place), rows_sum(place * score)
    trace = rest[0][0:1] + rest[1][1:2] + rest[2][2:3]
    cross = turned[0][0:1] + turned[1][1:2] + turned[2][2:3]
    drift = score * (square * count - 2.0 * rows_sum(place * first) + trace) - square * scores
    drift += both * first + place * (
        rows_sum(place * scores) + rows_sum(score * first) - both * count - cross
    )
    ends = []
    for i in range(3):
        here = slice(i, i + 1)
        drift += 2.0 * place[here] * turned[i] - score[here] * rest[i]
        ends.append(rows_sum(place * turned[i]) + rest[i][3:4])
    return drift - jnp.where(row == 0, ends[0], jnp.where(row == 1, ends[1], ends[2]))


def widened(block):
    return jnp.concatenate([block[0], jnp.zeros_like(block[0])], axis=0)


def prepared(whole, live):
    weight = jnp.where(live, whole[3:4], 0.0)
    parts = grid_parts(jnp.where(row_of(whole) < 3, whole * SCALE, 0.0))
    place = parts[0] + parts[1] + parts[2]
    key, query = distance_features(parts)
    return weight, place, key.T, query, weighted_rows(weight, place)


def split_blobs(exponent, split):
    for group in range(0, exponent.shape[0], GROUP):
        rows = pl.ds(group, GROUP)
        store_split(split, rows, jnp.exp2(exponent[rows, :]))


def split_distances(exponent, split):
    for group in range(0, exponent.shape[0], GROUP):
        rows = pl.ds(group, GROUP)
        negative = jnp.minimum(exponent[rows, :], -TINY)
        store_split(split, rows, negative * lax.rsqrt(-negative))


def diagonal_tiles(start, width):
    half = width // 2
    return [(start, half, start, half, 0), (start + half, half, start, width, half)]


def add_blobs(tile, split, moments, sums_ref):
    key, keys, query, queries, turned = tile
    sums_ref[:, pl.ds(query, queries)] += sum_rows(moments(key, keys), split)
    if turned:
        sums_ref[:, pl.ds(key, keys)] += sum_columns(moments(query, turned), split.at[:, 0:turned])


def add_distances(tile, split, fluxes, totals_ref):
    key, keys, query, queries, turned = tile

    def rows():
        upper, lower = sum_rows_less(fluxes(key, keys), split)
        totals_ref[:, pl.ds(query, queries)] += upper + lower

    def columns():
        upper, lower = sum_columns_less(fluxes(query, turned), split.at[:, 0:turned])
        totals_ref[:, pl.ds(key, keys)] += upper + lower

    return rows, columns if turned else lambda: None


def stage(tiles, exponent, moments, sums_ref, exponent_refs, split_refs, distance_refs,
          after=lambda index: None):
    def buffer(index):
        _, keys, _, queries, _ = tiles[index]
        return exponent_refs[index % len(exponent_refs)].at[0:keys, 0:queries]

    buffer(0)[...] = exponent(tiles[0])
    for index, tile in enumerate(tiles):
        if index + 1 < len(tiles):
            buffer(index + 1)[...] = exponent(tiles[index + 1])
        split = split_refs[index % 2].at[0 : 2 * tile[1], 0 : tile[3]]
        split_blobs(buffer(index), split)
        add_blobs(tile, split, moments, sums_ref)
        if distance_refs is not None:
            split_distances(buffer(index), distance_refs[index])
        after(index)


def looked_up(refs, width, axis):
    def read(start, size):
        at = pl.ds(start % width, size)
        ref = refs[start // width]
        return ref[at, :] if axis == 0 else ref[:, at]

    return read


def exponent_of(keys, queries):
    return lambda tile: product(keys(tile[0], tile[1]), queries(tile[2], tile[3]))


def lanes_of(source, width):
    return lax.broadcasted_iota(jnp.int32, (1, width), 1) + source * width


def owner_of(sources):
    here = lax.axis_index("sharers")
    return sum(jnp.where(here == i, source, 0) for i, source in enumerate(sources))


def own_kernel(filled, block, key_out, query_out, moment_out, sums_out, first_out, second_out,
               *scratch):
    width = block.shape[2]
    live = lanes_of(lax.axis_index("sharers"), width) < filled[...]
    _, _, key, query, moment = prepared(widened(block), live)
    key_out[...] = key
    query_out[...] = query
    moment_out[...] = moment
    sums_out[...] = jnp.zeros_like(sums_out)
    exponent = exponent_of(looked_up([key_out], width, 0), looked_up([query_out], width, 1))
    moments = looked_up([moment_out], width, 1)
    tiles = diagonal_tiles(0, width)
    stage(tiles, exponent, moments, sums_out, scratch[:2], scratch[2:], (first_out, second_out))


def next_kernel(sources, filled, block, own_key, own_query, own_moment, own_sums, key_out,
                query_out, moment_out, sums_out, *refs):
    width = block.shape[2]
    live = lanes_of(owner_of(sources), width) < filled[...]
    _, _, key, query, moment = prepared(widened(block), live)
    key_out[...] = key
    query_out[...] = query
    moment_out[...] = moment
    sums_out[:, 0:width] = own_sums[...]
    sums_out[:, width:] = jnp.zeros_like(own_sums)
    exponent = exponent_of(
        looked_up([own_key, key_out], width, 0), looked_up([own_query, query_out], width, 1)
    )
    moments = looked_up([own_moment, moment_out], width, 1)
    tiles = square_tiles(width, 0, width) + diagonal_tiles(width, width)
    distances, scratch = refs[: len(tiles)], refs[len(tiles) :]
    stage(tiles, exponent, moments, sums_out, scratch[:2], scratch[2:], distances)


def feature_shapes(width):
    return [
        jax.ShapeDtypeStruct((width, DISTANCE_ROWS), bf16),
        jax.ShapeDtypeStruct((DISTANCE_ROWS, width), bf16),
        jax.ShapeDtypeStruct((16, width), bf16),
    ]


def diagonal_shapes(width):
    half = width // 2
    return [
        jax.ShapeDtypeStruct((2 * half, half), bf16),
        jax.ShapeDtypeStruct((2 * half, width), bf16),
    ]


def stage_scratch(width):
    half = width // 2
    return [pltpu.VMEM((half, width), f32)] * 2 + [pltpu.VMEM((width, width), bf16)] * 2


def own_part(filled, block):
    width = block.shape[2]
    vector = pl.BlockSpec(memory_space=pltpu.VMEM)
    shapes = feature_shapes(width) + [jax.ShapeDtypeStruct((16, width), f32)] + diagonal_shapes(width)
    return pl.pallas_call(
        own_kernel,
        out_shape=shapes,
        in_specs=[vector] * 2,
        out_specs=[vector] * len(shapes),
        scratch_shapes=stage_scratch(width),
        compiler_params=pltpu.CompilerParams(vmem_limit_bytes=16 << 20),
        name="own",
    )(filled, block)


def next_part(filled, block, features, sums, sources):
    width = block.shape[2]
    vector = pl.BlockSpec(memory_space=pltpu.VMEM)
    shapes = feature_shapes(width) + [jax.ShapeDtypeStruct((16, 2 * width), f32)]
    shapes += [jax.ShapeDtypeStruct((width, width), bf16)] * 2 + diagonal_shapes(width)
    return pl.pallas_call(
        functools.partial(next_kernel, sources),
        out_shape=shapes,
        in_specs=[vector] * 6,
        out_specs=[vector] * len(shapes),
        scratch_shapes=stage_scratch(width),
        compiler_params=pltpu.CompilerParams(vmem_limit_bytes=20 << 20),
        name="next",
    )(filled, block, *features, sums)


def square_tiles(key, query, width):
    half = width // 2
    return [(key + part, half, query, width, width) for part in (0, half)]


def late_tiles(count, width):
    tiles, late = [], range(2, count)
    for query in late:
        for key in range(2):
            tiles += square_tiles(key * width, query * width, width)
    for query in late:
        for key in range(2, query):
            tiles += square_tiles(key * width, query * width, width)
    for query in late:
        tiles += diagonal_tiles(query * width, width)
    return tiles


def scored(weight, place, sums):
    vector, live = row_of(place) < 3, weight > 0.0
    density_sum = jnp.where(live, sums[3:4], 1.0)
    pull = place * density_sum - sums
    return jnp.where(vector & live, pull / (-SCALE * EPS * EPS * density_sum), 0.0)


def whole_cell(blocks, live):
    weight = jnp.concatenate(
        [jnp.where(on, block[0, 3:4], 0.0) for on, block in zip(live, blocks)], axis=1
    )
    whole = jnp.concatenate([widened(block) for block in blocks], axis=1)
    vector = row_of(whole) < 3
    parts = grid_parts(jnp.where(vector, whole * SCALE, 0.0))
    place = parts[0] + parts[1] + parts[2]
    middle = jnp.sum(place * weight, axis=1, keepdims=True)
    middle = middle / jnp.sum(weight, axis=1, keepdims=True)
    return weight, place, jnp.where(vector, place - middle, 0.0)


def drift_of(total, centred, score, weight, total_slots):
    drift = drift_sum(total, centred, score)
    live = (row_of(drift) < 3) & (weight > 0.0)
    return jnp.where(live, drift * (1.0 / (SCALE * SCALE * SCALE * total_slots)), 0.0)


def finish(blocks, score, drifts, outs):
    scores_out, drift_out, start_out, speed_out = outs
    width = blocks[0].shape[2]
    square = functools.reduce(jnp.maximum, [rows_sum(drift * drift) for drift in drifts])
    largest = jnp.max(square, axis=1, keepdims=True)
    speed_out[...] = jnp.broadcast_to(jnp.sqrt(largest), speed_out.shape)
    scores_out[...] = score
    for part in range(width // 128):
        lanes = slice(part * 128, part * 128 + 128)
        for axis in range(3):
            drift_out[axis, part : part + 1, :] = drifts[0][axis : axis + 1, lanes]
            start_out[axis, part : part + 1, :] = blocks[0][0, axis : axis + 1, lanes]


def sweep_kernel(sources, *refs):
    count = len(sources)
    filled, blocks, refs = refs[0], refs[1 : count + 1], list(refs[count + 1 :])
    own, following, refs = refs[:5], refs[5:13], refs[13:]
    outs, (key_ref, query_ref, moment_ref, sums_ref, totals_ref), refs = (
        refs[:4], refs[4:9], refs[9:]
    )
    flux_refs, refs = refs[:count], refs[count:]
    width = blocks[0].shape[2]
    half = 2 * width
    split_refs, refs = refs[:2], refs[2:]
    exponent_refs, distance_refs = refs[: len(refs) // 2], refs[len(refs) // 2 :]

    live = [lanes_of(owner_of(source), width) < filled[...] for source in sources]
    late = range(2, count)
    for index in late:
        _, _, key, query, moment = prepared(widened(blocks[index]), live[index])
        lanes = pl.ds((index - 2) * width, width)
        key_ref[lanes, :] = key
        query_ref[:, lanes] = query
        moment_ref[:, lanes] = moment
    weight, place, centred = whole_cell(blocks, live)
    lanes = [pl.ds((index - 2) * width, width) for index in late]
    keys = [own[0], following[0]] + [key_ref.at[lane, :] for lane in lanes]
    queries = [own[1], following[1]] + [query_ref.at[:, lane] for lane in lanes]
    moments = [own[2], following[2]] + [moment_ref.at[:, lane] for lane in lanes]
    exponent = exponent_of(looked_up(keys, width, 0), looked_up(queries, width, 1))

    sums_ref[:, 0:half] = following[3][...]
    sums_ref[:, half:] = jnp.zeros_like(sums_ref[:, half:])
    tiles = late_tiles(count, width)
    totals_ref[...] = jnp.zeros_like(totals_ref)
    lanes = [slice(index * width, index * width + width) for index in range(count)]
    scores = [None] * count
    fluxes = looked_up(flux_refs, width, 1)

    def score_blocks(*indices):
        for index in indices:
            at = lanes[index]
            scores[index] = scored(weight[:, at], place[:, at], joined(sums_ref[:, at]))
            flux_refs[index][...] = drift_rows(weight[:, at], centred[:, at], scores[index])

    mixed = sum(tile[0] < half for tile in tiles)

    def after(index):
        if index == mixed - 1:
            score_blocks(0, 1)

    stage(
        tiles, exponent, looked_up(moments, width, 1), sums_ref, exponent_refs, split_refs, None,
        after,
    )
    early = diagonal_tiles(0, width) + square_tiles(width, 0, width)
    early += diagonal_tiles(width, width)
    for tile, distances in zip(early, own[3:5] + following[4:8]):
        for job in add_distances(tile, distances, fluxes, totals_ref):
            job()
    score_blocks(*range(2, count))

    total_slots = count * width
    drifts = [None] * count

    def drift_block(index):
        at = lanes[index]
        drifts[index] = drift_of(
            totals_ref[:, at], centred[:, at], scores[index], weight[:, at], total_slots
        )

    turns = []
    for index in range(mixed):
        split_distances(exponent_refs[index], distance_refs[index])
        rows, columns = add_distances(tiles[index], distance_refs[index], fluxes, totals_ref)
        rows()
        turns.append((tiles[index][0], columns))
    for index in range(2):
        for key, columns in turns:
            if key // width == index:
                columns()
        drift_block(index)
    for index in range(mixed, len(tiles)):
        split_distances(exponent_refs[index], distance_refs[index])
        for job in add_distances(tiles[index], distance_refs[index], fluxes, totals_ref):
            job()
    for index in range(2, count):
        drift_block(index)
    finish(blocks, scores[0], drifts, outs)


def sweep_shapes(width, copies):
    parts = jax.ShapeDtypeStruct((3, width // 128, 128), f32)
    speeds = jax.ShapeDtypeStruct((copies, 128), f32)
    return [jax.ShapeDtypeStruct((8, width), f32), parts, parts, speeds]


def sweep(filled, blocks, sources):
    count, width = len(blocks), blocks[0].shape[2]
    slots, late = count * width, (count - 2) * width
    own = own_part(filled, blocks[0])
    following = next_part(filled, blocks[1], own[:3], own[3], sources[1])
    early = [*own[:3], *own[4:], *following]
    vector = pl.BlockSpec(memory_space=pltpu.VMEM)
    distances = [pltpu.VMEM((2 * tile[1], tile[3]), bf16) for tile in late_tiles(count, width)]
    return pl.pallas_call(
        functools.partial(sweep_kernel, sources),
        out_shape=sweep_shapes(width, 1),
        in_specs=[vector] * (1 + count + len(early)),
        out_specs=[vector] * 4,
        scratch_shapes=[
            pltpu.VMEM((late, DISTANCE_ROWS), bf16),
            pltpu.VMEM((DISTANCE_ROWS, late), bf16),
            pltpu.VMEM((16, late), bf16),
            pltpu.VMEM((16, slots), f32),
            pltpu.VMEM((DRIFT_ROWS // 2, slots), f32),
        ]
        + [pltpu.VMEM((DRIFT_ROWS, width), bf16)] * count
        + [pltpu.VMEM((width, width), bf16)] * 2
        + [pltpu.VMEM((tile[1], tile[3]), f32) for tile in late_tiles(count, width)]
        + distances,
        compiler_params=pltpu.CompilerParams(vmem_limit_bytes=24 << 20),
        name="sweep",
    )(filled, *blocks, *early)


def long_kernel(sources, filled, *refs):
    count = len(sources)
    blocks, outs, refs = refs[:count], refs[count : count + 4], refs[count + 4 :]
    key_ref, query_ref, moment_ref, flux_ref, sums_ref, totals_ref, exponent_ref, split_ref = refs
    width = blocks[0].shape[2]
    live = [lanes_of(owner_of(source), width) < filled[...] for source in sources]
    for index, (block, on) in enumerate(zip(blocks, live)):
        _, _, key, query, moment = prepared(widened(block), on)
        lanes = pl.ds(index * width, width)
        key_ref[lanes, :] = key
        query_ref[:, lanes] = query
        moment_ref[:, lanes] = moment
    weight, place, centred = whole_cell(blocks, live)
    sums_ref[...] = jnp.zeros_like(sums_ref)
    totals_ref[...] = jnp.zeros_like(totals_ref)

    def block_tile(key, query, both):
        start, first = (pl.multiple_of(block * width, width) for block in (key, query))
        return (start, width, first, width, width if both else 0)

    def fill(tile):
        key, keys, query, queries, _ = tile
        exponent_ref[...] = product(key_ref[pl.ds(key, keys), :], query_ref[:, pl.ds(query, queries)])

    def blobs(key, query, both):
        tile = block_tile(key, query, both)
        fill(tile)
        split_blobs(exponent_ref, split_ref)
        add_blobs(tile, split_ref, lambda at, size: moment_ref[:, pl.ds(at, size)], sums_ref)

    @pl.loop(0, count)
    def _(query):
        blobs(query, query, False)

        @pl.loop(query + 1, count)
        def _(key):
            blobs(key, query, True)

    score = scored(weight, place, joined(sums_ref[...]))
    flux_ref[...] = drift_rows(weight, centred, score)

    @pl.loop(0, count)
    def _(key):
        tile = block_tile(key, 0, False)
        fill(tile)
        split_distances(exponent_ref, split_ref)
        for job in add_distances(
            tile, split_ref, lambda at, size: flux_ref[:, pl.ds(at, size)], totals_ref
        ):
            job()

    own = slice(0, width)
    drift = drift_of(
        totals_ref[...], centred[:, own], score[:, own], weight[:, own], count * width
    )
    finish(blocks, score[:, own], [drift], outs)


def long_sweep(filled, blocks, sources, copies):
    count, width = len(blocks), blocks[0].shape[2]
    slots = count * width
    vector = pl.BlockSpec(memory_space=pltpu.VMEM)
    return pl.pallas_call(
        functools.partial(long_kernel, sources),
        out_shape=sweep_shapes(width, copies),
        in_specs=[vector] * (1 + count),
        out_specs=[vector] * 4,
        scratch_shapes=[
            pltpu.VMEM((slots, DISTANCE_ROWS), bf16),
            pltpu.VMEM((DISTANCE_ROWS, slots), bf16),
            pltpu.VMEM((16, slots), bf16),
            pltpu.VMEM((DRIFT_ROWS, slots), bf16),
            pltpu.VMEM((16, slots), f32),
            pltpu.VMEM((DRIFT_ROWS // 2, width), f32),
            pltpu.VMEM((width, width), f32),
            pltpu.VMEM((2 * width, width), bf16),
        ],
        compiler_params=pltpu.CompilerParams(vmem_limit_bytes=(16 << 20) + slots * 2688),
        name="sweep",
    )(filled, *blocks)


def swapped(value, axis, step):
    pairs = [(i, i ^ step) for i in range(lax.axis_size(axis))]
    return lax.ppermute(value, axis, pairs)


def bits(size):
    return [1 << bit for bit in range(size.bit_length() - 1)]


ROUNDS = ((2, 3, 1, 0), (3, 2, 0, 1), (1, 0, 3, 2))


def gathered(block):
    size = lax.axis_size("sharers")
    if size == len(ROUNDS) + 1:
        blocks, sources = [block], [tuple(range(size))]
        for targets in ROUNDS:
            blocks.append(lax.ppermute(block, "sharers", list(enumerate(targets))))
            sources.append(tuple(targets.index(i) for i in range(size)))
        return blocks, sources
    for step in bits(size):
        block = jnp.concatenate([block, swapped(block, "sharers", step)], axis=0)
    sources = [tuple(i ^ step for i in range(size)) for step in range(size)]
    return [block[i : i + 1] for i in range(size)], sources


def local(velocities, weights, counts):
    filled = counts.reshape(1, 1)
    blocks, sources = gathered(jnp.concatenate([velocities, weights[:, None]], axis=1))
    if len(blocks) == len(ROUNDS) + 1:
        scores, drift, start, speeds = sweep(filled, blocks, sources)
        for step in bits(lax.axis_size("cells")):
            speeds = jnp.maximum(speeds, swapped(speeds, "cells", 2 * step - 1))
        largest = speeds
    else:
        axes = ("cells", "sharers")
        scores, drift, start, speeds = long_sweep(filled, blocks, sources, lax.axis_size(axes))
        largest = jnp.max(lax.all_to_all(speeds[:, None], axes, 0, 0, tiled=True), axis=0)
    time_step = 0.5 / (largest + 1e-06)
    moved = start + time_step[None] * drift
    return moved.reshape(velocities.shape), scores[None, 0:3]


def solution(mesh):
    in_specs = (
        P(("groups", "cells"), None, "sharers"),
        P(("groups", "cells"), "sharers"),
        P(("groups", "cells")),
    )
    out_specs = (P(("groups", "cells"), None, "sharers"), P(("groups", "cells"), None, "sharers"))
    return jax.shard_map(local, mesh=mesh, in_specs=in_specs, out_specs=out_specs, check_vma=False)
```

```python
import functools
import functools
import math

import jax
import jax.numpy as jnp
from jax import lax
from jax.experimental import pallas as pl
from jax.experimental.pallas import tpu as pltpu
from jax.sharding import PartitionSpec as P

EPS = 0.35
SCALE = math.sqrt(math.log2(math.e) / (2.0 * EPS * EPS))
GRID = 4.0
TINY = 1e-30
GROUP = 32
DISTANCE_ROWS = 96
DRIFT_ROWS = 64
bf16, f32 = jnp.bfloat16, jnp.float32


def round_bf16(value):
    return value.astype(bf16).astype(f32)


def pieces(value, count):
    parts = []
    for _ in range(count):
        part = round_bf16(value)
        parts.append(part)
        value = value - part
    return parts


def row_of(value):
    return lax.broadcasted_iota(jnp.int32, value.shape, 0)


def rows_sum(value):
    return jnp.sum(value, axis=0, keepdims=True)


def stacked(groups):
    if len(groups) % 2:
        groups = groups + [jnp.zeros_like(groups[0])]
    return jnp.concatenate(groups, axis=0).astype(bf16)


def scalar_groups(value, like):
    row = row_of(like)
    first, second, third = pieces(value, 3)
    low = jnp.where(row == 0, first, jnp.where(row == 1, second, jnp.where(row == 2, third, 0.0)))
    high = jnp.where(row == 3, first, jnp.where(row == 4, second, jnp.where(row == 5, third, 0.0)))
    ones_low, ones_high = row < 3, (row >= 3) & (row < 6)
    return jnp.where(ones_high, 1.0, low), jnp.where(ones_low, 1.0, high)


def grid_parts(place):
    coarse = jnp.floor(place * GRID + 0.5) * (1.0 / GRID)
    return [coarse] + pieces(place - coarse, 2)


def distance_features(parts):
    coarse, fine, rest = parts
    minor = fine + rest
    query_norm, key_norm = scalar_groups(-rows_sum(coarse * coarse), coarse)
    query_less, key_less = scalar_groups(-rows_sum(minor * (2.0 * coarse + minor)), coarse)
    key = [coarse, key_norm, coarse, coarse, fine, rest, key_less, fine, fine, rest, rest]
    coarse, fine, rest = coarse * 2.0, fine * 2.0, rest * 2.0
    query = [coarse, query_norm, fine, rest, coarse, coarse, query_less, fine, rest, fine, rest]
    return stacked(key), stacked(query)


def weighted_rows(weight, value):
    row = row_of(value)
    whole = jnp.where(row < 3, value, jnp.where(row == 3, 1.0, 0.0)) * weight
    first, second, third = pieces(whole, 3)
    return stacked([first, second + pltpu.roll(third, 4, 0)])


def product(left, right):
    return jnp.dot(left, right, preferred_element_type=f32)


def store_split(ref, rows, matrix):
    half = ref.shape[0] // 2
    upper = matrix.astype(bf16)
    ref[rows, :] = upper
    ref[pl.ds(half + rows.start, rows.size), :] = (matrix - upper.astype(f32)).astype(bf16)


def sum_rows(left, ref):
    return product(jnp.concatenate([left, left], axis=1), ref[...])


def sum_columns(left, ref):
    both = lax.dot_general(left, ref[...], (((1,), (1,)), ((), ())), preferred_element_type=f32)
    half = ref.shape[0] // 2
    return both[:, :half] + both[:, half:]


def joined(total):
    upper, lower = total[0:8], total[8:16]
    return upper + lower + pltpu.roll(lower, 4, 0)


def drift_rows(weight, place, score):
    row = row_of(place)
    base = place + jnp.where(row == 3, 1.0, 0.0) + pltpu.roll(score, 4, 0)
    cubic = rows_sum(place * place) * score - rows_sum(place * score) * place
    groups = [weight * base]
    for i in range(3):
        here = slice(i, i + 1)
        groups.append(weight * jnp.where(row == 3, cubic[here], place[here] * base))
    return stacked(sum(map(list, zip(*[pieces(group, 2) for group in groups])), []))


def drift_sum(total, place, score):
    row = row_of(place)
    total = total[: DRIFT_ROWS // 2] + total[DRIFT_ROWS // 2 :]
    first, *rest = [total[8 * i : 8 * i + 8] for i in range(4)]
    turned = [pltpu.roll(group, 4, 0) for group in rest]
    count, scores = first[3:4], pltpu.roll(first, 4, 0)
    square, both = rows_sum(place * place), rows_sum(place * score)
    trace = rest[0][0:1] + rest[1][1:2] + rest[2][2:3]
    cross = turned[0][0:1] + turned[1][1:2] + turned[2][2:3]
    drift = score * (square * count - 2.0 * rows_sum(place * first) + trace) - square * scores
    drift += both * first + place * (
        rows_sum(place * scores) + rows_sum(score * first) - both * count - cross
    )
    ends = []
    for i in range(3):
        here = slice(i, i + 1)
        drift += 2.0 * place[here] * turned[i] - score[here] * rest[i]
        ends.append(rows_sum(place * turned[i]) + rest[i][3:4])
    return drift - jnp.where(row == 0, ends[0], jnp.where(row == 1, ends[1], ends[2]))


def widened(block):
    return jnp.concatenate([block[0], jnp.zeros_like(block[0])], axis=0)


def prepared(whole, live):
    weight = jnp.where(live, whole[3:4], 0.0)
    parts = grid_parts(jnp.where(row_of(whole) < 3, whole * SCALE, 0.0))
    place = parts[0] + parts[1] + parts[2]
    key, query = distance_features(parts)
    return weight, place, key.T, query, weighted_rows(weight, place)


def split_blobs(exponent, split):
    for group in range(0, exponent.shape[0], GROUP):
        rows = pl.ds(group, GROUP)
        store_split(split, rows, jnp.exp2(exponent[rows, :]))


def split_distances(exponent, split):
    for group in range(0, exponent.shape[0], GROUP):
        rows = pl.ds(group, GROUP)
        negative = jnp.minimum(exponent[rows, :], -TINY)
        store_split(split, rows, negative * lax.rsqrt(-negative))


def diagonal_tiles(start, width):
    half = width // 2
    return [(start, half, start, half, 0), (start + half, half, start, width, half)]


def add_blobs(tile, split, moments, sums_ref):
    key, keys, query, queries, turned = tile
    sums_ref[:, pl.ds(query, queries)] += sum_rows(moments(key, keys), split)
    if turned:
        sums_ref[:, pl.ds(key, keys)] += sum_columns(moments(query, turned), split.at[:, 0:turned])


def add_distances(tile, split, fluxes, totals_ref):
    key, keys, query, queries, turned = tile

    def rows():
        totals_ref[:, pl.ds(query, queries)] += sum_rows(fluxes(key, keys), split)

    def columns():
        left, right = fluxes(query, turned), split.at[:, 0:turned]
        totals_ref[:, pl.ds(key, keys)] += sum_columns(left, right)

    return rows, columns if turned else lambda: None


def stage(tiles, exponent, moments, sums_ref, exponent_refs, split_refs, distance_refs,
          after=lambda index: None):
    def buffer(index):
        _, keys, _, queries, _ = tiles[index]
        return exponent_refs[index % len(exponent_refs)].at[0:keys, 0:queries]

    buffer(0)[...] = exponent(tiles[0])
    for index, tile in enumerate(tiles):
        if index + 1 < len(tiles):
            buffer(index + 1)[...] = exponent(tiles[index + 1])
        split = split_refs[index % 2].at[0 : 2 * tile[1], 0 : tile[3]]
        split_blobs(buffer(index), split)
        add_blobs(tile, split, moments, sums_ref)
        if distance_refs is not None:
            split_distances(buffer(index), distance_refs[index])
        after(index)


def looked_up(refs, width, axis):
    def read(start, size):
        at = pl.ds(start % width, size)
        ref = refs[start // width]
        return ref[at, :] if axis == 0 else ref[:, at]

    return read


def exponent_of(keys, queries):
    return lambda tile: product(keys(tile[0], tile[1]), queries(tile[2], tile[3]))


def lanes_of(source, width):
    return lax.broadcasted_iota(jnp.int32, (1, width), 1) + source * width


def owner_of(sources):
    here = lax.axis_index("sharers")
    return sum(jnp.where(here == i, source, 0) for i, source in enumerate(sources))


def own_kernel(filled, block, key_out, query_out, moment_out, sums_out, first_out, second_out,
               *scratch):
    width = block.shape[2]
    live = lanes_of(lax.axis_index("sharers"), width) < filled[...]
    _, _, key, query, moment = prepared(widened(block), live)
    key_out[...] = key
    query_out[...] = query
    moment_out[...] = moment
    sums_out[...] = jnp.zeros_like(sums_out)
    exponent = exponent_of(looked_up([key_out], width, 0), looked_up([query_out], width, 1))
    moments = looked_up([moment_out], width, 1)
    tiles = diagonal_tiles(0, width)
    stage(tiles, exponent, moments, sums_out, scratch[:2], scratch[2:], (first_out, second_out))


def next_kernel(sources, filled, block, own_key, own_query, own_moment, own_sums, key_out,
                query_out, moment_out, sums_out, *refs):
    width = block.shape[2]
    live = lanes_of(owner_of(sources), width) < filled[...]
    _, _, key, query, moment = prepared(widened(block), live)
    key_out[...] = key
    query_out[...] = query
    moment_out[...] = moment
    sums_out[:, 0:width] = own_sums[...]
    sums_out[:, width:] = jnp.zeros_like(own_sums)
    exponent = exponent_of(
        looked_up([own_key, key_out], width, 0), looked_up([own_query, query_out], width, 1)
    )
    moments = looked_up([own_moment, moment_out], width, 1)
    tiles = square_tiles(width, 0, width) + diagonal_tiles(width, width)
    distances, scratch = refs[: len(tiles)], refs[len(tiles) :]
    stage(tiles, exponent, moments, sums_out, scratch[:2], scratch[2:], distances)


def feature_shapes(width):
    return [
        jax.ShapeDtypeStruct((width, DISTANCE_ROWS), bf16),
        jax.ShapeDtypeStruct((DISTANCE_ROWS, width), bf16),
        jax.ShapeDtypeStruct((16, width), bf16),
    ]


def diagonal_shapes(width):
    half = width // 2
    return [
        jax.ShapeDtypeStruct((2 * half, half), bf16),
        jax.ShapeDtypeStruct((2 * half, width), bf16),
    ]


def stage_scratch(width):
    half = width // 2
    return [pltpu.VMEM((half, width), f32)] * 2 + [pltpu.VMEM((width, width), bf16)] * 2


def own_part(filled, block):
    width = block.shape[2]
    vector = pl.BlockSpec(memory_space=pltpu.VMEM)
    shapes = feature_shapes(width) + [jax.ShapeDtypeStruct((16, width), f32)] + diagonal_shapes(width)
    return pl.pallas_call(
        own_kernel,
        out_shape=shapes,
        in_specs=[vector] * 2,
        out_specs=[vector] * len(shapes),
        scratch_shapes=stage_scratch(width),
        compiler_params=pltpu.CompilerParams(vmem_limit_bytes=16 << 20),
        name="own",
    )(filled, block)


def next_part(filled, block, features, sums, sources):
    width = block.shape[2]
    vector = pl.BlockSpec(memory_space=pltpu.VMEM)
    shapes = feature_shapes(width) + [jax.ShapeDtypeStruct((16, 2 * width), f32)]
    shapes += [jax.ShapeDtypeStruct((width, width), bf16)] * 2 + diagonal_shapes(width)
    return pl.pallas_call(
        functools.partial(next_kernel, sources),
        out_shape=shapes,
        in_specs=[vector] * 6,
        out_specs=[vector] * len(shapes),
        scratch_shapes=stage_scratch(width),
        compiler_params=pltpu.CompilerParams(vmem_limit_bytes=20 << 20),
        name="next",
    )(filled, block, *features, sums)


def square_tiles(key, query, width):
    half = width // 2
    return [(key + part, half, query, width, width) for part in (0, half)]


def late_tiles(count, width):
    tiles, late = [], range(2, count)
    for query in late:
        for key in range(2):
            tiles += square_tiles(key * width, query * width, width)
    for query in late:
        for key in range(2, query):
            tiles += square_tiles(key * width, query * width, width)
    for query in late:
        tiles += diagonal_tiles(query * width, width)
    return tiles


def scored(weight, place, sums):
    vector, live = row_of(place) < 3, weight > 0.0
    density_sum = jnp.where(live, sums[3:4], 1.0)
    pull = place * density_sum - sums
    return jnp.where(vector & live, pull / (-SCALE * EPS * EPS * density_sum), 0.0)


def whole_cell(blocks, live):
    weight = jnp.concatenate(
        [jnp.where(on, block[0, 3:4], 0.0) for on, block in zip(live, blocks)], axis=1
    )
    whole = jnp.concatenate([widened(block) for block in blocks], axis=1)
    vector = row_of(whole) < 3
    parts = grid_parts(jnp.where(vector, whole * SCALE, 0.0))
    place = parts[0] + parts[1] + parts[2]
    middle = jnp.sum(place * weight, axis=1, keepdims=True)
    middle = middle / jnp.sum(weight, axis=1, keepdims=True)
    return weight, place, jnp.where(vector, place - middle, 0.0)


def drift_of(total, centred, score, weight, total_slots):
    drift = drift_sum(total, centred, score)
    live = (row_of(drift) < 3) & (weight > 0.0)
    return jnp.where(live, drift * (1.0 / (SCALE * SCALE * SCALE * total_slots)), 0.0)


def finish(blocks, score, drifts, outs):
    scores_out, drift_out, start_out, speed_out = outs
    width = blocks[0].shape[2]
    square = functools.reduce(jnp.maximum, [rows_sum(drift * drift) for drift in drifts])
    largest = jnp.max(square, axis=1, keepdims=True)
    speed_out[...] = jnp.broadcast_to(jnp.sqrt(largest), speed_out.shape)
    scores_out[...] = score
    for part in range(width // 128):
        lanes = slice(part * 128, part * 128 + 128)
        for axis in range(3):
            drift_out[axis, part : part + 1, :] = drifts[0][axis : axis + 1, lanes]
            start_out[axis, part : part + 1, :] = blocks[0][0, axis : axis + 1, lanes]


def sweep_kernel(sources, *refs):
    count = len(sources)
    filled, blocks, refs = refs[0], refs[1 : count + 1], list(refs[count + 1 :])
    own, following, refs = refs[:5], refs[5:13], refs[13:]
    outs, (key_ref, query_ref, moment_ref, sums_ref, totals_ref), refs = (
        refs[:4], refs[4:9], refs[9:]
    )
    flux_refs, refs = refs[:count], refs[count:]
    width = blocks[0].shape[2]
    half = 2 * width
    split_refs, refs = refs[:2], refs[2:]
    exponent_refs, distance_refs = refs[: len(refs) // 2], refs[len(refs) // 2 :]

    live = [lanes_of(owner_of(source), width) < filled[...] for source in sources]
    late = range(2, count)
    for index in late:
        _, _, key, query, moment = prepared(widened(blocks[index]), live[index])
        lanes = pl.ds((index - 2) * width, width)
        key_ref[lanes, :] = key
        query_ref[:, lanes] = query
        moment_ref[:, lanes] = moment
    weight, place, centred = whole_cell(blocks, live)
    lanes = [pl.ds((index - 2) * width, width) for index in late]
    keys = [own[0], following[0]] + [key_ref.at[lane, :] for lane in lanes]
    queries = [own[1], following[1]] + [query_ref.at[:, lane] for lane in lanes]
    moments = [own[2], following[2]] + [moment_ref.at[:, lane] for lane in lanes]
    exponent = exponent_of(looked_up(keys, width, 0), looked_up(queries, width, 1))

    sums_ref[:, 0:half] = following[3][...]
    sums_ref[:, half:] = jnp.zeros_like(sums_ref[:, half:])
    tiles = late_tiles(count, width)
    totals_ref[...] = jnp.zeros_like(totals_ref)
    lanes = [slice(index * width, index * width + width) for index in range(count)]
    scores = [None] * count
    fluxes = looked_up(flux_refs, width, 1)

    def score_blocks(*indices):
        for index in indices:
            at = lanes[index]
            scores[index] = scored(weight[:, at], place[:, at], joined(sums_ref[:, at]))
            flux_refs[index][...] = drift_rows(weight[:, at], centred[:, at], scores[index])

    mixed = sum(tile[0] < half for tile in tiles)

    def after(index):
        if index == mixed - 1:
            score_blocks(0, 1)

    stage(
        tiles, exponent, looked_up(moments, width, 1), sums_ref, exponent_refs, split_refs, None,
        after,
    )
    early = diagonal_tiles(0, width) + square_tiles(width, 0, width)
    early += diagonal_tiles(width, width)
    for tile, distances in zip(early, own[3:5] + following[4:8]):
        for job in add_distances(tile, distances, fluxes, totals_ref):
            job()
    score_blocks(*range(2, count))

    total_slots = count * width
    drifts = [None] * count

    def drift_block(index):
        at = lanes[index]
        drifts[index] = drift_of(
            totals_ref[:, at], centred[:, at], scores[index], weight[:, at], total_slots
        )

    turns = []
    for index in range(mixed):
        split_distances(exponent_refs[index], distance_refs[index])
        rows, columns = add_distances(tiles[index], distance_refs[index], fluxes, totals_ref)
        rows()
        turns.append((tiles[index][0], columns))
    for index in range(2):
        for key, columns in turns:
            if key // width == index:
                columns()
        drift_block(index)
    for index in range(mixed, len(tiles)):
        split_distances(exponent_refs[index], distance_refs[index])
        for job in add_distances(tiles[index], distance_refs[index], fluxes, totals_ref):
            job()
    for index in range(2, count):
        drift_block(index)
    finish(blocks, scores[0], drifts, outs)


def sweep_shapes(width, copies):
    parts = jax.ShapeDtypeStruct((3, width // 128, 128), f32)
    speeds = jax.ShapeDtypeStruct((copies, 128), f32)
    return [jax.ShapeDtypeStruct((8, width), f32), parts, parts, speeds]


def sweep(filled, blocks, sources):
    count, width = len(blocks), blocks[0].shape[2]
    slots, late = count * width, (count - 2) * width
    own = own_part(filled, blocks[0])
    following = next_part(filled, blocks[1], own[:3], own[3], sources[1])
    early = [*own[:3], *own[4:], *following]
    vector = pl.BlockSpec(memory_space=pltpu.VMEM)
    distances = [pltpu.VMEM((2 * tile[1], tile[3]), bf16) for tile in late_tiles(count, width)]
    return pl.pallas_call(
        functools.partial(sweep_kernel, sources),
        out_shape=sweep_shapes(width, 1),
        in_specs=[vector] * (1 + count + len(early)),
        out_specs=[vector] * 4,
        scratch_shapes=[
            pltpu.VMEM((late, DISTANCE_ROWS), bf16),
            pltpu.VMEM((DISTANCE_ROWS, late), bf16),
            pltpu.VMEM((16, late), bf16),
            pltpu.VMEM((16, slots), f32),
            pltpu.VMEM((DRIFT_ROWS, slots), f32),
        ]
        + [pltpu.VMEM((DRIFT_ROWS, width), bf16)] * count
        + [pltpu.VMEM((width, width), bf16)] * 2
        + [pltpu.VMEM((tile[1], tile[3]), f32) for tile in late_tiles(count, width)]
        + distances,
        compiler_params=pltpu.CompilerParams(vmem_limit_bytes=24 << 20),
        name="sweep",
    )(filled, *blocks, *early)


def long_kernel(sources, filled, *refs):
    count = len(sources)
    blocks, outs, refs = refs[:count], refs[count : count + 4], refs[count + 4 :]
    key_ref, query_ref, moment_ref, flux_ref, sums_ref, totals_ref, exponent_ref, split_ref = refs
    width = blocks[0].shape[2]
    live = [lanes_of(owner_of(source), width) < filled[...] for source in sources]
    for index, (block, on) in enumerate(zip(blocks, live)):
        _, _, key, query, moment = prepared(widened(block), on)
        lanes = pl.ds(index * width, width)
        key_ref[lanes, :] = key
        query_ref[:, lanes] = query
        moment_ref[:, lanes] = moment
    weight, place, centred = whole_cell(blocks, live)
    sums_ref[...] = jnp.zeros_like(sums_ref)
    totals_ref[...] = jnp.zeros_like(totals_ref)

    def block_tile(key, query, both):
        start, first = (pl.multiple_of(block * width, width) for block in (key, query))
        return (start, width, first, width, width if both else 0)

    def fill(tile):
        key, keys, query, queries, _ = tile
        exponent_ref[...] = product(key_ref[pl.ds(key, keys), :], query_ref[:, pl.ds(query, queries)])

    def blobs(key, query, both):
        tile = block_tile(key, query, both)
        fill(tile)
        split_blobs(exponent_ref, split_ref)
        add_blobs(tile, split_ref, lambda at, size: moment_ref[:, pl.ds(at, size)], sums_ref)

    @pl.loop(0, count)
    def _(query):
        blobs(query, query, False)

        @pl.loop(query + 1, count)
        def _(key):
            blobs(key, query, True)

    score = scored(weight, place, joined(sums_ref[...]))
    flux_ref[...] = drift_rows(weight, centred, score)

    @pl.loop(0, count)
    def _(key):
        tile = block_tile(key, 0, False)
        fill(tile)
        split_distances(exponent_ref, split_ref)
        for job in add_distances(
            tile, split_ref, lambda at, size: flux_ref[:, pl.ds(at, size)], totals_ref
        ):
            job()

    own = slice(0, width)
    drift = drift_of(
        totals_ref[...], centred[:, own], score[:, own], weight[:, own], count * width
    )
    finish(blocks, score[:, own], [drift], outs)


def long_sweep(filled, blocks, sources, copies):
    count, width = len(blocks), blocks[0].shape[2]
    slots = count * width
    vector = pl.BlockSpec(memory_space=pltpu.VMEM)
    return pl.pallas_call(
        functools.partial(long_kernel, sources),
        out_shape=sweep_shapes(width, copies),
        in_specs=[vector] * (1 + count),
        out_specs=[vector] * 4,
        scratch_shapes=[
            pltpu.VMEM((slots, DISTANCE_ROWS), bf16),
            pltpu.VMEM((DISTANCE_ROWS, slots), bf16),
            pltpu.VMEM((16, slots), bf16),
            pltpu.VMEM((DRIFT_ROWS, slots), bf16),
            pltpu.VMEM((16, slots), f32),
            pltpu.VMEM((DRIFT_ROWS, width), f32),
            pltpu.VMEM((width, width), f32),
            pltpu.VMEM((2 * width, width), bf16),
        ],
        compiler_params=pltpu.CompilerParams(vmem_limit_bytes=(16 << 20) + slots * 2688),
        name="sweep",
    )(filled, *blocks)


def swapped(value, axis, step):
    pairs = [(i, i ^ step) for i in range(lax.axis_size(axis))]
    return lax.ppermute(value, axis, pairs)


def bits(size):
    return [1 << bit for bit in range(size.bit_length() - 1)]


ROUNDS = ((2, 3, 1, 0), (3, 2, 0, 1), (1, 0, 3, 2))


def gathered(block):
    size = lax.axis_size("sharers")
    if size == len(ROUNDS) + 1:
        blocks, sources = [block], [tuple(range(size))]
        for targets in ROUNDS:
            blocks.append(lax.ppermute(block, "sharers", list(enumerate(targets))))
            sources.append(tuple(targets.index(i) for i in range(size)))
        return blocks, sources
    for step in bits(size):
        block = jnp.concatenate([block, swapped(block, "sharers", step)], axis=0)
    sources = [tuple(i ^ step for i in range(size)) for step in range(size)]
    return [block[i : i + 1] for i in range(size)], sources


def local(velocities, weights, counts):
    filled = counts.reshape(1, 1)
    blocks, sources = gathered(jnp.concatenate([velocities, weights[:, None]], axis=1))
    if len(blocks) == len(ROUNDS) + 1:
        scores, drift, start, speeds = sweep(filled, blocks, sources)
        for step in bits(lax.axis_size("cells")):
            speeds = jnp.maximum(speeds, swapped(speeds, "cells", 2 * step - 1))
        largest = speeds
    else:
        axes = ("cells", "sharers")
        scores, drift, start, speeds = long_sweep(filled, blocks, sources, lax.axis_size(axes))
        largest = jnp.max(lax.all_to_all(speeds[:, None], axes, 0, 0, tiled=True), axis=0)
    time_step = 0.5 / (largest + 1e-06)
    moved = start + time_step[None] * drift
    return moved.reshape(velocities.shape), scores[None, 0:3]


def solution(mesh):
    in_specs = (
        P(("groups", "cells"), None, "sharers"),
        P(("groups", "cells"), "sharers"),
        P(("groups", "cells")),
    )
    out_specs = (P(("groups", "cells"), None, "sharers"), P(("groups", "cells"), None, "sharers"))
    return jax.shard_map(local, mesh=mesh, in_specs=in_specs, out_specs=out_specs, check_vma=False)
```

```python
import functools
import functools
import math

import jax
import jax.numpy as jnp
from jax import lax
from jax.experimental import pallas as pl
from jax.experimental.pallas import tpu as pltpu
from jax.sharding import PartitionSpec as P

EPS = 0.35
SCALE = math.sqrt(math.log2(math.e) / (2.0 * EPS * EPS))
GRID = 4.0
TINY = 1e-30
GROUP = 32
DISTANCE_ROWS = 96
DRIFT_ROWS = 64
bf16, f32 = jnp.bfloat16, jnp.float32


def round_bf16(value):
    return value.astype(bf16).astype(f32)


def pieces(value, count):
    parts = []
    for _ in range(count):
        part = round_bf16(value)
        parts.append(part)
        value = value - part
    return parts


def row_of(value):
    return lax.broadcasted_iota(jnp.int32, value.shape, 0)


def rows_sum(value):
    return jnp.sum(value, axis=0, keepdims=True)


def stacked(groups):
    if len(groups) % 2:
        groups = groups + [jnp.zeros_like(groups[0])]
    return jnp.concatenate(groups, axis=0).astype(bf16)


def scalar_groups(value, like):
    row = row_of(like)
    first, second, third = pieces(value, 3)
    low = jnp.where(row == 0, first, jnp.where(row == 1, second, jnp.where(row == 2, third, 0.0)))
    high = jnp.where(row == 3, first, jnp.where(row == 4, second, jnp.where(row == 5, third, 0.0)))
    ones_low, ones_high = row < 3, (row >= 3) & (row < 6)
    return jnp.where(ones_high, 1.0, low), jnp.where(ones_low, 1.0, high)


def grid_parts(place):
    coarse = jnp.floor(place * GRID + 0.5) * (1.0 / GRID)
    return [coarse] + pieces(place - coarse, 2)


def distance_features(parts):
    coarse, fine, rest = parts
    minor = fine + rest
    query_norm, key_norm = scalar_groups(-rows_sum(coarse * coarse), coarse)
    query_less, key_less = scalar_groups(-rows_sum(minor * (2.0 * coarse + minor)), coarse)
    key = [coarse, key_norm, coarse, coarse, fine, rest, key_less, fine, fine, rest, rest]
    coarse, fine, rest = coarse * 2.0, fine * 2.0, rest * 2.0
    query = [coarse, query_norm, fine, rest, coarse, coarse, query_less, fine, rest, fine, rest]
    return stacked(key), stacked(query)


def weighted_rows(weight, value):
    row = row_of(value)
    whole = jnp.where(row < 3, value, jnp.where(row == 3, 1.0, 0.0)) * weight
    first, second, third = pieces(whole, 3)
    return stacked([first, second + pltpu.roll(third, 4, 0)])


def product(left, right):
    return jnp.dot(left, right, preferred_element_type=f32)


def store_split(ref, rows, matrix):
    half = ref.shape[0] // 2
    upper = matrix.astype(bf16)
    ref[rows, :] = upper
    ref[pl.ds(half + rows.start, rows.size), :] = (matrix - upper.astype(f32)).astype(bf16)


def sum_rows(left, ref):
    return product(jnp.concatenate([left, left], axis=1), ref[...])


def sum_columns(left, ref):
    both = lax.dot_general(left, ref[...], (((1,), (1,)), ((), ())), preferred_element_type=f32)
    half = ref.shape[0] // 2
    return both[:, :half] + both[:, half:]


def sum_rows_less(left, ref):
    half = ref.shape[0] // 2
    both = product(left, ref[:half, :])
    few = left.shape[0] // 2
    return both[:few] + product(left[:few], ref[half:, :]), both[few:]


def sum_columns_less(left, ref):
    half, few = ref.shape[0] // 2, left.shape[0] // 2
    turned = (((1,), (1,)), ((), ()))
    both = lax.dot_general(left, ref[:half, :], turned, preferred_element_type=f32)
    less = lax.dot_general(left[:few], ref[half:, :], turned, preferred_element_type=f32)
    return both[:few] + less, both[few:]


def joined(total):
    upper, lower = total[0:8], total[8:16]
    return upper + lower + pltpu.roll(lower, 4, 0)


def drift_rows(weight, place, score):
    row = row_of(place)
    base = place + jnp.where(row == 3, 1.0, 0.0) + pltpu.roll(score, 4, 0)
    cubic = rows_sum(place * place) * score - rows_sum(place * score) * place
    groups = [weight * base]
    for i in range(3):
        here = slice(i, i + 1)
        groups.append(weight * jnp.where(row == 3, cubic[here], place[here] * base))
    return stacked(sum(map(list, zip(*[pieces(group, 2) for group in groups])), []))


def drift_sum(total, place, score):
    row = row_of(place)
    first, *rest = [total[8 * i : 8 * i + 8] for i in range(4)]
    turned = [pltpu.roll(group, 4, 0) for group in rest]
    count, scores = first[3:4], pltpu.roll(first, 4, 0)
    square, both = rows_sum(place * place), rows_sum(place * score)
    trace = rest[0][0:1] + rest[1][1:2] + rest[2][2:3]
    cross = turned[0][0:1] + turned[1][1:2] + turned[2][2:3]
    drift = score * (square * count - 2.0 * rows_sum(place * first) + trace) - square * scores
    drift += both * first + place * (
        rows_sum(place * scores) + rows_sum(score * first) - both * count - cross
    )
    ends = []
    for i in range(3):
        here = slice(i, i + 1)
        drift += 2.0 * place[here] * turned[i] - score[here] * rest[i]
        ends.append(rows_sum(place * turned[i]) + rest[i][3:4])
    return drift - jnp.where(row == 0, ends[0], jnp.where(row == 1, ends[1], ends[2]))


def widened(block):
    return jnp.concatenate([block[0], jnp.zeros_like(block[0])], axis=0)


def prepared(whole, live):
    weight = jnp.where(live, whole[3:4], 0.0)
    parts = grid_parts(jnp.where(row_of(whole) < 3, whole * SCALE, 0.0))
    place = parts[0] + parts[1] + parts[2]
    key, query = distance_features(parts)
    return weight, place, key.T, query, weighted_rows(weight, place)


def split_blobs(exponent, split):
    for group in range(0, exponent.shape[0], GROUP):
        rows = pl.ds(group, GROUP)
        store_split(split, rows, jnp.exp2(exponent[rows, :]))


def split_distances(exponent, split):
    for group in range(0, exponent.shape[0], GROUP):
        rows = pl.ds(group, GROUP)
        negative = jnp.minimum(exponent[rows, :], -TINY)
        store_split(split, rows, negative * lax.rsqrt(-negative))


def diagonal_tiles(start, width):
    half = width // 2
    return [(start, half, start, half, 0), (start + half, half, start, width, half)]


def add_blobs(tile, split, moments, sums_ref):
    key, keys, query, queries, turned = tile
    sums_ref[:, pl.ds(query, queries)] += sum_rows(moments(key, keys), split)
    if turned:
        sums_ref[:, pl.ds(key, keys)] += sum_columns(moments(query, turned), split.at[:, 0:turned])


def add_distances(tile, split, fluxes, totals_ref):
    key, keys, query, queries, turned = tile

    def rows():
        upper, lower = sum_rows_less(fluxes(key, keys), split)
        totals_ref[:, pl.ds(query, queries)] += upper + lower

    def columns():
        upper, lower = sum_columns_less(fluxes(query, turned), split.at[:, 0:turned])
        totals_ref[:, pl.ds(key, keys)] += upper + lower

    return rows, columns if turned else lambda: None


def stage(tiles, exponent, moments, sums_ref, exponent_refs, split_refs, distance_refs,
          after=lambda index: None):
    def buffer(index):
        _, keys, _, queries, _ = tiles[index]
        return exponent_refs[index % len(exponent_refs)].at[0:keys, 0:queries]

    buffer(0)[...] = exponent(tiles[0])
    for index, tile in enumerate(tiles):
        if index + 1 < len(tiles):
            buffer(index + 1)[...] = exponent(tiles[index + 1])
        split = split_refs[index % 2].at[0 : 2 * tile[1], 0 : tile[3]]
        split_blobs(buffer(index), split)
        add_blobs(tile, split, moments, sums_ref)
        if distance_refs is not None:
            split_distances(buffer(index), distance_refs[index])
        after(index)


def looked_up(refs, width, axis):
    def read(start, size):
        at = pl.ds(start % width, size)
        ref = refs[start // width]
        return ref[at, :] if axis == 0 else ref[:, at]

    return read


def exponent_of(keys, queries):
    return lambda tile: product(keys(tile[0], tile[1]), queries(tile[2], tile[3]))


def lanes_of(source, width):
    return lax.broadcasted_iota(jnp.int32, (1, width), 1) + source * width


def owner_of(sources):
    here = lax.axis_index("sharers")
    return sum(jnp.where(here == i, source, 0) for i, source in enumerate(sources))


def own_kernel(filled, block, key_out, query_out, moment_out, sums_out, first_out, second_out,
               *scratch):
    width = block.shape[2]
    live = lanes_of(lax.axis_index("sharers"), width) < filled[...]
    _, _, key, query, moment = prepared(widened(block), live)
    key_out[...] = key
    query_out[...] = query
    moment_out[...] = moment
    sums_out[...] = jnp.zeros_like(sums_out)
    exponent = exponent_of(looked_up([key_out], width, 0), looked_up([query_out], width, 1))
    moments = looked_up([moment_out], width, 1)
    tiles = diagonal_tiles(0, width)
    stage(tiles, exponent, moments, sums_out, scratch[:2], scratch[2:], (first_out, second_out))


def next_kernel(sources, filled, block, own_key, own_query, own_moment, own_sums, key_out,
                query_out, moment_out, sums_out, *refs):
    width = block.shape[2]
    live = lanes_of(owner_of(sources), width) < filled[...]
    _, _, key, query, moment = prepared(widened(block), live)
    key_out[...] = key
    query_out[...] = query
    moment_out[...] = moment
    sums_out[:, 0:width] = own_sums[...]
    sums_out[:, width:] = jnp.zeros_like(own_sums)
    exponent = exponent_of(
        looked_up([own_key, key_out], width, 0), looked_up([own_query, query_out], width, 1)
    )
    moments = looked_up([own_moment, moment_out], width, 1)
    tiles = square_tiles(width, 0, width) + diagonal_tiles(width, width)
    distances, scratch = refs[: len(tiles)], refs[len(tiles) :]
    stage(tiles, exponent, moments, sums_out, scratch[:2], scratch[2:], distances)


def feature_shapes(width):
    return [
        jax.ShapeDtypeStruct((width, DISTANCE_ROWS), bf16),
        jax.ShapeDtypeStruct((DISTANCE_ROWS, width), bf16),
        jax.ShapeDtypeStruct((16, width), bf16),
    ]


def diagonal_shapes(width):
    half = width // 2
    return [
        jax.ShapeDtypeStruct((2 * half, half), bf16),
        jax.ShapeDtypeStruct((2 * half, width), bf16),
    ]


def stage_scratch(width):
    half = width // 2
    return [pltpu.VMEM((half, width), f32)] * 2 + [pltpu.VMEM((width, width), bf16)] * 2


def own_part(filled, block):
    width = block.shape[2]
    vector = pl.BlockSpec(memory_space=pltpu.VMEM)
    shapes = feature_shapes(width) + [jax.ShapeDtypeStruct((16, width), f32)] + diagonal_shapes(width)
    return pl.pallas_call(
        own_kernel,
        out_shape=shapes,
        in_specs=[vector] * 2,
        out_specs=[vector] * len(shapes),
        scratch_shapes=stage_scratch(width),
        compiler_params=pltpu.CompilerParams(vmem_limit_bytes=16 << 20),
        name="own",
    )(filled, block)


def next_part(filled, block, features, sums, sources):
    width = block.shape[2]
    vector = pl.BlockSpec(memory_space=pltpu.VMEM)
    shapes = feature_shapes(width) + [jax.ShapeDtypeStruct((16, 2 * width), f32)]
    shapes += [jax.ShapeDtypeStruct((width, width), bf16)] * 2 + diagonal_shapes(width)
    return pl.pallas_call(
        functools.partial(next_kernel, sources),
        out_shape=shapes,
        in_specs=[vector] * 6,
        out_specs=[vector] * len(shapes),
        scratch_shapes=stage_scratch(width),
        compiler_params=pltpu.CompilerParams(vmem_limit_bytes=20 << 20),
        name="next",
    )(filled, block, *features, sums)


def square_tiles(key, query, width, cuts=2):
    part = width // cuts
    return [(key + at, part, query, width, width) for at in range(0, width, part)]


def late_tiles(count, width):
    tiles, late = [], range(2, count)
    for query in late:
        for key in range(2):
            tiles += square_tiles(key * width, query * width, width, 4)
    for query in late:
        for key in range(2, query):
            tiles += square_tiles(key * width, query * width, width, 4)
    for query in late:
        tiles += diagonal_tiles(query * width, width)
    return tiles


def scored(weight, place, sums):
    vector, live = row_of(place) < 3, weight > 0.0
    density_sum = jnp.where(live, sums[3:4], 1.0)
    pull = place * density_sum - sums
    return jnp.where(vector & live, pull / (-SCALE * EPS * EPS * density_sum), 0.0)


def whole_cell(blocks, live):
    weight = jnp.concatenate(
        [jnp.where(on, block[0, 3:4], 0.0) for on, block in zip(live, blocks)], axis=1
    )
    whole = jnp.concatenate([widened(block) for block in blocks], axis=1)
    vector = row_of(whole) < 3
    parts = grid_parts(jnp.where(vector, whole * SCALE, 0.0))
    place = parts[0] + parts[1] + parts[2]
    middle = jnp.sum(place * weight, axis=1, keepdims=True)
    middle = middle / jnp.sum(weight, axis=1, keepdims=True)
    return weight, place, jnp.where(vector, place - middle, 0.0)


def drift_of(total, centred, score, weight, total_slots):
    drift = drift_sum(total, centred, score)
    live = (row_of(drift) < 3) & (weight > 0.0)
    return jnp.where(live, drift * (1.0 / (SCALE * SCALE * SCALE * total_slots)), 0.0)


def finish(blocks, score, drifts, outs):
    scores_out, drift_out, start_out, speed_out = outs
    width = blocks[0].shape[2]
    square = functools.reduce(jnp.maximum, [rows_sum(drift * drift) for drift in drifts])
    largest = jnp.max(square, axis=1, keepdims=True)
    speed_out[...] = jnp.broadcast_to(jnp.sqrt(largest), speed_out.shape)
    scores_out[...] = score
    for part in range(width // 128):
        lanes = slice(part * 128, part * 128 + 128)
        for axis in range(3):
            drift_out[axis, part : part + 1, :] = drifts[0][axis : axis + 1, lanes]
            start_out[axis, part : part + 1, :] = blocks[0][0, axis : axis + 1, lanes]


def sweep_kernel(sources, *refs):
    count = len(sources)
    filled, blocks, refs = refs[0], refs[1 : count + 1], list(refs[count + 1 :])
    own, following, refs = refs[:5], refs[5:13], refs[13:]
    outs, (key_ref, query_ref, moment_ref, sums_ref, totals_ref), refs = (
        refs[:4], refs[4:9], refs[9:]
    )
    flux_refs, refs = refs[:count], refs[count:]
    width = blocks[0].shape[2]
    half = 2 * width
    split_refs, refs = refs[:2], refs[2:]
    exponent_refs, distance_refs = refs[: len(refs) // 2], refs[len(refs) // 2 :]

    live = [lanes_of(owner_of(source), width) < filled[...] for source in sources]
    late = range(2, count)
    for index in late:
        _, _, key, query, moment = prepared(widened(blocks[index]), live[index])
        lanes = pl.ds((index - 2) * width, width)
        key_ref[lanes, :] = key
        query_ref[:, lanes] = query
        moment_ref[:, lanes] = moment
    weight, place, centred = whole_cell(blocks, live)
    lanes = [pl.ds((index - 2) * width, width) for index in late]
    keys = [own[0], following[0]] + [key_ref.at[lane, :] for lane in lanes]
    queries = [own[1], following[1]] + [query_ref.at[:, lane] for lane in lanes]
    moments = [own[2], following[2]] + [moment_ref.at[:, lane] for lane in lanes]
    exponent = exponent_of(looked_up(keys, width, 0), looked_up(queries, width, 1))

    sums_ref[:, 0:half] = following[3][...]
    sums_ref[:, half:] = jnp.zeros_like(sums_ref[:, half:])
    tiles = late_tiles(count, width)
    totals_ref[...] = jnp.zeros_like(totals_ref)
    lanes = [slice(index * width, index * width + width) for index in range(count)]
    scores = [None] * count
    fluxes = looked_up(flux_refs, width, 1)

    def score_blocks(*indices):
        for index in indices:
            at = lanes[index]
            scores[index] = scored(weight[:, at], place[:, at], joined(sums_ref[:, at]))
            flux_refs[index][...] = drift_rows(weight[:, at], centred[:, at], scores[index])

    mixed = sum(tile[0] < half for tile in tiles)

    def after(index):
        if index == mixed - 1:
            score_blocks(0, 1)

    stage(
        tiles, exponent, looked_up(moments, width, 1), sums_ref, exponent_refs, split_refs, None,
        after,
    )
    early = diagonal_tiles(0, width) + square_tiles(width, 0, width)
    early += diagonal_tiles(width, width)
    for tile, distances in zip(early, own[3:5] + following[4:8]):
        for job in add_distances(tile, distances, fluxes, totals_ref):
            job()
    score_blocks(*range(2, count))

    total_slots = count * width
    drifts = [None] * count

    def drift_block(index):
        at = lanes[index]
        drifts[index] = drift_of(
            totals_ref[:, at], centred[:, at], scores[index], weight[:, at], total_slots
        )

    turns = []
    for index in range(mixed):
        split_distances(exponent_refs[index], distance_refs[index])
        rows, columns = add_distances(tiles[index], distance_refs[index], fluxes, totals_ref)
        rows()
        turns.append((tiles[index][0], columns))
    for index in range(2):
        for key, columns in turns:
            if key // width == index:
                columns()
        drift_block(index)
    for index in range(mixed, len(tiles)):
        split_distances(exponent_refs[index], distance_refs[index])
        for job in add_distances(tiles[index], distance_refs[index], fluxes, totals_ref):
            job()
    for index in range(2, count):
        drift_block(index)
    finish(blocks, scores[0], drifts, outs)


def sweep_shapes(width, copies):
    parts = jax.ShapeDtypeStruct((3, width // 128, 128), f32)
    speeds = jax.ShapeDtypeStruct((copies, 128), f32)
    return [jax.ShapeDtypeStruct((8, width), f32), parts, parts, speeds]


def sweep(filled, blocks, sources):
    count, width = len(blocks), blocks[0].shape[2]
    slots, late = count * width, (count - 2) * width
    own = own_part(filled, blocks[0])
    following = next_part(filled, blocks[1], own[:3], own[3], sources[1])
    early = [*own[:3], *own[4:], *following]
    vector = pl.BlockSpec(memory_space=pltpu.VMEM)
    distances = [pltpu.VMEM((2 * tile[1], tile[3]), bf16) for tile in late_tiles(count, width)]
    return pl.pallas_call(
        functools.partial(sweep_kernel, sources),
        out_shape=sweep_shapes(width, 1),
        in_specs=[vector] * (1 + count + len(early)),
        out_specs=[vector] * 4,
        scratch_shapes=[
            pltpu.VMEM((late, DISTANCE_ROWS), bf16),
            pltpu.VMEM((DISTANCE_ROWS, late), bf16),
            pltpu.VMEM((16, late), bf16),
            pltpu.VMEM((16, slots), f32),
            pltpu.VMEM((DRIFT_ROWS // 2, slots), f32),
        ]
        + [pltpu.VMEM((DRIFT_ROWS, width), bf16)] * count
        + [pltpu.VMEM((width, width), bf16)] * 2
        + [pltpu.VMEM((tile[1], tile[3]), f32) for tile in late_tiles(count, width)]
        + distances,
        compiler_params=pltpu.CompilerParams(vmem_limit_bytes=24 << 20),
        name="sweep",
    )(filled, *blocks, *early)


def long_kernel(sources, filled, *refs):
    count = len(sources)
    blocks, outs, refs = refs[:count], refs[count : count + 4], refs[count + 4 :]
    key_ref, query_ref, moment_ref, flux_ref, sums_ref, totals_ref, exponent_ref, split_ref = refs
    width = blocks[0].shape[2]
    live = [lanes_of(owner_of(source), width) < filled[...] for source in sources]
    for index, (block, on) in enumerate(zip(blocks, live)):
        _, _, key, query, moment = prepared(widened(block), on)
        lanes = pl.ds(index * width, width)
        key_ref[lanes, :] = key
        query_ref[:, lanes] = query
        moment_ref[:, lanes] = moment
    weight, place, centred = whole_cell(blocks, live)
    sums_ref[...] = jnp.zeros_like(sums_ref)
    totals_ref[...] = jnp.zeros_like(totals_ref)

    def block_tile(key, query, both):
        start, first = (pl.multiple_of(block * width, width) for block in (key, query))
        return (start, width, first, width, width if both else 0)

    def fill(tile):
        key, keys, query, queries, _ = tile
        exponent_ref[...] = product(key_ref[pl.ds(key, keys), :], query_ref[:, pl.ds(query, queries)])

    def blobs(key, query, both):
        tile = block_tile(key, query, both)
        fill(tile)
        split_blobs(exponent_ref, split_ref)
        add_blobs(tile, split_ref, lambda at, size: moment_ref[:, pl.ds(at, size)], sums_ref)

    @pl.loop(0, count)
    def _(query):
        blobs(query, query, False)

        @pl.loop(query + 1, count)
        def _(key):
            blobs(key, query, True)

    score = scored(weight, place, joined(sums_ref[...]))
    flux_ref[...] = drift_rows(weight, centred, score)

    @pl.loop(0, count)
    def _(key):
        tile = block_tile(key, 0, False)
        fill(tile)
        split_distances(exponent_ref, split_ref)
        for job in add_distances(
            tile, split_ref, lambda at, size: flux_ref[:, pl.ds(at, size)], totals_ref
        ):
            job()

    own = slice(0, width)
    drift = drift_of(
        totals_ref[...], centred[:, own], score[:, own], weight[:, own], count * width
    )
    finish(blocks, score[:, own], [drift], outs)


def long_sweep(filled, blocks, sources, copies):
    count, width = len(blocks), blocks[0].shape[2]
    slots = count * width
    vector = pl.BlockSpec(memory_space=pltpu.VMEM)
    return pl.pallas_call(
        functools.partial(long_kernel, sources),
        out_shape=sweep_shapes(width, copies),
        in_specs=[vector] * (1 + count),
        out_specs=[vector] * 4,
        scratch_shapes=[
            pltpu.VMEM((slots, DISTANCE_ROWS), bf16),
            pltpu.VMEM((DISTANCE_ROWS, slots), bf16),
            pltpu.VMEM((16, slots), bf16),
            pltpu.VMEM((DRIFT_ROWS, slots), bf16),
            pltpu.VMEM((16, slots), f32),
            pltpu.VMEM((DRIFT_ROWS // 2, width), f32),
            pltpu.VMEM((width, width), f32),
            pltpu.VMEM((2 * width, width), bf16),
        ],
        compiler_params=pltpu.CompilerParams(vmem_limit_bytes=(16 << 20) + slots * 2688),
        name="sweep",
    )(filled, *blocks)


def swapped(value, axis, step):
    pairs = [(i, i ^ step) for i in range(lax.axis_size(axis))]
    return lax.ppermute(value, axis, pairs)


def bits(size):
    return [1 << bit for bit in range(size.bit_length() - 1)]


ROUNDS = ((2, 3, 1, 0), (3, 2, 0, 1), (1, 0, 3, 2))


def gathered(block):
    size = lax.axis_size("sharers")
    if size == len(ROUNDS) + 1:
        blocks, sources = [block], [tuple(range(size))]
        for targets in ROUNDS:
            blocks.append(lax.ppermute(block, "sharers", list(enumerate(targets))))
            sources.append(tuple(targets.index(i) for i in range(size)))
        return blocks, sources
    for step in bits(size):
        block = jnp.concatenate([block, swapped(block, "sharers", step)], axis=0)
    sources = [tuple(i ^ step for i in range(size)) for step in range(size)]
    return [block[i : i + 1] for i in range(size)], sources


def local(velocities, weights, counts):
    filled = counts.reshape(1, 1)
    blocks, sources = gathered(jnp.concatenate([velocities, weights[:, None]], axis=1))
    if len(blocks) == len(ROUNDS) + 1:
        scores, drift, start, speeds = sweep(filled, blocks, sources)
        for step in bits(lax.axis_size("cells")):
            speeds = jnp.maximum(speeds, swapped(speeds, "cells", 2 * step - 1))
        largest = speeds
    else:
        axes = ("cells", "sharers")
        scores, drift, start, speeds = long_sweep(filled, blocks, sources, lax.axis_size(axes))
        largest = jnp.max(lax.all_to_all(speeds[:, None], axes, 0, 0, tiled=True), axis=0)
    time_step = 0.5 / (largest + 1e-06)
    moved = start + time_step[None] * drift
    return moved.reshape(velocities.shape), scores[None, 0:3]


def solution(mesh):
    in_specs = (
        P(("groups", "cells"), None, "sharers"),
        P(("groups", "cells"), "sharers"),
        P(("groups", "cells")),
    )
    out_specs = (P(("groups", "cells"), None, "sharers"), P(("groups", "cells"), None, "sharers"))
    return jax.shard_map(local, mesh=mesh, in_specs=in_specs, out_specs=out_specs, check_vma=False)
```

```python
import functools
import functools
import math

import jax
import jax.numpy as jnp
from jax import lax
from jax.experimental import pallas as pl
from jax.experimental.pallas import tpu as pltpu
from jax.sharding import PartitionSpec as P

EPS = 0.35
SCALE = math.sqrt(math.log2(math.e) / (2.0 * EPS * EPS))
GRID = 4.0
TINY = 1e-30
GROUP = 32
DISTANCE_ROWS = 96
DRIFT_ROWS = 64
bf16, f32 = jnp.bfloat16, jnp.float32


def round_bf16(value):
    return value.astype(bf16).astype(f32)


def pieces(value, count):
    parts = []
    for _ in range(count):
        part = round_bf16(value)
        parts.append(part)
        value = value - part
    return parts


def row_of(value):
    return lax.broadcasted_iota(jnp.int32, value.shape, 0)


def rows_sum(value):
    return jnp.sum(value, axis=0, keepdims=True)


def stacked(groups):
    if len(groups) % 2:
        groups = groups + [jnp.zeros_like(groups[0])]
    return jnp.concatenate(groups, axis=0).astype(bf16)


def scalar_groups(value, like):
    row = row_of(like)
    first, second, third = pieces(value, 3)
    low = jnp.where(row == 0, first, jnp.where(row == 1, second, jnp.where(row == 2, third, 0.0)))
    high = jnp.where(row == 3, first, jnp.where(row == 4, second, jnp.where(row == 5, third, 0.0)))
    ones_low, ones_high = row < 3, (row >= 3) & (row < 6)
    return jnp.where(ones_high, 1.0, low), jnp.where(ones_low, 1.0, high)


def grid_parts(place):
    coarse = jnp.floor(place * GRID + 0.5) * (1.0 / GRID)
    return [coarse] + pieces(place - coarse, 2)


def distance_features(parts):
    coarse, fine, rest = parts
    minor = fine + rest
    query_norm, key_norm = scalar_groups(-rows_sum(coarse * coarse), coarse)
    query_less, key_less = scalar_groups(-rows_sum(minor * (2.0 * coarse + minor)), coarse)
    key = [coarse, key_norm, coarse, coarse, fine, rest, key_less, fine, fine, rest, rest]
    coarse, fine, rest = coarse * 2.0, fine * 2.0, rest * 2.0
    query = [coarse, query_norm, fine, rest, coarse, coarse, query_less, fine, rest, fine, rest]
    return stacked(key), stacked(query)


def weighted_rows(weight, value):
    row = row_of(value)
    whole = jnp.where(row < 3, value, jnp.where(row == 3, 1.0, 0.0)) * weight
    first, second, third = pieces(whole, 3)
    return stacked([first, second + pltpu.roll(third, 4, 0)])


def product(left, right):
    return jnp.dot(left, right, preferred_element_type=f32)


def store_split(ref, rows, matrix):
    half = ref.shape[0] // 2
    upper = matrix.astype(bf16)
    ref[rows, :] = upper
    ref[pl.ds(half + rows.start, rows.size), :] = (matrix - upper.astype(f32)).astype(bf16)


def sum_rows(left, ref):
    return product(jnp.concatenate([left, left], axis=1), ref[...])


def sum_columns(left, ref):
    both = lax.dot_general(left, ref[...], (((1,), (1,)), ((), ())), preferred_element_type=f32)
    half = ref.shape[0] // 2
    return both[:, :half] + both[:, half:]


def sum_rows_less(left, ref):
    half = ref.shape[0] // 2
    both = product(left, ref[:half, :])
    few = left.shape[0] // 2
    return both[:few] + product(left[:few], ref[half:, :]), both[few:]


def sum_columns_less(left, ref):
    half, few = ref.shape[0] // 2, left.shape[0] // 2
    turned = (((1,), (1,)), ((), ()))
    both = lax.dot_general(left, ref[:half, :], turned, preferred_element_type=f32)
    less = lax.dot_general(left[:few], ref[half:, :], turned, preferred_element_type=f32)
    return both[:few] + less, both[few:]


def joined(total):
    upper, lower = total[0:8], total[8:16]
    return upper + lower + pltpu.roll(lower, 4, 0)


def drift_rows(weight, place, score):
    row = row_of(place)
    base = place + jnp.where(row == 3, 1.0, 0.0) + pltpu.roll(score, 4, 0)
    cubic = rows_sum(place * place) * score - rows_sum(place * score) * place
    groups = [weight * base]
    for i in range(3):
        here = slice(i, i + 1)
        groups.append(weight * jnp.where(row == 3, cubic[here], place[here] * base))
    return stacked(sum(map(list, zip(*[pieces(group, 2) for group in groups])), []))


def drift_sum(total, place, score):
    row = row_of(place)
    first, *rest = [total[8 * i : 8 * i + 8] for i in range(4)]
    turned = [pltpu.roll(group, 4, 0) for group in rest]
    count, scores = first[3:4], pltpu.roll(first, 4, 0)
    square, both = rows_sum(place * place), rows_sum(place * score)
    trace = rest[0][0:1] + rest[1][1:2] + rest[2][2:3]
    cross = turned[0][0:1] + turned[1][1:2] + turned[2][2:3]
    drift = score * (square * count - 2.0 * rows_sum(place * first) + trace) - square * scores
    drift += both * first + place * (
        rows_sum(place * scores) + rows_sum(score * first) - both * count - cross
    )
    ends = []
    for i in range(3):
        here = slice(i, i + 1)
        drift += 2.0 * place[here] * turned[i] - score[here] * rest[i]
        ends.append(rows_sum(place * turned[i]) + rest[i][3:4])
    return drift - jnp.where(row == 0, ends[0], jnp.where(row == 1, ends[1], ends[2]))


def widened(block):
    return jnp.concatenate([block[0], jnp.zeros_like(block[0])], axis=0)


def prepared(whole, live):
    weight = jnp.where(live, whole[3:4], 0.0)
    parts = grid_parts(jnp.where(row_of(whole) < 3, whole * SCALE, 0.0))
    place = parts[0] + parts[1] + parts[2]
    key, query = distance_features(parts)
    return weight, place, key.T, query, weighted_rows(weight, place)


def split_blobs(exponent, split):
    for group in range(0, exponent.shape[0], GROUP):
        rows = pl.ds(group, GROUP)
        store_split(split, rows, jnp.exp2(exponent[rows, :]))


def split_distances(exponent, split):
    for group in range(0, exponent.shape[0], GROUP):
        rows = pl.ds(group, GROUP)
        negative = jnp.minimum(exponent[rows, :], -TINY)
        store_split(split, rows, negative * lax.rsqrt(-negative))


def diagonal_tiles(start, width):
    half = width // 2
    return [(start, half, start, half, 0), (start + half, half, start, width, half)]


def add_blobs(tile, split, moments, sums_ref):
    key, keys, query, queries, turned = tile
    sums_ref[:, pl.ds(query, queries)] += sum_rows(moments(key, keys), split)
    if turned:
        sums_ref[:, pl.ds(key, keys)] += sum_columns(moments(query, turned), split.at[:, 0:turned])


def add_distances(tile, split, fluxes, totals_ref):
    key, keys, query, queries, turned = tile

    def rows():
        upper, lower = sum_rows_less(fluxes(key, keys), split)
        totals_ref[:, pl.ds(query, queries)] += upper + lower

    def columns():
        upper, lower = sum_columns_less(fluxes(query, turned), split.at[:, 0:turned])
        totals_ref[:, pl.ds(key, keys)] += upper + lower

    return rows, columns if turned else lambda: None


def stage(tiles, exponent, moments, sums_ref, exponent_refs, split_refs, distance_refs,
          after=lambda index: None):
    def buffer(index):
        _, keys, _, queries, _ = tiles[index]
        return exponent_refs[index % len(exponent_refs)].at[0:keys, 0:queries]

    buffer(0)[...] = exponent(tiles[0])
    for index, tile in enumerate(tiles):
        if index + 1 < len(tiles):
            buffer(index + 1)[...] = exponent(tiles[index + 1])
        split = split_refs[index % len(split_refs)].at[0 : 2 * tile[1], 0 : tile[3]]
        split_blobs(buffer(index), split)
        add_blobs(tile, split, moments, sums_ref)
        if distance_refs is not None:
            split_distances(buffer(index), distance_refs[index])
        after(index)


def looked_up(refs, width, axis):
    def read(start, size):
        at = pl.ds(start % width, size)
        ref = refs[start // width]
        return ref[at, :] if axis == 0 else ref[:, at]

    return read


def exponent_of(keys, queries):
    return lambda tile: product(keys(tile[0], tile[1]), queries(tile[2], tile[3]))


def lanes_of(source, width):
    return lax.broadcasted_iota(jnp.int32, (1, width), 1) + source * width


def owner_of(sources):
    here = lax.axis_index("sharers")
    return sum(jnp.where(here == i, source, 0) for i, source in enumerate(sources))


def own_kernel(filled, block, key_out, query_out, moment_out, sums_out, first_out, second_out,
               *scratch):
    width = block.shape[2]
    live = lanes_of(lax.axis_index("sharers"), width) < filled[...]
    _, _, key, query, moment = prepared(widened(block), live)
    key_out[...] = key
    query_out[...] = query
    moment_out[...] = moment
    sums_out[...] = jnp.zeros_like(sums_out)
    exponent = exponent_of(looked_up([key_out], width, 0), looked_up([query_out], width, 1))
    moments = looked_up([moment_out], width, 1)
    tiles = diagonal_tiles(0, width)
    stage(tiles, exponent, moments, sums_out, scratch[:2], scratch[2:], (first_out, second_out))


def next_kernel(sources, filled, block, own_key, own_query, own_moment, own_sums, key_out,
                query_out, moment_out, sums_out, *refs):
    width = block.shape[2]
    live = lanes_of(owner_of(sources), width) < filled[...]
    _, _, key, query, moment = prepared(widened(block), live)
    key_out[...] = key
    query_out[...] = query
    moment_out[...] = moment
    sums_out[:, 0:width] = own_sums[...]
    sums_out[:, width:] = jnp.zeros_like(own_sums)
    exponent = exponent_of(
        looked_up([own_key, key_out], width, 0), looked_up([own_query, query_out], width, 1)
    )
    moments = looked_up([own_moment, moment_out], width, 1)
    tiles = square_tiles(width, 0, width) + diagonal_tiles(width, width)
    distances, scratch = refs[: len(tiles)], refs[len(tiles) :]
    stage(tiles, exponent, moments, sums_out, scratch[:2], scratch[2:], distances)


def feature_shapes(width):
    return [
        jax.ShapeDtypeStruct((width, DISTANCE_ROWS), bf16),
        jax.ShapeDtypeStruct((DISTANCE_ROWS, width), bf16),
        jax.ShapeDtypeStruct((16, width), bf16),
    ]


def diagonal_shapes(width):
    half = width // 2
    return [
        jax.ShapeDtypeStruct((2 * half, half), bf16),
        jax.ShapeDtypeStruct((2 * half, width), bf16),
    ]


def stage_scratch(width):
    half = width // 2
    return [pltpu.VMEM((half, width), f32)] * 2 + [pltpu.VMEM((width, width), bf16)] * 2


def own_part(filled, block):
    width = block.shape[2]
    vector = pl.BlockSpec(memory_space=pltpu.VMEM)
    shapes = feature_shapes(width) + [jax.ShapeDtypeStruct((16, width), f32)] + diagonal_shapes(width)
    return pl.pallas_call(
        own_kernel,
        out_shape=shapes,
        in_specs=[vector] * 2,
        out_specs=[vector] * len(shapes),
        scratch_shapes=stage_scratch(width),
        compiler_params=pltpu.CompilerParams(vmem_limit_bytes=16 << 20),
        name="own",
    )(filled, block)


def next_part(filled, block, features, sums, sources):
    width = block.shape[2]
    vector = pl.BlockSpec(memory_space=pltpu.VMEM)
    shapes = feature_shapes(width) + [jax.ShapeDtypeStruct((16, 2 * width), f32)]
    shapes += [jax.ShapeDtypeStruct((width, width), bf16)] * 2 + diagonal_shapes(width)
    return pl.pallas_call(
        functools.partial(next_kernel, sources),
        out_shape=shapes,
        in_specs=[vector] * 6,
        out_specs=[vector] * len(shapes),
        scratch_shapes=stage_scratch(width),
        compiler_params=pltpu.CompilerParams(vmem_limit_bytes=20 << 20),
        name="next",
    )(filled, block, *features, sums)


def square_tiles(key, query, width):
    half = width // 2
    return [(key + part, half, query, width, width) for part in (0, half)]


def late_tiles(count, width):
    tiles, late = [], range(2, count)
    for query in late:
        for key in range(2):
            tiles += square_tiles(key * width, query * width, width)
    for query in late:
        for key in range(2, query):
            tiles += square_tiles(key * width, query * width, width)
    for query in late:
        tiles += diagonal_tiles(query * width, width)
    return tiles


def scored(weight, place, sums):
    vector, live = row_of(place) < 3, weight > 0.0
    density_sum = jnp.where(live, sums[3:4], 1.0)
    pull = place * density_sum - sums
    return jnp.where(vector & live, pull / (-SCALE * EPS * EPS * density_sum), 0.0)


def whole_cell(blocks, live):
    weight = jnp.concatenate(
        [jnp.where(on, block[0, 3:4], 0.0) for on, block in zip(live, blocks)], axis=1
    )
    whole = jnp.concatenate([widened(block) for block in blocks], axis=1)
    vector = row_of(whole) < 3
    parts = grid_parts(jnp.where(vector, whole * SCALE, 0.0))
    place = parts[0] + parts[1] + parts[2]
    middle = jnp.sum(place * weight, axis=1, keepdims=True)
    middle = middle / jnp.sum(weight, axis=1, keepdims=True)
    return weight, place, jnp.where(vector, place - middle, 0.0)


def drift_of(total, centred, score, weight, total_slots):
    drift = drift_sum(total, centred, score)
    live = (row_of(drift) < 3) & (weight > 0.0)
    return jnp.where(live, drift * (1.0 / (SCALE * SCALE * SCALE * total_slots)), 0.0)


def finish(blocks, score, drifts, outs):
    scores_out, drift_out, start_out, speed_out = outs
    width = blocks[0].shape[2]
    square = functools.reduce(jnp.maximum, [rows_sum(drift * drift) for drift in drifts])
    largest = jnp.max(square, axis=1, keepdims=True)
    speed_out[...] = jnp.broadcast_to(jnp.sqrt(largest), speed_out.shape)
    scores_out[...] = score
    for part in range(width // 128):
        lanes = slice(part * 128, part * 128 + 128)
        for axis in range(3):
            drift_out[axis, part : part + 1, :] = drifts[0][axis : axis + 1, lanes]
            start_out[axis, part : part + 1, :] = blocks[0][0, axis : axis + 1, lanes]


def sweep_kernel(sources, *refs):
    count = len(sources)
    filled, blocks, refs = refs[0], refs[1 : count + 1], list(refs[count + 1 :])
    own, following, refs = refs[:5], refs[5:13], refs[13:]
    outs, (key_ref, query_ref, moment_ref, sums_ref, totals_ref), refs = (
        refs[:4], refs[4:9], refs[9:]
    )
    flux_refs, refs = refs[:count], refs[count:]
    width = blocks[0].shape[2]
    half = 2 * width
    split_refs, refs = refs[:4], refs[4:]
    exponent_refs, distance_refs = refs[: len(refs) // 2], refs[len(refs) // 2 :]

    live = [lanes_of(owner_of(source), width) < filled[...] for source in sources]
    late = range(2, count)
    for index in late:
        _, _, key, query, moment = prepared(widened(blocks[index]), live[index])
        lanes = pl.ds((index - 2) * width, width)
        key_ref[lanes, :] = key
        query_ref[:, lanes] = query
        moment_ref[:, lanes] = moment
    weight, place, centred = whole_cell(blocks, live)
    lanes = [pl.ds((index - 2) * width, width) for index in late]
    keys = [own[0], following[0]] + [key_ref.at[lane, :] for lane in lanes]
    queries = [own[1], following[1]] + [query_ref.at[:, lane] for lane in lanes]
    moments = [own[2], following[2]] + [moment_ref.at[:, lane] for lane in lanes]
    exponent = exponent_of(looked_up(keys, width, 0), looked_up(queries, width, 1))

    sums_ref[:, 0:half] = following[3][...]
    sums_ref[:, half:] = jnp.zeros_like(sums_ref[:, half:])
    tiles = late_tiles(count, width)
    totals_ref[...] = jnp.zeros_like(totals_ref)
    lanes = [slice(index * width, index * width + width) for index in range(count)]
    scores = [None] * count
    fluxes = looked_up(flux_refs, width, 1)

    def score_blocks(*indices):
        for index in indices:
            at = lanes[index]
            scores[index] = scored(weight[:, at], place[:, at], joined(sums_ref[:, at]))
            flux_refs[index][...] = drift_rows(weight[:, at], centred[:, at], scores[index])

    mixed = sum(tile[0] < half for tile in tiles)

    def after(index):
        if index == mixed - 1:
            score_blocks(0, 1)

    stage(
        tiles, exponent, looked_up(moments, width, 1), sums_ref, exponent_refs, split_refs, None,
        after,
    )
    early = diagonal_tiles(0, width) + square_tiles(width, 0, width)
    early += diagonal_tiles(width, width)
    for tile, distances in zip(early, own[3:5] + following[4:8]):
        for job in add_distances(tile, distances, fluxes, totals_ref):
            job()
    score_blocks(*range(2, count))

    total_slots = count * width
    drifts = [None] * count

    def drift_block(index):
        at = lanes[index]
        drifts[index] = drift_of(
            totals_ref[:, at], centred[:, at], scores[index], weight[:, at], total_slots
        )

    turns = []
    for index in range(mixed):
        split_distances(exponent_refs[index], distance_refs[index])
        rows, columns = add_distances(tiles[index], distance_refs[index], fluxes, totals_ref)
        rows()
        turns.append((tiles[index][0], columns))
    for index in range(2):
        for key, columns in turns:
            if key // width == index:
                columns()
        drift_block(index)
    for index in range(mixed, len(tiles)):
        split_distances(exponent_refs[index], distance_refs[index])
        for job in add_distances(tiles[index], distance_refs[index], fluxes, totals_ref):
            job()
    for index in range(2, count):
        drift_block(index)
    finish(blocks, scores[0], drifts, outs)


def sweep_shapes(width, copies):
    parts = jax.ShapeDtypeStruct((3, width // 128, 128), f32)
    speeds = jax.ShapeDtypeStruct((copies, 128), f32)
    return [jax.ShapeDtypeStruct((8, width), f32), parts, parts, speeds]


def sweep(filled, blocks, sources):
    count, width = len(blocks), blocks[0].shape[2]
    slots, late = count * width, (count - 2) * width
    own = own_part(filled, blocks[0])
    following = next_part(filled, blocks[1], own[:3], own[3], sources[1])
    early = [*own[:3], *own[4:], *following]
    vector = pl.BlockSpec(memory_space=pltpu.VMEM)
    distances = [pltpu.VMEM((2 * tile[1], tile[3]), bf16) for tile in late_tiles(count, width)]
    return pl.pallas_call(
        functools.partial(sweep_kernel, sources),
        out_shape=sweep_shapes(width, 1),
        in_specs=[vector] * (1 + count + len(early)),
        out_specs=[vector] * 4,
        scratch_shapes=[
            pltpu.VMEM((late, DISTANCE_ROWS), bf16),
            pltpu.VMEM((DISTANCE_ROWS, late), bf16),
            pltpu.VMEM((16, late), bf16),
            pltpu.VMEM((16, slots), f32),
            pltpu.VMEM((DRIFT_ROWS // 2, slots), f32),
        ]
        + [pltpu.VMEM((DRIFT_ROWS, width), bf16)] * count
        + [pltpu.VMEM((width, width), bf16)] * 4
        + [pltpu.VMEM((tile[1], tile[3]), f32) for tile in late_tiles(count, width)]
        + distances,
        compiler_params=pltpu.CompilerParams(vmem_limit_bytes=24 << 20),
        name="sweep",
    )(filled, *blocks, *early)


def long_kernel(sources, filled, *refs):
    count = len(sources)
    blocks, outs, refs = refs[:count], refs[count : count + 4], refs[count + 4 :]
    key_ref, query_ref, moment_ref, flux_ref, sums_ref, totals_ref, exponent_ref, split_ref = refs
    width = blocks[0].shape[2]
    live = [lanes_of(owner_of(source), width) < filled[...] for source in sources]
    for index, (block, on) in enumerate(zip(blocks, live)):
        _, _, key, query, moment = prepared(widened(block), on)
        lanes = pl.ds(index * width, width)
        key_ref[lanes, :] = key
        query_ref[:, lanes] = query
        moment_ref[:, lanes] = moment
    weight, place, centred = whole_cell(blocks, live)
    sums_ref[...] = jnp.zeros_like(sums_ref)
    totals_ref[...] = jnp.zeros_like(totals_ref)

    def block_tile(key, query, both):
        start, first = (pl.multiple_of(block * width, width) for block in (key, query))
        return (start, width, first, width, width if both else 0)

    def fill(tile):
        key, keys, query, queries, _ = tile
        exponent_ref[...] = product(key_ref[pl.ds(key, keys), :], query_ref[:, pl.ds(query, queries)])

    def blobs(key, query, both):
        tile = block_tile(key, query, both)
        fill(tile)
        split_blobs(exponent_ref, split_ref)
        add_blobs(tile, split_ref, lambda at, size: moment_ref[:, pl.ds(at, size)], sums_ref)

    @pl.loop(0, count)
    def _(query):
        blobs(query, query, False)

        @pl.loop(query + 1, count)
        def _(key):
            blobs(key, query, True)

    score = scored(weight, place, joined(sums_ref[...]))
    flux_ref[...] = drift_rows(weight, centred, score)

    @pl.loop(0, count)
    def _(key):
        tile = block_tile(key, 0, False)
        fill(tile)
        split_distances(exponent_ref, split_ref)
        for job in add_distances(
            tile, split_ref, lambda at, size: flux_ref[:, pl.ds(at, size)], totals_ref
        ):
            job()

    own = slice(0, width)
    drift = drift_of(
        totals_ref[...], centred[:, own], score[:, own], weight[:, own], count * width
    )
    finish(blocks, score[:, own], [drift], outs)


def long_sweep(filled, blocks, sources, copies):
    count, width = len(blocks), blocks[0].shape[2]
    slots = count * width
    vector = pl.BlockSpec(memory_space=pltpu.VMEM)
    return pl.pallas_call(
        functools.partial(long_kernel, sources),
        out_shape=sweep_shapes(width, copies),
        in_specs=[vector] * (1 + count),
        out_specs=[vector] * 4,
        scratch_shapes=[
            pltpu.VMEM((slots, DISTANCE_ROWS), bf16),
            pltpu.VMEM((DISTANCE_ROWS, slots), bf16),
            pltpu.VMEM((16, slots), bf16),
            pltpu.VMEM((DRIFT_ROWS, slots), bf16),
            pltpu.VMEM((16, slots), f32),
            pltpu.VMEM((DRIFT_ROWS // 2, width), f32),
            pltpu.VMEM((width, width), f32),
            pltpu.VMEM((2 * width, width), bf16),
        ],
        compiler_params=pltpu.CompilerParams(vmem_limit_bytes=(16 << 20) + slots * 2688),
        name="sweep",
    )(filled, *blocks)


def swapped(value, axis, step):
    pairs = [(i, i ^ step) for i in range(lax.axis_size(axis))]
    return lax.ppermute(value, axis, pairs)


def bits(size):
    return [1 << bit for bit in range(size.bit_length() - 1)]


ROUNDS = ((2, 3, 1, 0), (3, 2, 0, 1), (1, 0, 3, 2))


def gathered(block):
    size = lax.axis_size("sharers")
    if size == len(ROUNDS) + 1:
        blocks, sources = [block], [tuple(range(size))]
        for targets in ROUNDS:
            blocks.append(lax.ppermute(block, "sharers", list(enumerate(targets))))
            sources.append(tuple(targets.index(i) for i in range(size)))
        return blocks, sources
    for step in bits(size):
        block = jnp.concatenate([block, swapped(block, "sharers", step)], axis=0)
    sources = [tuple(i ^ step for i in range(size)) for step in range(size)]
    return [block[i : i + 1] for i in range(size)], sources


def local(velocities, weights, counts):
    filled = counts.reshape(1, 1)
    blocks, sources = gathered(jnp.concatenate([velocities, weights[:, None]], axis=1))
    if len(blocks) == len(ROUNDS) + 1:
        scores, drift, start, speeds = sweep(filled, blocks, sources)
        for step in bits(lax.axis_size("cells")):
            speeds = jnp.maximum(speeds, swapped(speeds, "cells", 2 * step - 1))
        largest = speeds
    else:
        axes = ("cells", "sharers")
        scores, drift, start, speeds = long_sweep(filled, blocks, sources, lax.axis_size(axes))
        largest = jnp.max(lax.all_to_all(speeds[:, None], axes, 0, 0, tiled=True), axis=0)
    time_step = 0.5 / (largest + 1e-06)
    moved = start + time_step[None] * drift
    return moved.reshape(velocities.shape), scores[None, 0:3]


def solution(mesh):
    in_specs = (
        P(("groups", "cells"), None, "sharers"),
        P(("groups", "cells"), "sharers"),
        P(("groups", "cells")),
    )
    out_specs = (P(("groups", "cells"), None, "sharers"), P(("groups", "cells"), None, "sharers"))
    return jax.shard_map(local, mesh=mesh, in_specs=in_specs, out_specs=out_specs, check_vma=False)
```

```python
import functools
import functools
import math

import jax
import jax.numpy as jnp
from jax import lax
from jax.experimental import pallas as pl
from jax.experimental.pallas import tpu as pltpu
from jax.sharding import PartitionSpec as P

EPS = 0.35
SCALE = math.sqrt(math.log2(math.e) / (2.0 * EPS * EPS))
GRID = 4.0
TINY = 1e-30
GROUP = 32
DISTANCE_ROWS = 64
DRIFT_ROWS = 64
bf16, f32 = jnp.bfloat16, jnp.float32


def round_bf16(value):
    return value.astype(bf16).astype(f32)


def pieces(value, count):
    parts = []
    for _ in range(count):
        part = round_bf16(value)
        parts.append(part)
        value = value - part
    return parts


def row_of(value):
    return lax.broadcasted_iota(jnp.int32, value.shape, 0)


def rows_sum(value):
    return jnp.sum(value, axis=0, keepdims=True)


def stacked(groups):
    if len(groups) % 2:
        groups = groups + [jnp.zeros_like(groups[0])]
    return jnp.concatenate(groups, axis=0).astype(bf16)


def scalar_groups(value, like):
    row = row_of(like)
    first, second, third = pieces(value, 3)
    low = jnp.where(row == 0, first, jnp.where(row == 1, second, jnp.where(row == 2, third, 0.0)))
    high = jnp.where(row == 3, first, jnp.where(row == 4, second, jnp.where(row == 5, third, 0.0)))
    ones_low, ones_high = row < 3, (row >= 3) & (row < 6)
    return jnp.where(ones_high, 1.0, low), jnp.where(ones_low, 1.0, high)


def grid_parts(place):
    coarse = jnp.floor(place * GRID + 0.5) * (1.0 / GRID)
    return [coarse] + pieces(place - coarse, 2)


def distance_features(parts):
    coarse, fine, rest = parts
    minor = fine + rest
    query_norm, key_norm = scalar_groups(-rows_sum(coarse * coarse), coarse)
    query_less, key_less = scalar_groups(-rows_sum(minor * (2.0 * coarse + minor)), coarse)
    key = [coarse, key_norm, paired(coarse, coarse), paired(fine, rest), key_less]
    key += [paired(fine, fine), paired(rest, rest)]
    coarse, fine, rest = coarse * 2.0, fine * 2.0, rest * 2.0
    query = [coarse, query_norm, paired(fine, rest), paired(coarse, coarse), query_less]
    query += [paired(fine, rest)] * 2
    return stacked(key), stacked(query)


def paired(first, second):
    return first + pltpu.roll(second, 4, 0)


def weighted_rows(weight, value):
    row = row_of(value)
    whole = jnp.where(row < 3, value, jnp.where(row == 3, 1.0, 0.0)) * weight
    first, second, third = pieces(whole, 3)
    return stacked([first, second + pltpu.roll(third, 4, 0)])


def product(left, right):
    return jnp.dot(left, right, preferred_element_type=f32)


def store_split(ref, rows, matrix):
    half = ref.shape[0] // 2
    upper = matrix.astype(bf16)
    ref[rows, :] = upper
    ref[pl.ds(half + rows.start, rows.size), :] = (matrix - upper.astype(f32)).astype(bf16)


def sum_rows(left, ref):
    return product(jnp.concatenate([left, left], axis=1), ref[...])


def sum_columns(left, ref):
    both = lax.dot_general(left, ref[...], (((1,), (1,)), ((), ())), preferred_element_type=f32)
    half = ref.shape[0] // 2
    return both[:, :half] + both[:, half:]


def sum_rows_less(left, ref):
    half = ref.shape[0] // 2
    both = product(left, ref[:half, :])
    few = left.shape[0] // 2
    return both[:few] + product(left[:few], ref[half:, :]), both[few:]


def sum_columns_less(left, ref):
    half, few = ref.shape[0] // 2, left.shape[0] // 2
    turned = (((1,), (1,)), ((), ()))
    both = lax.dot_general(left, ref[:half, :], turned, preferred_element_type=f32)
    less = lax.dot_general(left[:few], ref[half:, :], turned, preferred_element_type=f32)
    return both[:few] + less, both[few:]


def joined(total):
    upper, lower = total[0:8], total[8:16]
    return upper + lower + pltpu.roll(lower, 4, 0)


def drift_rows(weight, place, score):
    row = row_of(place)
    base = place + jnp.where(row == 3, 1.0, 0.0) + pltpu.roll(score, 4, 0)
    cubic = rows_sum(place * place) * score - rows_sum(place * score) * place
    groups = [weight * base]
    for i in range(3):
        here = slice(i, i + 1)
        groups.append(weight * jnp.where(row == 3, cubic[here], place[here] * base))
    return stacked(sum(map(list, zip(*[pieces(group, 2) for group in groups])), []))


def drift_sum(total, place, score):
    row = row_of(place)
    first, *rest = [total[8 * i : 8 * i + 8] for i in range(4)]
    turned = [pltpu.roll(group, 4, 0) for group in rest]
    count, scores = first[3:4], pltpu.roll(first, 4, 0)
    square, both = rows_sum(place * place), rows_sum(place * score)
    trace = rest[0][0:1] + rest[1][1:2] + rest[2][2:3]
    cross = turned[0][0:1] + turned[1][1:2] + turned[2][2:3]
    drift = score * (square * count - 2.0 * rows_sum(place * first) + trace) - square * scores
    drift += both * first + place * (
        rows_sum(place * scores) + rows_sum(score * first) - both * count - cross
    )
    ends = []
    for i in range(3):
        here = slice(i, i + 1)
        drift += 2.0 * place[here] * turned[i] - score[here] * rest[i]
        ends.append(rows_sum(place * turned[i]) + rest[i][3:4])
    return drift - jnp.where(row == 0, ends[0], jnp.where(row == 1, ends[1], ends[2]))


def widened(block):
    return jnp.concatenate([block[0], jnp.zeros_like(block[0])], axis=0)


def prepared(whole, live):
    weight = jnp.where(live, whole[3:4], 0.0)
    parts = grid_parts(jnp.where(row_of(whole) < 3, whole * SCALE, 0.0))
    place = parts[0] + parts[1] + parts[2]
    key, query = distance_features(parts)
    return weight, place, key.T, query, weighted_rows(weight, place)


def split_blobs(exponent, split):
    for group in range(0, exponent.shape[0], GROUP):
        rows = pl.ds(group, GROUP)
        store_split(split, rows, jnp.exp2(exponent[rows, :]))


def split_distances(exponent, split):
    for group in range(0, exponent.shape[0], GROUP):
        rows = pl.ds(group, GROUP)
        negative = jnp.minimum(exponent[rows, :], -TINY)
        store_split(split, rows, negative * lax.rsqrt(-negative))


def diagonal_tiles(start, width):
    half = width // 2
    return [(start, half, start, half, 0), (start + half, half, start, width, half)]


def add_blobs(tile, split, moments, sums_ref):
    key, keys, query, queries, turned = tile
    sums_ref[:, pl.ds(query, queries)] += sum_rows(moments(key, keys), split)
    if turned:
        sums_ref[:, pl.ds(key, keys)] += sum_columns(moments(query, turned), split.at[:, 0:turned])


def add_distances(tile, split, fluxes, totals_ref):
    key, keys, query, queries, turned = tile

    def rows():
        upper, lower = sum_rows_less(fluxes(key, keys), split)
        totals_ref[:, pl.ds(query, queries)] += upper + lower

    def columns():
        upper, lower = sum_columns_less(fluxes(query, turned), split.at[:, 0:turned])
        totals_ref[:, pl.ds(key, keys)] += upper + lower

    return rows, columns if turned else lambda: None


def stage(tiles, exponent, moments, sums_ref, exponent_refs, split_refs, distance_refs,
          after=lambda index: None):
    def buffer(index):
        _, keys, _, queries, _ = tiles[index]
        return exponent_refs[index % len(exponent_refs)].at[0:keys, 0:queries]

    buffer(0)[...] = exponent(tiles[0])
    for index, tile in enumerate(tiles):
        if index + 1 < len(tiles):
            buffer(index + 1)[...] = exponent(tiles[index + 1])
        split = split_refs[index % 2].at[0 : 2 * tile[1], 0 : tile[3]]
        split_blobs(buffer(index), split)
        add_blobs(tile, split, moments, sums_ref)
        if distance_refs is not None:
            split_distances(buffer(index), distance_refs[index])
        after(index)


def looked_up(refs, width, axis):
    def read(start, size):
        at = pl.ds(start % width, size)
        ref = refs[start // width]
        return ref[at, :] if axis == 0 else ref[:, at]

    return read


def exponent_of(keys, queries):
    return lambda tile: product(keys(tile[0], tile[1]), queries(tile[2], tile[3]))


def lanes_of(source, width):
    return lax.broadcasted_iota(jnp.int32, (1, width), 1) + source * width


def owner_of(sources):
    here = lax.axis_index("sharers")
    return sum(jnp.where(here == i, source, 0) for i, source in enumerate(sources))


def own_kernel(filled, block, key_out, query_out, moment_out, sums_out, first_out, second_out,
               *scratch):
    width = block.shape[2]
    live = lanes_of(lax.axis_index("sharers"), width) < filled[...]
    _, _, key, query, moment = prepared(widened(block), live)
    key_out[...] = key
    query_out[...] = query
    moment_out[...] = moment
    sums_out[...] = jnp.zeros_like(sums_out)
    exponent = exponent_of(looked_up([key_out], width, 0), looked_up([query_out], width, 1))
    moments = looked_up([moment_out], width, 1)
    tiles = diagonal_tiles(0, width)
    stage(tiles, exponent, moments, sums_out, scratch[:2], scratch[2:], (first_out, second_out))


def next_kernel(sources, filled, block, own_key, own_query, own_moment, own_sums, key_out,
                query_out, moment_out, sums_out, *refs):
    width = block.shape[2]
    live = lanes_of(owner_of(sources), width) < filled[...]
    _, _, key, query, moment = prepared(widened(block), live)
    key_out[...] = key
    query_out[...] = query
    moment_out[...] = moment
    sums_out[:, 0:width] = own_sums[...]
    sums_out[:, width:] = jnp.zeros_like(own_sums)
    exponent = exponent_of(
        looked_up([own_key, key_out], width, 0), looked_up([own_query, query_out], width, 1)
    )
    moments = looked_up([own_moment, moment_out], width, 1)
    tiles = square_tiles(width, 0, width) + diagonal_tiles(width, width)
    distances, scratch = refs[: len(tiles)], refs[len(tiles) :]
    stage(tiles, exponent, moments, sums_out, scratch[:2], scratch[2:], distances)


def feature_shapes(width):
    return [
        jax.ShapeDtypeStruct((width, DISTANCE_ROWS), bf16),
        jax.ShapeDtypeStruct((DISTANCE_ROWS, width), bf16),
        jax.ShapeDtypeStruct((16, width), bf16),
    ]


def diagonal_shapes(width):
    half = width // 2
    return [
        jax.ShapeDtypeStruct((2 * half, half), bf16),
        jax.ShapeDtypeStruct((2 * half, width), bf16),
    ]


def stage_scratch(width):
    half = width // 2
    return [pltpu.VMEM((half, width), f32)] * 2 + [pltpu.VMEM((width, width), bf16)] * 2


def own_part(filled, block):
    width = block.shape[2]
    vector = pl.BlockSpec(memory_space=pltpu.VMEM)
    shapes = feature_shapes(width) + [jax.ShapeDtypeStruct((16, width), f32)] + diagonal_shapes(width)
    return pl.pallas_call(
        own_kernel,
        out_shape=shapes,
        in_specs=[vector] * 2,
        out_specs=[vector] * len(shapes),
        scratch_shapes=stage_scratch(width),
        compiler_params=pltpu.CompilerParams(vmem_limit_bytes=16 << 20),
        name="own",
    )(filled, block)


def next_part(filled, block, features, sums, sources):
    width = block.shape[2]
    vector = pl.BlockSpec(memory_space=pltpu.VMEM)
    shapes = feature_shapes(width) + [jax.ShapeDtypeStruct((16, 2 * width), f32)]
    shapes += [jax.ShapeDtypeStruct((width, width), bf16)] * 2 + diagonal_shapes(width)
    return pl.pallas_call(
        functools.partial(next_kernel, sources),
        out_shape=shapes,
        in_specs=[vector] * 6,
        out_specs=[vector] * len(shapes),
        scratch_shapes=stage_scratch(width),
        compiler_params=pltpu.CompilerParams(vmem_limit_bytes=20 << 20),
        name="next",
    )(filled, block, *features, sums)


def square_tiles(key, query, width):
    half = width // 2
    return [(key + part, half, query, width, width) for part in (0, half)]


def late_tiles(count, width):
    tiles, late = [], range(2, count)
    for query in late:
        for key in range(2):
            tiles += square_tiles(key * width, query * width, width)
    for query in late:
        for key in range(2, query):
            tiles += square_tiles(key * width, query * width, width)
    for query in late:
        tiles += diagonal_tiles(query * width, width)
    return tiles


def scored(weight, place, sums):
    vector, live = row_of(place) < 3, weight > 0.0
    density_sum = jnp.where(live, sums[3:4], 1.0)
    pull = place * density_sum - sums
    return jnp.where(vector & live, pull / (-SCALE * EPS * EPS * density_sum), 0.0)


def whole_cell(blocks, live):
    weight = jnp.concatenate(
        [jnp.where(on, block[0, 3:4], 0.0) for on, block in zip(live, blocks)], axis=1
    )
    whole = jnp.concatenate([widened(block) for block in blocks], axis=1)
    vector = row_of(whole) < 3
    parts = grid_parts(jnp.where(vector, whole * SCALE, 0.0))
    place = parts[0] + parts[1] + parts[2]
    middle = jnp.sum(place * weight, axis=1, keepdims=True)
    middle = middle / jnp.sum(weight, axis=1, keepdims=True)
    return weight, place, jnp.where(vector, place - middle, 0.0)


def drift_of(total, centred, score, weight, total_slots):
    drift = drift_sum(total, centred, score)
    live = (row_of(drift) < 3) & (weight > 0.0)
    return jnp.where(live, drift * (1.0 / (SCALE * SCALE * SCALE * total_slots)), 0.0)


def finish(blocks, score, drifts, outs):
    scores_out, drift_out, start_out, speed_out = outs
    width = blocks[0].shape[2]
    square = functools.reduce(jnp.maximum, [rows_sum(drift * drift) for drift in drifts])
    largest = jnp.max(square, axis=1, keepdims=True)
    speed_out[...] = jnp.broadcast_to(jnp.sqrt(largest), speed_out.shape)
    scores_out[...] = score
    for part in range(width // 128):
        lanes = slice(part * 128, part * 128 + 128)
        for axis in range(3):
            drift_out[axis, part : part + 1, :] = drifts[0][axis : axis + 1, lanes]
            start_out[axis, part : part + 1, :] = blocks[0][0, axis : axis + 1, lanes]


def sweep_kernel(sources, *refs):
    count = len(sources)
    filled, blocks, refs = refs[0], refs[1 : count + 1], list(refs[count + 1 :])
    own, following, refs = refs[:5], refs[5:13], refs[13:]
    outs, (key_ref, query_ref, moment_ref, sums_ref, totals_ref), refs = (
        refs[:4], refs[4:9], refs[9:]
    )
    flux_refs, refs = refs[:count], refs[count:]
    width = blocks[0].shape[2]
    half = 2 * width
    split_refs, refs = refs[:2], refs[2:]
    exponent_refs, distance_refs = refs[: len(refs) // 2], refs[len(refs) // 2 :]

    live = [lanes_of(owner_of(source), width) < filled[...] for source in sources]
    late = range(2, count)
    for index in late:
        _, _, key, query, moment = prepared(widened(blocks[index]), live[index])
        lanes = pl.ds((index - 2) * width, width)
        key_ref[lanes, :] = key
        query_ref[:, lanes] = query
        moment_ref[:, lanes] = moment
    weight, place, centred = whole_cell(blocks, live)
    lanes = [pl.ds((index - 2) * width, width) for index in late]
    keys = [own[0], following[0]] + [key_ref.at[lane, :] for lane in lanes]
    queries = [own[1], following[1]] + [query_ref.at[:, lane] for lane in lanes]
    moments = [own[2], following[2]] + [moment_ref.at[:, lane] for lane in lanes]
    exponent = exponent_of(looked_up(keys, width, 0), looked_up(queries, width, 1))

    sums_ref[:, 0:half] = following[3][...]
    sums_ref[:, half:] = jnp.zeros_like(sums_ref[:, half:])
    tiles = late_tiles(count, width)
    totals_ref[...] = jnp.zeros_like(totals_ref)
    lanes = [slice(index * width, index * width + width) for index in range(count)]
    scores = [None] * count
    fluxes = looked_up(flux_refs, width, 1)

    def score_blocks(*indices):
        for index in indices:
            at = lanes[index]
            scores[index] = scored(weight[:, at], place[:, at], joined(sums_ref[:, at]))
            flux_refs[index][...] = drift_rows(weight[:, at], centred[:, at], scores[index])

    mixed = sum(tile[0] < half for tile in tiles)

    def after(index):
        if index == mixed - 1:
            score_blocks(0, 1)

    stage(
        tiles, exponent, looked_up(moments, width, 1), sums_ref, exponent_refs, split_refs, None,
        after,
    )
    early = diagonal_tiles(0, width) + square_tiles(width, 0, width)
    early += diagonal_tiles(width, width)
    for tile, distances in zip(early, own[3:5] + following[4:8]):
        for job in add_distances(tile, distances, fluxes, totals_ref):
            job()
    score_blocks(*range(2, count))

    total_slots = count * width
    drifts = [None] * count

    def drift_block(index):
        at = lanes[index]
        drifts[index] = drift_of(
            totals_ref[:, at], centred[:, at], scores[index], weight[:, at], total_slots
        )

    turns = []
    for index in range(mixed):
        split_distances(exponent_refs[index], distance_refs[index])
        rows, columns = add_distances(tiles[index], distance_refs[index], fluxes, totals_ref)
        rows()
        turns.append((tiles[index][0], columns))
    for index in range(2):
        for key, columns in turns:
            if key // width == index:
                columns()
        drift_block(index)
    for index in range(mixed, len(tiles)):
        split_distances(exponent_refs[index], distance_refs[index])
        for job in add_distances(tiles[index], distance_refs[index], fluxes, totals_ref):
            job()
    for index in range(2, count):
        drift_block(index)
    finish(blocks, scores[0], drifts, outs)


def sweep_shapes(width, copies):
    parts = jax.ShapeDtypeStruct((3, width // 128, 128), f32)
    speeds = jax.ShapeDtypeStruct((copies, 128), f32)
    return [jax.ShapeDtypeStruct((8, width), f32), parts, parts, speeds]


def sweep(filled, blocks, sources):
    count, width = len(blocks), blocks[0].shape[2]
    slots, late = count * width, (count - 2) * width
    own = own_part(filled, blocks[0])
    following = next_part(filled, blocks[1], own[:3], own[3], sources[1])
    early = [*own[:3], *own[4:], *following]
    vector = pl.BlockSpec(memory_space=pltpu.VMEM)
    distances = [pltpu.VMEM((2 * tile[1], tile[3]), bf16) for tile in late_tiles(count, width)]
    return pl.pallas_call(
        functools.partial(sweep_kernel, sources),
        out_shape=sweep_shapes(width, 1),
        in_specs=[vector] * (1 + count + len(early)),
        out_specs=[vector] * 4,
        scratch_shapes=[
            pltpu.VMEM((late, DISTANCE_ROWS), bf16),
            pltpu.VMEM((DISTANCE_ROWS, late), bf16),
            pltpu.VMEM((16, late), bf16),
            pltpu.VMEM((16, slots), f32),
            pltpu.VMEM((DRIFT_ROWS // 2, slots), f32),
        ]
        + [pltpu.VMEM((DRIFT_ROWS, width), bf16)] * count
        + [pltpu.VMEM((width, width), bf16)] * 2
        + [pltpu.VMEM((tile[1], tile[3]), f32) for tile in late_tiles(count, width)]
        + distances,
        compiler_params=pltpu.CompilerParams(vmem_limit_bytes=24 << 20),
        name="sweep",
    )(filled, *blocks, *early)


def long_kernel(sources, filled, *refs):
    count = len(sources)
    blocks, outs, refs = refs[:count], refs[count : count + 4], refs[count + 4 :]
    key_ref, query_ref, moment_ref, flux_ref, sums_ref, totals_ref, exponent_ref, split_ref = refs
    width = blocks[0].shape[2]
    live = [lanes_of(owner_of(source), width) < filled[...] for source in sources]
    for index, (block, on) in enumerate(zip(blocks, live)):
        _, _, key, query, moment = prepared(widened(block), on)
        lanes = pl.ds(index * width, width)
        key_ref[lanes, :] = key
        query_ref[:, lanes] = query
        moment_ref[:, lanes] = moment
    weight, place, centred = whole_cell(blocks, live)
    sums_ref[...] = jnp.zeros_like(sums_ref)
    totals_ref[...] = jnp.zeros_like(totals_ref)

    def block_tile(key, query, both):
        start, first = (pl.multiple_of(block * width, width) for block in (key, query))
        return (start, width, first, width, width if both else 0)

    def fill(tile):
        key, keys, query, queries, _ = tile
        exponent_ref[...] = product(key_ref[pl.ds(key, keys), :], query_ref[:, pl.ds(query, queries)])

    def blobs(key, query, both):
        tile = block_tile(key, query, both)
        fill(tile)
        split_blobs(exponent_ref, split_ref)
        add_blobs(tile, split_ref, lambda at, size: moment_ref[:, pl.ds(at, size)], sums_ref)

    @pl.loop(0, count)
    def _(query):
        blobs(query, query, False)

        @pl.loop(query + 1, count)
        def _(key):
            blobs(key, query, True)

    score = scored(weight, place, joined(sums_ref[...]))
    flux_ref[...] = drift_rows(weight, centred, score)

    @pl.loop(0, count)
    def _(key):
        tile = block_tile(key, 0, False)
        fill(tile)
        split_distances(exponent_ref, split_ref)
        for job in add_distances(
            tile, split_ref, lambda at, size: flux_ref[:, pl.ds(at, size)], totals_ref
        ):
            job()

    own = slice(0, width)
    drift = drift_of(
        totals_ref[...], centred[:, own], score[:, own], weight[:, own], count * width
    )
    finish(blocks, score[:, own], [drift], outs)


def long_sweep(filled, blocks, sources, copies):
    count, width = len(blocks), blocks[0].shape[2]
    slots = count * width
    vector = pl.BlockSpec(memory_space=pltpu.VMEM)
    return pl.pallas_call(
        functools.partial(long_kernel, sources),
        out_shape=sweep_shapes(width, copies),
        in_specs=[vector] * (1 + count),
        out_specs=[vector] * 4,
        scratch_shapes=[
            pltpu.VMEM((slots, DISTANCE_ROWS), bf16),
            pltpu.VMEM((DISTANCE_ROWS, slots), bf16),
            pltpu.VMEM((16, slots), bf16),
            pltpu.VMEM((DRIFT_ROWS, slots), bf16),
            pltpu.VMEM((16, slots), f32),
            pltpu.VMEM((DRIFT_ROWS // 2, width), f32),
            pltpu.VMEM((width, width), f32),
            pltpu.VMEM((2 * width, width), bf16),
        ],
        compiler_params=pltpu.CompilerParams(vmem_limit_bytes=(16 << 20) + slots * 2688),
        name="sweep",
    )(filled, *blocks)


def swapped(value, axis, step):
    pairs = [(i, i ^ step) for i in range(lax.axis_size(axis))]
    return lax.ppermute(value, axis, pairs)


def bits(size):
    return [1 << bit for bit in range(size.bit_length() - 1)]


ROUNDS = ((2, 3, 1, 0), (3, 2, 0, 1), (1, 0, 3, 2))


def gathered(block):
    size = lax.axis_size("sharers")
    if size == len(ROUNDS) + 1:
        blocks, sources = [block], [tuple(range(size))]
        for targets in ROUNDS:
            blocks.append(lax.ppermute(block, "sharers", list(enumerate(targets))))
            sources.append(tuple(targets.index(i) for i in range(size)))
        return blocks, sources
    for step in bits(size):
        block = jnp.concatenate([block, swapped(block, "sharers", step)], axis=0)
    sources = [tuple(i ^ step for i in range(size)) for step in range(size)]
    return [block[i : i + 1] for i in range(size)], sources


def local(velocities, weights, counts):
    filled = counts.reshape(1, 1)
    blocks, sources = gathered(jnp.concatenate([velocities, weights[:, None]], axis=1))
    if len(blocks) == len(ROUNDS) + 1:
        scores, drift, start, speeds = sweep(filled, blocks, sources)
        for step in bits(lax.axis_size("cells")):
            speeds = jnp.maximum(speeds, swapped(speeds, "cells", 2 * step - 1))
        largest = speeds
    else:
        axes = ("cells", "sharers")
        scores, drift, start, speeds = long_sweep(filled, blocks, sources, lax.axis_size(axes))
        largest = jnp.max(lax.all_to_all(speeds[:, None], axes, 0, 0, tiled=True), axis=0)
    time_step = 0.5 / (largest + 1e-06)
    moved = start + time_step[None] * drift
    return moved.reshape(velocities.shape), scores[None, 0:3]


def solution(mesh):
    in_specs = (
        P(("groups", "cells"), None, "sharers"),
        P(("groups", "cells"), "sharers"),
        P(("groups", "cells")),
    )
    out_specs = (P(("groups", "cells"), None, "sharers"), P(("groups", "cells"), None, "sharers"))
    return jax.shard_map(local, mesh=mesh, in_specs=in_specs, out_specs=out_specs, check_vma=False)
```

```python
import functools
import functools
import math

import jax
import jax.numpy as jnp
from jax import lax
from jax.experimental import pallas as pl
from jax.experimental.pallas import tpu as pltpu
from jax.sharding import PartitionSpec as P

EPS = 0.35
SCALE = math.sqrt(math.log2(math.e) / (2.0 * EPS * EPS))
GRID = 4.0
TINY = 1e-30
GROUP = 32
DISTANCE_ROWS = 96
DRIFT_ROWS = 64
bf16, f32 = jnp.bfloat16, jnp.float32


def round_bf16(value):
    return value.astype(bf16).astype(f32)


def pieces(value, count):
    parts = []
    for _ in range(count):
        part = round_bf16(value)
        parts.append(part)
        value = value - part
    return parts


def row_of(value):
    return lax.broadcasted_iota(jnp.int32, value.shape, 0)


def rows_sum(value):
    return jnp.sum(value, axis=0, keepdims=True)


def stacked(groups):
    if len(groups) % 2:
        groups = groups + [jnp.zeros_like(groups[0])]
    return jnp.concatenate(groups, axis=0).astype(bf16)


def scalar_groups(value, like):
    row = row_of(like)
    first, second, third = pieces(value, 3)
    low = jnp.where(row == 0, first, jnp.where(row == 1, second, jnp.where(row == 2, third, 0.0)))
    high = jnp.where(row == 3, first, jnp.where(row == 4, second, jnp.where(row == 5, third, 0.0)))
    ones_low, ones_high = row < 3, (row >= 3) & (row < 6)
    return jnp.where(ones_high, 1.0, low), jnp.where(ones_low, 1.0, high)


def grid_parts(place):
    coarse = jnp.floor(place * GRID + 0.5) * (1.0 / GRID)
    return [coarse] + pieces(place - coarse, 2)


def distance_features(parts):
    coarse, fine, rest = parts
    minor = fine + rest
    query_norm, key_norm = scalar_groups(-rows_sum(coarse * coarse), coarse)
    query_less, key_less = scalar_groups(-rows_sum(minor * (2.0 * coarse + minor)), coarse)
    key = [coarse, key_norm, coarse, coarse, fine, rest, key_less, fine, fine, rest, rest]
    coarse, fine, rest = coarse * 2.0, fine * 2.0, rest * 2.0
    query = [coarse, query_norm, fine, rest, coarse, coarse, query_less, fine, rest, fine, rest]
    return stacked(key), stacked(query)


def weighted_rows(weight, value):
    row = row_of(value)
    whole = jnp.where(row < 3, value, jnp.where(row == 3, 1.0, 0.0)) * weight
    first, second, third = pieces(whole, 3)
    return stacked([first, second + pltpu.roll(third, 4, 0)])


def product(left, right):
    return jnp.dot(left, right, preferred_element_type=f32)


def store_split(ref, rows, matrix):
    half = ref.shape[0] // 2
    upper = matrix.astype(bf16)
    ref[rows, :] = upper
    ref[pl.ds(half + rows.start, rows.size), :] = (matrix - upper.astype(f32)).astype(bf16)


def sum_rows(left, ref):
    return product(jnp.concatenate([left, left], axis=1), ref[...])


def sum_columns(left, ref):
    both = lax.dot_general(left, ref[...], (((1,), (1,)), ((), ())), preferred_element_type=f32)
    half = ref.shape[0] // 2
    return both[:, :half] + both[:, half:]


def sum_rows_less(left, ref):
    half = ref.shape[0] // 2
    both = product(left, ref[:half, :])
    few = left.shape[0] // 2
    return both[:few] + product(left[:few], ref[half:, :]), both[few:]


def sum_columns_less(left, ref):
    half, few = ref.shape[0] // 2, left.shape[0] // 2
    turned = (((1,), (1,)), ((), ()))
    both = lax.dot_general(left, ref[:half, :], turned, preferred_element_type=f32)
    less = lax.dot_general(left[:few], ref[half:, :], turned, preferred_element_type=f32)
    return both[:few] + less, both[few:]


def joined(total):
    upper, lower = total[0:8], total[8:16]
    return upper + lower + pltpu.roll(lower, 4, 0)


def drift_rows(weight, place, score):
    row = row_of(place)
    base = place + jnp.where(row == 3, 1.0, 0.0) + pltpu.roll(score, 4, 0)
    cubic = rows_sum(place * place) * score - rows_sum(place * score) * place
    groups = [weight * base]
    for i in range(3):
        here = slice(i, i + 1)
        groups.append(weight * jnp.where(row == 3, cubic[here], place[here] * base))
    return stacked(sum(map(list, zip(*[pieces(group, 2) for group in groups])), []))


def drift_sum(total, place, score):
    row = row_of(place)
    first, *rest = [total[8 * i : 8 * i + 8] for i in range(4)]
    turned = [pltpu.roll(group, 4, 0) for group in rest]
    count, scores = first[3:4], pltpu.roll(first, 4, 0)
    square, both = rows_sum(place * place), rows_sum(place * score)
    trace = rest[0][0:1] + rest[1][1:2] + rest[2][2:3]
    cross = turned[0][0:1] + turned[1][1:2] + turned[2][2:3]
    drift = score * (square * count - 2.0 * rows_sum(place * first) + trace) - square * scores
    drift += both * first + place * (
        rows_sum(place * scores) + rows_sum(score * first) - both * count - cross
    )
    ends = []
    for i in range(3):
        here = slice(i, i + 1)
        drift += 2.0 * place[here] * turned[i] - score[here] * rest[i]
        ends.append(rows_sum(place * turned[i]) + rest[i][3:4])
    return drift - jnp.where(row == 0, ends[0], jnp.where(row == 1, ends[1], ends[2]))


def widened(block):
    return jnp.concatenate([block[0], jnp.zeros_like(block[0])], axis=0)


def prepared(whole, live):
    weight = jnp.where(live, whole[3:4], 0.0)
    parts = grid_parts(jnp.where(row_of(whole) < 3, whole * SCALE, 0.0))
    place = parts[0] + parts[1] + parts[2]
    key, query = distance_features(parts)
    return weight, place, key.T, query, weighted_rows(weight, place)


def split_blobs(exponent, split):
    for group in range(0, exponent.shape[0], GROUP):
        rows = pl.ds(group, GROUP)
        store_split(split, rows, jnp.exp2(exponent[rows, :]))


def split_distances(exponent, split):
    for group in range(0, exponent.shape[0], GROUP):
        rows = pl.ds(group, GROUP)
        negative = jnp.minimum(exponent[rows, :], -TINY)
        store_split(split, rows, negative * lax.rsqrt(-negative))


def diagonal_tiles(start, width):
    half = width // 2
    return [(start, half, start, half, 0), (start + half, half, start, width, half)]


def add_blobs(tile, split, moments, sums_ref):
    key, keys, query, queries, turned = tile
    sums_ref[:, pl.ds(query, queries)] += sum_rows(moments(key, keys), split)
    if turned:
        sums_ref[:, pl.ds(key, keys)] += sum_columns(moments(query, turned), split.at[:, 0:turned])


def add_distances(tile, split, fluxes, totals_ref):
    key, keys, query, queries, turned = tile

    def rows():
        upper, lower = sum_rows_less(fluxes(key, keys), split)
        totals_ref[:, pl.ds(query, queries)] += upper + lower

    def columns():
        upper, lower = sum_columns_less(fluxes(query, turned), split.at[:, 0:turned])
        totals_ref[:, pl.ds(key, keys)] += upper + lower

    return rows, columns if turned else lambda: None


def stage(tiles, exponent, moments, sums_ref, exponent_refs, split_refs, distance_refs,
          after=lambda index: None):
    def buffer(index):
        _, keys, _, queries, _ = tiles[index]
        return exponent_refs[index % len(exponent_refs)].at[0:keys, 0:queries]

    ahead = 2 if len(exponent_refs) > 2 else 1
    for index in range(ahead):
        buffer(index)[...] = exponent(tiles[index])
    for index, tile in enumerate(tiles):
        if index + ahead < len(tiles):
            buffer(index + ahead)[...] = exponent(tiles[index + ahead])
        split = split_refs[index % 2].at[0 : 2 * tile[1], 0 : tile[3]]
        split_blobs(buffer(index), split)
        add_blobs(tile, split, moments, sums_ref)
        if distance_refs is not None:
            split_distances(buffer(index), distance_refs[index])
        after(index)


def looked_up(refs, width, axis):
    def read(start, size):
        at = pl.ds(start % width, size)
        ref = refs[start // width]
        return ref[at, :] if axis == 0 else ref[:, at]

    return read


def exponent_of(keys, queries):
    return lambda tile: product(keys(tile[0], tile[1]), queries(tile[2], tile[3]))


def lanes_of(source, width):
    return lax.broadcasted_iota(jnp.int32, (1, width), 1) + source * width


def owner_of(sources):
    here = lax.axis_index("sharers")
    return sum(jnp.where(here == i, source, 0) for i, source in enumerate(sources))


def own_kernel(filled, block, key_out, query_out, moment_out, sums_out, first_out, second_out,
               *scratch):
    width = block.shape[2]
    live = lanes_of(lax.axis_index("sharers"), width) < filled[...]
    _, _, key, query, moment = prepared(widened(block), live)
    key_out[...] = key
    query_out[...] = query
    moment_out[...] = moment
    sums_out[...] = jnp.zeros_like(sums_out)
    exponent = exponent_of(looked_up([key_out], width, 0), looked_up([query_out], width, 1))
    moments = looked_up([moment_out], width, 1)
    tiles = diagonal_tiles(0, width)
    stage(tiles, exponent, moments, sums_out, scratch[:2], scratch[2:], (first_out, second_out))


def next_kernel(sources, filled, block, own_key, own_query, own_moment, own_sums, key_out,
                query_out, moment_out, sums_out, *refs):
    width = block.shape[2]
    live = lanes_of(owner_of(sources), width) < filled[...]
    _, _, key, query, moment = prepared(widened(block), live)
    key_out[...] = key
    query_out[...] = query
    moment_out[...] = moment
    sums_out[:, 0:width] = own_sums[...]
    sums_out[:, width:] = jnp.zeros_like(own_sums)
    exponent = exponent_of(
        looked_up([own_key, key_out], width, 0), looked_up([own_query, query_out], width, 1)
    )
    moments = looked_up([own_moment, moment_out], width, 1)
    tiles = square_tiles(width, 0, width) + diagonal_tiles(width, width)
    distances, scratch = refs[: len(tiles)], refs[len(tiles) :]
    stage(tiles, exponent, moments, sums_out, scratch[:2], scratch[2:], distances)


def feature_shapes(width):
    return [
        jax.ShapeDtypeStruct((width, DISTANCE_ROWS), bf16),
        jax.ShapeDtypeStruct((DISTANCE_ROWS, width), bf16),
        jax.ShapeDtypeStruct((16, width), bf16),
    ]


def diagonal_shapes(width):
    half = width // 2
    return [
        jax.ShapeDtypeStruct((2 * half, half), bf16),
        jax.ShapeDtypeStruct((2 * half, width), bf16),
    ]


def stage_scratch(width):
    half = width // 2
    return [pltpu.VMEM((half, width), f32)] * 2 + [pltpu.VMEM((width, width), bf16)] * 2


def own_part(filled, block):
    width = block.shape[2]
    vector = pl.BlockSpec(memory_space=pltpu.VMEM)
    shapes = feature_shapes(width) + [jax.ShapeDtypeStruct((16, width), f32)] + diagonal_shapes(width)
    return pl.pallas_call(
        own_kernel,
        out_shape=shapes,
        in_specs=[vector] * 2,
        out_specs=[vector] * len(shapes),
        scratch_shapes=stage_scratch(width),
        compiler_params=pltpu.CompilerParams(vmem_limit_bytes=16 << 20),
        name="own",
    )(filled, block)


def next_part(filled, block, features, sums, sources):
    width = block.shape[2]
    vector = pl.BlockSpec(memory_space=pltpu.VMEM)
    shapes = feature_shapes(width) + [jax.ShapeDtypeStruct((16, 2 * width), f32)]
    shapes += [jax.ShapeDtypeStruct((width, width), bf16)] * 2 + diagonal_shapes(width)
    return pl.pallas_call(
        functools.partial(next_kernel, sources),
        out_shape=shapes,
        in_specs=[vector] * 6,
        out_specs=[vector] * len(shapes),
        scratch_shapes=stage_scratch(width),
        compiler_params=pltpu.CompilerParams(vmem_limit_bytes=20 << 20),
        name="next",
    )(filled, block, *features, sums)


def square_tiles(key, query, width):
    half = width // 2
    return [(key + part, half, query, width, width) for part in (0, half)]


def late_tiles(count, width):
    tiles, late = [], range(2, count)
    for query in late:
        for key in range(2):
            tiles += square_tiles(key * width, query * width, width)
    for query in late:
        for key in range(2, query):
            tiles += square_tiles(key * width, query * width, width)
    for query in late:
        tiles += diagonal_tiles(query * width, width)
    return tiles


def scored(weight, place, sums):
    vector, live = row_of(place) < 3, weight > 0.0
    density_sum = jnp.where(live, sums[3:4], 1.0)
    pull = place * density_sum - sums
    return jnp.where(vector & live, pull / (-SCALE * EPS * EPS * density_sum), 0.0)


def whole_cell(blocks, live):
    weight = jnp.concatenate(
        [jnp.where(on, block[0, 3:4], 0.0) for on, block in zip(live, blocks)], axis=1
    )
    whole = jnp.concatenate([widened(block) for block in blocks], axis=1)
    vector = row_of(whole) < 3
    parts = grid_parts(jnp.where(vector, whole * SCALE, 0.0))
    place = parts[0] + parts[1] + parts[2]
    middle = jnp.sum(place * weight, axis=1, keepdims=True)
    middle = middle / jnp.sum(weight, axis=1, keepdims=True)
    return weight, place, jnp.where(vector, place - middle, 0.0)


def drift_of(total, centred, score, weight, total_slots):
    drift = drift_sum(total, centred, score)
    live = (row_of(drift) < 3) & (weight > 0.0)
    return jnp.where(live, drift * (1.0 / (SCALE * SCALE * SCALE * total_slots)), 0.0)


def finish(blocks, score, drifts, outs):
    scores_out, drift_out, start_out, speed_out = outs
    width = blocks[0].shape[2]
    square = functools.reduce(jnp.maximum, [rows_sum(drift * drift) for drift in drifts])
    largest = jnp.max(square, axis=1, keepdims=True)
    speed_out[...] = jnp.broadcast_to(jnp.sqrt(largest), speed_out.shape)
    scores_out[...] = score
    for part in range(width // 128):
        lanes = slice(part * 128, part * 128 + 128)
        for axis in range(3):
            drift_out[axis, part : part + 1, :] = drifts[0][axis : axis + 1, lanes]
            start_out[axis, part : part + 1, :] = blocks[0][0, axis : axis + 1, lanes]


def sweep_kernel(sources, *refs):
    count = len(sources)
    filled, blocks, refs = refs[0], refs[1 : count + 1], list(refs[count + 1 :])
    own, following, refs = refs[:5], refs[5:13], refs[13:]
    outs, (key_ref, query_ref, moment_ref, sums_ref, totals_ref), refs = (
        refs[:4], refs[4:9], refs[9:]
    )
    flux_refs, refs = refs[:count], refs[count:]
    width = blocks[0].shape[2]
    half = 2 * width
    split_refs, refs = refs[:2], refs[2:]
    exponent_refs, distance_refs = refs[: len(refs) // 2], refs[len(refs) // 2 :]

    live = [lanes_of(owner_of(source), width) < filled[...] for source in sources]
    late = range(2, count)
    for index in late:
        _, _, key, query, moment = prepared(widened(blocks[index]), live[index])
        lanes = pl.ds((index - 2) * width, width)
        key_ref[lanes, :] = key
        query_ref[:, lanes] = query
        moment_ref[:, lanes] = moment
    weight, place, centred = whole_cell(blocks, live)
    lanes = [pl.ds((index - 2) * width, width) for index in late]
    keys = [own[0], following[0]] + [key_ref.at[lane, :] for lane in lanes]
    queries = [own[1], following[1]] + [query_ref.at[:, lane] for lane in lanes]
    moments = [own[2], following[2]] + [moment_ref.at[:, lane] for lane in lanes]
    exponent = exponent_of(looked_up(keys, width, 0), looked_up(queries, width, 1))

    sums_ref[:, 0:half] = following[3][...]
    sums_ref[:, half:] = jnp.zeros_like(sums_ref[:, half:])
    tiles = late_tiles(count, width)
    totals_ref[...] = jnp.zeros_like(totals_ref)
    lanes = [slice(index * width, index * width + width) for index in range(count)]
    scores = [None] * count
    fluxes = looked_up(flux_refs, width, 1)

    def score_blocks(*indices):
        for index in indices:
            at = lanes[index]
            scores[index] = scored(weight[:, at], place[:, at], joined(sums_ref[:, at]))
            flux_refs[index][...] = drift_rows(weight[:, at], centred[:, at], scores[index])

    mixed = sum(tile[0] < half for tile in tiles)

    def after(index):
        if index == mixed - 1:
            score_blocks(0, 1)

    stage(
        tiles, exponent, looked_up(moments, width, 1), sums_ref, exponent_refs, split_refs, None,
        after,
    )
    early = diagonal_tiles(0, width) + square_tiles(width, 0, width)
    early += diagonal_tiles(width, width)
    for tile, distances in zip(early, own[3:5] + following[4:8]):
        for job in add_distances(tile, distances, fluxes, totals_ref):
            job()
    score_blocks(*range(2, count))

    total_slots = count * width
    drifts = [None] * count

    def drift_block(index):
        at = lanes[index]
        drifts[index] = drift_of(
            totals_ref[:, at], centred[:, at], scores[index], weight[:, at], total_slots
        )

    turns = []
    for index in range(mixed):
        split_distances(exponent_refs[index], distance_refs[index])
        rows, columns = add_distances(tiles[index], distance_refs[index], fluxes, totals_ref)
        rows()
        turns.append((tiles[index][0], columns))
    for index in range(2):
        for key, columns in turns:
            if key // width == index:
                columns()
        drift_block(index)
    for index in range(mixed, len(tiles)):
        split_distances(exponent_refs[index], distance_refs[index])
        for job in add_distances(tiles[index], distance_refs[index], fluxes, totals_ref):
            job()
    for index in range(2, count):
        drift_block(index)
    finish(blocks, scores[0], drifts, outs)


def sweep_shapes(width, copies):
    parts = jax.ShapeDtypeStruct((3, width // 128, 128), f32)
    speeds = jax.ShapeDtypeStruct((copies, 128), f32)
    return [jax.ShapeDtypeStruct((8, width), f32), parts, parts, speeds]


def sweep(filled, blocks, sources):
    count, width = len(blocks), blocks[0].shape[2]
    slots, late = count * width, (count - 2) * width
    own = own_part(filled, blocks[0])
    following = next_part(filled, blocks[1], own[:3], own[3], sources[1])
    early = [*own[:3], *own[4:], *following]
    vector = pl.BlockSpec(memory_space=pltpu.VMEM)
    distances = [pltpu.VMEM((2 * tile[1], tile[3]), bf16) for tile in late_tiles(count, width)]
    return pl.pallas_call(
        functools.partial(sweep_kernel, sources),
        out_shape=sweep_shapes(width, 1),
        in_specs=[vector] * (1 + count + len(early)),
        out_specs=[vector] * 4,
        scratch_shapes=[
            pltpu.VMEM((late, DISTANCE_ROWS), bf16),
            pltpu.VMEM((DISTANCE_ROWS, late), bf16),
            pltpu.VMEM((16, late), bf16),
            pltpu.VMEM((16, slots), f32),
            pltpu.VMEM((DRIFT_ROWS // 2, slots), f32),
        ]
        + [pltpu.VMEM((DRIFT_ROWS, width), bf16)] * count
        + [pltpu.VMEM((width, width), bf16)] * 2
        + [pltpu.VMEM((tile[1], tile[3]), f32) for tile in late_tiles(count, width)]
        + distances,
        compiler_params=pltpu.CompilerParams(vmem_limit_bytes=24 << 20),
        name="sweep",
    )(filled, *blocks, *early)


def long_kernel(sources, filled, *refs):
    count = len(sources)
    blocks, outs, refs = refs[:count], refs[count : count + 4], refs[count + 4 :]
    key_ref, query_ref, moment_ref, flux_ref, sums_ref, totals_ref, exponent_ref, split_ref = refs
    width = blocks[0].shape[2]
    live = [lanes_of(owner_of(source), width) < filled[...] for source in sources]
    for index, (block, on) in enumerate(zip(blocks, live)):
        _, _, key, query, moment = prepared(widened(block), on)
        lanes = pl.ds(index * width, width)
        key_ref[lanes, :] = key
        query_ref[:, lanes] = query
        moment_ref[:, lanes] = moment
    weight, place, centred = whole_cell(blocks, live)
    sums_ref[...] = jnp.zeros_like(sums_ref)
    totals_ref[...] = jnp.zeros_like(totals_ref)

    def block_tile(key, query, both):
        start, first = (pl.multiple_of(block * width, width) for block in (key, query))
        return (start, width, first, width, width if both else 0)

    def fill(tile):
        key, keys, query, queries, _ = tile
        exponent_ref[...] = product(key_ref[pl.ds(key, keys), :], query_ref[:, pl.ds(query, queries)])

    def blobs(key, query, both):
        tile = block_tile(key, query, both)
        fill(tile)
        split_blobs(exponent_ref, split_ref)
        add_blobs(tile, split_ref, lambda at, size: moment_ref[:, pl.ds(at, size)], sums_ref)

    @pl.loop(0, count)
    def _(query):
        blobs(query, query, False)

        @pl.loop(query + 1, count)
        def _(key):
            blobs(key, query, True)

    score = scored(weight, place, joined(sums_ref[...]))
    flux_ref[...] = drift_rows(weight, centred, score)

    @pl.loop(0, count)
    def _(key):
        tile = block_tile(key, 0, False)
        fill(tile)
        split_distances(exponent_ref, split_ref)
        for job in add_distances(
            tile, split_ref, lambda at, size: flux_ref[:, pl.ds(at, size)], totals_ref
        ):
            job()

    own = slice(0, width)
    drift = drift_of(
        totals_ref[...], centred[:, own], score[:, own], weight[:, own], count * width
    )
    finish(blocks, score[:, own], [drift], outs)


def long_sweep(filled, blocks, sources, copies):
    count, width = len(blocks), blocks[0].shape[2]
    slots = count * width
    vector = pl.BlockSpec(memory_space=pltpu.VMEM)
    return pl.pallas_call(
        functools.partial(long_kernel, sources),
        out_shape=sweep_shapes(width, copies),
        in_specs=[vector] * (1 + count),
        out_specs=[vector] * 4,
        scratch_shapes=[
            pltpu.VMEM((slots, DISTANCE_ROWS), bf16),
            pltpu.VMEM((DISTANCE_ROWS, slots), bf16),
            pltpu.VMEM((16, slots), bf16),
            pltpu.VMEM((DRIFT_ROWS, slots), bf16),
            pltpu.VMEM((16, slots), f32),
            pltpu.VMEM((DRIFT_ROWS // 2, width), f32),
            pltpu.VMEM((width, width), f32),
            pltpu.VMEM((2 * width, width), bf16),
        ],
        compiler_params=pltpu.CompilerParams(vmem_limit_bytes=(16 << 20) + slots * 2688),
        name="sweep",
    )(filled, *blocks)


def swapped(value, axis, step):
    pairs = [(i, i ^ step) for i in range(lax.axis_size(axis))]
    return lax.ppermute(value, axis, pairs)


def bits(size):
    return [1 << bit for bit in range(size.bit_length() - 1)]


ROUNDS = ((2, 3, 1, 0), (3, 2, 0, 1), (1, 0, 3, 2))


def gathered(block):
    size = lax.axis_size("sharers")
    if size == len(ROUNDS) + 1:
        blocks, sources = [block], [tuple(range(size))]
        for targets in ROUNDS:
            blocks.append(lax.ppermute(block, "sharers", list(enumerate(targets))))
            sources.append(tuple(targets.index(i) for i in range(size)))
        return blocks, sources
    for step in bits(size):
        block = jnp.concatenate([block, swapped(block, "sharers", step)], axis=0)
    sources = [tuple(i ^ step for i in range(size)) for step in range(size)]
    return [block[i : i + 1] for i in range(size)], sources


def local(velocities, weights, counts):
    filled = counts.reshape(1, 1)
    blocks, sources = gathered(jnp.concatenate([velocities, weights[:, None]], axis=1))
    if len(blocks) == len(ROUNDS) + 1:
        scores, drift, start, speeds = sweep(filled, blocks, sources)
        for step in bits(lax.axis_size("cells")):
            speeds = jnp.maximum(speeds, swapped(speeds, "cells", 2 * step - 1))
        largest = speeds
    else:
        axes = ("cells", "sharers")
        scores, drift, start, speeds = long_sweep(filled, blocks, sources, lax.axis_size(axes))
        largest = jnp.max(lax.all_to_all(speeds[:, None], axes, 0, 0, tiled=True), axis=0)
    time_step = 0.5 / (largest + 1e-06)
    moved = start + time_step[None] * drift
    return moved.reshape(velocities.shape), scores[None, 0:3]


def solution(mesh):
    in_specs = (
        P(("groups", "cells"), None, "sharers"),
        P(("groups", "cells"), "sharers"),
        P(("groups", "cells")),
    )
    out_specs = (P(("groups", "cells"), None, "sharers"), P(("groups", "cells"), None, "sharers"))
    return jax.shard_map(local, mesh=mesh, in_specs=in_specs, out_specs=out_specs, check_vma=False)
```

```python
import functools
import functools
import math

import jax
import jax.numpy as jnp
from jax import lax
from jax.experimental import pallas as pl
from jax.experimental.pallas import tpu as pltpu
from jax.sharding import PartitionSpec as P

EPS = 0.35
SCALE = math.sqrt(math.log2(math.e) / (2.0 * EPS * EPS))
GRID = 4.0
TINY = 1e-30
GROUP = 16
DISTANCE_ROWS = 96
DRIFT_ROWS = 64
bf16, f32 = jnp.bfloat16, jnp.float32


def round_bf16(value):
    return value.astype(bf16).astype(f32)


def pieces(value, count):
    parts = []
    for _ in range(count):
        part = round_bf16(value)
        parts.append(part)
        value = value - part
    return parts


def row_of(value):
    return lax.broadcasted_iota(jnp.int32, value.shape, 0)


def rows_sum(value):
    return jnp.sum(value, axis=0, keepdims=True)


def stacked(groups):
    if len(groups) % 2:
        groups = groups + [jnp.zeros_like(groups[0])]
    return jnp.concatenate(groups, axis=0).astype(bf16)


def scalar_groups(value, like):
    row = row_of(like)
    first, second, third = pieces(value, 3)
    low = jnp.where(row == 0, first, jnp.where(row == 1, second, jnp.where(row == 2, third, 0.0)))
    high = jnp.where(row == 3, first, jnp.where(row == 4, second, jnp.where(row == 5, third, 0.0)))
    ones_low, ones_high = row < 3, (row >= 3) & (row < 6)
    return jnp.where(ones_high, 1.0, low), jnp.where(ones_low, 1.0, high)


def grid_parts(place):
    coarse = jnp.floor(place * GRID + 0.5) * (1.0 / GRID)
    return [coarse] + pieces(place - coarse, 2)


def distance_features(parts):
    coarse, fine, rest = parts
    minor = fine + rest
    query_norm, key_norm = scalar_groups(-rows_sum(coarse * coarse), coarse)
    query_less, key_less = scalar_groups(-rows_sum(minor * (2.0 * coarse + minor)), coarse)
    key = [coarse, key_norm, coarse, coarse, fine, rest, key_less, fine, fine, rest, rest]
    coarse, fine, rest = coarse * 2.0, fine * 2.0, rest * 2.0
    query = [coarse, query_norm, fine, rest, coarse, coarse, query_less, fine, rest, fine, rest]
    return stacked(key), stacked(query)


def weighted_rows(weight, value):
    row = row_of(value)
    whole = jnp.where(row < 3, value, jnp.where(row == 3, 1.0, 0.0)) * weight
    first, second, third = pieces(whole, 3)
    return stacked([first, second + pltpu.roll(third, 4, 0)])


def product(left, right):
    return jnp.dot(left, right, preferred_element_type=f32)


def store_split(ref, rows, matrix):
    half = ref.shape[0] // 2
    upper = matrix.astype(bf16)
    ref[rows, :] = upper
    ref[pl.ds(half + rows.start, rows.size), :] = (matrix - upper.astype(f32)).astype(bf16)


def sum_rows(left, ref):
    return product(jnp.concatenate([left, left], axis=1), ref[...])


def sum_columns(left, ref):
    both = lax.dot_general(left, ref[...], (((1,), (1,)), ((), ())), preferred_element_type=f32)
    half = ref.shape[0] // 2
    return both[:, :half] + both[:, half:]


def sum_rows_less(left, ref):
    half = ref.shape[0] // 2
    both = product(left, ref[:half, :])
    few = left.shape[0] // 2
    return both[:few] + product(left[:few], ref[half:, :]), both[few:]


def sum_columns_less(left, ref):
    half, few = ref.shape[0] // 2, left.shape[0] // 2
    turned = (((1,), (1,)), ((), ()))
    both = lax.dot_general(left, ref[:half, :], turned, preferred_element_type=f32)
    less = lax.dot_general(left[:few], ref[half:, :], turned, preferred_element_type=f32)
    return both[:few] + less, both[few:]


def joined(total):
    upper, lower = total[0:8], total[8:16]
    return upper + lower + pltpu.roll(lower, 4, 0)


def drift_rows(weight, place, score):
    row = row_of(place)
    base = place + jnp.where(row == 3, 1.0, 0.0) + pltpu.roll(score, 4, 0)
    cubic = rows_sum(place * place) * score - rows_sum(place * score) * place
    groups = [weight * base]
    for i in range(3):
        here = slice(i, i + 1)
        groups.append(weight * jnp.where(row == 3, cubic[here], place[here] * base))
    return stacked(sum(map(list, zip(*[pieces(group, 2) for group in groups])), []))


def drift_sum(total, place, score):
    row = row_of(place)
    first, *rest = [total[8 * i : 8 * i + 8] for i in range(4)]
    turned = [pltpu.roll(group, 4, 0) for group in rest]
    count, scores = first[3:4], pltpu.roll(first, 4, 0)
    square, both = rows_sum(place * place), rows_sum(place * score)
    trace = rest[0][0:1] + rest[1][1:2] + rest[2][2:3]
    cross = turned[0][0:1] + turned[1][1:2] + turned[2][2:3]
    drift = score * (square * count - 2.0 * rows_sum(place * first) + trace) - square * scores
    drift += both * first + place * (
        rows_sum(place * scores) + rows_sum(score * first) - both * count - cross
    )
    ends = []
    for i in range(3):
        here = slice(i, i + 1)
        drift += 2.0 * place[here] * turned[i] - score[here] * rest[i]
        ends.append(rows_sum(place * turned[i]) + rest[i][3:4])
    return drift - jnp.where(row == 0, ends[0], jnp.where(row == 1, ends[1], ends[2]))


def widened(block):
    return jnp.concatenate([block[0], jnp.zeros_like(block[0])], axis=0)


def prepared(whole, live):
    weight = jnp.where(live, whole[3:4], 0.0)
    parts = grid_parts(jnp.where(row_of(whole) < 3, whole * SCALE, 0.0))
    place = parts[0] + parts[1] + parts[2]
    key, query = distance_features(parts)
    return weight, place, key.T, query, weighted_rows(weight, place)


def split_blobs(exponent, split):
    for group in range(0, exponent.shape[0], GROUP):
        rows = pl.ds(group, GROUP)
        store_split(split, rows, jnp.exp2(exponent[rows, :]))


def split_distances(exponent, split):
    for group in range(0, exponent.shape[0], GROUP):
        rows = pl.ds(group, GROUP)
        negative = jnp.minimum(exponent[rows, :], -TINY)
        store_split(split, rows, negative * lax.rsqrt(-negative))


def diagonal_tiles(start, width):
    half = width // 2
    return [(start, half, start, half, 0), (start + half, half, start, width, half)]


def add_blobs(tile, split, moments, sums_ref):
    key, keys, query, queries, turned = tile
    sums_ref[:, pl.ds(query, queries)] += sum_rows(moments(key, keys), split)
    if turned:
        sums_ref[:, pl.ds(key, keys)] += sum_columns(moments(query, turned), split.at[:, 0:turned])


def add_distances(tile, split, fluxes, totals_ref):
    key, keys, query, queries, turned = tile

    def rows():
        upper, lower = sum_rows_less(fluxes(key, keys), split)
        totals_ref[:, pl.ds(query, queries)] += upper + lower

    def columns():
        upper, lower = sum_columns_less(fluxes(query, turned), split.at[:, 0:turned])
        totals_ref[:, pl.ds(key, keys)] += upper + lower

    return rows, columns if turned else lambda: None


def stage(tiles, exponent, moments, sums_ref, exponent_refs, split_refs, distance_refs,
          after=lambda index: None):
    def buffer(index):
        _, keys, _, queries, _ = tiles[index]
        return exponent_refs[index % len(exponent_refs)].at[0:keys, 0:queries]

    buffer(0)[...] = exponent(tiles[0])
    for index, tile in enumerate(tiles):
        if index + 1 < len(tiles):
            buffer(index + 1)[...] = exponent(tiles[index + 1])
        split = split_refs[index % 2].at[0 : 2 * tile[1], 0 : tile[3]]
        split_blobs(buffer(index), split)
        add_blobs(tile, split, moments, sums_ref)
        if distance_refs is not None:
            split_distances(buffer(index), distance_refs[index])
        after(index)


def looked_up(refs, width, axis):
    def read(start, size):
        at = pl.ds(start % width, size)
        ref = refs[start // width]
        return ref[at, :] if axis == 0 else ref[:, at]

    return read


def exponent_of(keys, queries):
    return lambda tile: product(keys(tile[0], tile[1]), queries(tile[2], tile[3]))


def lanes_of(source, width):
    return lax.broadcasted_iota(jnp.int32, (1, width), 1) + source * width


def owner_of(sources):
    here = lax.axis_index("sharers")
    return sum(jnp.where(here == i, source, 0) for i, source in enumerate(sources))


def own_kernel(filled, block, key_out, query_out, moment_out, sums_out, first_out, second_out,
               *scratch):
    width = block.shape[2]
    live = lanes_of(lax.axis_index("sharers"), width) < filled[...]
    _, _, key, query, moment = prepared(widened(block), live)
    key_out[...] = key
    query_out[...] = query
    moment_out[...] = moment
    sums_out[...] = jnp.zeros_like(sums_out)
    exponent = exponent_of(looked_up([key_out], width, 0), looked_up([query_out], width, 1))
    moments = looked_up([moment_out], width, 1)
    tiles = diagonal_tiles(0, width)
    stage(tiles, exponent, moments, sums_out, scratch[:2], scratch[2:], (first_out, second_out))


def next_kernel(sources, filled, block, own_key, own_query, own_moment, own_sums, key_out,
                query_out, moment_out, sums_out, *refs):
    width = block.shape[2]
    live = lanes_of(owner_of(sources), width) < filled[...]
    _, _, key, query, moment = prepared(widened(block), live)
    key_out[...] = key
    query_out[...] = query
    moment_out[...] = moment
    sums_out[:, 0:width] = own_sums[...]
    sums_out[:, width:] = jnp.zeros_like(own_sums)
    exponent = exponent_of(
        looked_up([own_key, key_out], width, 0), looked_up([own_query, query_out], width, 1)
    )
    moments = looked_up([own_moment, moment_out], width, 1)
    tiles = square_tiles(width, 0, width) + diagonal_tiles(width, width)
    distances, scratch = refs[: len(tiles)], refs[len(tiles) :]
    stage(tiles, exponent, moments, sums_out, scratch[:2], scratch[2:], distances)


def feature_shapes(width):
    return [
        jax.ShapeDtypeStruct((width, DISTANCE_ROWS), bf16),
        jax.ShapeDtypeStruct((DISTANCE_ROWS, width), bf16),
        jax.ShapeDtypeStruct((16, width), bf16),
    ]


def diagonal_shapes(width):
    half = width // 2
    return [
        jax.ShapeDtypeStruct((2 * half, half), bf16),
        jax.ShapeDtypeStruct((2 * half, width), bf16),
    ]


def stage_scratch(width):
    half = width // 2
    return [pltpu.VMEM((half, width), f32)] * 2 + [pltpu.VMEM((width, width), bf16)] * 2


def own_part(filled, block):
    width = block.shape[2]
    vector = pl.BlockSpec(memory_space=pltpu.VMEM)
    shapes = feature_shapes(width) + [jax.ShapeDtypeStruct((16, width), f32)] + diagonal_shapes(width)
    return pl.pallas_call(
        own_kernel,
        out_shape=shapes,
        in_specs=[vector] * 2,
        out_specs=[vector] * len(shapes),
        scratch_shapes=stage_scratch(width),
        compiler_params=pltpu.CompilerParams(vmem_limit_bytes=16 << 20),
        name="own",
    )(filled, block)


def next_part(filled, block, features, sums, sources):
    width = block.shape[2]
    vector = pl.BlockSpec(memory_space=pltpu.VMEM)
    shapes = feature_shapes(width) + [jax.ShapeDtypeStruct((16, 2 * width), f32)]
    shapes += [jax.ShapeDtypeStruct((width, width), bf16)] * 2 + diagonal_shapes(width)
    return pl.pallas_call(
        functools.partial(next_kernel, sources),
        out_shape=shapes,
        in_specs=[vector] * 6,
        out_specs=[vector] * len(shapes),
        scratch_shapes=stage_scratch(width),
        compiler_params=pltpu.CompilerParams(vmem_limit_bytes=20 << 20),
        name="next",
    )(filled, block, *features, sums)


def square_tiles(key, query, width):
    half = width // 2
    return [(key + part, half, query, width, width) for part in (0, half)]


def late_tiles(count, width):
    tiles, late = [], range(2, count)
    for query in late:
        for key in range(2):
            tiles += square_tiles(key * width, query * width, width)
    for query in late:
        for key in range(2, query):
            tiles += square_tiles(key * width, query * width, width)
    for query in late:
        tiles += diagonal_tiles(query * width, width)
    return tiles


def scored(weight, place, sums):
    vector, live = row_of(place) < 3, weight > 0.0
    density_sum = jnp.where(live, sums[3:4], 1.0)
    pull = place * density_sum - sums
    return jnp.where(vector & live, pull / (-SCALE * EPS * EPS * density_sum), 0.0)


def whole_cell(blocks, live):
    weight = jnp.concatenate(
        [jnp.where(on, block[0, 3:4], 0.0) for on, block in zip(live, blocks)], axis=1
    )
    whole = jnp.concatenate([widened(block) for block in blocks], axis=1)
    vector = row_of(whole) < 3
    parts = grid_parts(jnp.where(vector, whole * SCALE, 0.0))
    place = parts[0] + parts[1] + parts[2]
    middle = jnp.sum(place * weight, axis=1, keepdims=True)
    middle = middle / jnp.sum(weight, axis=1, keepdims=True)
    return weight, place, jnp.where(vector, place - middle, 0.0)


def drift_of(total, centred, score, weight, total_slots):
    drift = drift_sum(total, centred, score)
    live = (row_of(drift) < 3) & (weight > 0.0)
    return jnp.where(live, drift * (1.0 / (SCALE * SCALE * SCALE * total_slots)), 0.0)


def finish(blocks, score, drifts, outs):
    scores_out, drift_out, start_out, speed_out = outs
    width = blocks[0].shape[2]
    square = functools.reduce(jnp.maximum, [rows_sum(drift * drift) for drift in drifts])
    largest = jnp.max(square, axis=1, keepdims=True)
    speed_out[...] = jnp.broadcast_to(jnp.sqrt(largest), speed_out.shape)
    scores_out[...] = score
    for part in range(width // 128):
        lanes = slice(part * 128, part * 128 + 128)
        for axis in range(3):
            drift_out[axis, part : part + 1, :] = drifts[0][axis : axis + 1, lanes]
            start_out[axis, part : part + 1, :] = blocks[0][0, axis : axis + 1, lanes]


def sweep_kernel(sources, *refs):
    count = len(sources)
    filled, blocks, refs = refs[0], refs[1 : count + 1], list(refs[count + 1 :])
    own, following, refs = refs[:5], refs[5:13], refs[13:]
    outs, (key_ref, query_ref, moment_ref, sums_ref, totals_ref), refs = (
        refs[:4], refs[4:9], refs[9:]
    )
    flux_refs, refs = refs[:count], refs[count:]
    width = blocks[0].shape[2]
    half = 2 * width
    split_refs, refs = refs[:2], refs[2:]
    exponent_refs, distance_refs = refs[: len(refs) // 2], refs[len(refs) // 2 :]

    live = [lanes_of(owner_of(source), width) < filled[...] for source in sources]
    late = range(2, count)
    for index in late:
        _, _, key, query, moment = prepared(widened(blocks[index]), live[index])
        lanes = pl.ds((index - 2) * width, width)
        key_ref[lanes, :] = key
        query_ref[:, lanes] = query
        moment_ref[:, lanes] = moment
    weight, place, centred = whole_cell(blocks, live)
    lanes = [pl.ds((index - 2) * width, width) for index in late]
    keys = [own[0], following[0]] + [key_ref.at[lane, :] for lane in lanes]
    queries = [own[1], following[1]] + [query_ref.at[:, lane] for lane in lanes]
    moments = [own[2], following[2]] + [moment_ref.at[:, lane] for lane in lanes]
    exponent = exponent_of(looked_up(keys, width, 0), looked_up(queries, width, 1))

    sums_ref[:, 0:half] = following[3][...]
    sums_ref[:, half:] = jnp.zeros_like(sums_ref[:, half:])
    tiles = late_tiles(count, width)
    totals_ref[...] = jnp.zeros_like(totals_ref)
    lanes = [slice(index * width, index * width + width) for index in range(count)]
    scores = [None] * count
    fluxes = looked_up(flux_refs, width, 1)

    def score_blocks(*indices):
        for index in indices:
            at = lanes[index]
            scores[index] = scored(weight[:, at], place[:, at], joined(sums_ref[:, at]))
            flux_refs[index][...] = drift_rows(weight[:, at], centred[:, at], scores[index])

    mixed = sum(tile[0] < half for tile in tiles)

    def after(index):
        if index == mixed - 1:
            score_blocks(0, 1)

    stage(
        tiles, exponent, looked_up(moments, width, 1), sums_ref, exponent_refs, split_refs, None,
        after,
    )
    early = diagonal_tiles(0, width) + square_tiles(width, 0, width)
    early += diagonal_tiles(width, width)
    for tile, distances in zip(early, own[3:5] + following[4:8]):
        for job in add_distances(tile, distances, fluxes, totals_ref):
            job()
    score_blocks(*range(2, count))

    total_slots = count * width
    drifts = [None] * count

    def drift_block(index):
        at = lanes[index]
        drifts[index] = drift_of(
            totals_ref[:, at], centred[:, at], scores[index], weight[:, at], total_slots
        )

    turns = []
    for index in range(mixed):
        split_distances(exponent_refs[index], distance_refs[index])
        rows, columns = add_distances(tiles[index], distance_refs[index], fluxes, totals_ref)
        rows()
        turns.append((tiles[index][0], columns))
    for index in range(2):
        for key, columns in turns:
            if key // width == index:
                columns()
        drift_block(index)
    for index in range(mixed, len(tiles)):
        split_distances(exponent_refs[index], distance_refs[index])
        for job in add_distances(tiles[index], distance_refs[index], fluxes, totals_ref):
            job()
    for index in range(2, count):
        drift_block(index)
    finish(blocks, scores[0], drifts, outs)


def sweep_shapes(width, copies):
    parts = jax.ShapeDtypeStruct((3, width // 128, 128), f32)
    speeds = jax.ShapeDtypeStruct((copies, 128), f32)
    return [jax.ShapeDtypeStruct((8, width), f32), parts, parts, speeds]


def sweep(filled, blocks, sources):
    count, width = len(blocks), blocks[0].shape[2]
    slots, late = count * width, (count - 2) * width
    own = own_part(filled, blocks[0])
    following = next_part(filled, blocks[1], own[:3], own[3], sources[1])
    early = [*own[:3], *own[4:], *following]
    vector = pl.BlockSpec(memory_space=pltpu.VMEM)
    distances = [pltpu.VMEM((2 * tile[1], tile[3]), bf16) for tile in late_tiles(count, width)]
    return pl.pallas_call(
        functools.partial(sweep_kernel, sources),
        out_shape=sweep_shapes(width, 1),
        in_specs=[vector] * (1 + count + len(early)),
        out_specs=[vector] * 4,
        scratch_shapes=[
            pltpu.VMEM((late, DISTANCE_ROWS), bf16),
            pltpu.VMEM((DISTANCE_ROWS, late), bf16),
            pltpu.VMEM((16, late), bf16),
            pltpu.VMEM((16, slots), f32),
            pltpu.VMEM((DRIFT_ROWS // 2, slots), f32),
        ]
        + [pltpu.VMEM((DRIFT_ROWS, width), bf16)] * count
        + [pltpu.VMEM((width, width), bf16)] * 2
        + [pltpu.VMEM((tile[1], tile[3]), f32) for tile in late_tiles(count, width)]
        + distances,
        compiler_params=pltpu.CompilerParams(vmem_limit_bytes=24 << 20),
        name="sweep",
    )(filled, *blocks, *early)


def long_kernel(sources, filled, *refs):
    count = len(sources)
    blocks, outs, refs = refs[:count], refs[count : count + 4], refs[count + 4 :]
    key_ref, query_ref, moment_ref, flux_ref, sums_ref, totals_ref, exponent_ref, split_ref = refs
    width = blocks[0].shape[2]
    live = [lanes_of(owner_of(source), width) < filled[...] for source in sources]
    for index, (block, on) in enumerate(zip(blocks, live)):
        _, _, key, query, moment = prepared(widened(block), on)
        lanes = pl.ds(index * width, width)
        key_ref[lanes, :] = key
        query_ref[:, lanes] = query
        moment_ref[:, lanes] = moment
    weight, place, centred = whole_cell(blocks, live)
    sums_ref[...] = jnp.zeros_like(sums_ref)
    totals_ref[...] = jnp.zeros_like(totals_ref)

    def block_tile(key, query, both):
        start, first = (pl.multiple_of(block * width, width) for block in (key, query))
        return (start, width, first, width, width if both else 0)

    def fill(tile):
        key, keys, query, queries, _ = tile
        exponent_ref[...] = product(key_ref[pl.ds(key, keys), :], query_ref[:, pl.ds(query, queries)])

    def blobs(key, query, both):
        tile = block_tile(key, query, both)
        fill(tile)
        split_blobs(exponent_ref, split_ref)
        add_blobs(tile, split_ref, lambda at, size: moment_ref[:, pl.ds(at, size)], sums_ref)

    @pl.loop(0, count)
    def _(query):
        blobs(query, query, False)

        @pl.loop(query + 1, count)
        def _(key):
            blobs(key, query, True)

    score = scored(weight, place, joined(sums_ref[...]))
    flux_ref[...] = drift_rows(weight, centred, score)

    @pl.loop(0, count)
    def _(key):
        tile = block_tile(key, 0, False)
        fill(tile)
        split_distances(exponent_ref, split_ref)
        for job in add_distances(
            tile, split_ref, lambda at, size: flux_ref[:, pl.ds(at, size)], totals_ref
        ):
            job()

    own = slice(0, width)
    drift = drift_of(
        totals_ref[...], centred[:, own], score[:, own], weight[:, own], count * width
    )
    finish(blocks, score[:, own], [drift], outs)


def long_sweep(filled, blocks, sources, copies):
    count, width = len(blocks), blocks[0].shape[2]
    slots = count * width
    vector = pl.BlockSpec(memory_space=pltpu.VMEM)
    return pl.pallas_call(
        functools.partial(long_kernel, sources),
        out_shape=sweep_shapes(width, copies),
        in_specs=[vector] * (1 + count),
        out_specs=[vector] * 4,
        scratch_shapes=[
            pltpu.VMEM((slots, DISTANCE_ROWS), bf16),
            pltpu.VMEM((DISTANCE_ROWS, slots), bf16),
            pltpu.VMEM((16, slots), bf16),
            pltpu.VMEM((DRIFT_ROWS, slots), bf16),
            pltpu.VMEM((16, slots), f32),
            pltpu.VMEM((DRIFT_ROWS // 2, width), f32),
            pltpu.VMEM((width, width), f32),
            pltpu.VMEM((2 * width, width), bf16),
        ],
        compiler_params=pltpu.CompilerParams(vmem_limit_bytes=(16 << 20) + slots * 2688),
        name="sweep",
    )(filled, *blocks)


def swapped(value, axis, step):
    pairs = [(i, i ^ step) for i in range(lax.axis_size(axis))]
    return lax.ppermute(value, axis, pairs)


def bits(size):
    return [1 << bit for bit in range(size.bit_length() - 1)]


ROUNDS = ((2, 3, 1, 0), (3, 2, 0, 1), (1, 0, 3, 2))


def gathered(block):
    size = lax.axis_size("sharers")
    if size == len(ROUNDS) + 1:
        blocks, sources = [block], [tuple(range(size))]
        for targets in ROUNDS:
            blocks.append(lax.ppermute(block, "sharers", list(enumerate(targets))))
            sources.append(tuple(targets.index(i) for i in range(size)))
        return blocks, sources
    for step in bits(size):
        block = jnp.concatenate([block, swapped(block, "sharers", step)], axis=0)
    sources = [tuple(i ^ step for i in range(size)) for step in range(size)]
    return [block[i : i + 1] for i in range(size)], sources


def local(velocities, weights, counts):
    filled = counts.reshape(1, 1)
    blocks, sources = gathered(jnp.concatenate([velocities, weights[:, None]], axis=1))
    if len(blocks) == len(ROUNDS) + 1:
        scores, drift, start, speeds = sweep(filled, blocks, sources)
        for step in bits(lax.axis_size("cells")):
            speeds = jnp.maximum(speeds, swapped(speeds, "cells", 2 * step - 1))
        largest = speeds
    else:
        axes = ("cells", "sharers")
        scores, drift, start, speeds = long_sweep(filled, blocks, sources, lax.axis_size(axes))
        largest = jnp.max(lax.all_to_all(speeds[:, None], axes, 0, 0, tiled=True), axis=0)
    time_step = 0.5 / (largest + 1e-06)
    moved = start + time_step[None] * drift
    return moved.reshape(velocities.shape), scores[None, 0:3]


def solution(mesh):
    in_specs = (
        P(("groups", "cells"), None, "sharers"),
        P(("groups", "cells"), "sharers"),
        P(("groups", "cells")),
    )
    out_specs = (P(("groups", "cells"), None, "sharers"), P(("groups", "cells"), None, "sharers"))
    return jax.shard_map(local, mesh=mesh, in_specs=in_specs, out_specs=out_specs, check_vma=False)
```
